32 devices in a mesh: dp: 16 (over z, x, core), seq: 2 (over y).
Axes of the slice: x: 2, y: 2, z: 4, core: 2. Of those that a mesh axis runs over, the one named last changes fastest.
Arguments:
- tokens: bfloat16 [32, 1024, 768], P('dp', 'seq'), may hold values from -6 to 6
- time_embedding: bfloat16 [32, 128], P('dp'), may hold values from -6 to 6
- prefix_length: int32 [32], P('dp'), may hold values from 0 to 511
- suffix_mask: int32 [32, 1024], P('dp', 'seq'), may hold values 0 or 1
- cotangent: bfloat16 [32, 1024, 768], P('dp', 'seq'), may hold values from -6 to 6
- modulation_weight: bfloat16 [4608, 128], replicated, may hold values from -0.5 to 0.5
- modulation_bias: bfloat16 [4608], replicated, may hold values from -3 to 3
- attention_gain: bfloat16 [768], replicated, may hold values from 0.099609375 to 1.8984375
- attention_in: bfloat16 [768, 2304], replicated, may hold values from -0.15625 to 0.15625
- attention_out: bfloat16 [768, 768], replicated, may hold values from -1.75 to 1.75
- feed_gain: bfloat16 [768], replicated, may hold values from 0.099609375 to 1.8984375
- feed_up: bfloat16 [768, 3072], replicated, may hold values from -0.21875 to 0.21875
- feed_up_bias: bfloat16 [3072], replicated, may hold values from -3 to 3
- feed_down: bfloat16 [3072, 768], replicated, may hold values from -0.109375 to 0.109375
- feed_down_bias: bfloat16 [768], replicated, may hold values from -3 to 3
Outputs:
- block_output: bfloat16 [32, 1024, 768], P('dp', 'seq')
- tokens_grad: bfloat16 [32, 1024, 768], P('dp', 'seq')
- time_grad: float32 [32, 128], P('dp')
- modulation_weight_grad: float32 [4608, 128], P('dp')
- modulation_bias_grad: float32 [4608], P('dp')
- attention_gain_grad: float32 [768], P('dp')
- attention_in_grad: float32 [768, 2304], P('dp')
- attention_out_grad: float32 [768, 768], P('dp')
- feed_gain_grad: float32 [768], P('dp')
- feed_up_grad: float32 [768, 3072], P('dp')
- feed_up_bias_grad: float32 [3072], P('dp')
- feed_down_grad: float32 [3072, 768], P('dp')
- feed_down_bias_grad: float32 [768], P('dp')
The draws below stay inside these ranges and needn't reach their ends.
All inputs are finite; a program needn't handle non-finite values. No bound on the sum of `suffix_mask` on one device may be relied on, other than what follows from the above.
Results may differ from the reference program's by a relative error of at most 0.015.
The reference program's roundings to bfloat16 on the way count: a program that leaves them out, or rounds other values in their place, can miss the bound.
Values may be sent and summed in bfloat16 or wider, within the bound.
A program may use at most 256 MiB of HBM per device.

```python
import jax
import jax.numpy as jnp
from jax import lax

D = 768
HEADS = 12
HD = 64
FF = 3072
COND = 128
LENGTH = 1024
SEQS = 32


def set_ends(entries, rng, low, top_value):
    place = [jax.random.randint(jax.random.fold_in(rng, axis), (), 0, length) for axis, length in enumerate(entries.shape)]
    widest = entries.shape.index(max(entries.shape))
    beside = place[:widest] + [(place[widest] + 1) % entries.shape[widest]] + place[widest + 1:]
    return entries.at[tuple(place)].set(low).at[tuple(beside)].set(top_value)


def block_levels(stream_key, shape, cuts, smallest, high):
    def one(axis_at, shards_of):
        heights = jax.random.uniform(jax.random.fold_in(jax.random.fold_in(stream_key, 6), axis_at), (shards_of,), jnp.float32, smallest / len(cuts), high / len(cuts))
        return jnp.repeat(jnp.exp(heights), shape[axis_at] // shards_of).reshape((-1,) + (1,) * (len(shape) - axis_at - 1))

    loudness = one(*cuts[0])
    for cut in cuts[1:]:
        loudness = loudness * one(*cut)
    return loudness


def normal_values(rng, shape, scale, reach, cuts=(), held_as=jnp.bfloat16):
    level = block_levels(rng, shape, cuts, -0.22, 0.18) if cuts else 1.0
    values = jax.random.normal(rng, shape, jnp.float32) * scale * level
    return jnp.minimum(jnp.maximum(values, -reach), reach).astype(held_as)


def setup_inputs(seed: int = 0) -> dict:
    key_list = jax.random.split(jax.random.key(seed), 16)
    tokens = normal_values(key_list[0], (SEQS, LENGTH, D), 1.0, 6.0, ((0, 16), (1, 2)))
    time_embedding = normal_values(key_list[1], (SEQS, COND), 1.0, 6.0, ((0, 16),))
    prefix_length = set_ends(jax.random.randint(key_list[2], (SEQS,), 0, LENGTH // 2), jax.random.fold_in(key_list[2], 1), 0, (LENGTH // 2) - 1).astype(jnp.int32)
    suffix_mask = set_ends((jax.random.randint(key_list[3], (SEQS, LENGTH), 0, 2) < 1).astype(jnp.int32), jax.random.fold_in(key_list[3], 1), 0, 1)
    cotangent = normal_values(key_list[4], (SEQS, LENGTH, D), 1.0, 6.0, ((0, 16), (1, 2)))
    modulation_weight = normal_values(key_list[5], (6 * D, COND), COND ** -0.5, 0.5)
    modulation_bias = normal_values(key_list[6], (6 * D,), 0.5, 3.0)
    attention_gain = jnp.clip(1.0 + 0.18 * jax.random.normal(key_list[7], (D,), jnp.float32), 0.099609375, 1.8984375).astype(jnp.bfloat16)
    attention_in = normal_values(key_list[8], (D, 3 * D), (2 * D) ** -0.5, 0.15625)
    attention_out = normal_values(key_list[9], (D, D), (D // 64) ** -0.5, 1.75)
    feed_gain = jnp.clip(1.0 + 0.18 * jax.random.normal(key_list[10], (D,), jnp.float32), 0.099609375, 1.8984375).astype(jnp.bfloat16)
    feed_up = normal_values(key_list[11], (D, FF), D ** -0.5, 0.21875)
    feed_up_bias = normal_values(key_list[12], (FF,), 0.5, 3.0)
    feed_down = normal_values(key_list[13], (FF, D), FF ** -0.5, 0.109375)
    feed_down_bias = normal_values(key_list[14], (D,), 0.5, 3.0)
    return dict(tokens=tokens, time_embedding=time_embedding, prefix_length=prefix_length, suffix_mask=suffix_mask, cotangent=cotangent, modulation_weight=modulation_weight, modulation_bias=modulation_bias, attention_gain=attention_gain, attention_in=attention_in, attention_out=attention_out, feed_gain=feed_gain, feed_up=feed_up, feed_up_bias=feed_up_bias, feed_down=feed_down, feed_down_bias=feed_down_bias)


@jax.custom_vjp
def low(v):
    return lax.optimization_barrier(v.astype(jnp.bfloat16)).astype(jnp.float32)

@jax.custom_vjp
def low_back(v):
    return v

def low_keep(v):
    return (low(v), None)

def low_pass(kept, grad):
    return (grad,)

def back_keep(v):
    return (v, None)

def back_low(kept, grad):
    return (low(grad),)
low.defvjp(low_keep, low_pass)
low_back.defvjp(back_keep, back_low)
highest = lax.Precision.HIGHEST

def normalize(values):
    centre = values - lax.optimization_barrier(jnp.mean(values, -1, keepdims=True))
    spread = lax.optimization_barrier(jnp.mean(centre * centre, -1, keepdims=True))
    return centre * lax.rsqrt(spread + 1e-05)

def rotate(values, cosine, sines):
    halves = values.shape[-1] // 2
    former = values[..., :halves]
    latter = values[..., halves:]
    cosine = cosine[:, None, :]
    sines = sines[:, None, :]
    return jnp.concatenate([former * cosine - latter * sines, latter * cosine + former * sines], -1)

def attend(query_rows, key_rows, value_rows):
    length = query_rows.shape[0]
    block_rows = min(512, length)
    grouped = query_rows.reshape(length // block_rows, block_rows, query_rows.shape[1], query_rows.shape[2])

    def one_block(query_block):
        scores = low_back(jnp.einsum('qhd,khd->hqk', query_block, key_rows, precision=highest) * 0.125)
        probability = jax.nn.softmax(scores, axis=-1)
        return jnp.einsum('hqk,khd->qhd', low(probability), value_rows, precision=highest)
    result = lax.map(jax.checkpoint(one_block), grouped)
    return result.reshape(query_rows.shape)

def layer(tokens, embedding, modulation_weight, modulation_bias, attention_gain, attention_in, attention_out, feed_gain, feed_up, feed_up_bias, feed_down, feed_down_bias):
    length = tokens.shape[0]
    model_width = tokens.shape[1]
    modulation = jnp.dot(modulation_weight, embedding, precision=highest) + modulation_bias
    shift_one, scale_one, gate_one, shift_two, scale_two, gate_two = jnp.split(modulation, 6)
    first_input = low(normalize(tokens) * attention_gain * (1.0 + scale_one) + shift_one)
    projected = low_back(jnp.dot(first_input, attention_in, precision=highest)).reshape(length, 3, HEADS, HD)
    positions = jnp.arange(length, dtype=jnp.float32)
    inverse = 10000.0 ** (-jnp.arange(HD // 2, dtype=jnp.float32) * 2.0 / HD)
    angles = positions[:, None] * inverse[None, :]
    cosine = jnp.cos(angles)
    sines = jnp.sin(angles)
    query_rows = low_back(low(rotate(projected[:, 0], cosine, sines)))
    key_rows = low_back(low(rotate(projected[:, 1], cosine, sines)))
    value_rows = low_back(low(projected[:, 2]))
    attended = low_back(low(attend(query_rows, key_rows, value_rows).reshape(length, model_width)))
    branch_one = low_back(jnp.dot(attended, attention_out, precision=highest))
    middle = tokens + gate_one * branch_one
    second_input = low(normalize(middle) * feed_gain * (1.0 + scale_two) + shift_two)
    hidden = low_back(jnp.dot(second_input, feed_up, precision=highest) + feed_up_bias)
    activated = low(jax.nn.gelu(hidden, approximate=True))
    branch_two = low_back(jnp.dot(activated, feed_down, precision=highest) + feed_down_bias)
    return middle + gate_two * branch_two

def reference(tokens, time_embedding, prefix_length, suffix_mask, cotangent, modulation_weight, modulation_bias, attention_gain, attention_in, attention_out, feed_gain, feed_up, feed_up_bias, feed_down, feed_down_bias):
    weights = tuple((w.astype(jnp.float32) for w in (modulation_weight, modulation_bias, attention_gain, attention_in, attention_out, feed_gain, feed_up, feed_up_bias, feed_down, feed_down_bias)))
    positions = jnp.arange(LENGTH, dtype=jnp.int32)

    def one_sequence(summed, inputs):
        seq_tokens, embedding, prefix, mask_row, seq_cotangent = inputs
        live_rows = jnp.where((positions >= prefix) & (mask_row == 1), 1.0, 0.0).astype(jnp.float32)
        output, backward = jax.vjp(layer, seq_tokens.astype(jnp.float32), embedding.astype(jnp.float32), *weights)
        grads = backward(seq_cotangent.astype(jnp.float32) * live_rows[:, None])
        summed = tuple((a + b for a, b in zip(summed, grads[2:])))
        return (summed, (output.astype(jnp.bfloat16), grads[0].astype(jnp.bfloat16), grads[1]))
    zeros = tuple((jnp.zeros_like(w) for w in weights))
    summed, (outputs, tokens_grad, time_grad) = lax.scan(one_sequence, zeros, (tokens, time_embedding, prefix_length, suffix_mask, cotangent))
    return (outputs, tokens_grad, time_grad, summed[0], summed[1], summed[2], summed[3], summed[4], summed[5], summed[6], summed[7], summed[8], summed[9])
```

```python
from functools import partial

import jax
import jax.numpy as jnp
import numpy as np
from jax import lax
from jax.experimental import pallas as pl
from jax.experimental.pallas import tpu as pltpu
from jax.sharding import PartitionSpec as P

HEADS = 12
HD = 64


highest = lax.Precision.HIGHEST


def as_sent(shard):

    def short(part):
        return part.astype(jnp.bfloat16) if part.dtype == jnp.float32 else part

    return jax.tree.map(short, shard)


def normalize(values):
    centre = values - jnp.mean(values, -1, keepdims=True)
    spread = jnp.mean(centre * centre, -1, keepdims=True)
    return centre * lax.rsqrt(spread + 1e-05)


def modulate(values, scaling, shifts, scales):
    return normalize(values) * scaling * (1.0 + scales) + shifts


def rotate(values, cosine, sines, direction):
    halves = values.shape[-1] // 2
    former = values[..., :halves]
    latter = values[..., halves:]
    cosine = cosine[None, :, None, :]
    sines = direction * sines[None, :, None, :]
    return jnp.concatenate([former * cosine - latter * sines, latter * cosine + former * sines], -1)


def attend_forward(stacked):
    query_rows = stacked[:, 0]
    key_rows = stacked[:, 1]
    value_rows = stacked[:, 2]
    length = query_rows.shape[0]
    block_rows = min(512, length)
    pieces = []
    logsums = []
    for offset in range(0, length, block_rows):
        query_block = query_rows[offset : offset + block_rows]
        scores = (
            jnp.einsum("qhd,khd->hqk", query_block, key_rows, preferred_element_type=jnp.float32)
            * 0.125
        )
        largest = jnp.max(scores, -1, keepdims=True)
        exponentials = jnp.exp(scores - largest)
        totals = jnp.sum(exponentials, -1, keepdims=True)
        probability = (exponentials / totals).astype(jnp.bfloat16)
        pieces.append(
            jnp.einsum("hqk,khd->qhd", probability, value_rows, preferred_element_type=jnp.float32)
        )
        logsums.append((largest + jnp.log(totals))[..., 0])
    return (jnp.concatenate(pieces, 0).astype(jnp.bfloat16), jnp.concatenate(logsums, 1))


def attend_backward(operands):
    stacked, grad_attended, logsums = operands
    query_rows = stacked[:, 0]
    key_rows = stacked[:, 1]
    value_rows = stacked[:, 2]
    length = query_rows.shape[0]
    block_rows = min(512, length)
    grad_query = []
    grad_keys = jnp.zeros(key_rows.shape, jnp.float32)
    grad_values = jnp.zeros(value_rows.shape, jnp.float32)
    for offset in range(0, length, block_rows):
        query_block = query_rows[offset : offset + block_rows]
        grad_block = grad_attended[offset : offset + block_rows]
        scores = (
            jnp.einsum("qhd,khd->hqk", query_block, key_rows, preferred_element_type=jnp.float32)
            * 0.125
        )
        probability = jnp.exp(scores - logsums[:, offset : offset + block_rows, None])
        grad_probs = jnp.einsum(
            "qhd,khd->hqk", grad_block, value_rows, preferred_element_type=jnp.float32
        )
        row_dots = jnp.sum(probability * grad_probs, -1, keepdims=True)
        grad_scores = (probability * (grad_probs - row_dots)).astype(jnp.bfloat16)
        grad_query.append(
            (
                jnp.einsum(
                    "hqk,khd->qhd", grad_scores, key_rows, preferred_element_type=jnp.float32
                )
                * 0.125
            ).astype(jnp.bfloat16)
        )
        grad_keys = grad_keys + jnp.einsum(
            "hqk,qhd->khd", grad_scores, query_block, preferred_element_type=jnp.float32
        )
        grad_values = grad_values + jnp.einsum(
            "hqk,qhd->khd",
            probability.astype(jnp.bfloat16),
            grad_block,
            preferred_element_type=jnp.float32,
        )
    return jnp.stack(
        [
            jnp.concatenate(grad_query, 0),
            (grad_keys * 0.125).astype(jnp.bfloat16),
            grad_values.astype(jnp.bfloat16),
        ],
        1,
    )


def general_body(
    tokens,
    time_embedding,
    prefix_length,
    suffix_mask,
    cotangent,
    modulation_weight,
    modulation_bias,
    attention_gain,
    attention_in,
    attention_out,
    feed_gain,
    feed_up,
    feed_up_bias,
    feed_down,
    feed_down_bias,
):
    sequences, local_len, model_width = tokens.shape
    groups = lax.axis_size("seq")
    data_size = lax.axis_size("dp")
    length = local_len * groups
    heads_local = HEADS // groups
    group_width = model_width // groups
    modulation = jnp.einsum(
        "sc,oc->so", time_embedding, modulation_weight, preferred_element_type=jnp.float32
    ) + modulation_bias.astype(jnp.float32)
    shift_one, scale_one, gate_one, shift_two, scale_two, gate_two = [
        portion[:, None, :] for portion in jnp.split(modulation, 6, axis=1)
    ]
    inputs = tokens.astype(jnp.float32)
    first_float, first_back = jax.vjp(
        modulate, inputs, attention_gain.astype(jnp.float32), shift_one, scale_one
    )
    first_input = first_float.astype(jnp.bfloat16)
    projected = jnp.einsum(
        "spd,de->spe", first_input, attention_in, preferred_element_type=jnp.float32
    ).reshape(sequences, local_len, 3, HEADS, HD)
    position_ints = lax.axis_index("seq") * local_len + jnp.arange(local_len, dtype=jnp.int32)
    positions = position_ints.astype(jnp.float32)
    inverse = 10000.0 ** (-jnp.arange(HD // 2, dtype=jnp.float32) * 2.0 / HD)
    angles = positions[:, None] * inverse[None, :]
    cosine = jnp.cos(angles)
    sines = jnp.sin(angles)
    rotated = jnp.stack(
        [
            rotate(projected[:, :, 0], cosine, sines, 1.0),
            rotate(projected[:, :, 1], cosine, sines, 1.0),
            projected[:, :, 2],
        ],
        2,
    ).astype(jnp.bfloat16)
    by_heads = lax.all_to_all(
        rotated.reshape(sequences, local_len, 3, groups, group_width),
        "seq",
        split_axis=3,
        concat_axis=1,
        tiled=True,
    )
    by_heads = by_heads.reshape(sequences, length, 3, heads_local, HD)
    attended_heads, logsums = lax.map(attend_forward, by_heads)
    attended = lax.all_to_all(
        as_sent(attended_heads.reshape(sequences, length, 1, group_width)),
        "seq",
        split_axis=1,
        concat_axis=2,
        tiled=True,
    )
    attended = attended.reshape(sequences, local_len, model_width)
    branch_one = jnp.einsum(
        "spd,de->spe", attended, attention_out, preferred_element_type=jnp.float32
    )
    middle = inputs + gate_one * branch_one
    second_float, second_back = jax.vjp(
        modulate, middle, feed_gain.astype(jnp.float32), shift_two, scale_two
    )
    second_input = second_float.astype(jnp.bfloat16)
    hidden = jnp.einsum(
        "spd,df->spf", second_input, feed_up, preferred_element_type=jnp.float32
    ) + feed_up_bias.astype(jnp.float32)
    activated_float, gelu_back = jax.vjp(partial(jax.nn.gelu, approximate=True), hidden)
    activated = activated_float.astype(jnp.bfloat16)
    branch_two = jnp.einsum(
        "spf,fd->spd", activated, feed_down, preferred_element_type=jnp.float32
    ) + feed_down_bias.astype(jnp.float32)
    block_output = (middle + gate_two * branch_two).astype(jnp.bfloat16)
    live_rows = ((position_ints[None, :] >= prefix_length[:, None]) & (suffix_mask == 1)).astype(
        jnp.float32
    )
    grad_output = cotangent.astype(jnp.float32) * live_rows[:, :, None]
    grad_gate_two = jnp.sum(grad_output * branch_two, axis=1)
    grad_branch_two = (gate_two * grad_output).astype(jnp.bfloat16)
    feed_down_bias_grad = jnp.sum(grad_branch_two.astype(jnp.float32), axis=(0, 1))
    feed_down_grad = jnp.einsum(
        "spf,spd->fd", activated, grad_branch_two, preferred_element_type=jnp.float32
    )
    grad_activated = jnp.einsum(
        "spd,fd->spf", grad_branch_two, feed_down, preferred_element_type=jnp.float32
    )
    grad_hidden = gelu_back(grad_activated)[0].astype(jnp.bfloat16)
    feed_up_bias_grad = jnp.sum(grad_hidden.astype(jnp.float32), axis=(0, 1))
    feed_up_grad = jnp.einsum(
        "spd,spf->df", second_input, grad_hidden, preferred_element_type=jnp.float32
    )
    grad_second = jnp.einsum(
        "spf,df->spd", grad_hidden, feed_up, preferred_element_type=jnp.float32
    )
    grad_from_norm, feed_gain_grad, grad_shift_two, grad_scale_two = second_back(grad_second)
    grad_middle = grad_output + grad_from_norm
    grad_gate_one = jnp.sum(grad_middle * branch_one, axis=1)
    grad_branch_one = (gate_one * grad_middle).astype(jnp.bfloat16)
    attention_out_grad = jnp.einsum(
        "spd,spe->de", attended, grad_branch_one, preferred_element_type=jnp.float32
    )
    grad_attended = jnp.einsum(
        "spe,de->spd", grad_branch_one, attention_out, preferred_element_type=jnp.float32
    ).astype(jnp.bfloat16)
    grad_heads = lax.all_to_all(
        grad_attended.reshape(sequences, local_len, groups, group_width),
        "seq",
        split_axis=2,
        concat_axis=1,
        tiled=True,
    )
    grad_heads = grad_heads.reshape(sequences, length, heads_local, HD)
    grad_stacked = lax.map(attend_backward, (by_heads, grad_heads, logsums))
    grad_positions = lax.all_to_all(
        as_sent(grad_stacked.reshape(sequences, length, 3, 1, group_width)),
        "seq",
        split_axis=1,
        concat_axis=3,
        tiled=True,
    )
    grad_positions = grad_positions.reshape(sequences, local_len, 3, HEADS, HD).astype(jnp.float32)
    grad_projected = jnp.stack(
        [
            rotate(grad_positions[:, :, 0], cosine, sines, -1.0),
            rotate(grad_positions[:, :, 1], cosine, sines, -1.0),
            grad_positions[:, :, 2],
        ],
        2,
    ).astype(jnp.bfloat16)
    grad_projected = grad_projected.reshape(sequences, local_len, 3 * model_width)
    attention_in_grad = jnp.einsum(
        "spd,spe->de", first_input, grad_projected, preferred_element_type=jnp.float32
    )
    grad_first = jnp.einsum(
        "spe,de->spd", grad_projected, attention_in, preferred_element_type=jnp.float32
    )
    grad_tokens_norm, attention_gain_grad, grad_shift_one, grad_scale_one = first_back(grad_first)
    tokens_grad = (grad_middle + grad_tokens_norm).astype(jnp.bfloat16)
    grad_modulation = jnp.concatenate(
        [
            grad_shift_one[:, 0],
            grad_scale_one[:, 0],
            grad_gate_one,
            grad_shift_two[:, 0],
            grad_scale_two[:, 0],
            grad_gate_two,
        ],
        1,
    )
    modulation_total = lax.psum(grad_modulation.astype(jnp.bfloat16), "seq").astype(jnp.float32)
    time_grad = jnp.einsum(
        "so,oc->sc", modulation_total, modulation_weight.astype(jnp.float32), precision=highest
    )
    modulation_weight_grad = jnp.einsum(
        "so,sc->oc", grad_modulation, time_embedding.astype(jnp.float32), precision=highest
    )
    modulation_bias_grad = jnp.sum(grad_modulation, axis=0)
    gradients = (
        modulation_weight_grad,
        modulation_bias_grad,
        attention_gain_grad,
        attention_in_grad,
        attention_out_grad,
        feed_gain_grad,
        feed_up_grad,
        feed_up_bias_grad,
        feed_down_grad,
        feed_down_bias_grad,
    )
    flattened = tuple((g.reshape(data_size, -1) for g in gradients))
    shares = lax.psum_scatter(flattened, "dp", scatter_dimension=0, tiled=True)
    summed = jax.tree.map(lambda part: part.astype(jnp.float32), lax.psum(as_sent(shares), "seq"))
    shards = tuple(
        (s.reshape((g.shape[0] // data_size,) + g.shape[1:]) for s, g in zip(summed, gradients))
    )
    return (
        block_output,
        tokens_grad,
        time_grad,
        shards[0],
        shards[1],
        shards[2],
        shards[3],
        shards[4],
        shards[5],
        shards[6],
        shards[7],
        shards[8],
        shards[9],
    )


T_ROWS = 256
MIB = 1 << 20


def dot(a, b, ca, cb):
    return lax.dot_general(a, b, (((ca,), (cb,)), ((), ())), preferred_element_type=jnp.float32)


def params(limit=60):
    return pltpu.CompilerParams(vmem_limit_bytes=limit * MIB)


def norm_rows(values):
    centre = values - jnp.mean(values, -1, keepdims=True)
    inverse = lax.rsqrt(jnp.mean(centre * centre, -1, keepdims=True) + 1e-05)
    return centre * inverse, inverse


def swap_halves(values, lane):
    left = pltpu.roll(values, 96, 1)
    right = pltpu.roll(values, 32, 1)
    return jnp.where(lane % 64 < 32, left, right)


def project_kernel(own_ref, other_ref, mod_ref, gain_ref, weight_ref, cos_ref, sin_ref, first_ref, qkv_ref):
    rows = T_ROWS
    half = own_ref.shape[0]
    model = own_ref.shape[1]
    lane = lax.broadcasted_iota(jnp.int32, (rows, 128), 1)
    scaling = gain_ref[...] * (1.0 + mod_ref[1:2])
    shifts = mod_ref[0:1]
    for chunk in range(2 * half // rows):
        at = chunk * rows
        source = own_ref if at < half else other_ref
        values = source[at % half : at % half + rows].astype(jnp.float32)
        normed, _ = norm_rows(values)
        first = (normed * scaling + shifts).astype(jnp.bfloat16)
        first_ref[at : at + rows] = first
        for part in range(3):
            projected = dot(first, weight_ref[:, part * model : (part + 1) * model], 1, 0)
            for block in range(model // 128):
                piece = projected[:, block * 128 : (block + 1) * 128]
                if part < 2:
                    piece = piece * cos_ref[at : at + rows] + swap_halves(piece, lane) * sin_ref[at : at + rows]
                piece = piece.astype(jnp.bfloat16)
                if part == 0:
                    piece = piece * 0.125
                column = part * model + block * 128
                qkv_ref[at : at + rows, column : column + 128] = piece


def attend_kernel(q_ref, k_ref, v_ref, out_ref, exp_ref, inv_ref):
    rows = T_ROWS
    length = q_ref.shape[0]
    lane = lax.broadcasted_iota(jnp.int32, (rows, 128), 1)
    keys = k_ref[...]
    values = jnp.concatenate([v_ref[...], jnp.ones((length, 128), jnp.bfloat16)], 1)
    for chunk in range(length // rows):
        at = slice(chunk * rows, (chunk + 1) * rows)
        queries = q_ref[at]
        outs = []
        inverses = []
        for head in range(2):
            mine = jnp.where((lane < 64) == (head == 0), queries, jnp.zeros_like(queries))
            scores = dot(mine, keys, 1, 1)
            largest = jnp.max(scores, -1, keepdims=True)
            exps = jnp.exp(scores - largest).astype(jnp.bfloat16)
            exp_ref[head, at] = exps
            summed = dot(exps, values, 1, 0)
            inverse = 1.0 / summed[:, 128:256]
            outs.append(summed[:, 0:128] * inverse)
            inverses.append(inverse)
        out_ref[at] = jnp.where(lane < 64, outs[0], outs[1]).astype(jnp.bfloat16)
        inv_ref[at] = jnp.where(lane < 64, inverses[0], inverses[1])


def attend_back_kernel(q_ref, k_ref, v_ref, out_ref, grad_ref, exp_ref, inv_ref, cos_ref, sin_ref, dq_ref, dk_ref, dv_ref, ds_ref, dq_sum):
    rows = T_ROWS
    length = q_ref.shape[0]
    lane = lax.broadcasted_iota(jnp.int32, (rows, 128), 1)
    keys = k_ref[...]
    values = v_ref[...]
    scaled = grad_ref[...].astype(jnp.float32) * inv_ref[...]
    products = scaled * out_ref[...].astype(jnp.float32)
    scaled = scaled.astype(jnp.bfloat16)
    scaled_t = scaled.T
    queries_t = q_ref[...].T
    grad_k = []
    grad_v = []
    for head in range(2):
        for chunk in range(length // rows):
            at = slice(chunk * rows, (chunk + 1) * rows)
            mask = (lane < 64) == (head == 0)
            mine = jnp.where(mask, scaled[at], jnp.zeros((rows, 128), jnp.bfloat16))
            row_dots = jnp.sum(jnp.where(mask, products[at], 0.0), -1, keepdims=True)
            grad_p = dot(mine, values, 1, 1)
            grad_s = (exp_ref[head, at].astype(jnp.float32) * (grad_p - row_dots)).astype(jnp.bfloat16)
            ds_ref[at] = grad_s
            grad_q = dot(grad_s, keys, 1, 0) * 0.125
            if head == 0:
                dq_sum[at] = grad_q
            else:
                dq_sum[at] = jnp.where(lane < 64, dq_sum[at], grad_q)
        grad_v.append(dot(scaled_t[64 * head : 64 * head + 64], exp_ref[head], 1, 0))
        grad_k.append(dot(queries_t[64 * head : 64 * head + 64], ds_ref[...], 1, 0))
    dv_ref[...] = jnp.concatenate(grad_v, 0).astype(jnp.bfloat16).T
    grad_keys = jnp.concatenate(grad_k, 0).astype(jnp.bfloat16).T
    for chunk in range(length // rows):
        at = slice(chunk * rows, (chunk + 1) * rows)
        for source, target in ((dq_sum[at].astype(jnp.bfloat16), dq_ref), (grad_keys[at], dk_ref)):
            piece = source.astype(jnp.float32)
            target[at] = (piece * cos_ref[at] - swap_halves(piece, lane) * sin_ref[at]).astype(jnp.bfloat16)


def share(core, grad, keep_ref, send_ref, *at):
    first, second = grad
    keep_ref[at] = jnp.where(core == 0, first, second)
    send_ref[at] = jnp.where(core == 0, second, first)


def middle_kernel(
    core_ref,
    own_ref,
    other_ref,
    own_cot_ref,
    other_cot_ref,
    attended_ref,
    mod_ref,
    gain_ref,
    out_weight_ref,
    up_ref,
    up_bias_ref,
    down_ref,
    down_bias_ref,
    own_out_ref,
    other_out_ref,
    grad_middle_ref,
    grad_attended_ref,
    rows_ref,
    up_bias_grad_ref,
    down_keep_ref,
    down_send_ref,
    up_keep_ref,
    up_send_ref,
    out_keep_ref,
    out_send_ref,
    branch_one,
    second,
    second_t,
    grad_two,
    sum_two,
    sum_second,
    act,
    grad_hidden,
):
    rows = T_ROWS
    step = pl.program_id(0)
    core = core_ref[0]
    half, model = own_ref.shape
    length = 2 * half
    scaling = gain_ref[...] * (1.0 + mod_ref[4:5])
    gate_one = mod_ref[2:3]
    shift_two = mod_ref[3:4]
    gate_two = mod_ref[5:6]

    def pick(first_ref, second_ref, chunk):
        at = chunk * rows
        return (first_ref if at < half else second_ref)[at % half : at % half + rows]

    @pl.when(step == 0)
    def _():
        bias_grad = jnp.zeros((1, model), jnp.float32)
        for chunk in range(length // rows):
            at = slice(chunk * rows, (chunk + 1) * rows)
            branch = dot(attended_ref[at], out_weight_ref[...], 1, 0)
            branch_one[at] = branch
            middle = pick(own_ref, other_ref, chunk).astype(jnp.float32) + gate_one * branch
            normed, _ = norm_rows(middle)
            rounded = (normed * scaling + shift_two).astype(jnp.bfloat16)
            second[at] = rounded
            second_t[:, at] = rounded.T
            grad = (gate_two * pick(own_cot_ref, other_cot_ref, chunk).astype(jnp.float32)).astype(jnp.bfloat16)
            grad_two[at] = grad
            bias_grad = bias_grad + jnp.sum(grad.astype(jnp.float32), 0, keepdims=True)
        rows_ref[5:6] = bias_grad

    up = up_ref[...]
    down = down_ref[...]
    width = up.shape[1]
    bias_sum = jnp.zeros((1, width), jnp.float32)
    for chunk in range(length // rows):
        at = slice(chunk * rows, (chunk + 1) * rows)
        hidden = dot(second[at], up, 1, 0) + up_bias_ref[...]
        squared = hidden * hidden
        tanh = jnp.tanh(hidden * (0.7978845608028654 + 0.035677408136300125 * squared))
        gate = 0.5 + 0.5 * tanh
        activated = (hidden * gate).astype(jnp.bfloat16)
        slope = gate + (0.5 * hidden) * (1.0 - tanh * tanh) * (0.7978845608028654 + 0.10703222440890037 * squared)
        act[at] = activated
        grad = (slope * dot(grad_two[at], down, 1, 1)).astype(jnp.bfloat16)
        grad_hidden[at] = grad
        bias_sum = bias_sum + jnp.sum(grad.astype(jnp.float32), 0, keepdims=True)
        forward = dot(activated, down, 1, 0)
        backward = dot(grad, up, 1, 1)

        @pl.when(step == 0)
        def _():
            sum_two[at] = forward
            sum_second[at] = backward

        @pl.when(step > 0)
        def _():
            sum_two[at] += forward
            sum_second[at] += backward

    up_bias_grad_ref[...] = bias_sum
    down_grad = dot(act[...], grad_two[...], 0, 0).astype(jnp.bfloat16).reshape(down_keep_ref.shape[0], 2, -1, model)
    share(core, (down_grad[:, 0], down_grad[:, 1]), down_keep_ref, down_send_ref, Ellipsis)
    up_grad = dot(second_t[...], grad_hidden[...], 1, 0).astype(jnp.bfloat16).reshape(up_keep_ref.shape[0], 2, -1, width)
    share(core, (up_grad[:, 0], up_grad[:, 1]), up_keep_ref, up_send_ref, Ellipsis)

    @pl.when(step == pl.num_programs(0) - 1)
    def _():
        sums = [jnp.zeros((1, model), jnp.float32) for _ in range(4)]
        for chunk in range(length // rows):
            at = slice(chunk * rows, (chunk + 1) * rows)
            branch = branch_one[at]
            middle = pick(own_ref, other_ref, chunk).astype(jnp.float32) + gate_one * branch
            normed, inverse = norm_rows(middle)
            branch_two = sum_two[at] + down_bias_ref[...]
            output = (middle + gate_two * branch_two).astype(jnp.bfloat16)
            place = (chunk * rows) % half
            (own_out_ref if chunk * rows < half else other_out_ref)[place : place + rows] = output
            cot = pick(own_cot_ref, other_cot_ref, chunk).astype(jnp.float32)
            grad = sum_second[at]
            weighted = grad * normed
            scaled = grad * scaling
            inner = jnp.mean(weighted * scaling, -1, keepdims=True)
            grad_middle = cot + (scaled - jnp.mean(scaled, -1, keepdims=True) - normed * inner) * inverse
            grad_middle_ref[at] = grad_middle
            grad_one = (gate_one * grad_middle).astype(jnp.bfloat16)
            grad_two[at] = grad_one
            grad_attended_ref[at] = dot(grad_one, out_weight_ref[...], 1, 1).astype(jnp.bfloat16)
            for i, term in enumerate((grad_middle * branch, grad, weighted, cot * branch_two)):
                sums[i] = sums[i] + jnp.sum(term, 0, keepdims=True)
        rows_ref[0:1] = sums[0]
        rows_ref[1:2] = sums[1]
        rows_ref[2:3] = sums[2] * gain_ref[...]
        rows_ref[3:4] = sums[3]
        rows_ref[4:5] = sums[2] * (1.0 + mod_ref[4:5])
        out_grad = dot(attended_ref[...], grad_two[...], 0, 0).astype(jnp.bfloat16)
        out_grad = out_grad.reshape(out_keep_ref.shape[0], 2, -1, model)
        share(core, (out_grad[:, 0], out_grad[:, 1]), out_keep_ref, out_send_ref, Ellipsis)


def entry_kernel(core_ref, grad_ref, weight_ref, first_ref, own_ref, other_ref, grad_middle_ref, mod_ref, gain_ref, own_out_ref, other_out_ref, rows_ref, keep_ref, send_ref, total, first_t):
    rows = T_ROWS
    step = pl.program_id(0)
    core = core_ref[0]
    half, model = own_ref.shape
    length = 2 * half
    scaling = gain_ref[...] * (1.0 + mod_ref[1:2])

    @pl.when(step == 0)
    def _():
        first_t[...] = first_ref[...].T

    weight_grad = dot(first_t[...], grad_ref[...], 1, 0).astype(jnp.bfloat16).reshape(keep_ref.shape[0], 2, -1, model)
    share(core, (weight_grad[:, 0], weight_grad[:, 1]), keep_ref, send_ref, Ellipsis)
    for chunk in range(length // rows):
        at = slice(chunk * rows, (chunk + 1) * rows)
        grad = dot(grad_ref[at], weight_ref[...], 1, 1)

        @pl.when(step == 0)
        def _():
            total[at] = grad

        @pl.when(step > 0)
        def _():
            total[at] += grad

    @pl.when(step == pl.num_programs(0) - 1)
    def _():
        sums = [jnp.zeros((1, model), jnp.float32) for _ in range(2)]
        for chunk in range(length // rows):
            at = slice(chunk * rows, (chunk + 1) * rows)
            place = (chunk * rows) % half
            mine = chunk * rows < half
            values = (own_ref if mine else other_ref)[place : place + rows].astype(jnp.float32)
            normed, inverse = norm_rows(values)
            grad = total[at]
            weighted = grad * normed
            scaled = grad * scaling
            inner = jnp.mean(weighted * scaling, -1, keepdims=True)
            result = grad_middle_ref[at] + (scaled - jnp.mean(scaled, -1, keepdims=True) - normed * inner) * inverse
            (own_out_ref if mine else other_out_ref)[place : place + rows] = result.astype(jnp.bfloat16)
            for i, term in enumerate((grad, weighted)):
                sums[i] = sums[i] + jnp.sum(term, 0, keepdims=True)
        rows_ref[0:1] = sums[0]
        rows_ref[1:2] = sums[1] * gain_ref[...]
        rows_ref[2:3] = sums[1] * (1.0 + mod_ref[1:2])


def turn_tables(length):
    inverse = 10000.0 ** (-np.arange(HD // 2, dtype=np.float64) * 2.0 / HD)
    angles = np.arange(length, dtype=np.float64)[:, None] * inverse[None, :]
    cosine = np.tile(np.cos(angles), (1, 4))
    sines = np.sin(angles)
    sines = np.concatenate([-sines, sines, -sines, sines], 1)
    both = [np.stack([t, np.roll(t, -(length // 2), 0)]).astype(np.float32) for t in (cosine, sines)]
    return jnp.asarray(both[0]), jnp.asarray(both[1])


def call(kernel, grid, place, in_specs, out_specs, out_shape, scratch, operands, name, flops, moved):
    return pl.pallas_call(
        kernel,
        grid_spec=pltpu.PrefetchScalarGridSpec(
            num_scalar_prefetch=1, grid=grid, in_specs=in_specs, out_specs=out_specs, scratch_shapes=scratch
        ),
        out_shape=out_shape,
        compiler_params=params(),
        cost_estimate=pl.CostEstimate(flops=flops, bytes_accessed=moved, transcendentals=0),
        name=name,
    )(place, *operands)


def whole(*shape):
    return pl.BlockSpec(shape, lambda i, p: (0,) * len(shape))


def swap_pairs(size, bit):
    return [(i, i ^ bit) for i in range(size)]


def reduce_pieces(keep, send, dp, size):
    terms = [keep, lax.ppermute(send, "dp", swap_pairs(size, 1))]
    bit = 1
    count = size // 2
    order = []
    while count > 1:
        bit *= 2
        count //= 2
        order.append(bit)
        mine = (dp // bit) % 2
        split = [t.reshape(count, 2, *t.shape[1:]) for t in terms]
        other = sum(lax.dynamic_index_in_dim(t, 1 - mine, 1, False).astype(jnp.float32) for t in split)
        got = lax.ppermute(other.astype(jnp.bfloat16), "dp", swap_pairs(size, bit))
        terms = [lax.dynamic_index_in_dim(t, mine, 1, False) for t in split] + [got]
    total = sum(t[0].astype(jnp.float32) for t in terms).astype(jnp.bfloat16)
    got = lax.ppermute(total, "seq", swap_pairs(2, 1))
    return total.astype(jnp.float32) + got.astype(jnp.float32)


def fast_body(
    tokens,
    time_embedding,
    prefix_length,
    suffix_mask,
    cotangent,
    modulation_weight,
    modulation_bias,
    attention_gain,
    attention_in,
    attention_out,
    feed_gain,
    feed_up,
    feed_up_bias,
    feed_down,
    feed_down_bias,
):
    bf16 = jnp.bfloat16
    f32 = jnp.float32
    _, half, model = tokens.shape
    length = 2 * half
    hidden_width = feed_up.shape[1]
    size = lax.axis_size("dp")
    me = lax.axis_index("seq")
    dp = lax.axis_index("dp")
    place = jnp.stack([dp % 2, me]).astype(jnp.int32)
    swap = swap_pairs(2, 1)
    shape = jax.ShapeDtypeStruct

    def mine(array):
        return lax.dynamic_index_in_dim(array, me, 0, False)

    def theirs(array):
        return lax.dynamic_index_in_dim(array, 1 - me, 0, False)

    own = mine(tokens)
    other = lax.ppermute(theirs(tokens), "seq", swap)
    positions = me * half + jnp.arange(half, dtype=jnp.int32)
    live = (positions[None, :] >= prefix_length[:, None]) & (suffix_mask == 1)
    live_cot = jnp.where(live[:, :, None], cotangent, jnp.zeros_like(cotangent))
    own_cot = mine(live_cot)
    other_cot = lax.ppermute(theirs(live_cot), "seq", swap)
    all_embeddings = lax.all_gather(time_embedding, "dp", axis=0, tiled=True)

    modulation = jnp.einsum(
        "c,oc->o", mine(time_embedding), modulation_weight, preferred_element_type=f32
    ) + modulation_bias.astype(f32)
    modulation = modulation.reshape(6, model)
    gain_one = attention_gain.astype(f32)[None]
    gain_two = feed_gain.astype(f32)[None]
    cosine, sines = turn_tables(length)
    table = pl.BlockSpec((None, length, 128), lambda i, p: (p[1], 0, 0))

    first_input, qkv = call(
        lambda p, *refs: project_kernel(*refs),
        (1,),
        place,
        [whole(half, model)] * 2 + [whole(6, model), whole(1, model), whole(model, 3 * model), table, table],
        [whole(length, model), whole(length, 3 * model)],
        [shape((length, model), bf16), shape((length, 3 * model), bf16)],
        [],
        (own, other, modulation, gain_one, attention_in, cosine, sines),
        "project",
        2 * length * model * 3 * model,
        8 * MIB,
    )

    def column(k):
        return pl.BlockSpec((length, 128), lambda h, p: (0, h + k))

    pairs = model // 128
    exps_block = pl.BlockSpec((2, length, length), lambda h, p: (h, 0, 0))
    attended, exps, inverses = call(
        lambda p, *refs: attend_kernel(*refs),
        (pairs,),
        place,
        [column(0), column(pairs), column(2 * pairs)],
        [column(0), exps_block, column(0)],
        [shape((length, model), bf16), shape((HEADS, length, length), bf16), shape((length, model), f32)],
        [],
        (qkv, qkv, qkv),
        "attend",
        16 * length * length * model,
        32 * MIB,
    )

    tiles = 4
    width = hidden_width // tiles
    groups = size // 2
    share_rows = hidden_width // size
    model_rows = model // size
    down_block = pl.BlockSpec((groups // tiles, share_rows, model), lambda j, p: (j, 0, 0))
    up_block = pl.BlockSpec((groups, model_rows, width), lambda j, p: (0, 0, j))
    out_block = whole(groups, model_rows, model)
    (
        own_out,
        other_out,
        grad_middle,
        grad_attended,
        mid_rows,
        up_bias_grad,
        down_keep,
        down_send,
        up_keep,
        up_send,
        out_keep,
        out_send,
    ) = call(
        middle_kernel,
        (tiles,),
        place,
        [whole(half, model)] * 4
        + [
            whole(length, model),
            whole(6, model),
            whole(1, model),
            whole(model, model),
            pl.BlockSpec((model, width), lambda j, p: (0, j)),
            pl.BlockSpec((1, width), lambda j, p: (0, j)),
            pl.BlockSpec((width, model), lambda j, p: (j, 0)),
            whole(1, model),
        ],
        [
            whole(half, model),
            whole(half, model),
            whole(length, model),
            whole(length, model),
            whole(6, model),
            pl.BlockSpec((1, width), lambda j, p: (0, j)),
            down_block,
            down_block,
            up_block,
            up_block,
            out_block,
            out_block,
        ],
        [shape((half, model), bf16)] * 2
        + [shape((length, model), f32), shape((length, model), bf16), shape((6, model), f32), shape((1, hidden_width), f32)]
        + [shape((groups, share_rows, model), bf16)] * 2
        + [shape((groups, model_rows, hidden_width), bf16)] * 2
        + [shape((groups, model_rows, model), bf16)] * 2,
        [
            pltpu.VMEM((length, model), f32),
            pltpu.VMEM((length, model), bf16),
            pltpu.VMEM((model, length), bf16),
            pltpu.VMEM((length, model), bf16),
            pltpu.VMEM((length, model), f32),
            pltpu.VMEM((length, model), f32),
            pltpu.VMEM((length, width), bf16),
            pltpu.VMEM((length, width), bf16),
        ],
        (
            own,
            other,
            own_cot,
            other_cot,
            attended,
            modulation,
            gain_two,
            attention_out,
            feed_up,
            feed_up_bias.astype(f32)[None],
            feed_down,
            feed_down_bias.astype(f32)[None],
        ),
        "middle",
        12 * length * model * hidden_width + 6 * length * model * model,
        36 * MIB,
    )
    got_out = lax.ppermute(other_out, "seq", swap)
    down_grad = reduce_pieces(down_keep, down_send, dp, size)
    up_grad = reduce_pieces(up_keep, up_send, dp, size)
    out_grad = reduce_pieces(out_keep, out_send, dp, size)

    grads = call(
        lambda p, *refs: attend_back_kernel(*refs),
        (pairs,),
        place,
        [column(0), column(pairs), column(2 * pairs), column(0), column(0), exps_block, column(0), table, table],
        [column(0)] * 3,
        [shape((length, model), bf16)] * 3,
        [pltpu.VMEM((length, length), bf16), pltpu.VMEM((length, 128), f32)],
        (qkv, qkv, qkv, attended, grad_attended, exps, inverses, cosine, sines),
        "attend_back",
        32 * length * length * model,
        40 * MIB,
    )
    grad_projected = jnp.concatenate(grads, 1)

    in_block = pl.BlockSpec((groups, model_rows, model), lambda i, p: (0, 0, i))
    own_grad, other_grad, in_rows, in_keep, in_send = call(
        entry_kernel,
        (3,),
        place,
        [
            pl.BlockSpec((length, model), lambda i, p: (0, i)),
            pl.BlockSpec((model, model), lambda i, p: (0, i)),
            whole(length, model),
            whole(half, model),
            whole(half, model),
            whole(length, model),
            whole(6, model),
            whole(1, model),
        ],
        [whole(half, model), whole(half, model), whole(3, model), in_block, in_block],
        [shape((half, model), bf16)] * 2
        + [shape((3, model), f32)]
        + [shape((groups, model_rows, 3 * model), bf16)] * 2,
        [pltpu.VMEM((length, model), f32), pltpu.VMEM((model, length), bf16)],
        (grad_projected, attention_in, first_input, own, other, grad_middle, modulation, gain_one),
        "entry",
        4 * length * model * 3 * model,
        20 * MIB,
    )
    got_grad = lax.ppermute(other_grad, "seq", swap)
    in_grad = reduce_pieces(in_keep, in_send, dp, size)

    def assemble(kept, got):
        return jnp.where(me == 0, jnp.stack([kept, got]), jnp.stack([got, kept]))

    block_output = assemble(own_out, got_out)
    tokens_grad = assemble(own_grad, got_grad)

    grad_modulation = jnp.concatenate([in_rows[0:2], mid_rows[0:4]]).reshape(-1)
    own_time = jnp.einsum("o,oc->c", grad_modulation, modulation_weight.astype(f32), precision=highest)
    time_grad = assemble(own_time, lax.ppermute(own_time, "seq", swap))

    vectors = jnp.concatenate([grad_modulation, in_rows[2], mid_rows[4], up_bias_grad[0], mid_rows[5]])
    everyone = lax.all_gather(vectors, ("dp", "seq"), axis=0)

    def shard_of(start, width):
        rows = width // size
        return lax.dynamic_slice_in_dim(everyone, start + dp * rows, rows, 1)

    modulation_part = shard_of(0, 6 * model)
    modulation_weight_grad = jnp.einsum("so,sc->oc", modulation_part, all_embeddings.astype(f32), precision=highest)
    starts = (6 * model, 7 * model, 8 * model, 8 * model + hidden_width)
    widths = (model, model, hidden_width, model)
    gain_grad, feed_gain_grad, feed_up_bias_grad, feed_down_bias_grad = [
        jnp.sum(shard_of(a, w), 0) for a, w in zip(starts, widths)
    ]
    return (
        block_output,
        tokens_grad,
        time_grad,
        modulation_weight_grad,
        jnp.sum(modulation_part, 0),
        gain_grad,
        in_grad,
        out_grad,
        feed_gain_grad,
        up_grad,
        feed_up_bias_grad,
        down_grad,
        feed_down_bias_grad,
    )


def body(tokens, *rest):
    sequences, half, model = tokens.shape
    size = lax.axis_size("dp")
    fits = size & (size - 1) == 0 and size >= 8 and model % (16 * size) == 0 and half % T_ROWS == 0
    fits = fits and lax.axis_size("seq") == 2 and sequences == 2
    return (fast_body if fits else general_body)(tokens, *rest)


def solution(mesh):
    return jax.shard_map(
        body,
        mesh=mesh,
        in_specs=(
            P("dp", "seq", None),
            P("dp", None),
            P("dp"),
            P("dp", "seq"),
            P("dp", "seq", None),
            P(),
            P(),
            P(),
            P(),
            P(),
            P(),
            P(),
            P(),
            P(),
            P(),
        ),
        out_specs=(
            P("dp", "seq", None),
            P("dp", "seq", None),
            P("dp", None),
            P("dp", None),
            P("dp"),
            P("dp"),
            P("dp", None),
            P("dp", None),
            P("dp"),
            P("dp", None),
            P("dp"),
            P("dp", None),
            P("dp"),
        ),
        check_vma=False,
    )
```

```python
import functools
from functools import partial

import jax
import jax.numpy as jnp
import numpy as np
from jax import lax
from jax.experimental import pallas as pl
from jax.experimental.pallas import tpu as pltpu
from jax.sharding import PartitionSpec as P

HEADS = 12
HD = 64


highest = lax.Precision.HIGHEST


def as_sent(shard):

    def short(part):
        return part.astype(jnp.bfloat16) if part.dtype == jnp.float32 else part

    return jax.tree.map(short, shard)


def normalize(values):
    centre = values - jnp.mean(values, -1, keepdims=True)
    spread = jnp.mean(centre * centre, -1, keepdims=True)
    return centre * lax.rsqrt(spread + 1e-05)


def modulate(values, scaling, shifts, scales):
    return normalize(values) * scaling * (1.0 + scales) + shifts


def rotate(values, cosine, sines, direction):
    halves = values.shape[-1] // 2
    former = values[..., :halves]
    latter = values[..., halves:]
    cosine = cosine[None, :, None, :]
    sines = direction * sines[None, :, None, :]
    return jnp.concatenate([former * cosine - latter * sines, latter * cosine + former * sines], -1)


def attend_forward(stacked):
    query_rows = stacked[:, 0]
    key_rows = stacked[:, 1]
    value_rows = stacked[:, 2]
    length = query_rows.shape[0]
    block_rows = min(512, length)
    pieces = []
    logsums = []
    for offset in range(0, length, block_rows):
        query_block = query_rows[offset : offset + block_rows]
        scores = (
            jnp.einsum("qhd,khd->hqk", query_block, key_rows, preferred_element_type=jnp.float32)
            * 0.125
        )
        largest = jnp.max(scores, -1, keepdims=True)
        exponentials = jnp.exp(scores - largest)
        totals = jnp.sum(exponentials, -1, keepdims=True)
        probability = (exponentials / totals).astype(jnp.bfloat16)
        pieces.append(
            jnp.einsum("hqk,khd->qhd", probability, value_rows, preferred_element_type=jnp.float32)
        )
        logsums.append((largest + jnp.log(totals))[..., 0])
    return (jnp.concatenate(pieces, 0).astype(jnp.bfloat16), jnp.concatenate(logsums, 1))


def attend_backward(operands):
    stacked, grad_attended, logsums = operands
    query_rows = stacked[:, 0]
    key_rows = stacked[:, 1]
    value_rows = stacked[:, 2]
    length = query_rows.shape[0]
    block_rows = min(512, length)
    grad_query = []
    grad_keys = jnp.zeros(key_rows.shape, jnp.float32)
    grad_values = jnp.zeros(value_rows.shape, jnp.float32)
    for offset in range(0, length, block_rows):
        query_block = query_rows[offset : offset + block_rows]
        grad_block = grad_attended[offset : offset + block_rows]
        scores = (
            jnp.einsum("qhd,khd->hqk", query_block, key_rows, preferred_element_type=jnp.float32)
            * 0.125
        )
        probability = jnp.exp(scores - logsums[:, offset : offset + block_rows, None])
        grad_probs = jnp.einsum(
            "qhd,khd->hqk", grad_block, value_rows, preferred_element_type=jnp.float32
        )
        row_dots = jnp.sum(probability * grad_probs, -1, keepdims=True)
        grad_scores = (probability * (grad_probs - row_dots)).astype(jnp.bfloat16)
        grad_query.append(
            (
                jnp.einsum(
                    "hqk,khd->qhd", grad_scores, key_rows, preferred_element_type=jnp.float32
                )
                * 0.125
            ).astype(jnp.bfloat16)
        )
        grad_keys = grad_keys + jnp.einsum(
            "hqk,qhd->khd", grad_scores, query_block, preferred_element_type=jnp.float32
        )
        grad_values = grad_values + jnp.einsum(
            "hqk,qhd->khd",
            probability.astype(jnp.bfloat16),
            grad_block,
            preferred_element_type=jnp.float32,
        )
    return jnp.stack(
        [
            jnp.concatenate(grad_query, 0),
            (grad_keys * 0.125).astype(jnp.bfloat16),
            grad_values.astype(jnp.bfloat16),
        ],
        1,
    )


def general_body(
    tokens,
    time_embedding,
    prefix_length,
    suffix_mask,
    cotangent,
    modulation_weight,
    modulation_bias,
    attention_gain,
    attention_in,
    attention_out,
    feed_gain,
    feed_up,
    feed_up_bias,
    feed_down,
    feed_down_bias,
):
    sequences, local_len, model_width = tokens.shape
    groups = lax.axis_size("seq")
    data_size = lax.axis_size("dp")
    length = local_len * groups
    heads_local = HEADS // groups
    group_width = model_width // groups
    modulation = jnp.einsum(
        "sc,oc->so", time_embedding, modulation_weight, preferred_element_type=jnp.float32
    ) + modulation_bias.astype(jnp.float32)
    shift_one, scale_one, gate_one, shift_two, scale_two, gate_two = [
        portion[:, None, :] for portion in jnp.split(modulation, 6, axis=1)
    ]
    inputs = tokens.astype(jnp.float32)
    first_float, first_back = jax.vjp(
        modulate, inputs, attention_gain.astype(jnp.float32), shift_one, scale_one
    )
    first_input = first_float.astype(jnp.bfloat16)
    projected = jnp.einsum(
        "spd,de->spe", first_input, attention_in, preferred_element_type=jnp.float32
    ).reshape(sequences, local_len, 3, HEADS, HD)
    position_ints = lax.axis_index("seq") * local_len + jnp.arange(local_len, dtype=jnp.int32)
    positions = position_ints.astype(jnp.float32)
    inverse = 10000.0 ** (-jnp.arange(HD // 2, dtype=jnp.float32) * 2.0 / HD)
    angles = positions[:, None] * inverse[None, :]
    cosine = jnp.cos(angles)
    sines = jnp.sin(angles)
    rotated = jnp.stack(
        [
            rotate(projected[:, :, 0], cosine, sines, 1.0),
            rotate(projected[:, :, 1], cosine, sines, 1.0),
            projected[:, :, 2],
        ],
        2,
    ).astype(jnp.bfloat16)
    by_heads = lax.all_to_all(
        rotated.reshape(sequences, local_len, 3, groups, group_width),
        "seq",
        split_axis=3,
        concat_axis=1,
        tiled=True,
    )
    by_heads = by_heads.reshape(sequences, length, 3, heads_local, HD)
    attended_heads, logsums = lax.map(attend_forward, by_heads)
    attended = lax.all_to_all(
        as_sent(attended_heads.reshape(sequences, length, 1, group_width)),
        "seq",
        split_axis=1,
        concat_axis=2,
        tiled=True,
    )
    attended = attended.reshape(sequences, local_len, model_width)
    branch_one = jnp.einsum(
        "spd,de->spe", attended, attention_out, preferred_element_type=jnp.float32
    )
    middle = inputs + gate_one * branch_one
    second_float, second_back = jax.vjp(
        modulate, middle, feed_gain.astype(jnp.float32), shift_two, scale_two
    )
    second_input = second_float.astype(jnp.bfloat16)
    hidden = jnp.einsum(
        "spd,df->spf", second_input, feed_up, preferred_element_type=jnp.float32
    ) + feed_up_bias.astype(jnp.float32)
    activated_float, gelu_back = jax.vjp(partial(jax.nn.gelu, approximate=True), hidden)
    activated = activated_float.astype(jnp.bfloat16)
    branch_two = jnp.einsum(
        "spf,fd->spd", activated, feed_down, preferred_element_type=jnp.float32
    ) + feed_down_bias.astype(jnp.float32)
    block_output = (middle + gate_two * branch_two).astype(jnp.bfloat16)
    live_rows = ((position_ints[None, :] >= prefix_length[:, None]) & (suffix_mask == 1)).astype(
        jnp.float32
    )
    grad_output = cotangent.astype(jnp.float32) * live_rows[:, :, None]
    grad_gate_two = jnp.sum(grad_output * branch_two, axis=1)
    grad_branch_two = (gate_two * grad_output).astype(jnp.bfloat16)
    feed_down_bias_grad = jnp.sum(grad_branch_two.astype(jnp.float32), axis=(0, 1))
    feed_down_grad = jnp.einsum(
        "spf,spd->fd", activated, grad_branch_two, preferred_element_type=jnp.float32
    )
    grad_activated = jnp.einsum(
        "spd,fd->spf", grad_branch_two, feed_down, preferred_element_type=jnp.float32
    )
    grad_hidden = gelu_back(grad_activated)[0].astype(jnp.bfloat16)
    feed_up_bias_grad = jnp.sum(grad_hidden.astype(jnp.float32), axis=(0, 1))
    feed_up_grad = jnp.einsum(
        "spd,spf->df", second_input, grad_hidden, preferred_element_type=jnp.float32
    )
    grad_second = jnp.einsum(
        "spf,df->spd", grad_hidden, feed_up, preferred_element_type=jnp.float32
    )
    grad_from_norm, feed_gain_grad, grad_shift_two, grad_scale_two = second_back(grad_second)
    grad_middle = grad_output + grad_from_norm
    grad_gate_one = jnp.sum(grad_middle * branch_one, axis=1)
    grad_branch_one = (gate_one * grad_middle).astype(jnp.bfloat16)
    attention_out_grad = jnp.einsum(
        "spd,spe->de", attended, grad_branch_one, preferred_element_type=jnp.float32
    )
    grad_attended = jnp.einsum(
        "spe,de->spd", grad_branch_one, attention_out, preferred_element_type=jnp.float32
    ).astype(jnp.bfloat16)
    grad_heads = lax.all_to_all(
        grad_attended.reshape(sequences, local_len, groups, group_width),
        "seq",
        split_axis=2,
        concat_axis=1,
        tiled=True,
    )
    grad_heads = grad_heads.reshape(sequences, length, heads_local, HD)
    grad_stacked = lax.map(attend_backward, (by_heads, grad_heads, logsums))
    grad_positions = lax.all_to_all(
        as_sent(grad_stacked.reshape(sequences, length, 3, 1, group_width)),
        "seq",
        split_axis=1,
        concat_axis=3,
        tiled=True,
    )
    grad_positions = grad_positions.reshape(sequences, local_len, 3, HEADS, HD).astype(jnp.float32)
    grad_projected = jnp.stack(
        [
            rotate(grad_positions[:, :, 0], cosine, sines, -1.0),
            rotate(grad_positions[:, :, 1], cosine, sines, -1.0),
            grad_positions[:, :, 2],
        ],
        2,
    ).astype(jnp.bfloat16)
    grad_projected = grad_projected.reshape(sequences, local_len, 3 * model_width)
    attention_in_grad = jnp.einsum(
        "spd,spe->de", first_input, grad_projected, preferred_element_type=jnp.float32
    )
    grad_first = jnp.einsum(
        "spe,de->spd", grad_projected, attention_in, preferred_element_type=jnp.float32
    )
    grad_tokens_norm, attention_gain_grad, grad_shift_one, grad_scale_one = first_back(grad_first)
    tokens_grad = (grad_middle + grad_tokens_norm).astype(jnp.bfloat16)
    grad_modulation = jnp.concatenate(
        [
            grad_shift_one[:, 0],
            grad_scale_one[:, 0],
            grad_gate_one,
            grad_shift_two[:, 0],
            grad_scale_two[:, 0],
            grad_gate_two,
        ],
        1,
    )
    modulation_total = lax.psum(grad_modulation.astype(jnp.bfloat16), "seq").astype(jnp.float32)
    time_grad = jnp.einsum(
        "so,oc->sc", modulation_total, modulation_weight.astype(jnp.float32), precision=highest
    )
    modulation_weight_grad = jnp.einsum(
        "so,sc->oc", grad_modulation, time_embedding.astype(jnp.float32), precision=highest
    )
    modulation_bias_grad = jnp.sum(grad_modulation, axis=0)
    gradients = (
        modulation_weight_grad,
        modulation_bias_grad,
        attention_gain_grad,
        attention_in_grad,
        attention_out_grad,
        feed_gain_grad,
        feed_up_grad,
        feed_up_bias_grad,
        feed_down_grad,
        feed_down_bias_grad,
    )
    flattened = tuple((g.reshape(data_size, -1) for g in gradients))
    shares = lax.psum_scatter(flattened, "dp", scatter_dimension=0, tiled=True)
    summed = jax.tree.map(lambda part: part.astype(jnp.float32), lax.psum(as_sent(shares), "seq"))
    shards = tuple(
        (s.reshape((g.shape[0] // data_size,) + g.shape[1:]) for s, g in zip(summed, gradients))
    )
    return (
        block_output,
        tokens_grad,
        time_grad,
        shards[0],
        shards[1],
        shards[2],
        shards[3],
        shards[4],
        shards[5],
        shards[6],
        shards[7],
        shards[8],
        shards[9],
    )


T_ROWS = 256
MIB = 1 << 20


def dot(a, b, ca, cb):
    return lax.dot_general(a, b, (((ca,), (cb,)), ((), ())), preferred_element_type=jnp.float32)


def params(limit=60):
    return pltpu.CompilerParams(vmem_limit_bytes=limit * MIB)


def norm_rows(values):
    centre = values - jnp.mean(values, -1, keepdims=True)
    inverse = lax.rsqrt(jnp.mean(centre * centre, -1, keepdims=True) + 1e-05)
    return centre * inverse, inverse


def swap_halves(values, lane):
    left = pltpu.roll(values, 96, 1)
    right = pltpu.roll(values, 32, 1)
    return jnp.where(lane % 64 < 32, left, right)


def project_kernel(source_ref, mod_ref, gain_ref, weight_ref, cos_ref, sin_ref, first_t_ref, qkv_ref):
    rows, model = source_ref.shape
    lane = lax.broadcasted_iota(jnp.int32, (rows, 128), 1)
    scaling = gain_ref[...] * (1.0 + mod_ref[1:2])
    normed, _ = norm_rows(source_ref[...].astype(jnp.float32))
    first = (normed * scaling + mod_ref[0:1]).astype(jnp.bfloat16)
    first_t_ref[...] = first.T
    for part in range(3):
        projected = dot(first, weight_ref[:, part * model : (part + 1) * model], 1, 0)
        for block in range(model // 128):
            piece = projected[:, block * 128 : (block + 1) * 128]
            if part < 2:
                piece = piece * cos_ref[...] + swap_halves(piece, lane) * sin_ref[...]
            piece = piece.astype(jnp.bfloat16)
            if part == 0:
                piece = piece * 0.125
            column = part * model + block * 128
            qkv_ref[:, column : column + 128] = piece


def attend_kernel(q_ref, k_ref, v_ref, out_ref, exp_ref, inv_ref):
    rows = T_ROWS
    length = q_ref.shape[0]
    lane = lax.broadcasted_iota(jnp.int32, (rows, 128), 1)
    keys = k_ref[...]
    values = jnp.concatenate([v_ref[...], jnp.ones((length, 128), jnp.bfloat16)], 1)
    for chunk in range(length // rows):
        at = slice(chunk * rows, (chunk + 1) * rows)
        queries = q_ref[at]
        outs = []
        inverses = []
        for head in range(2):
            mine = jnp.where((lane < 64) == (head == 0), queries, jnp.zeros_like(queries))
            scores = dot(mine, keys, 1, 1)
            largest = jnp.max(scores, -1, keepdims=True)
            exps = jnp.exp(scores - largest).astype(jnp.bfloat16)
            exp_ref[head, at] = exps
            summed = dot(exps, values, 1, 0)
            inverse = 1.0 / summed[:, 128:256]
            outs.append(summed[:, 0:128] * inverse)
            inverses.append(inverse)
        out_ref[at] = jnp.where(lane < 64, outs[0], outs[1]).astype(jnp.bfloat16)
        inv_ref[at] = jnp.where(lane < 64, inverses[0], inverses[1])


def share(core, grad, keep_ref, send_ref, *at):
    first, second = grad
    keep_ref[at] = jnp.where(core == 0, first, second)
    send_ref[at] = jnp.where(core == 0, second, first)


def middle_kernel(
    core_ref,
    own_ref,
    other_ref,
    own_cot_ref,
    other_cot_ref,
    attended_ref,
    mod_ref,
    gain_ref,
    out_weight_ref,
    up_ref,
    up_bias_ref,
    down_ref,
    down_bias_ref,
    own_out_ref,
    other_out_ref,
    grad_middle_ref,
    grad_attended_ref,
    rows_ref,
    up_bias_grad_ref,
    down_keep_ref,
    down_send_ref,
    up_keep_ref,
    up_send_ref,
    out_keep_ref,
    out_send_ref,
    branch_one,
    attended_t,
    second,
    second_t,
    grad_two,
    sum_two,
    sum_second,
    act_t,
    grad_hidden,
):
    rows = T_ROWS
    step = pl.program_id(0)
    core = core_ref[0]
    half, model = own_ref.shape
    length = 2 * half
    scaling = gain_ref[...] * (1.0 + mod_ref[4:5])
    gate_one = mod_ref[2:3]
    shift_two = mod_ref[3:4]
    gate_two = mod_ref[5:6]

    def pick(first_ref, second_ref, chunk):
        at = chunk * rows
        return (first_ref if at < half else second_ref)[at % half : at % half + rows]

    @pl.when(step == 0)
    def _():
        bias_grad = jnp.zeros((1, model), jnp.float32)
        for chunk in range(length // rows):
            at = slice(chunk * rows, (chunk + 1) * rows)
            branch = dot(attended_ref[at], out_weight_ref[...], 1, 0)
            branch_one[at] = branch
            attended_t[:, at] = attended_ref[at].T
            sum_two[at] = jnp.zeros((rows, model), jnp.float32)
            sum_second[at] = jnp.zeros((rows, model), jnp.float32)
            middle = pick(own_ref, other_ref, chunk).astype(jnp.float32) + gate_one * branch
            normed, _ = norm_rows(middle)
            rounded = (normed * scaling + shift_two).astype(jnp.bfloat16)
            second[at] = rounded
            second_t[:, at] = rounded.T
            grad = (gate_two * pick(own_cot_ref, other_cot_ref, chunk).astype(jnp.float32)).astype(jnp.bfloat16)
            grad_two[at] = grad
            bias_grad = bias_grad + jnp.sum(grad.astype(jnp.float32), 0, keepdims=True)
        rows_ref[5:6] = bias_grad

    up = up_ref[...]
    down = down_ref[...]
    width = up.shape[1]
    bias_sum = jnp.zeros((1, width), jnp.float32)
    for chunk in range(length // rows):
        at = slice(chunk * rows, (chunk + 1) * rows)
        hidden = dot(second[at], up, 1, 0) + up_bias_ref[...]
        squared = hidden * hidden
        tanh = jnp.tanh(hidden * (0.7978845608028654 + 0.035677408136300125 * squared))
        gate = 0.5 + 0.5 * tanh
        activated = (hidden * gate).astype(jnp.bfloat16)
        slope = gate + (0.5 * hidden) * (1.0 - tanh * tanh) * (0.7978845608028654 + 0.10703222440890037 * squared)
        act_t[:, at] = activated.T
        grad = (slope * dot(grad_two[at], down, 1, 1)).astype(jnp.bfloat16)
        grad_hidden[at] = grad
        bias_sum = bias_sum + jnp.sum(grad.astype(jnp.float32), 0, keepdims=True)
        sum_two[at] += dot(activated, down, 1, 0)
        sum_second[at] += dot(grad, up, 1, 1)

    up_bias_grad_ref[...] = bias_sum
    down_grad = dot(act_t[...], grad_two[...], 1, 0).astype(jnp.bfloat16).reshape(down_keep_ref.shape[0], 2, -1, model)
    share(core, (down_grad[:, 0], down_grad[:, 1]), down_keep_ref, down_send_ref, Ellipsis)
    up_grad = dot(second_t[...], grad_hidden[...], 1, 0).astype(jnp.bfloat16).reshape(up_keep_ref.shape[0], 2, -1, width)
    share(core, (up_grad[:, 0], up_grad[:, 1]), up_keep_ref, up_send_ref, Ellipsis)

    @pl.when(step == pl.num_programs(0) - 1)
    def _():
        sums = [jnp.zeros((1, model), jnp.float32) for _ in range(4)]
        for chunk in range(length // rows):
            at = slice(chunk * rows, (chunk + 1) * rows)
            branch = branch_one[at]
            middle = pick(own_ref, other_ref, chunk).astype(jnp.float32) + gate_one * branch
            normed, inverse = norm_rows(middle)
            branch_two = sum_two[at] + down_bias_ref[...]
            output = (middle + gate_two * branch_two).astype(jnp.bfloat16)
            place = (chunk * rows) % half
            (own_out_ref if chunk * rows < half else other_out_ref)[place : place + rows] = output
            cot = pick(own_cot_ref, other_cot_ref, chunk).astype(jnp.float32)
            grad = sum_second[at]
            weighted = grad * normed
            scaled = grad * scaling
            inner = jnp.mean(weighted * scaling, -1, keepdims=True)
            grad_middle = cot + (scaled - jnp.mean(scaled, -1, keepdims=True) - normed * inner) * inverse
            grad_middle_ref[at] = grad_middle
            grad_one = (gate_one * grad_middle).astype(jnp.bfloat16)
            grad_two[at] = grad_one
            grad_attended_ref[at] = dot(grad_one, out_weight_ref[...], 1, 1).astype(jnp.bfloat16)
            for i, term in enumerate((grad_middle * branch, grad, weighted, cot * branch_two)):
                sums[i] = sums[i] + jnp.sum(term, 0, keepdims=True)
        rows_ref[0:1] = sums[0]
        rows_ref[1:2] = sums[1]
        rows_ref[2:3] = sums[2] * gain_ref[...]
        rows_ref[3:4] = sums[3]
        rows_ref[4:5] = sums[2] * (1.0 + mod_ref[4:5])
        out_grad = dot(attended_t[...], grad_two[...], 1, 0).astype(jnp.bfloat16)
        out_grad = out_grad.reshape(out_keep_ref.shape[0], 2, -1, model)
        share(core, (out_grad[:, 0], out_grad[:, 1]), out_keep_ref, out_send_ref, Ellipsis)


class Links:
    def __init__(self):
        dp = lax.axis_index("dp")
        self.me = lax.axis_index("seq")
        self.bit = {"C": dp % 2, "X": (dp // 2) % 2, "Z": (dp // 4) % 2, "W": (dp // 8) % 2, "Y": self.me}
        self.partner = {
            name: (dp + jump * (1 - 2 * self.bit[name]), self.me)
            for name, jump in (("C", 1), ("X", 2), ("Z", 4), ("W", 8))
        }
        self.partner["Y"] = (dp, 1 - self.me)


def remote(source, target, sems, slot, device):
    return pltpu.make_async_remote_copy(
        src_ref=source,
        dst_ref=target,
        send_sem=sems.at[0, slot],
        recv_sem=sems.at[1, slot],
        device_id=device,
        device_id_type=pl.DeviceIdType.MESH,
    )


def stage_shapes(rows, order):
    count = 8
    shapes = []
    for kind in order:
        if kind == "Y":
            rows //= 2
        else:
            count //= 2
        shapes.append((count, rows))
    shapes.append((1, rows))
    return shapes


def piece_scratch(rows, order, width, sent):
    shapes = [(8, rows)] * (3 if sent else 2)
    for shape in stage_shapes(rows, order):
        shapes += [shape] * 2
    return [pltpu.VMEM((count, r, width), jnp.bfloat16) for count, r in shapes]


class Piece:
    def __init__(self, links, refs, rows, order, sems, slot, source=None):
        refs = list(refs)
        self.links = links
        self.sems = sems
        self.slot = slot
        self.order = list(order)
        self.rows = rows
        self.split = False
        self.keep = refs.pop(0)
        first = refs.pop(0)
        self.source = source if source is not None else refs.pop(0)
        self.buffers = refs
        self.left = ["W", "Z", "X"]
        self.terms = [(self.keep, list(self.left), False)]
        copy = (self.source, first, sems, slot, links.partner["C"])
        self.slot += 1
        self.copies = [copy]
        self.flying = (copy, first, list(self.left), False)

    def launch(self, source, target, kind, bits):
        copy = (source, target, self.sems, self.slot, self.links.partner[kind])
        self.slot += 1
        remote(*copy).start()
        self.copies.append(copy)
        self.flying = (copy, target, list(bits), self.split)

    def begin(self):
        remote(*self.copies[0]).start()

    def arrive(self):
        copy, target, bits, split = self.flying
        remote(*copy).wait_recv()
        self.terms.append((target, bits, split))

    def index(self, bits, values):
        at = 0
        for bit in bits:
            at = at * 2 + values[bit]
        return at

    def add(self, out, kind):
        links = self.links
        left = [bit for bit in self.left if bit != kind]
        rows = out.shape[1]
        block = 48
        for combo in range(1 << len(left)):
            values = dict(links.bit)
            for place, bit in enumerate(left):
                values[bit] = (combo >> (len(left) - 1 - place)) & 1
            if kind is not None and kind != "Y":
                values[kind] = 1 - links.bit[kind]
            indices = [self.index(bits, values) for _, bits, _ in self.terms]

            def some(i, carry, indices=indices, combo=combo):
                start = pl.multiple_of(i * block, 16)
                total = None
                for (ref, _, split), at in zip(self.terms, indices):
                    begin = start
                    if not split and (kind == "Y" or self.split):
                        half = (1 - links.me) if kind == "Y" else links.me
                        begin = pl.multiple_of(half * rows + i * block, 16)
                    term = ref[at, pl.ds(begin, block), :].astype(jnp.float32)
                    total = term if total is None else total + term
                out[combo, pl.ds(start, block), :] = total.astype(jnp.bfloat16)
                return carry

            lax.fori_loop(0, rows // block, some, 0)

    def step(self):
        self.arrive()
        kind = self.order.pop(0)
        out, target = self.buffers.pop(0), self.buffers.pop(0)
        self.add(out, kind)
        if kind == "Y":
            self.split = True
        else:
            self.left.remove(kind)
        self.launch(out, target, kind, self.left)

    def last(self):
        self.arrive()
        self.total, self.got = self.buffers.pop(0), self.buffers.pop(0)
        self.add(self.total, None)
        self.launch(self.total, self.got, "Y", [])

    def result(self, store):
        remote(*self.flying[0]).wait_recv()
        rows = self.total.shape[1]
        total = self.total[0].astype(jnp.float32)
        got = self.got[0].astype(jnp.float32)
        if self.split:
            store(pl.ds(pl.multiple_of(self.links.me * rows, 8), rows), total)
            store(pl.ds(pl.multiple_of((1 - self.links.me) * rows, 8), rows), got)
        else:
            store(slice(0, rows), total + got)


BACK_PIECES = (("down", 192, "YXZW"), ("up", 192, "XZW"), ("out", 48, "ZXW"), ("in0", 48, "ZXW"), ("in1", 48, "ZXW"), ("in2", 48, "XZW"))
BACK_COPIES = sum(2 + len(order) for _, _, order in BACK_PIECES)


def back_kernel(
    q_ref,
    k_ref,
    v_ref,
    out_ref,
    grad_ref,
    exp_ref,
    inv_ref,
    cos_ref,
    sin_ref,
    first_t_ref,
    weight_ref,
    own_ref,
    other_ref,
    grad_middle_ref,
    mod_ref,
    gain_ref,
    down_keep,
    down_send,
    up_keep,
    up_send,
    out_keep,
    out_send,
    tokens_grad_ref,
    rows_ref,
    down_ref,
    up_ref,
    out_grad_ref,
    in_ref,
    ds_ref,
    dq_sum,
    proj,
    tokens_stage,
    sems,
    local_sems,
    *buffers,
):
    rows = T_ROWS
    step = pl.program_id(0)
    length = q_ref.shape[0]
    half, model = other_ref.shape
    links = Links()
    core = links.bit["C"]
    pieces = []
    buffers = list(buffers)
    slot = 0
    sources = [down_send, up_send, out_send, None, None, None]
    for (_, piece_rows, order), source in zip(BACK_PIECES, sources):
        count = 2 * len(order) + 4 + (source is None)
        pieces.append(Piece(links, buffers[:count], piece_rows, order, sems, slot, source))
        buffers = buffers[count:]
        slot += 2 + len(order)
    down, up, out, *ins = pieces

    def fetches():
        pairs = ((down_keep, down), (up_keep, up), (out_keep, out))
        return [pltpu.make_async_copy(s, p.keep, local_sems.at[i]) for i, (s, p) in enumerate(pairs)]

    @pl.when(step == 0)
    def _():
        barrier = pltpu.get_barrier_semaphore()
        for name in "CXZWY":
            pl.semaphore_signal(
                barrier, inc=1, device_id=links.partner[name], device_id_type=pl.DeviceIdType.MESH
            )
        pl.semaphore_wait(barrier, 5)
        for piece in (down, up, out):
            piece.begin()
        for copy in fetches():
            copy.start()

    def at_step(number):
        return pl.when(step == number)

    @at_step(2)
    def _():
        for copy in fetches():
            copy.wait()
        down.step()
        up.step()
        out.step()

    @at_step(3)
    def _():
        ins[0].step()

    @at_step(5)
    def _():
        ins[1].step()

    lane = lax.broadcasted_iota(jnp.int32, (rows, 128), 1)

    @pl.when(step < 6)
    def _():
        keys = k_ref[...]
        values = v_ref[...]
        scaled = grad_ref[...].astype(jnp.float32) * inv_ref[...]
        products = scaled * out_ref[...].astype(jnp.float32)
        scaled = scaled.astype(jnp.bfloat16)
        scaled_t = scaled.T
        queries_t = q_ref[...].T
        grad_k = []
        grad_v = []
        for head in range(2):
            for chunk in range(length // rows):
                at = slice(chunk * rows, (chunk + 1) * rows)
                mask = (lane < 64) == (head == 0)
                mine = jnp.where(mask, scaled[at], jnp.zeros((rows, 128), jnp.bfloat16))
                row_dots = jnp.sum(jnp.where(mask, products[at], 0.0), -1, keepdims=True)
                grad_p = dot(mine, values, 1, 1)
                grad_s = (exp_ref[head, at].astype(jnp.float32) * (grad_p - row_dots)).astype(jnp.bfloat16)
                ds_ref[at] = grad_s
                grad_q = dot(grad_s, keys, 1, 0) * 0.125
                if head == 0:
                    dq_sum[at] = grad_q
                else:
                    dq_sum[at] = jnp.where(lane < 64, dq_sum[at], grad_q)
            grad_v.append(dot(scaled_t[64 * head : 64 * head + 64], exp_ref[head], 1, 0))
            grad_k.append(dot(queries_t[64 * head : 64 * head + 64], ds_ref[...], 1, 0))
        columns = [pl.ds(pl.multiple_of(part * model + step * 128, 128), 128) for part in range(3)]
        proj[:, columns[2]] = jnp.concatenate(grad_v, 0).astype(jnp.bfloat16).T
        grad_keys = jnp.concatenate(grad_k, 0).astype(jnp.bfloat16).T
        for chunk in range(length // rows):
            at = slice(chunk * rows, (chunk + 1) * rows)
            for part, source in enumerate((dq_sum[at].astype(jnp.bfloat16), grad_keys[at])):
                piece = source.astype(jnp.float32)
                turned = piece * cos_ref[at] - swap_halves(piece, lane) * sin_ref[at]
                proj[at, columns[part]] = turned.astype(jnp.bfloat16)

    def weight_part(group):
        piece = ins[group]
        span = model // 3
        for part in range(3):
            column = part * model + group * span
            grad = dot(first_t_ref[...], proj[:, column : column + span], 1, 0).astype(jnp.bfloat16)
            grad = grad.reshape(8, 2, -1, span)
            share(core, (grad[:, 0], grad[:, 1]), piece.keep, piece.source, Ellipsis, slice(part * span, (part + 1) * span))
        piece.begin()

    for group in range(3):
        at_step(2 * group + 1)(functools.partial(weight_part, group))

    scaling = gain_ref[...] * (1.0 + mod_ref[1:2])

    def entry(values_ref, base):
        sums = [jnp.zeros((1, model), jnp.float32) for _ in range(2)]
        for chunk in range(half // rows):
            at = slice(base + chunk * rows, base + (chunk + 1) * rows)
            local = slice(chunk * rows, (chunk + 1) * rows)
            grad = dot(proj[at], weight_ref[...], 1, 1)
            normed, inverse = norm_rows(values_ref[local].astype(jnp.float32))
            weighted = grad * normed
            scaled = grad * scaling
            inner = jnp.mean(weighted * scaling, -1, keepdims=True)
            result = grad_middle_ref[local] + (scaled - jnp.mean(scaled, -1, keepdims=True) - normed * inner) * inverse
            tokens_stage[at] = result.astype(jnp.bfloat16)
            for i, term in enumerate((grad, weighted)):
                sums[i] = sums[i] + jnp.sum(term, 0, keepdims=True)
        return jnp.concatenate(sums, 0)

    def away():
        target = tokens_grad_ref.at[links.me]
        return remote(tokens_stage.at[pl.ds(half, half)], target, sems, BACK_COPIES, links.partner["Y"])

    def home():
        return pltpu.make_async_copy(tokens_stage.at[pl.ds(0, half)], tokens_grad_ref.at[links.me], local_sems.at[3])

    @at_step(6)
    def _():
        rows_ref[...] = entry(other_ref, half)
        away().start()
        ins[2].step()
        ins[0].step()
        ins[1].step()
        out.step()

    @at_step(7)
    def _():
        rows_ref[...] += entry(own_ref, 0)
        home().start()
        down.step()
        up.step()
        for piece in (ins[0], out, ins[1], ins[2]):
            piece.step()
        down.step()
        for piece in (ins[0], out, ins[1]):
            piece.last()
        up.step()
        ins[2].step()
        down.step()
        ins[2].last()
        down.last()
        up.last()
        span = model // 3
        for group in range(3):
            def store(at, value, group=group):
                for part in range(3):
                    column = part * model + group * span
                    in_ref[at, column : column + span] = value[:, part * span : (part + 1) * span]

            ins[group].result(store)

        def store_out(at, value):
            out_grad_ref[at] = value

        out.result(store_out)

        def store_down(at, value):
            down_ref[at] = value

        down.result(store_down)

        def store_up(at, value):
            count = up_ref.shape[0]
            for tile in range(up_ref.shape[1] // model):
                up_ref[:, tile * model : (tile + 1) * model] = value[tile * count : (tile + 1) * count]

        up.result(store_up)
        home().wait()
        away().wait()
        for piece in pieces:
            for copy in piece.copies:
                remote(*copy).wait_send()


def turn_tables(length):
    inverse = 10000.0 ** (-np.arange(HD // 2, dtype=np.float64) * 2.0 / HD)
    angles = np.arange(length, dtype=np.float64)[:, None] * inverse[None, :]
    cosine = np.tile(np.cos(angles), (1, 4))
    sines = np.sin(angles)
    sines = np.concatenate([-sines, sines, -sines, sines], 1)
    both = [np.stack([t, np.roll(t, -(length // 2), 0)]).astype(np.float32) for t in (cosine, sines)]
    return jnp.asarray(both[0]), jnp.asarray(both[1])


def call(kernel, grid, place, in_specs, out_specs, out_shape, scratch, operands, name, flops, moved, after=(), alias=()):
    count = len(in_specs) + 1
    extra = len(after) + len(alias)
    in_specs = in_specs + [pl.BlockSpec(memory_space=pl.ANY)] * extra

    def inner(*refs):
        kernel(*refs[:count], *refs[count + extra :])

    start = count + len(after)
    first_out = len(out_shape) - len(alias)
    operands = (*operands, *after, *alias)
    return pl.pallas_call(
        inner,
        input_output_aliases={start + i: first_out + i for i in range(len(alias))},
        grid_spec=pltpu.PrefetchScalarGridSpec(
            num_scalar_prefetch=1, grid=grid, in_specs=in_specs, out_specs=out_specs, scratch_shapes=scratch
        ),
        out_shape=out_shape,
        compiler_params=params(),
        cost_estimate=pl.CostEstimate(flops=flops, bytes_accessed=moved, transcendentals=0),
        name=name,
    )(place, *operands)


def whole(*shape):
    return pl.BlockSpec(shape, lambda i, p: (0,) * len(shape))


def swap_pairs(size, bit):
    return [(i, i ^ bit) for i in range(size)]


def fast_body(
    tokens,
    time_embedding,
    prefix_length,
    suffix_mask,
    cotangent,
    modulation_weight,
    modulation_bias,
    attention_gain,
    attention_in,
    attention_out,
    feed_gain,
    feed_up,
    feed_up_bias,
    feed_down,
    feed_down_bias,
):
    bf16 = jnp.bfloat16
    f32 = jnp.float32
    _, half, model = tokens.shape
    length = 2 * half
    hidden_width = feed_up.shape[1]
    size = lax.axis_size("dp")
    me = lax.axis_index("seq")
    dp = lax.axis_index("dp")
    place = jnp.stack([dp % 2, me]).astype(jnp.int32)
    swap = swap_pairs(2, 1)
    shape = jax.ShapeDtypeStruct

    def mine(array):
        return lax.dynamic_index_in_dim(array, me, 0, False)

    def theirs(array):
        return lax.dynamic_index_in_dim(array, 1 - me, 0, False)

    other = lax.ppermute(theirs(tokens), "seq", swap)
    positions = me * half + jnp.arange(half, dtype=jnp.int32)
    live = (positions[None, :] >= prefix_length[:, None]) & (suffix_mask == 1)
    live_cot = jnp.where(live[:, :, None], cotangent, jnp.zeros_like(cotangent))
    own_cot = mine(live_cot)
    other_cot = lax.ppermute(theirs(live_cot), "seq", swap)

    modulation = jnp.einsum(
        "c,oc->o", mine(time_embedding), modulation_weight, preferred_element_type=f32
    ) + modulation_bias.astype(f32)
    modulation = modulation.reshape(6, model)
    gain_one = attention_gain.astype(f32)[None]
    gain_two = feed_gain.astype(f32)[None]
    cosine, sines = turn_tables(length)
    table = pl.BlockSpec((None, length, 128), lambda i, p: (p[1], 0, 0))
    own_rows = pl.BlockSpec((None, half, model), lambda i, p: (p[1], 0, 0))
    blocks = half // T_ROWS

    def project(source, spec, start, alias):
        turn = pl.BlockSpec((None, T_ROWS, 128), lambda i, p: (p[1], i + start, 0))
        return call(
            lambda p, *refs: project_kernel(*refs),
            (blocks,),
            place,
            [spec, whole(6, model), whole(1, model), whole(model, 3 * model), turn, turn],
            [
                pl.BlockSpec((model, T_ROWS), lambda i, p: (0, i + start)),
                pl.BlockSpec((T_ROWS, 3 * model), lambda i, p: (i + start, 0)),
            ],
            [shape((model, length), bf16), shape((length, 3 * model), bf16)],
            [],
            (source, modulation, gain_one, attention_in, cosine, sines),
            "project",
            length * model * 3 * model,
            6 * MIB,
            alias=alias,
        )

    kept = project(tokens, pl.BlockSpec((None, T_ROWS, model), lambda i, p: (p[1], i, 0)), 0, ())
    first_t, qkv = project(other, pl.BlockSpec((T_ROWS, model), lambda i, p: (i, 0)), blocks, kept)
    def column(k):
        return pl.BlockSpec((length, 128), lambda h, p: (0, h + k))

    pairs = model // 128
    exps_block = pl.BlockSpec((2, length, length), lambda h, p: (h, 0, 0))
    attended, exps, inverses = call(
        lambda p, *refs: attend_kernel(*refs),
        (pairs,),
        place,
        [column(0), column(pairs), column(2 * pairs)],
        [column(0), exps_block, column(0)],
        [shape((length, model), bf16), shape((HEADS, length, length), bf16), shape((length, model), f32)],
        [],
        (qkv, qkv, qkv),
        "attend",
        16 * length * length * model,
        32 * MIB,
    )

    tiles = 4
    width = hidden_width // tiles
    groups = size // 2
    share_rows = hidden_width // size
    model_rows = model // size
    down_block = pl.BlockSpec((groups // tiles, share_rows, model), lambda j, p: (j, 0, 0))
    up_block = pl.BlockSpec((groups, None, model_rows, width), lambda j, p: (0, j, 0, 0))
    out_block = whole(groups, model_rows, model)
    (
        own_out,
        other_out,
        grad_middle,
        grad_attended,
        mid_rows,
        up_bias_grad,
        down_keep,
        down_send,
        up_keep,
        up_send,
        out_keep,
        out_send,
    ) = call(
        middle_kernel,
        (tiles,),
        place,
        [own_rows] + [whole(half, model)] * 3
        + [
            whole(length, model),
            whole(6, model),
            whole(1, model),
            whole(model, model),
            pl.BlockSpec((model, width), lambda j, p: (0, j)),
            pl.BlockSpec((1, width), lambda j, p: (0, j)),
            pl.BlockSpec((width, model), lambda j, p: (j, 0)),
            whole(1, model),
        ],
        [
            own_rows,
            whole(half, model),
            whole(length, model),
            whole(length, model),
            whole(6, model),
            pl.BlockSpec((1, width), lambda j, p: (0, j)),
            down_block,
            down_block,
            up_block,
            up_block,
            out_block,
            out_block,
        ],
        [shape((2, half, model), bf16), shape((half, model), bf16)]
        + [shape((length, model), f32), shape((length, model), bf16), shape((6, model), f32), shape((1, hidden_width), f32)]
        + [shape((groups, share_rows, model), bf16)] * 2
        + [shape((groups, tiles, model_rows, width), bf16)] * 2
        + [shape((groups, model_rows, model), bf16)] * 2,
        [
            pltpu.VMEM((length, model), f32),
            pltpu.VMEM((model, length), bf16),
            pltpu.VMEM((length, model), bf16),
            pltpu.VMEM((model, length), bf16),
            pltpu.VMEM((length, model), bf16),
            pltpu.VMEM((length, model), f32),
            pltpu.VMEM((length, model), f32),
            pltpu.VMEM((width, length), bf16),
            pltpu.VMEM((length, width), bf16),
        ],
        (
            tokens,
            other,
            own_cot,
            other_cot,
            attended,
            modulation,
            gain_two,
            attention_out,
            feed_up,
            feed_up_bias.astype(f32)[None],
            feed_down,
            feed_down_bias.astype(f32)[None],
        ),
        "middle",
        12 * length * model * hidden_width + 6 * length * model * model,
        36 * MIB,
    )
    got_out = lax.ppermute(other_out, "seq", swap)
    merge = (groups, hidden_width // size, model)

    def near(k):
        return pl.BlockSpec((length, 128), lambda h: (0, jnp.minimum(h, pairs - 1) + k))

    def fixed(*dims):
        return pl.BlockSpec(dims, lambda h: (0,) * len(dims), pipeline_mode=pl.Buffered(1))

    turn = pl.BlockSpec((None, length, 128), lambda h: (lax.axis_index("seq"), 0, 0), pipeline_mode=pl.Buffered(1))
    own_part = pl.BlockSpec((None, half, model), lambda h: (lax.axis_index("seq"), 0, 0), pipeline_mode=pl.Buffered(1))
    anywhere = pl.BlockSpec(memory_space=pl.ANY)
    scratch = [
        pltpu.VMEM((length, length), bf16),
        pltpu.VMEM((length, 128), f32),
        pltpu.VMEM((length, 3 * model), bf16),
        pltpu.VMEM((length, model), bf16),
        pltpu.SemaphoreType.DMA((2, BACK_COPIES + 1)),
        pltpu.SemaphoreType.DMA((4,)),
    ]
    for (_, piece_rows, order), sent in zip(BACK_PIECES, (False,) * 3 + (True,) * 3):
        scratch += piece_scratch(piece_rows, order, model, sent)
    tokens_grad, sums, down_grad, up_grad, out_grad, in_grad = pl.pallas_call(
        back_kernel,
        grid=(pairs + 2,),
        in_specs=[
            near(0),
            near(pairs),
            near(2 * pairs),
            near(0),
            near(0),
            pl.BlockSpec((2, length, length), lambda h: (jnp.minimum(h, pairs - 1), 0, 0)),
            near(0),
            turn,
            turn,
            fixed(model, length),
            fixed(model, 3 * model),
            own_part,
            fixed(half, model),
            pl.BlockSpec((half, model), lambda h: (jnp.where(h > pairs, 0, 1), 0)),
            fixed(6, model),
            fixed(1, model),
        ]
        + [anywhere] * 6,
        out_specs=[
            anywhere,
            fixed(2, model),
            fixed(hidden_width // size, model),
            fixed(model_rows, hidden_width),
            fixed(model_rows, model),
            fixed(model_rows, 3 * model),
        ],
        out_shape=[
            shape((2, half, model), bf16),
            shape((2, model), f32),
            shape((hidden_width // size, model), f32),
            shape((model_rows, hidden_width), f32),
            shape((model_rows, model), f32),
            shape((model_rows, 3 * model), f32),
        ],
        scratch_shapes=scratch,
        compiler_params=pltpu.CompilerParams(vmem_limit_bytes=63 * MIB, collective_id=0, has_side_effects=True),
        cost_estimate=pl.CostEstimate(flops=40 * length * length * model, bytes_accessed=60 * MIB, transcendentals=0),
        name="back",
    )(
        qkv,
        qkv,
        qkv,
        attended,
        grad_attended,
        exps,
        inverses,
        cosine,
        sines,
        first_t,
        attention_in,
        tokens,
        other,
        grad_middle,
        modulation,
        gain_one,
        down_keep,
        down_send,
        up_keep.reshape(merge),
        up_send.reshape(merge),
        out_keep,
        out_send,
    )
    in_rows = [sums[0], sums[1] * gain_one[0], sums[1] * (1.0 + modulation[1])]
    block_output = lax.dynamic_update_index_in_dim(own_out, got_out, 1 - me, 0)

    grad_modulation = jnp.concatenate([in_rows[0], in_rows[1], mid_rows[0:4].reshape(-1)])
    own_time = jnp.einsum("o,oc->c", grad_modulation, modulation_weight.astype(f32), precision=highest)
    got_time = lax.ppermute(own_time, "seq", swap)
    time_grad = jnp.where(me == 0, jnp.stack([own_time, got_time]), jnp.stack([got_time, own_time]))

    vectors = [grad_modulation, in_rows[2], mid_rows[4], up_bias_grad[0], mid_rows[5], mine(time_embedding).astype(f32)]
    vectors = jnp.concatenate(vectors)
    everyone = lax.all_gather(vectors, ("dp", "seq"), axis=0)

    def shard_of(start, width):
        rows = width // size
        return lax.dynamic_slice_in_dim(everyone, start + dp * rows, rows, 1)

    modulation_part = shard_of(0, 6 * model)
    modulation_weight_grad = jnp.einsum("so,sc->oc", modulation_part, everyone[:, 9 * model + hidden_width :], precision=highest)
    starts = (6 * model, 7 * model, 8 * model, 8 * model + hidden_width)
    widths = (model, model, hidden_width, model)
    gain_grad, feed_gain_grad, feed_up_bias_grad, feed_down_bias_grad = [
        jnp.sum(shard_of(a, w), 0) for a, w in zip(starts, widths)
    ]
    return (
        block_output,
        tokens_grad,
        time_grad,
        modulation_weight_grad,
        jnp.sum(modulation_part, 0),
        gain_grad,
        in_grad,
        out_grad,
        feed_gain_grad,
        up_grad,
        feed_up_bias_grad,
        down_grad,
        feed_down_bias_grad,
    )


def body(tokens, *rest):
    sequences, half, model = tokens.shape
    size = lax.axis_size("dp")
    fits = model % (16 * size) == 0 and half % T_ROWS == 0
    fits = fits and size == 16 and lax.axis_size("seq") == 2 and sequences == 2
    return (fast_body if fits else general_body)(tokens, *rest)


def solution(mesh):
    return jax.shard_map(
        body,
        mesh=mesh,
        in_specs=(
            P("dp", "seq", None),
            P("dp", None),
            P("dp"),
            P("dp", "seq"),
            P("dp", "seq", None),
            P(),
            P(),
            P(),
            P(),
            P(),
            P(),
            P(),
            P(),
            P(),
            P(),
        ),
        out_specs=(
            P("dp", "seq", None),
            P("dp", "seq", None),
            P("dp", None),
            P("dp", None),
            P("dp"),
            P("dp"),
            P("dp", None),
            P("dp", None),
            P("dp"),
            P("dp", None),
            P("dp"),
            P("dp", None),
            P("dp"),
        ),
        check_vma=False,
    )
```

```python
import functools
from functools import partial

import jax
import jax.numpy as jnp
import numpy as np
from jax import lax
from jax.experimental import pallas as pl
from jax.experimental.pallas import tpu as pltpu
from jax.sharding import PartitionSpec as P

HEADS = 12
HD = 64


highest = lax.Precision.HIGHEST


def as_sent(shard):

    def short(part):
        return part.astype(jnp.bfloat16) if part.dtype == jnp.float32 else part

    return jax.tree.map(short, shard)


def normalize(values):
    centre = values - jnp.mean(values, -1, keepdims=True)
    spread = jnp.mean(centre * centre, -1, keepdims=True)
    return centre * lax.rsqrt(spread + 1e-05)


def modulate(values, scaling, shifts, scales):
    return normalize(values) * scaling * (1.0 + scales) + shifts


def rotate(values, cosine, sines, direction):
    halves = values.shape[-1] // 2
    former = values[..., :halves]
    latter = values[..., halves:]
    cosine = cosine[None, :, None, :]
    sines = direction * sines[None, :, None, :]
    return jnp.concatenate([former * cosine - latter * sines, latter * cosine + former * sines], -1)


def attend_forward(stacked):
    query_rows = stacked[:, 0]
    key_rows = stacked[:, 1]
    value_rows = stacked[:, 2]
    length = query_rows.shape[0]
    block_rows = min(512, length)
    pieces = []
    logsums = []
    for offset in range(0, length, block_rows):
        query_block = query_rows[offset : offset + block_rows]
        scores = (
            jnp.einsum("qhd,khd->hqk", query_block, key_rows, preferred_element_type=jnp.float32)
            * 0.125
        )
        largest = jnp.max(scores, -1, keepdims=True)
        exponentials = jnp.exp(scores - largest)
        totals = jnp.sum(exponentials, -1, keepdims=True)
        probability = (exponentials / totals).astype(jnp.bfloat16)
        pieces.append(
            jnp.einsum("hqk,khd->qhd", probability, value_rows, preferred_element_type=jnp.float32)
        )
        logsums.append((largest + jnp.log(totals))[..., 0])
    return (jnp.concatenate(pieces, 0).astype(jnp.bfloat16), jnp.concatenate(logsums, 1))


def attend_backward(operands):
    stacked, grad_attended, logsums = operands
    query_rows = stacked[:, 0]
    key_rows = stacked[:, 1]
    value_rows = stacked[:, 2]
    length = query_rows.shape[0]
    block_rows = min(512, length)
    grad_query = []
    grad_keys = jnp.zeros(key_rows.shape, jnp.float32)
    grad_values = jnp.zeros(value_rows.shape, jnp.float32)
    for offset in range(0, length, block_rows):
        query_block = query_rows[offset : offset + block_rows]
        grad_block = grad_attended[offset : offset + block_rows]
        scores = (
            jnp.einsum("qhd,khd->hqk", query_block, key_rows, preferred_element_type=jnp.float32)
            * 0.125
        )
        probability = jnp.exp(scores - logsums[:, offset : offset + block_rows, None])
        grad_probs = jnp.einsum(
            "qhd,khd->hqk", grad_block, value_rows, preferred_element_type=jnp.float32
        )
        row_dots = jnp.sum(probability * grad_probs, -1, keepdims=True)
        grad_scores = (probability * (grad_probs - row_dots)).astype(jnp.bfloat16)
        grad_query.append(
            (
                jnp.einsum(
                    "hqk,khd->qhd", grad_scores, key_rows, preferred_element_type=jnp.float32
                )
                * 0.125
            ).astype(jnp.bfloat16)
        )
        grad_keys = grad_keys + jnp.einsum(
            "hqk,qhd->khd", grad_scores, query_block, preferred_element_type=jnp.float32
        )
        grad_values = grad_values + jnp.einsum(
            "hqk,qhd->khd",
            probability.astype(jnp.bfloat16),
            grad_block,
            preferred_element_type=jnp.float32,
        )
    return jnp.stack(
        [
            jnp.concatenate(grad_query, 0),
            (grad_keys * 0.125).astype(jnp.bfloat16),
            grad_values.astype(jnp.bfloat16),
        ],
        1,
    )


def general_body(
    tokens,
    time_embedding,
    prefix_length,
    suffix_mask,
    cotangent,
    modulation_weight,
    modulation_bias,
    attention_gain,
    attention_in,
    attention_out,
    feed_gain,
    feed_up,
    feed_up_bias,
    feed_down,
    feed_down_bias,
):
    sequences, local_len, model_width = tokens.shape
    groups = lax.axis_size("seq")
    data_size = lax.axis_size("dp")
    length = local_len * groups
    heads_local = HEADS // groups
    group_width = model_width // groups
    modulation = jnp.einsum(
        "sc,oc->so", time_embedding, modulation_weight, preferred_element_type=jnp.float32
    ) + modulation_bias.astype(jnp.float32)
    shift_one, scale_one, gate_one, shift_two, scale_two, gate_two = [
        portion[:, None, :] for portion in jnp.split(modulation, 6, axis=1)
    ]
    inputs = tokens.astype(jnp.float32)
    first_float, first_back = jax.vjp(
        modulate, inputs, attention_gain.astype(jnp.float32), shift_one, scale_one
    )
    first_input = first_float.astype(jnp.bfloat16)
    projected = jnp.einsum(
        "spd,de->spe", first_input, attention_in, preferred_element_type=jnp.float32
    ).reshape(sequences, local_len, 3, HEADS, HD)
    position_ints = lax.axis_index("seq") * local_len + jnp.arange(local_len, dtype=jnp.int32)
    positions = position_ints.astype(jnp.float32)
    inverse = 10000.0 ** (-jnp.arange(HD // 2, dtype=jnp.float32) * 2.0 / HD)
    angles = positions[:, None] * inverse[None, :]
    cosine = jnp.cos(angles)
    sines = jnp.sin(angles)
    rotated = jnp.stack(
        [
            rotate(projected[:, :, 0], cosine, sines, 1.0),
            rotate(projected[:, :, 1], cosine, sines, 1.0),
            projected[:, :, 2],
        ],
        2,
    ).astype(jnp.bfloat16)
    by_heads = lax.all_to_all(
        rotated.reshape(sequences, local_len, 3, groups, group_width),
        "seq",
        split_axis=3,
        concat_axis=1,
        tiled=True,
    )
    by_heads = by_heads.reshape(sequences, length, 3, heads_local, HD)
    attended_heads, logsums = lax.map(attend_forward, by_heads)
    attended = lax.all_to_all(
        as_sent(attended_heads.reshape(sequences, length, 1, group_width)),
        "seq",
        split_axis=1,
        concat_axis=2,
        tiled=True,
    )
    attended = attended.reshape(sequences, local_len, model_width)
    branch_one = jnp.einsum(
        "spd,de->spe", attended, attention_out, preferred_element_type=jnp.float32
    )
    middle = inputs + gate_one * branch_one
    second_float, second_back = jax.vjp(
        modulate, middle, feed_gain.astype(jnp.float32), shift_two, scale_two
    )
    second_input = second_float.astype(jnp.bfloat16)
    hidden = jnp.einsum(
        "spd,df->spf", second_input, feed_up, preferred_element_type=jnp.float32
    ) + feed_up_bias.astype(jnp.float32)
    activated_float, gelu_back = jax.vjp(partial(jax.nn.gelu, approximate=True), hidden)
    activated = activated_float.astype(jnp.bfloat16)
    branch_two = jnp.einsum(
        "spf,fd->spd", activated, feed_down, preferred_element_type=jnp.float32
    ) + feed_down_bias.astype(jnp.float32)
    block_output = (middle + gate_two * branch_two).astype(jnp.bfloat16)
    live_rows = ((position_ints[None, :] >= prefix_length[:, None]) & (suffix_mask == 1)).astype(
        jnp.float32
    )
    grad_output = cotangent.astype(jnp.float32) * live_rows[:, :, None]
    grad_gate_two = jnp.sum(grad_output * branch_two, axis=1)
    grad_branch_two = (gate_two * grad_output).astype(jnp.bfloat16)
    feed_down_bias_grad = jnp.sum(grad_branch_two.astype(jnp.float32), axis=(0, 1))
    feed_down_grad = jnp.einsum(
        "spf,spd->fd", activated, grad_branch_two, preferred_element_type=jnp.float32
    )
    grad_activated = jnp.einsum(
        "spd,fd->spf", grad_branch_two, feed_down, preferred_element_type=jnp.float32
    )
    grad_hidden = gelu_back(grad_activated)[0].astype(jnp.bfloat16)
    feed_up_bias_grad = jnp.sum(grad_hidden.astype(jnp.float32), axis=(0, 1))
    feed_up_grad = jnp.einsum(
        "spd,spf->df", second_input, grad_hidden, preferred_element_type=jnp.float32
    )
    grad_second = jnp.einsum(
        "spf,df->spd", grad_hidden, feed_up, preferred_element_type=jnp.float32
    )
    grad_from_norm, feed_gain_grad, grad_shift_two, grad_scale_two = second_back(grad_second)
    grad_middle = grad_output + grad_from_norm
    grad_gate_one = jnp.sum(grad_middle * branch_one, axis=1)
    grad_branch_one = (gate_one * grad_middle).astype(jnp.bfloat16)
    attention_out_grad = jnp.einsum(
        "spd,spe->de", attended, grad_branch_one, preferred_element_type=jnp.float32
    )
    grad_attended = jnp.einsum(
        "spe,de->spd", grad_branch_one, attention_out, preferred_element_type=jnp.float32
    ).astype(jnp.bfloat16)
    grad_heads = lax.all_to_all(
        grad_attended.reshape(sequences, local_len, groups, group_width),
        "seq",
        split_axis=2,
        concat_axis=1,
        tiled=True,
    )
    grad_heads = grad_heads.reshape(sequences, length, heads_local, HD)
    grad_stacked = lax.map(attend_backward, (by_heads, grad_heads, logsums))
    grad_positions = lax.all_to_all(
        as_sent(grad_stacked.reshape(sequences, length, 3, 1, group_width)),
        "seq",
        split_axis=1,
        concat_axis=3,
        tiled=True,
    )
    grad_positions = grad_positions.reshape(sequences, local_len, 3, HEADS, HD).astype(jnp.float32)
    grad_projected = jnp.stack(
        [
            rotate(grad_positions[:, :, 0], cosine, sines, -1.0),
            rotate(grad_positions[:, :, 1], cosine, sines, -1.0),
            grad_positions[:, :, 2],
        ],
        2,
    ).astype(jnp.bfloat16)
    grad_projected = grad_projected.reshape(sequences, local_len, 3 * model_width)
    attention_in_grad = jnp.einsum(
        "spd,spe->de", first_input, grad_projected, preferred_element_type=jnp.float32
    )
    grad_first = jnp.einsum(
        "spe,de->spd", grad_projected, attention_in, preferred_element_type=jnp.float32
    )
    grad_tokens_norm, attention_gain_grad, grad_shift_one, grad_scale_one = first_back(grad_first)
    tokens_grad = (grad_middle + grad_tokens_norm).astype(jnp.bfloat16)
    grad_modulation = jnp.concatenate(
        [
            grad_shift_one[:, 0],
            grad_scale_one[:, 0],
            grad_gate_one,
            grad_shift_two[:, 0],
            grad_scale_two[:, 0],
            grad_gate_two,
        ],
        1,
    )
    modulation_total = lax.psum(grad_modulation.astype(jnp.bfloat16), "seq").astype(jnp.float32)
    time_grad = jnp.einsum(
        "so,oc->sc", modulation_total, modulation_weight.astype(jnp.float32), precision=highest
    )
    modulation_weight_grad = jnp.einsum(
        "so,sc->oc", grad_modulation, time_embedding.astype(jnp.float32), precision=highest
    )
    modulation_bias_grad = jnp.sum(grad_modulation, axis=0)
    gradients = (
        modulation_weight_grad,
        modulation_bias_grad,
        attention_gain_grad,
        attention_in_grad,
        attention_out_grad,
        feed_gain_grad,
        feed_up_grad,
        feed_up_bias_grad,
        feed_down_grad,
        feed_down_bias_grad,
    )
    flattened = tuple((g.reshape(data_size, -1) for g in gradients))
    shares = lax.psum_scatter(flattened, "dp", scatter_dimension=0, tiled=True)
    summed = jax.tree.map(lambda part: part.astype(jnp.float32), lax.psum(as_sent(shares), "seq"))
    shards = tuple(
        (s.reshape((g.shape[0] // data_size,) + g.shape[1:]) for s, g in zip(summed, gradients))
    )
    return (
        block_output,
        tokens_grad,
        time_grad,
        shards[0],
        shards[1],
        shards[2],
        shards[3],
        shards[4],
        shards[5],
        shards[6],
        shards[7],
        shards[8],
        shards[9],
    )


T_ROWS = 256
MIDDLE_ROWS = 512
PROJECT_ROWS = 512
MIB = 1 << 20


def dot(a, b, ca, cb):
    return lax.dot_general(a, b, (((ca,), (cb,)), ((), ())), preferred_element_type=jnp.float32)


def params(limit=60):
    return pltpu.CompilerParams(vmem_limit_bytes=limit * MIB)


def norm_rows(values):
    centre = values - jnp.mean(values, -1, keepdims=True)
    inverse = lax.rsqrt(jnp.mean(centre * centre, -1, keepdims=True) + 1e-05)
    return centre * inverse, inverse


def swap_halves(values, lane):
    left = pltpu.roll(values, 96, 1)
    right = pltpu.roll(values, 32, 1)
    return jnp.where(lane % 64 < 32, left, right)


def project_kernel(source_ref, mod_ref, gain_ref, weight_ref, cos_ref, sin_ref, first_t_ref, qkv_ref):
    rows, model = source_ref.shape
    lane = lax.broadcasted_iota(jnp.int32, (rows, 128), 1)
    scaling = gain_ref[...] * (1.0 + mod_ref[1:2])
    normed, _ = norm_rows(source_ref[...].astype(jnp.float32))
    first = (normed * scaling + mod_ref[0:1]).astype(jnp.bfloat16)
    first_t_ref[...] = first.T
    for part in range(3):
        projected = dot(first, weight_ref[:, part * model : (part + 1) * model], 1, 0)
        for block in range(model // 128):
            piece = projected[:, block * 128 : (block + 1) * 128]
            if part < 2:
                piece = piece * cos_ref[...] + swap_halves(piece, lane) * sin_ref[...]
            piece = piece.astype(jnp.bfloat16)
            if part == 0:
                piece = piece * 0.125
            column = part * model + block * 128
            qkv_ref[:, column : column + 128] = piece


def attend_kernel(q_ref, k_ref, v_ref, out_ref, exp_ref, inv_ref):
    rows = 128
    length = q_ref.shape[0]
    lane = lax.broadcasted_iota(jnp.int32, (rows, 128), 1)
    keys = k_ref[...]
    values = jnp.concatenate([v_ref[...], jnp.ones((length, 128), jnp.bfloat16)], 1)
    for chunk in range(length // rows):
        at = slice(chunk * rows, (chunk + 1) * rows)
        queries = q_ref[at]
        outs = []
        inverses = []
        for head in range(2):
            mine = jnp.where((lane < 64) == (head == 0), queries, jnp.zeros_like(queries))
            scores = dot(mine, keys, 1, 1)
            largest = jnp.max(scores, -1, keepdims=True)
            exps = jnp.exp(scores - largest).astype(jnp.bfloat16)
            exp_ref[head, at] = exps
            summed = dot(exps, values, 1, 0)
            inverse = 1.0 / summed[:, 128:256]
            outs.append(summed[:, 0:128] * inverse)
            inverses.append(inverse)
        out_ref[at] = jnp.where(lane < 64, outs[0], outs[1]).astype(jnp.bfloat16)
        inv_ref[at] = jnp.where(lane < 64, inverses[0], inverses[1])


def share(core, grad, keep_ref, send_ref, *at):
    first, second = grad
    keep_ref[at] = jnp.where(core == 0, first, second)
    send_ref[at] = jnp.where(core == 0, second, first)


def middle_kernel(
    own_ref,
    other_ref,
    own_cot_ref,
    other_cot_ref,
    attended_ref,
    mod_ref,
    gain_ref,
    out_weight_ref,
    up_ref,
    up_bias_ref,
    down_ref,
    down_bias_ref,
    own_out_ref,
    other_out_ref,
    grad_middle_ref,
    grad_attended_ref,
    rows_ref,
    up_bias_grad_ref,
    down_sum_ref,
    down_tail_ref,
    upv_sum_ref,
    upx_sum_ref,
    out_keep_ref,
    out_send_ref,
    second_t,
    grad_two,
    sum_two,
    sum_second,
    act_t,
    down_keep,
    down_give,
    down_got,
    up_keep,
    up_give,
    up_got,
    down_half,
    down_half_got,
    down_part,
    down_part_got,
    up_part,
    up_part_got,
    up_half,
    up_half_got,
    sems,
):
    rows = MIDDLE_ROWS
    step = pl.program_id(0)
    links = Links()
    core = links.bit["C"]
    tiles = down_keep.shape[0]

    per_tile = 7
    last = tiles - 1

    def first_copies(tile):
        return [
            remote(give.at[tile], got.at[tile], sems, tile * per_tile + i, links.partner["C"])
            for i, (give, got) in enumerate(((down_give, down_got), (up_give, up_got)))
        ]

    def down_copy(tile):
        return remote(down_half.at[tile], down_half_got.at[tile], sems, tile * per_tile + 2, links.partner["Y"])

    def down_on_copy(tile):
        return remote(down_part.at[tile], down_part_got.at[tile], sems, tile * per_tile + 3, links.partner["X"])

    def up_copies(tile):
        return [
            remote(up_part.at[tile, i], up_part_got.at[tile, i], sems, tile * per_tile + 4 + i, links.partner[flip])
            for i, flip in enumerate(Z_FLIPS)
        ]

    def up_last_copy():
        return remote(up_half, up_half_got, sems, last * per_tile + 4, links.partner["X"])

    def total(*terms):
        return sum(term.astype(jnp.float32) for term in terms).astype(jnp.bfloat16)

    half_rows = down_half.shape[2]
    home = pl.ds(pl.multiple_of(links.me * half_rows, 16), half_rows)
    away = pl.ds(pl.multiple_of((1 - links.me) * half_rows, 16), half_rows)
    z_at = links.bit["W"] * 2 + links.bit["Z"]

    def flipped(flip):
        values = {bit: 1 - links.bit[bit] if bit in flip else links.bit[bit] for bit in "WZ"}
        return values["W"] * 2 + values["Z"]

    def send_on(tile, final):
        for copy in first_copies(tile):
            copy.wait_recv()
        for x in range(2):
            down_half[tile, x] = total(down_keep[tile, x, away], down_got[tile, x, away])
        down_copy(tile).start()
        if final:
            for z in range(4):
                other = 2 * z + 1 - links.bit["X"]
                up_half[z] = total(up_keep[tile, other], up_got[tile, other])
            up_last_copy().start()
        else:
            for i, flip in enumerate(Z_FLIPS):
                for x in range(2):
                    other = 2 * flipped(flip) + x
                    up_part[tile, i, x] = total(up_keep[tile, other], up_got[tile, other])
            for copy in up_copies(tile):
                copy.start()

    def send_down(tile):
        down_copy(tile).wait_recv()
        x = 1 - links.bit["X"]
        down_part[tile] = total(down_keep[tile, x, home], down_got[tile, x, home], down_half_got[tile, x])
        down_on_copy(tile).start()

    def settle(tile, final):
        if final:
            down_copy(tile).wait_recv()
            for x in range(2):
                down_tail_ref[x] = total(down_keep[tile, x, home], down_got[tile, x, home], down_half_got[tile, x])
        else:
            down_on_copy(tile).wait_recv()
            x = links.bit["X"]
            terms = (down_keep[tile, x, home], down_got[tile, x, home], down_half_got[tile, x], down_part_got[tile])
            down_sum_ref[tile] = total(*terms)
        if final:
            up_last_copy().wait_recv()
            for z in range(4):
                mine = 2 * z + links.bit["X"]
                upx_sum_ref[z] = total(up_keep[tile, mine], up_got[tile, mine], up_half_got[z])
        else:
            for copy in up_copies(tile):
                copy.wait_recv()
            for x in range(2):
                mine = 2 * z_at + x
                got = [up_part_got[tile, i, x] for i in range(3)]
                upv_sum_ref[x, tile] = total(up_keep[tile, mine], up_got[tile, mine], *got)

    @pl.when(step == 0)
    def _():
        links.greet()

    half, model = own_ref.shape
    length = 2 * half
    scaling = gain_ref[...] * (1.0 + mod_ref[4:5])
    gate_one = mod_ref[2:3]
    shift_two = mod_ref[3:4]
    gate_two = mod_ref[5:6]

    def pick(first_ref, second_ref, chunk):
        at = chunk * rows
        return (first_ref if at < half else second_ref)[at % half : at % half + rows]

    @pl.when(step == 0)
    def _():
        bias_grad = jnp.zeros((1, model), jnp.float32)
        for chunk in range(length // rows):
            at = slice(chunk * rows, (chunk + 1) * rows)
            branch = dot(attended_ref[at], out_weight_ref[...], 1, 0)
            grad_middle_ref[at] = branch
            sum_two[at] = jnp.zeros((rows, model), jnp.float32)
            sum_second[at] = jnp.zeros((rows, model), jnp.float32)
            middle = pick(own_ref, other_ref, chunk).astype(jnp.float32) + gate_one * branch
            normed, _ = norm_rows(middle)
            rounded = (normed * scaling + shift_two).astype(jnp.bfloat16)
            place = (chunk * rows) % half
            (own_out_ref if chunk * rows < half else other_out_ref)[place : place + rows] = rounded
            second_t[:, at] = rounded.T
            grad = (gate_two * pick(own_cot_ref, other_cot_ref, chunk).astype(jnp.float32)).astype(jnp.bfloat16)
            grad_two[at] = grad
            bias_grad = bias_grad + jnp.sum(grad.astype(jnp.float32), 0, keepdims=True)
        rows_ref[5:6] = bias_grad

    up = up_ref[...]
    down = down_ref[...]
    width = up.shape[1]
    bias_sum = jnp.zeros((1, width), jnp.float32)
    for chunk in range(length // rows):
        if chunk * rows == half:

            @pl.when(step > 0)
            def _():
                send_on(step - 1, False)

            @pl.when(step > 1)
            def _():
                send_down(step - 2)

        at = slice(chunk * rows, (chunk + 1) * rows)
        hidden = dot(pick(own_out_ref, other_out_ref, chunk), up, 1, 0) + up_bias_ref[...]
        squared = hidden * hidden
        tanh = jnp.tanh(hidden * (0.7978845608028654 + 0.035677408136300125 * squared))
        gate = 0.5 + 0.5 * tanh
        activated = (hidden * gate).astype(jnp.bfloat16)
        slope = gate + (0.5 * hidden) * (1.0 - tanh * tanh) * (0.7978845608028654 + 0.10703222440890037 * squared)
        act_t[:, at] = activated.T
        grad = (slope * dot(grad_two[at], down, 1, 1)).astype(jnp.bfloat16)
        grad_attended_ref[at] = grad
        bias_sum = bias_sum + jnp.sum(grad.astype(jnp.float32), 0, keepdims=True)
        sum_two[at] += dot(activated, down, 1, 0)
        sum_second[at] += dot(grad, up, 1, 1)

    up_bias_grad_ref[...] = bias_sum
    down_grad = dot(act_t[...], grad_two[...], 1, 0).astype(jnp.bfloat16).reshape(2, 2, -1, model)
    share(core, (down_grad[:, 0], down_grad[:, 1]), down_keep, down_give, step)
    up_grad = dot(second_t[...], grad_attended_ref[...], 1, 0).astype(jnp.bfloat16).reshape(up_keep.shape[1], 2, -1, width)
    share(core, (up_grad[:, 0], up_grad[:, 1]), up_keep, up_give, step)
    for copy in first_copies(step):
        copy.start()

    @pl.when(step == pl.num_programs(0) - 1)
    def _():
        sums = [jnp.zeros((1, model), jnp.float32) for _ in range(4)]
        for chunk in range(length // rows):
            at = slice(chunk * rows, (chunk + 1) * rows)
            branch = grad_middle_ref[at]
            middle = pick(own_ref, other_ref, chunk).astype(jnp.float32) + gate_one * branch
            normed, inverse = norm_rows(middle)
            branch_two = sum_two[at] + down_bias_ref[...]
            output = (middle + gate_two * branch_two).astype(jnp.bfloat16)
            place = (chunk * rows) % half
            (own_out_ref if chunk * rows < half else other_out_ref)[place : place + rows] = output
            cot = pick(own_cot_ref, other_cot_ref, chunk).astype(jnp.float32)
            grad = sum_second[at]
            weighted = grad * normed
            scaled = grad * scaling
            inner = jnp.mean(weighted * scaling, -1, keepdims=True)
            grad_middle = cot + (scaled - jnp.mean(scaled, -1, keepdims=True) - normed * inner) * inverse
            grad_middle_ref[at] = grad_middle
            grad_one = (gate_one * grad_middle).astype(jnp.bfloat16)
            grad_two[at] = grad_one
            act_t[:, at] = attended_ref[at].T
            grad_attended_ref[at] = dot(grad_one, out_weight_ref[...], 1, 1).astype(jnp.bfloat16)
            for i, term in enumerate((grad_middle * branch, grad, weighted, cot * branch_two)):
                sums[i] = sums[i] + jnp.sum(term, 0, keepdims=True)
            if (chunk + 1) * rows == half:
                send_on(last, True)
                send_down(last - 1)
        rows_ref[0:1] = sums[0]
        rows_ref[1:2] = sums[1]
        rows_ref[2:3] = sums[2] * gain_ref[...]
        rows_ref[3:4] = sums[3]
        rows_ref[4:5] = sums[2] * (1.0 + mod_ref[4:5])
        out_grad = dot(act_t[...], grad_two[...], 1, 0).astype(jnp.bfloat16)
        out_grad = out_grad.reshape(out_keep_ref.shape[0], 2, -1, model)
        share(core, (out_grad[:, 0], out_grad[:, 1]), out_keep_ref, out_send_ref, Ellipsis)
        for tile in range(last):
            settle(tile, False)
        settle(last, True)
        for tile in range(tiles):
            ups = [up_last_copy()] if tile == last else up_copies(tile)
            for copy in first_copies(tile) + [down_copy(tile)] + ([] if tile == last else [down_on_copy(tile)]) + ups:
                copy.wait_send()


Z_FLIPS = ("Z", "W", "ZW")


class Links:
    def __init__(self):
        dp = lax.axis_index("dp")
        self.me = lax.axis_index("seq")
        self.bit = {"C": dp % 2, "X": (dp // 2) % 2, "Z": (dp // 4) % 2, "W": (dp // 8) % 2, "Y": self.me}
        jump = {name: size * (1 - 2 * self.bit[name]) for name, size in (("C", 1), ("X", 2), ("Z", 4), ("W", 8))}
        self.partner = {name: (dp + jump[name], self.me) for name in "CXZW"}
        self.partner["ZW"] = (dp + jump["Z"] + jump["W"], self.me)
        self.partner["Y"] = (dp, 1 - self.me)

    def place(self):
        return self.me * 16 + self.bit["X"] * 8 + self.bit["W"] * 4 + self.bit["Z"] * 2 + self.bit["C"]

    def greet(self):
        barrier = pltpu.get_barrier_semaphore()
        for device in self.partner.values():
            pl.semaphore_signal(barrier, inc=1, device_id=device, device_id_type=pl.DeviceIdType.MESH)
        pl.semaphore_wait(barrier, len(self.partner))


def flips_of(kind):
    return Z_FLIPS if kind == "V" else (kind,)


def remote(source, target, sems, slot, device):
    return pltpu.make_async_remote_copy(
        src_ref=source,
        dst_ref=target,
        send_sem=sems.at[0, slot],
        recv_sem=sems.at[1, slot],
        device_id=device,
        device_id_type=pl.DeviceIdType.MESH,
    )


def piece_scratch(spec):
    _, rows, width, left, order, kind = spec
    count = 1 << len(left)
    shapes = [count] * (1 + ("summed", "given", "made").index(kind))
    for step in order:
        count //= 4 if step == "V" else 2
        shapes += [count * len(flips_of(step))] * 2
    shapes += [1] * 2
    return [pltpu.VMEM((c, rows, width), jnp.bfloat16) for c in shapes]


class Piece:
    def __init__(self, links, refs, spec, sems, slot, source=None, split=False):
        refs = list(refs)
        _, _, _, left, order, kind = spec
        self.links = links
        self.sems = sems
        self.slot = slot
        self.order = list(order)
        self.split = split
        self.left = list(left)
        self.keep = refs.pop(0)
        self.terms = [(self.keep, list(self.left))]
        self.copies = []
        self.flying = []
        if kind != "summed":
            first = refs.pop(0)
            self.source = refs.pop(0) if kind == "made" else source
            copy = (self.source, first, sems, slot, links.partner["C"])
            self.slot += 1
            self.copies.append(copy)
            self.flying = [(copy, first, list(self.left))]
        self.buffers = refs

    def launch(self, source, target, flip):
        copy = (source, target, self.sems, self.slot, self.links.partner[flip])
        self.slot += 1
        remote(*copy).start()
        self.copies.append(copy)
        self.flying.append((copy, target, list(self.left)))

    def begin(self):
        remote(*self.copies[0]).start()

    def arrive(self):
        for copy, target, bits in self.flying:
            remote(*copy).wait_recv()
            self.terms.append((target, bits))
        self.flying = []

    def index(self, bits, values):
        at = 0
        for bit in bits:
            at = at * 2 + values[bit]
        return at

    def add(self, out, flip):
        links = self.links
        rows = out.shape[1]
        block = 48
        for combo in range(1 << len(self.left)):
            values = dict(links.bit)
            for bit in flip:
                values[bit] = 1 - links.bit[bit]
            for place, bit in enumerate(self.left):
                values[bit] = (combo >> (len(self.left) - 1 - place)) & 1
            indices = [self.index(bits, values) for _, bits in self.terms]

            def some(i, carry, indices=indices, combo=combo):
                at = pl.ds(pl.multiple_of(i * block, 16), block)
                total = None
                for (ref, _), index in zip(self.terms, indices):
                    term = ref[index, at, :].astype(jnp.float32)
                    total = term if total is None else total + term
                out[combo, at, :] = total.astype(jnp.bfloat16)
                return carry

            lax.fori_loop(0, rows // block, some, 0)

    def step(self):
        self.arrive()
        kind = self.order.pop(0)
        out, target = self.buffers.pop(0), self.buffers.pop(0)
        for bit in "WZ" if kind == "V" else kind:
            self.left.remove(bit)
        count = 1 << len(self.left)
        for i, flip in enumerate(flips_of(kind)):
            part = pl.ds(i * count, count)
            self.add(out.at[part], flip)
            self.launch(out.at[part], target.at[part], flip)

    def last(self):
        self.arrive()
        self.total, self.got = self.buffers.pop(0), self.buffers.pop(0)
        self.add(self.total, "")
        self.launch(self.total, self.got, "Y")

    def result(self, store):
        remote(*self.flying[0][0]).wait_recv()
        rows = self.total.shape[1]
        total = self.total[0].astype(jnp.float32)
        got = self.got[0].astype(jnp.float32)
        if self.split:
            store(pl.ds(pl.multiple_of(self.links.me * rows, 8), rows), total)
            store(pl.ds(pl.multiple_of((1 - self.links.me) * rows, 8), rows), got)
        else:
            store(slice(0, rows), total + got)


CHUNKS = (3, 2, 1)
BACK_PIECES = (
    ("down", 96, 768, "WZ", "V", "summed"),
    ("upv", 144, 768, "X", "X", "summed"),
    ("upx", 48, 768, "WZ", "V", "summed"),
    ("out", 48, 768, "WZX", "XV", "given"),
    *((f"in{i}", 48, 384 * pairs, "WZX", "XV", "made") for i, pairs in enumerate(CHUNKS)),
)


def copies_of(spec):
    return sum(len(flips_of(kind)) for kind in spec[4]) + 1 + (spec[5] != "summed")


BACK_COPIES = sum(copies_of(spec) for spec in BACK_PIECES)
HOPS = (("C",), Z_FLIPS, ("X",), ("Y",))
SPREAD = "XZWCY"


def spread_copies(links, array, sems, slot, number):
    place = links.place()
    have = (1, 2, 8, 16)[number]
    part = array.at[pl.ds((place // have) * have, have)]
    slot += (0, 1, 4, 5)[number]
    return [remote(part, part, sems, slot + i, links.partner[flip]) for i, flip in enumerate(HOPS[number])]


def start_all(copies):
    for copy in copies:
        copy.start()


def receive_all(copies):
    for copy in copies:
        copy.wait_recv()


def back_kernel(
    q_ref,
    k_ref,
    v_ref,
    out_ref,
    grad_ref,
    exp_ref,
    inv_ref,
    cos_ref,
    sin_ref,
    first_t_hbm,
    weight_hbm,
    own_hbm,
    other_hbm,
    grad_middle_hbm,
    mod_ref,
    gain_ref,
    down_keep,
    down_tail_hbm,
    upv_keep,
    upx_keep,
    out_keep,
    out_send,
    mid_rows_ref,
    up_bias_ref,
    time_ref,
    mod_weight_hbm,
    other_block_ref,
    _,
    tokens_grad_ref,
    time_grad_ref,
    mod_weight_grad_ref,
    mod_bias_grad_ref,
    gain_grad_ref,
    feed_gain_grad_ref,
    up_bias_grad_ref,
    down_bias_grad_ref,
    down_ref,
    up_ref,
    out_grad_ref,
    in_ref,
    block_ref,
    first_t_ref,
    weight_ref,
    own_ref,
    other_ref,
    grad_middle_ref,
    mod_weight_ref,
    down_tail,
    down_tail_give,
    down_tail_got,
    ds_ref,
    dq_sum,
    proj,
    tokens_stage,
    rows_ref,
    early,
    late,
    running,
    running_got,
    by_vector,
    spread,
    spread_bias,
    turned,
    sems,
    local_sems,
    *buffers,
):
    rows = T_ROWS
    step = pl.program_id(0)
    length = q_ref.shape[0]
    half, model = other_ref.shape
    links = Links()
    core = links.bit["C"]
    pieces = []
    buffers = list(buffers)
    slot = 0
    for spec in BACK_PIECES:
        count = len(piece_scratch(spec))
        source = out_send if spec[0] == "out" else None
        pieces.append(Piece(links, buffers[:count], spec, sems, slot, source, spec[0] == "down"))
        buffers = buffers[count:]
        slot += copies_of(spec)
    down, upv, upx, out, *ins = pieces

    def fetches(first=0, end=11):
        pairs = (
            (upv_keep, upv.keep),
            (down_keep, down.keep.at[pl.ds(0, 3)]),
            (upx_keep, upx.keep),
            (out_keep, out.keep),
            (down_tail_hbm, down_tail),
            (first_t_hbm, first_t_ref),
            (weight_hbm, weight_ref),
            (other_hbm, other_ref),
            (grad_middle_hbm, grad_middle_ref),
            (own_hbm.at[links.me], own_ref),
            (mod_weight_hbm, mod_weight_ref),
        )
        return [pltpu.make_async_copy(a, b, local_sems.at[i]) for i, (a, b) in enumerate(pairs) if first <= i < end]

    place = links.place()
    dp = lax.axis_index("dp")
    early_slot = BACK_COPIES + 6
    quarter = half // 4
    late_slot = early_slot + 6
    running_slot = late_slot + 6
    tail_slot = running_slot + 5

    def running_copy(number):
        partner = links.partner[SPREAD[number]]
        return remote(running.at[number], running_got.at[number], sems, running_slot + number, partner)

    def tail_copy():
        return remote(down_tail_give, down_tail_got, sems, tail_slot, links.partner["X"])

    def block_copy(number):
        at = pl.ds(number * quarter, quarter)
        target = block_ref.at[links.me, at]
        return remote(other_block_ref.at[at], target, sems, BACK_COPIES + number, links.partner["Y"])

    def halves(target, at, first, values):
        middle = model // 2
        target[at, first : first + 1] = values[:, :middle]
        target[at, first + 1 : first + 2] = values[:, middle:]

    @pl.when(step == 0)
    def _():
        links.greet()
        for copy in fetches():
            copy.start()
        out.begin()
        for m in range(4):
            halves(early, place, 2 * m, mid_rows_ref[m : m + 1])
        running[0, 0:2] = mid_rows_ref[4:6]
        for tile in range(up_bias_ref.shape[1] // model):
            running[0, 2 + tile : 3 + tile] = up_bias_ref[:, tile * model : (tile + 1) * model]
        running[0, 6:8] = jnp.zeros((2, model), jnp.float32)
        start_all(spread_copies(links, early, sems, early_slot, 0))
        running_copy(0).start()

    for number in range(1, 6):

        @pl.when(step == number)
        def _(number=number):
            if number < 5:
                receive_all(spread_copies(links, early, sems, early_slot, number - 1))
                if number < 4:
                    start_all(spread_copies(links, early, sems, early_slot, number))
            running_copy(number - 1).wait_recv()
            running[number] = running[number - 1] + running_got[number - 1]
            if number < 5:
                running_copy(number).start()
                block_copy(number - 1).start()

    def at_step(number):
        return pl.when(step == number)

    def between():
        @at_step(0)
        def _():
            for copy in fetches(0, 5):
                copy.wait()
            down_tail_give[...] = down_tail[1 - links.bit["X"]]
            tail_copy().start()
            upv.step()
            upx.step()

        @at_step(1)
        def _():
            tail_copy().wait_recv()
            kept = down_tail[links.bit["X"]].astype(jnp.float32) + down_tail_got[...].astype(jnp.float32)
            down.keep[3] = kept.astype(jnp.bfloat16)
            down.step()
            out.step()

        @at_step(2)
        def _():
            for copy in fetches(5):
                copy.wait()
            upx.last()
            upv.last()

        @at_step(3)
        def _():
            ins[0].step()

        @at_step(4)
        def _():
            out.step()
            down.last()

        @at_step(5)
        def _():
            ins[1].step()
            ins[0].step()

    lane = lax.broadcasted_iota(jnp.int32, (rows, 128), 1)

    @pl.when(step < 6)
    def _():
        keys = k_ref[...]
        values = v_ref[...]
        scaled = grad_ref[...].astype(jnp.float32) * inv_ref[...]
        products = scaled * out_ref[...].astype(jnp.float32)
        scaled = scaled.astype(jnp.bfloat16)
        scaled_t = scaled.T
        queries_t = q_ref[...].T
        grad_k = []
        grad_v = []
        for head in range(2):
            if head == 1:
                between()
            for chunk in range(length // rows):
                at = slice(chunk * rows, (chunk + 1) * rows)
                mask = (lane < 64) == (head == 0)
                mine = jnp.where(mask, scaled[at], jnp.zeros((rows, 128), jnp.bfloat16))
                row_dots = jnp.sum(jnp.where(mask, products[at], 0.0), -1, keepdims=True)
                grad_p = dot(mine, values, 1, 1)
                grad_s = (exp_ref[head, at].astype(jnp.float32) * (grad_p - row_dots)).astype(jnp.bfloat16)
                ds_ref[at] = grad_s
                grad_q = dot(grad_s, keys, 1, 0) * 0.125
                if head == 0:
                    dq_sum[at] = grad_q
                else:
                    dq_sum[at] = jnp.where(lane < 64, dq_sum[at], grad_q)
            grad_v.append(dot(scaled_t[64 * head : 64 * head + 64], exp_ref[head], 1, 0))
            grad_k.append(dot(queries_t[64 * head : 64 * head + 64], ds_ref[...], 1, 0))
        columns = [pl.ds(pl.multiple_of(part * model + step * 128, 128), 128) for part in range(3)]
        proj[:, columns[2]] = jnp.concatenate(grad_v, 0).astype(jnp.bfloat16).T
        grad_keys = jnp.concatenate(grad_k, 0).astype(jnp.bfloat16).T
        for chunk in range(length // rows):
            at = slice(chunk * rows, (chunk + 1) * rows)
            for part, source in enumerate((dq_sum[at].astype(jnp.bfloat16), grad_keys[at])):
                piece = source.astype(jnp.float32)
                turned = piece * cos_ref[at] - swap_halves(piece, lane) * sin_ref[at]
                proj[at, columns[part]] = turned.astype(jnp.bfloat16)

    starts = [128 * sum(CHUNKS[:i]) for i in range(len(CHUNKS))]

    def weight_part(group):
        piece = ins[group]
        span = 128 * CHUNKS[group]
        for part in range(3):
            column = part * model + starts[group]
            grad = dot(first_t_ref[...], proj[:, column : column + span], 1, 0).astype(jnp.bfloat16)
            grad = grad.reshape(8, 2, -1, span)
            share(core, (grad[:, 0], grad[:, 1]), piece.keep, piece.source, Ellipsis, slice(part * span, (part + 1) * span))
        piece.begin()

    for group, number in enumerate((2, 4, 5)):
        at_step(number)(functools.partial(weight_part, group))

    scaling = gain_ref[...] * (1.0 + mod_ref[1:2])

    def entry(values_ref, base, chunk):
        at = slice(base + chunk * rows, base + (chunk + 1) * rows)
        local = slice(chunk * rows, (chunk + 1) * rows)
        grad = dot(proj[at], weight_ref[...], 1, 1)
        normed, inverse = norm_rows(values_ref[local].astype(jnp.float32))
        weighted = grad * normed
        scaled = grad * scaling
        inner = jnp.mean(weighted * scaling, -1, keepdims=True)
        result = grad_middle_ref[at] + (scaled - jnp.mean(scaled, -1, keepdims=True) - normed * inner) * inverse
        tokens_stage[at] = result.astype(jnp.bfloat16)
        return jnp.concatenate([jnp.sum(grad, 0, keepdims=True), jnp.sum(weighted, 0, keepdims=True)], 0)

    def away(chunk):
        source = tokens_stage.at[pl.ds(half + chunk * rows, rows)]
        target = tokens_grad_ref.at[links.me, pl.ds(chunk * rows, rows)]
        return remote(source, target, sems, BACK_COPIES + 4 + chunk, links.partner["Y"])

    def home():
        return pltpu.make_async_copy(tokens_stage.at[pl.ds(0, half)], tokens_grad_ref.at[links.me], local_sems.at[11])

    def vectors():
        middle = model // 2
        for m in range(6):
            source, row = (late, 2 * m) if m < 2 else (early, 2 * m - 4)
            by_vector[m, :, 0:middle] = source[:, row, :]
            by_vector[m, :, middle:model] = source[:, row + 1, :]
        ones = jnp.ones((32, 128), jnp.float32)
        factors = jnp.concatenate([late[:, 6, 0:128], ones], 1)
        unit = mod_weight_grad_ref.shape[0] // 6
        for part in range(6):
            at = dp * 6 + part
            product = lax.dot_general(
                by_vector[at // 16],
                factors,
                (((0,), (0,)), ((), ())),
                precision=highest,
                preferred_element_type=jnp.float32,
            )
            spread[...] = product
            kept = spread[pl.ds(pl.multiple_of((at % 16) * unit, 8), unit), :]
            mod_weight_grad_ref[part * unit : (part + 1) * unit] = kept[:, 0:128]
            spread_bias[part * unit : (part + 1) * unit] = kept[:, 128:256]
        mod_bias_grad_ref[...] = spread_bias[...].T[0:1]
        base = place % 16
        both = jnp.zeros((2, 128), jnp.float32)
        for m in range(6):
            rest = jnp.concatenate([by_vector[m, pl.ds(base, 1)], by_vector[m, pl.ds(base + 16, 1)]], 0)
            for _ in range(3):
                high = rest.astype(jnp.bfloat16)
                both = both + dot(high, mod_weight_ref[m * model : (m + 1) * model], 1, 0)
                rest = rest - high.astype(jnp.float32)
        time_grad_ref[...] = both
        gains = [jnp.sum(late[:, row, :], 0, keepdims=True) for row in (4, 5)]
        gains = jnp.concatenate(gains, 1)
        turned[...] = jnp.concatenate([running[5, 0:6], gains, gains], 0).T
        narrow = turned[pl.ds(pl.multiple_of(dp * unit, 8), unit), :].T
        feed_gain_grad_ref[...] = narrow[0:1]
        down_bias_grad_ref[...] = narrow[1:2]
        gain_grad_ref[...] = narrow[6:7]
        wide_rows = up_bias_grad_ref.shape[1]
        share_of = model // wide_rows
        wide = turned[pl.ds(pl.multiple_of((dp % share_of) * wide_rows, 8), wide_rows), :].T
        picked = jnp.zeros((1, wide_rows), jnp.float32)
        for tile in range(4):
            picked = jnp.where(dp // share_of == tile, wide[2 + tile : 3 + tile], picked)
        up_bias_grad_ref[...] = picked

    @at_step(6)
    def _():
        rows_ref[...] = entry(other_ref, half, 0)
        ins[2].step()
        away(0).start()
        rows_ref[...] += entry(other_ref, half, 1)
        out.last()
        away(1).start()
        ins[1].step()

    @at_step(7)
    def _():
        rows_ref[...] += entry(own_ref, 0, 0)
        ins[2].step()
        rows_ref[...] += entry(own_ref, 0, 1)
        home().start()
        scaling_one = 1.0 + mod_ref[1:2]
        halves(late, place, 0, rows_ref[0:1])
        halves(late, place, 2, rows_ref[1:2] * gain_ref[...])
        halves(late, place, 4, rows_ref[1:2] * scaling_one)
        embedding = time_ref[...].astype(jnp.float32)
        late[place, 6:7, 0:128] = jnp.where(links.me == 0, embedding[0:1], embedding[1:2])
        start_all(spread_copies(links, late, sems, late_slot, 0))
        hop = iter(range(4))

        def hop_on():
            number = next(hop)
            receive_all(spread_copies(links, late, sems, late_slot, number))
            if number < 3:
                start_all(spread_copies(links, late, sems, late_slot, number + 1))

        ins[0].last()
        hop_on()
        ins[1].last()
        hop_on()
        ins[2].last()
        hop_on()
        hop_on()
        vectors()
        for group in range(3):
            def store(at, value, group=group):
                span = 128 * CHUNKS[group]
                for part in range(3):
                    column = part * model + starts[group]
                    in_ref[at, column : column + span] = value[:, part * span : (part + 1) * span]

            ins[group].result(store)

        def store_out(at, value):
            out_grad_ref[at] = value

        out.result(store_out)

        def store_down(at, value):
            down_ref[at] = value

        down.result(store_down)

        def store_up(first):
            def store(at, value):
                count = up_ref.shape[0]
                for tile in range(value.shape[0] // count):
                    columns = slice((first + tile) * model, (first + tile + 1) * model)
                    up_ref[:, columns] = value[tile * count : (tile + 1) * count]

            return store

        upv.result(store_up(0))
        upx.result(store_up(3))
        home().wait()
        for chunk in range(half // rows):
            away(chunk).wait()
        for number in range(4):
            block_copy(number).wait()
        for number in range(4):
            for copy in spread_copies(links, early, sems, early_slot, number) + spread_copies(links, late, sems, late_slot, number):
                copy.wait_send()
        for number in range(5):
            running_copy(number).wait_send()
        tail_copy().wait_send()
        for piece in pieces:
            for copy in piece.copies:
                remote(*copy).wait_send()


def close_kernel(*refs):
    count = len(refs) // 2
    for source, target in zip(refs[:count], refs[count:]):
        target[...] = source[...]


def turn_tables(length):
    inverse = 10000.0 ** (-np.arange(HD // 2, dtype=np.float64) * 2.0 / HD)
    angles = np.arange(length, dtype=np.float64)[:, None] * inverse[None, :]
    cosine = np.tile(np.cos(angles), (1, 4))
    sines = np.sin(angles)
    sines = np.concatenate([-sines, sines, -sines, sines], 1)
    both = [np.stack([t, np.roll(t, -(length // 2), 0)]).astype(np.float32) for t in (cosine, sines)]
    return jnp.asarray(both[0]), jnp.asarray(both[1])


def call(kernel, grid, place, in_specs, out_specs, out_shape, scratch, operands, name, flops, moved, after=(), alias=()):
    count = len(in_specs) + 1
    extra = len(after) + len(alias)
    in_specs = in_specs + [pl.BlockSpec(memory_space=pl.ANY)] * extra

    def inner(*refs):
        kernel(*refs[:count], *refs[count + extra :])

    start = count + len(after)
    first_out = len(out_shape) - len(alias)
    operands = (*operands, *after, *alias)
    return pl.pallas_call(
        inner,
        input_output_aliases={start + i: first_out + i for i in range(len(alias))},
        grid_spec=pltpu.PrefetchScalarGridSpec(
            num_scalar_prefetch=1, grid=grid, in_specs=in_specs, out_specs=out_specs, scratch_shapes=scratch
        ),
        out_shape=out_shape,
        compiler_params=params(),
        cost_estimate=pl.CostEstimate(flops=flops, bytes_accessed=moved, transcendentals=0),
        name=name,
    )(place, *operands)


def whole(*shape):
    return pl.BlockSpec(shape, lambda i, p: (0,) * len(shape))


def swap_pairs(size, bit):
    return [(i, i ^ bit) for i in range(size)]


def fast_body(
    tokens,
    time_embedding,
    prefix_length,
    suffix_mask,
    cotangent,
    modulation_weight,
    modulation_bias,
    attention_gain,
    attention_in,
    attention_out,
    feed_gain,
    feed_up,
    feed_up_bias,
    feed_down,
    feed_down_bias,
):
    bf16 = jnp.bfloat16
    f32 = jnp.float32
    _, half, model = tokens.shape
    length = 2 * half
    hidden_width = feed_up.shape[1]
    size = lax.axis_size("dp")
    me = lax.axis_index("seq")
    dp = lax.axis_index("dp")
    place = jnp.stack([dp % 2, me]).astype(jnp.int32)
    swap = swap_pairs(2, 1)
    shape = jax.ShapeDtypeStruct

    def mine(array):
        return lax.dynamic_index_in_dim(array, me, 0, False)

    def theirs(array):
        return lax.dynamic_index_in_dim(array, 1 - me, 0, False)

    other = lax.ppermute(theirs(tokens), "seq", swap)
    positions = me * half + jnp.arange(half, dtype=jnp.int32)
    live = (positions[None, :] >= prefix_length[:, None]) & (suffix_mask == 1)
    live_cot = jnp.where(live[:, :, None], cotangent, jnp.zeros_like(cotangent))
    own_cot = mine(live_cot)
    other_cot = lax.ppermute(theirs(live_cot), "seq", swap)

    modulation = jnp.einsum(
        "c,oc->o", mine(time_embedding), modulation_weight, preferred_element_type=f32
    ) + modulation_bias.astype(f32)
    modulation = modulation.reshape(6, model)
    gain_one = attention_gain.astype(f32)[None]
    gain_two = feed_gain.astype(f32)[None]
    cosine, sines = turn_tables(length)
    table = pl.BlockSpec((None, length, 128), lambda i, p: (p[1], 0, 0))
    own_rows = pl.BlockSpec((None, half, model), lambda i, p: (p[1], 0, 0))
    blocks = half // PROJECT_ROWS

    def project(source, spec, start, alias):
        turn = pl.BlockSpec((None, PROJECT_ROWS, 128), lambda i, p: (p[1], i + start, 0))
        return call(
            lambda p, *refs: project_kernel(*refs),
            (blocks,),
            place,
            [spec, whole(6, model), whole(1, model), whole(model, 3 * model), turn, turn],
            [
                pl.BlockSpec((model, PROJECT_ROWS), lambda i, p: (0, i + start)),
                pl.BlockSpec((PROJECT_ROWS, 3 * model), lambda i, p: (i + start, 0)),
            ],
            [shape((model, length), bf16), shape((length, 3 * model), bf16)],
            [],
            (source, modulation, gain_one, attention_in, cosine, sines),
            "project",
            length * model * 3 * model,
            6 * MIB,
            alias=alias,
        )

    kept = project(tokens, pl.BlockSpec((None, PROJECT_ROWS, model), lambda i, p: (p[1], i, 0)), 0, ())
    first_t, qkv = project(other, pl.BlockSpec((PROJECT_ROWS, model), lambda i, p: (i, 0)), blocks, kept)
    def column(k):
        return pl.BlockSpec((length, 128), lambda h, p: (0, h + k))

    pairs = model // 128
    exps_block = pl.BlockSpec((2, length, length), lambda h, p: (h, 0, 0))
    attended, exps, inverses = call(
        lambda p, *refs: attend_kernel(*refs),
        (pairs,),
        place,
        [column(0), column(pairs), column(2 * pairs)],
        [column(0), exps_block, column(0)],
        [shape((length, model), bf16), shape((HEADS, length, length), bf16), shape((length, model), f32)],
        [],
        (qkv, qkv, qkv),
        "attend",
        16 * length * length * model,
        32 * MIB,
    )

    tiles = 4
    width = hidden_width // tiles
    groups = size // 2
    share_rows = hidden_width // size
    model_rows = model // size
    anywhere = pl.BlockSpec(memory_space=pl.ANY)

    def fixed(*dims):
        return pl.BlockSpec(dims, lambda h: (0,) * len(dims), pipeline_mode=pl.Buffered(1))

    own_part = pl.BlockSpec((None, half, model), lambda h: (lax.axis_index("seq"), 0, 0), pipeline_mode=pl.Buffered(1))
    up_tile = pl.BlockSpec((model, width), lambda j: (0, j))
    bias_tile = pl.BlockSpec((1, width), lambda j: (0, j))
    down_tile = pl.BlockSpec((width, model), lambda j: (j, 0))
    (
        own_out,
        other_out,
        grad_middle,
        grad_attended,
        mid_rows,
        up_bias_grad,
        down_sum,
        down_tail,
        upv_sum,
        upx_sum,
        out_keep,
        out_send,
    ) = pl.pallas_call(
        middle_kernel,
        grid=(tiles,),
        in_specs=[own_part]
        + [fixed(half, model)] * 3
        + [
            fixed(length, model),
            fixed(6, model),
            fixed(1, model),
            fixed(model, model),
            up_tile,
            bias_tile,
            down_tile,
            fixed(1, model),
        ],
        out_specs=[
            own_part,
            fixed(half, model),
            fixed(length, model),
            fixed(length, model),
            fixed(6, model),
            bias_tile,
            fixed(tiles - 1, share_rows // 2, model),
            fixed(2, share_rows // 2, model),
            fixed(2, tiles - 1, model_rows, model),
            fixed(4, model_rows, model),
            fixed(groups, model_rows, model),
            fixed(groups, model_rows, model),
        ],
        out_shape=[shape((2, half, model), bf16), shape((half, model), bf16)]
        + [shape((length, model), f32), shape((length, model), bf16), shape((6, model), f32), shape((1, hidden_width), f32)]
        + [shape((tiles - 1, share_rows // 2, model), bf16), shape((2, share_rows // 2, model), bf16), shape((2, tiles - 1, model_rows, model), bf16)]
        + [shape((4, model_rows, model), bf16)]
        + [shape((groups, model_rows, model), bf16)] * 2,
        scratch_shapes=[
            pltpu.VMEM((model, length), bf16),
            pltpu.VMEM((length, model), bf16),
            pltpu.VMEM((length, model), f32),
            pltpu.VMEM((length, model), f32),
            pltpu.VMEM((width, length), bf16),
        ]
        + [pltpu.VMEM((tiles, groups // tiles, share_rows, model), bf16)] * 3
        + [pltpu.VMEM((tiles, groups, model_rows, model), bf16)] * 3
        + [pltpu.VMEM((tiles, groups // tiles, share_rows // 2, model), bf16)] * 2
        + [pltpu.VMEM((tiles - 1, share_rows // 2, model), bf16)] * 2
        + [pltpu.VMEM((tiles - 1, 3, 2, model_rows, model), bf16)] * 2
        + [pltpu.VMEM((4, model_rows, model), bf16)] * 2
        + [pltpu.SemaphoreType.DMA((2, 7 * tiles))],
        compiler_params=pltpu.CompilerParams(vmem_limit_bytes=63 * MIB, collective_id=1, has_side_effects=True),
        cost_estimate=pl.CostEstimate(
            flops=12 * length * model * hidden_width + 6 * length * model * model, bytes_accessed=36 * MIB, transcendentals=0
        ),
        name="middle",
    )(
        tokens,
        other,
        own_cot,
        other_cot,
        attended,
        modulation,
        gain_two,
        attention_out,
        feed_up,
        feed_up_bias.astype(f32)[None],
        feed_down,
        feed_down_bias.astype(f32)[None],
    )
    merge = (2, (tiles - 1) * model_rows, model)

    def near(k):
        return pl.BlockSpec((length, 128), lambda h: (0, jnp.minimum(h, pairs - 1) + k))

    turn = pl.BlockSpec((None, length, 128), lambda h: (lax.axis_index("seq"), 0, 0), pipeline_mode=pl.Buffered(1))
    scratch = [
        pltpu.VMEM((model, length), bf16),
        pltpu.VMEM((model, 3 * model), bf16),
        pltpu.VMEM((half, model), bf16),
        pltpu.VMEM((half, model), bf16),
        pltpu.VMEM((length, model), f32),
        pltpu.VMEM((6 * model, 128), bf16),
        pltpu.VMEM((2, share_rows // 2, model), bf16),
        pltpu.VMEM((share_rows // 2, model), bf16),
        pltpu.VMEM((share_rows // 2, model), bf16),
        pltpu.VMEM((length, length), bf16),
        pltpu.VMEM((length, 128), f32),
        pltpu.VMEM((length, 3 * model), bf16),
        pltpu.VMEM((length, model), bf16),
        pltpu.VMEM((2, model), f32),
        pltpu.VMEM((2 * size, 8, model // 2), f32),
        pltpu.VMEM((2 * size, 8, model // 2), f32),
        pltpu.VMEM((6, 8, model), f32),
        pltpu.VMEM((5, 8, model), f32),
        pltpu.VMEM((6, 2 * size, model), f32),
        pltpu.VMEM((model, 256), f32),
        pltpu.VMEM((6 * model_rows, 128), f32),
        pltpu.VMEM((model, 8), f32),
        pltpu.SemaphoreType.DMA((2, BACK_COPIES + 24)),
        pltpu.SemaphoreType.DMA((12,)),
    ]
    for spec in BACK_PIECES:
        scratch += piece_scratch(spec)
    def cut(dims):
        if len(dims) == 3:
            return pl.BlockSpec((1, *dims[1:]), lambda i: (i, 0, 0))
        if dims[0] % 16:
            return pl.BlockSpec(dims, lambda i: (0, 0))
        return pl.BlockSpec((dims[0] // 2, dims[1]), lambda i: (i, 0))

    results = pl.pallas_call(
        back_kernel,
        grid=(pairs + 2,),
        in_specs=[
            near(0),
            near(pairs),
            near(2 * pairs),
            near(0),
            near(0),
            pl.BlockSpec((2, length, length), lambda h: (jnp.minimum(h, pairs - 1), 0, 0)),
            near(0),
            turn,
            turn,
            *[anywhere] * 5,
            fixed(6, model),
            fixed(1, model),
        ]
        + [anywhere] * 6
        + [fixed(6, model), fixed(1, hidden_width), fixed(2, 128), anywhere, anywhere, anywhere],
        out_specs=[
            anywhere,
            fixed(2, 128),
            fixed(6 * model_rows, 128),
            fixed(1, 6 * model_rows),
            fixed(1, model_rows),
            fixed(1, model_rows),
            fixed(1, hidden_width // size),
            fixed(1, model_rows),
            fixed(hidden_width // size, model),
            fixed(model_rows, hidden_width),
            fixed(model_rows, model),
            fixed(model_rows, 3 * model),
            anywhere,
        ],
        out_shape=[
            shape((2, half, model), bf16),
            shape((2, 128), f32),
            shape((6 * model_rows, 128), f32),
            shape((1, 6 * model_rows), f32),
            shape((1, model_rows), f32),
            shape((1, model_rows), f32),
            shape((1, hidden_width // size), f32),
            shape((1, model_rows), f32),
            shape((hidden_width // size, model), f32),
            shape((model_rows, hidden_width), f32),
            shape((model_rows, model), f32),
            shape((model_rows, 3 * model), f32),
            shape((2, half, model), bf16),
        ],
        input_output_aliases={27: 12},
        scratch_shapes=scratch,
        compiler_params=pltpu.CompilerParams(vmem_limit_bytes=63 * MIB, collective_id=0, has_side_effects=True),
        cost_estimate=pl.CostEstimate(flops=40 * length * length * model, bytes_accessed=60 * MIB, transcendentals=0),
        name="back",
    )(
        qkv,
        qkv,
        qkv,
        attended,
        grad_attended,
        exps,
        inverses,
        cosine,
        sines,
        first_t,
        attention_in,
        tokens,
        other,
        grad_middle,
        modulation,
        gain_one,
        down_sum,
        down_tail,
        upv_sum.reshape(merge),
        upx_sum,
        out_keep,
        out_send,
        mid_rows,
        up_bias_grad,
        time_embedding,
        modulation_weight,
        other_out,
        own_out,
    )
    (
        tokens_grad,
        time_grad,
        modulation_weight_grad,
        modulation_bias_grad,
        gain_grad,
        feed_gain_grad,
        feed_up_bias_grad,
        feed_down_bias_grad,
        down_grad,
        up_grad,
        out_grad,
        in_grad,
        block_output,
    ) = pl.pallas_call(
        close_kernel,
        grid=(2,),
        in_specs=[cut(r.shape) for r in results],
        out_specs=[cut(r.shape) for r in results],
        out_shape=[shape(r.shape, r.dtype) for r in results],
        compiler_params=params(62),
        name="close",
    )(*results)
    return (
        block_output,
        tokens_grad,
        time_grad,
        modulation_weight_grad,
        modulation_bias_grad[0],
        gain_grad[0],
        in_grad,
        out_grad,
        feed_gain_grad[0],
        up_grad,
        feed_up_bias_grad[0],
        down_grad,
        feed_down_bias_grad[0],
    )


def body(tokens, *rest):
    sequences, half, model = tokens.shape
    size = lax.axis_size("dp")
    fits = model % (16 * size) == 0 and half % T_ROWS == 0
    fits = fits and tokens.shape[1] % PROJECT_ROWS == 0 and rest[10].shape[1] == 4 * model and size == 16 and lax.axis_size("seq") == 2 and sequences == 2
    return (fast_body if fits else general_body)(tokens, *rest)


def solution(mesh):
    return jax.shard_map(
        body,
        mesh=mesh,
        in_specs=(
            P("dp", "seq", None),
            P("dp", None),
            P("dp"),
            P("dp", "seq"),
            P("dp", "seq", None),
            P(),
            P(),
            P(),
            P(),
            P(),
            P(),
            P(),
            P(),
            P(),
            P(),
        ),
        out_specs=(
            P("dp", "seq", None),
            P("dp", "seq", None),
            P("dp", None),
            P("dp", None),
            P("dp"),
            P("dp"),
            P("dp", None),
            P("dp", None),
            P("dp"),
            P("dp", None),
            P("dp"),
            P("dp", None),
            P("dp"),
        ),
        check_vma=False,
    )
```

```python
import functools
from functools import partial

import jax
import jax.numpy as jnp
import numpy as np
from jax import lax
from jax.experimental import pallas as pl
from jax.experimental.pallas import tpu as pltpu
from jax.sharding import PartitionSpec as P

HEADS = 12
HD = 64


highest = lax.Precision.HIGHEST


def as_sent(shard):

    def short(part):
        return part.astype(jnp.bfloat16) if part.dtype == jnp.float32 else part

    return jax.tree.map(short, shard)


def normalize(values):
    centre = values - jnp.mean(values, -1, keepdims=True)
    spread = jnp.mean(centre * centre, -1, keepdims=True)
    return centre * lax.rsqrt(spread + 1e-05)


def modulate(values, scaling, shifts, scales):
    return normalize(values) * scaling * (1.0 + scales) + shifts


def rotate(values, cosine, sines, direction):
    halves = values.shape[-1] // 2
    former = values[..., :halves]
    latter = values[..., halves:]
    cosine = cosine[None, :, None, :]
    sines = direction * sines[None, :, None, :]
    return jnp.concatenate([former * cosine - latter * sines, latter * cosine + former * sines], -1)


def attend_forward(stacked):
    query_rows = stacked[:, 0]
    key_rows = stacked[:, 1]
    value_rows = stacked[:, 2]
    length = query_rows.shape[0]
    block_rows = min(512, length)
    pieces = []
    logsums = []
    for offset in range(0, length, block_rows):
        query_block = query_rows[offset : offset + block_rows]
        scores = (
            jnp.einsum("qhd,khd->hqk", query_block, key_rows, preferred_element_type=jnp.float32)
            * 0.125
        )
        largest = jnp.max(scores, -1, keepdims=True)
        exponentials = jnp.exp(scores - largest)
        totals = jnp.sum(exponentials, -1, keepdims=True)
        probability = (exponentials / totals).astype(jnp.bfloat16)
        pieces.append(
            jnp.einsum("hqk,khd->qhd", probability, value_rows, preferred_element_type=jnp.float32)
        )
        logsums.append((largest + jnp.log(totals))[..., 0])
    return (jnp.concatenate(pieces, 0).astype(jnp.bfloat16), jnp.concatenate(logsums, 1))


def attend_backward(operands):
    stacked, grad_attended, logsums = operands
    query_rows = stacked[:, 0]
    key_rows = stacked[:, 1]
    value_rows = stacked[:, 2]
    length = query_rows.shape[0]
    block_rows = min(512, length)
    grad_query = []
    grad_keys = jnp.zeros(key_rows.shape, jnp.float32)
    grad_values = jnp.zeros(value_rows.shape, jnp.float32)
    for offset in range(0, length, block_rows):
        query_block = query_rows[offset : offset + block_rows]
        grad_block = grad_attended[offset : offset + block_rows]
        scores = (
            jnp.einsum("qhd,khd->hqk", query_block, key_rows, preferred_element_type=jnp.float32)
            * 0.125
        )
        probability = jnp.exp(scores - logsums[:, offset : offset + block_rows, None])
        grad_probs = jnp.einsum(
            "qhd,khd->hqk", grad_block, value_rows, preferred_element_type=jnp.float32
        )
        row_dots = jnp.sum(probability * grad_probs, -1, keepdims=True)
        grad_scores = (probability * (grad_probs - row_dots)).astype(jnp.bfloat16)
        grad_query.append(
            (
                jnp.einsum(
                    "hqk,khd->qhd", grad_scores, key_rows, preferred_element_type=jnp.float32
                )
                * 0.125
            ).astype(jnp.bfloat16)
        )
        grad_keys = grad_keys + jnp.einsum(
            "hqk,qhd->khd", grad_scores, query_block, preferred_element_type=jnp.float32
        )
        grad_values = grad_values + jnp.einsum(
            "hqk,qhd->khd",
            probability.astype(jnp.bfloat16),
            grad_block,
            preferred_element_type=jnp.float32,
        )
    return jnp.stack(
        [
            jnp.concatenate(grad_query, 0),
            (grad_keys * 0.125).astype(jnp.bfloat16),
            grad_values.astype(jnp.bfloat16),
        ],
        1,
    )


def general_body(
    tokens,
    time_embedding,
    prefix_length,
    suffix_mask,
    cotangent,
    modulation_weight,
    modulation_bias,
    attention_gain,
    attention_in,
    attention_out,
    feed_gain,
    feed_up,
    feed_up_bias,
    feed_down,
    feed_down_bias,
):
    sequences, local_len, model_width = tokens.shape
    groups = lax.axis_size("seq")
    data_size = lax.axis_size("dp")
    length = local_len * groups
    heads_local = HEADS // groups
    group_width = model_width // groups
    modulation = jnp.einsum(
        "sc,oc->so", time_embedding, modulation_weight, preferred_element_type=jnp.float32
    ) + modulation_bias.astype(jnp.float32)
    shift_one, scale_one, gate_one, shift_two, scale_two, gate_two = [
        portion[:, None, :] for portion in jnp.split(modulation, 6, axis=1)
    ]
    inputs = tokens.astype(jnp.float32)
    first_float, first_back = jax.vjp(
        modulate, inputs, attention_gain.astype(jnp.float32), shift_one, scale_one
    )
    first_input = first_float.astype(jnp.bfloat16)
    projected = jnp.einsum(
        "spd,de->spe", first_input, attention_in, preferred_element_type=jnp.float32
    ).reshape(sequences, local_len, 3, HEADS, HD)
    position_ints = lax.axis_index("seq") * local_len + jnp.arange(local_len, dtype=jnp.int32)
    positions = position_ints.astype(jnp.float32)
    inverse = 10000.0 ** (-jnp.arange(HD // 2, dtype=jnp.float32) * 2.0 / HD)
    angles = positions[:, None] * inverse[None, :]
    cosine = jnp.cos(angles)
    sines = jnp.sin(angles)
    rotated = jnp.stack(
        [
            rotate(projected[:, :, 0], cosine, sines, 1.0),
            rotate(projected[:, :, 1], cosine, sines, 1.0),
            projected[:, :, 2],
        ],
        2,
    ).astype(jnp.bfloat16)
    by_heads = lax.all_to_all(
        rotated.reshape(sequences, local_len, 3, groups, group_width),
        "seq",
        split_axis=3,
        concat_axis=1,
        tiled=True,
    )
    by_heads = by_heads.reshape(sequences, length, 3, heads_local, HD)
    attended_heads, logsums = lax.map(attend_forward, by_heads)
    attended = lax.all_to_all(
        as_sent(attended_heads.reshape(sequences, length, 1, group_width)),
        "seq",
        split_axis=1,
        concat_axis=2,
        tiled=True,
    )
    attended = attended.reshape(sequences, local_len, model_width)
    branch_one = jnp.einsum(
        "spd,de->spe", attended, attention_out, preferred_element_type=jnp.float32
    )
    middle = inputs + gate_one * branch_one
    second_float, second_back = jax.vjp(
        modulate, middle, feed_gain.astype(jnp.float32), shift_two, scale_two
    )
    second_input = second_float.astype(jnp.bfloat16)
    hidden = jnp.einsum(
        "spd,df->spf", second_input, feed_up, preferred_element_type=jnp.float32
    ) + feed_up_bias.astype(jnp.float32)
    activated_float, gelu_back = jax.vjp(partial(jax.nn.gelu, approximate=True), hidden)
    activated = activated_float.astype(jnp.bfloat16)
    branch_two = jnp.einsum(
        "spf,fd->spd", activated, feed_down, preferred_element_type=jnp.float32
    ) + feed_down_bias.astype(jnp.float32)
    block_output = (middle + gate_two * branch_two).astype(jnp.bfloat16)
    live_rows = ((position_ints[None, :] >= prefix_length[:, None]) & (suffix_mask == 1)).astype(
        jnp.float32
    )
    grad_output = cotangent.astype(jnp.float32) * live_rows[:, :, None]
    grad_gate_two = jnp.sum(grad_output * branch_two, axis=1)
    grad_branch_two = (gate_two * grad_output).astype(jnp.bfloat16)
    feed_down_bias_grad = jnp.sum(grad_branch_two.astype(jnp.float32), axis=(0, 1))
    feed_down_grad = jnp.einsum(
        "spf,spd->fd", activated, grad_branch_two, preferred_element_type=jnp.float32
    )
    grad_activated = jnp.einsum(
        "spd,fd->spf", grad_branch_two, feed_down, preferred_element_type=jnp.float32
    )
    grad_hidden = gelu_back(grad_activated)[0].astype(jnp.bfloat16)
    feed_up_bias_grad = jnp.sum(grad_hidden.astype(jnp.float32), axis=(0, 1))
    feed_up_grad = jnp.einsum(
        "spd,spf->df", second_input, grad_hidden, preferred_element_type=jnp.float32
    )
    grad_second = jnp.einsum(
        "spf,df->spd", grad_hidden, feed_up, preferred_element_type=jnp.float32
    )
    grad_from_norm, feed_gain_grad, grad_shift_two, grad_scale_two = second_back(grad_second)
    grad_middle = grad_output + grad_from_norm
    grad_gate_one = jnp.sum(grad_middle * branch_one, axis=1)
    grad_branch_one = (gate_one * grad_middle).astype(jnp.bfloat16)
    attention_out_grad = jnp.einsum(
        "spd,spe->de", attended, grad_branch_one, preferred_element_type=jnp.float32
    )
    grad_attended = jnp.einsum(
        "spe,de->spd", grad_branch_one, attention_out, preferred_element_type=jnp.float32
    ).astype(jnp.bfloat16)
    grad_heads = lax.all_to_all(
        grad_attended.reshape(sequences, local_len, groups, group_width),
        "seq",
        split_axis=2,
        concat_axis=1,
        tiled=True,
    )
    grad_heads = grad_heads.reshape(sequences, length, heads_local, HD)
    grad_stacked = lax.map(attend_backward, (by_heads, grad_heads, logsums))
    grad_positions = lax.all_to_all(
        as_sent(grad_stacked.reshape(sequences, length, 3, 1, group_width)),
        "seq",
        split_axis=1,
        concat_axis=3,
        tiled=True,
    )
    grad_positions = grad_positions.reshape(sequences, local_len, 3, HEADS, HD).astype(jnp.float32)
    grad_projected = jnp.stack(
        [
            rotate(grad_positions[:, :, 0], cosine, sines, -1.0),
            rotate(grad_positions[:, :, 1], cosine, sines, -1.0),
            grad_positions[:, :, 2],
        ],
        2,
    ).astype(jnp.bfloat16)
    grad_projected = grad_projected.reshape(sequences, local_len, 3 * model_width)
    attention_in_grad = jnp.einsum(
        "spd,spe->de", first_input, grad_projected, preferred_element_type=jnp.float32
    )
    grad_first = jnp.einsum(
        "spe,de->spd", grad_projected, attention_in, preferred_element_type=jnp.float32
    )
    grad_tokens_norm, attention_gain_grad, grad_shift_one, grad_scale_one = first_back(grad_first)
    tokens_grad = (grad_middle + grad_tokens_norm).astype(jnp.bfloat16)
    grad_modulation = jnp.concatenate(
        [
            grad_shift_one[:, 0],
            grad_scale_one[:, 0],
            grad_gate_one,
            grad_shift_two[:, 0],
            grad_scale_two[:, 0],
            grad_gate_two,
        ],
        1,
    )
    modulation_total = lax.psum(grad_modulation.astype(jnp.bfloat16), "seq").astype(jnp.float32)
    time_grad = jnp.einsum(
        "so,oc->sc", modulation_total, modulation_weight.astype(jnp.float32), precision=highest
    )
    modulation_weight_grad = jnp.einsum(
        "so,sc->oc", grad_modulation, time_embedding.astype(jnp.float32), precision=highest
    )
    modulation_bias_grad = jnp.sum(grad_modulation, axis=0)
    gradients = (
        modulation_weight_grad,
        modulation_bias_grad,
        attention_gain_grad,
        attention_in_grad,
        attention_out_grad,
        feed_gain_grad,
        feed_up_grad,
        feed_up_bias_grad,
        feed_down_grad,
        feed_down_bias_grad,
    )
    flattened = tuple((g.reshape(data_size, -1) for g in gradients))
    shares = lax.psum_scatter(flattened, "dp", scatter_dimension=0, tiled=True)
    summed = jax.tree.map(lambda part: part.astype(jnp.float32), lax.psum(as_sent(shares), "seq"))
    shards = tuple(
        (s.reshape((g.shape[0] // data_size,) + g.shape[1:]) for s, g in zip(summed, gradients))
    )
    return (
        block_output,
        tokens_grad,
        time_grad,
        shards[0],
        shards[1],
        shards[2],
        shards[3],
        shards[4],
        shards[5],
        shards[6],
        shards[7],
        shards[8],
        shards[9],
    )


T_ROWS = 256
MIDDLE_ROWS = 256
MIB = 1 << 20


def dot(a, b, ca, cb):
    return lax.dot_general(a, b, (((ca,), (cb,)), ((), ())), preferred_element_type=jnp.float32)


def params(limit=60):
    return pltpu.CompilerParams(vmem_limit_bytes=limit * MIB)


def norm_rows(values):
    centre = values - jnp.mean(values, -1, keepdims=True)
    inverse = lax.rsqrt(jnp.mean(centre * centre, -1, keepdims=True) + 1e-05)
    return centre * inverse, inverse


def swap_halves(values, lane):
    left = pltpu.roll(values, 96, 1)
    right = pltpu.roll(values, 32, 1)
    return jnp.where(lane % 64 < 32, left, right)


def attend_kernel(
    prefix_ref,
    q_ref,
    k_ref,
    v_ref,
    mask_ref,
    cot_hbm,
    out_ref,
    exp_ref,
    inv_ref,
    own_live_ref,
    other_live_ref,
    other_cot_hbm,
    give,
    got,
    sems,
):
    rows = 128
    step = pl.program_id(0)
    links = Links()
    half = mask_ref.shape[1]
    partner = links.partner["Y"]

    def exchanges():
        return [
            remote(give, got, sems, 0, partner),
            remote(cot_hbm.at[1 - links.me], other_cot_hbm, sems, 1, partner),
        ]

    @pl.when(step == 0)
    def _():
        position = links.me * half + lax.broadcasted_iota(jnp.int32, (1, half), 1)
        live = [
            jnp.where((position >= prefix_ref[i]) & (mask_ref[i : i + 1] == 1), 1.0, 0.0) for i in range(2)
        ]
        wide = [jnp.broadcast_to(row, (8, half)) for row in live]
        own_live_ref[...] = jnp.where(links.me == 0, wide[0], wide[1])
        give[...] = jnp.where(links.me == 0, wide[1], wide[0])
        links.greet(("Y",))
        start_all(exchanges())

    length = q_ref.shape[0]
    lane = lax.broadcasted_iota(jnp.int32, (rows, 128), 1)
    keys = k_ref[...]
    values = jnp.concatenate([v_ref[...], jnp.ones((length, 128), jnp.bfloat16)], 1)
    for chunk in range(length // rows):
        at = slice(chunk * rows, (chunk + 1) * rows)
        queries = q_ref[at]
        outs = []
        inverses = []
        for head in range(2):
            mine = jnp.where((lane < 64) == (head == 0), queries, jnp.zeros_like(queries))
            scores = dot(mine, keys, 1, 1)
            largest = jnp.max(scores, -1, keepdims=True)
            exps = jnp.exp(scores - largest).astype(jnp.bfloat16)
            exp_ref[head, at] = exps
            summed = dot(exps, values, 1, 0)
            inverse = 1.0 / summed[:, 128:256]
            outs.append(summed[:, 0:128] * inverse)
            inverses.append(inverse)
        out_ref[at] = jnp.where(lane < 64, outs[0], outs[1]).astype(jnp.bfloat16)
        inv_ref[at] = jnp.where(lane < 64, inverses[0], inverses[1])

    @pl.when(step == pl.num_programs(0) - 1)
    def _():
        for copy in exchanges():
            copy.wait()
        other_live_ref[...] = got[...]


def share(core, grad, keep_ref, send_ref, *at):
    first, second = grad
    keep_ref[at] = jnp.where(core == 0, first, second)
    send_ref[at] = jnp.where(core == 0, second, first)


def middle_kernel(
    own_ref,
    other_ref,
    own_cot_ref,
    other_cot_ref,
    own_live_ref,
    other_live_ref,
    attended_ref,
    mod_ref,
    gain_ref,
    out_weight_ref,
    up_ref,
    up_bias_ref,
    down_ref,
    down_bias_ref,
    own_out_ref,
    other_out_ref,
    grad_middle_ref,
    grad_attended_ref,
    rows_ref,
    up_bias_grad_ref,
    down_sum_ref,
    down_tail_ref,
    upv_sum_ref,
    upx_sum_ref,
    out_keep_ref,
    out_send_ref,
    second_t,
    grad_two,
    sum_two,
    sum_second,
    act_t,
    down_keep,
    down_give,
    down_got,
    up_keep,
    up_give,
    up_got,
    down_half,
    down_half_got,
    down_part,
    down_part_got,
    up_part,
    up_part_got,
    up_half,
    up_half_got,
    sems,
):
    rows = MIDDLE_ROWS
    step = pl.program_id(0)
    links = Links()
    core = links.bit["C"]
    tiles = down_keep.shape[0]

    per_tile = 7
    last = tiles - 1

    def first_copies(tile):
        return [
            remote(give.at[tile], got.at[tile], sems, tile * per_tile + i, links.partner["C"])
            for i, (give, got) in enumerate(((down_give, down_got), (up_give, up_got)))
        ]

    def down_copy(tile):
        return remote(down_half.at[tile], down_half_got.at[tile], sems, tile * per_tile + 2, links.partner["Y"])

    def down_on_copy(tile):
        return remote(down_part.at[tile], down_part_got.at[tile], sems, tile * per_tile + 3, links.partner["X"])

    def up_copies(tile):
        return [
            remote(up_part.at[tile, i], up_part_got.at[tile, i], sems, tile * per_tile + 4 + i, links.partner[flip])
            for i, flip in enumerate(Z_FLIPS)
        ]

    def up_last_copy():
        return remote(up_half, up_half_got, sems, last * per_tile + 4, links.partner["X"])

    def total(*terms):
        return sum(term.astype(jnp.float32) for term in terms).astype(jnp.bfloat16)

    half_rows = down_half.shape[2]
    home = pl.ds(pl.multiple_of(links.me * half_rows, 16), half_rows)
    away = pl.ds(pl.multiple_of((1 - links.me) * half_rows, 16), half_rows)
    z_at = links.bit["W"] * 2 + links.bit["Z"]

    def flipped(flip):
        values = {bit: 1 - links.bit[bit] if bit in flip else links.bit[bit] for bit in "WZ"}
        return values["W"] * 2 + values["Z"]

    def send_on(tile, final):
        for copy in first_copies(tile):
            copy.wait_recv()
        for x in range(2):
            down_half[tile, x] = total(down_keep[tile, x, away], down_got[tile, x, away])
        down_copy(tile).start()
        if final:
            for z in range(4):
                other = 2 * z + 1 - links.bit["X"]
                up_half[z] = total(up_keep[tile, other], up_got[tile, other])
            up_last_copy().start()
        else:
            for i, flip in enumerate(Z_FLIPS):
                for x in range(2):
                    other = 2 * flipped(flip) + x
                    up_part[tile, i, x] = total(up_keep[tile, other], up_got[tile, other])
            for copy in up_copies(tile):
                copy.start()

    def send_down(tile):
        down_copy(tile).wait_recv()
        x = 1 - links.bit["X"]
        down_part[tile] = total(down_keep[tile, x, home], down_got[tile, x, home], down_half_got[tile, x])
        down_on_copy(tile).start()

    def settle(tile, final):
        if final:
            down_copy(tile).wait_recv()
            for x in range(2):
                down_tail_ref[x] = total(down_keep[tile, x, home], down_got[tile, x, home], down_half_got[tile, x])
        else:
            down_on_copy(tile).wait_recv()
            x = links.bit["X"]
            terms = (down_keep[tile, x, home], down_got[tile, x, home], down_half_got[tile, x], down_part_got[tile])
            down_sum_ref[tile] = total(*terms)
        if final:
            up_last_copy().wait_recv()
            for z in range(4):
                mine = 2 * z + links.bit["X"]
                upx_sum_ref[z] = total(up_keep[tile, mine], up_got[tile, mine], up_half_got[z])
        else:
            for copy in up_copies(tile):
                copy.wait_recv()
            for x in range(2):
                mine = 2 * z_at + x
                got = [up_part_got[tile, i, x] for i in range(3)]
                upv_sum_ref[x, tile] = total(up_keep[tile, mine], up_got[tile, mine], *got)

    @pl.when(step == 0)
    def _():
        links.greet()

    half, model = own_ref.shape
    length = 2 * half
    scaling = gain_ref[...] * (1.0 + mod_ref[4:5])
    gate_one = mod_ref[2:3]
    shift_two = mod_ref[3:4]
    gate_two = mod_ref[5:6]

    def pick(first_ref, second_ref, chunk):
        at = chunk * rows
        return (first_ref if at < half else second_ref)[at % half : at % half + rows]

    def live_cot(chunk):
        at = (chunk * rows) % half
        live = (own_live_ref if chunk * rows < half else other_live_ref)[...].T[at : at + rows, 0:1]
        return pick(own_cot_ref, other_cot_ref, chunk).astype(jnp.float32) * live

    @pl.when(step == 0)
    def _():
        bias_grad = jnp.zeros((1, model), jnp.float32)
        for chunk in range(length // rows):
            at = slice(chunk * rows, (chunk + 1) * rows)
            branch = dot(attended_ref[at], out_weight_ref[...], 1, 0)
            grad_middle_ref[at] = branch
            sum_two[at] = jnp.zeros((rows, model), jnp.float32)
            sum_second[at] = jnp.zeros((rows, model), jnp.float32)
            middle = pick(own_ref, other_ref, chunk).astype(jnp.float32) + gate_one * branch
            normed, _ = norm_rows(middle)
            rounded = (normed * scaling + shift_two).astype(jnp.bfloat16)
            place = (chunk * rows) % half
            (own_out_ref if chunk * rows < half else other_out_ref)[place : place + rows] = rounded
            second_t[:, at] = rounded.T
            grad = (gate_two * live_cot(chunk)).astype(jnp.bfloat16)
            grad_two[at] = grad
            bias_grad = bias_grad + jnp.sum(grad.astype(jnp.float32), 0, keepdims=True)
        rows_ref[5:6] = bias_grad

    up = up_ref[...]
    down = down_ref[...]
    width = up.shape[1]
    bias_sum = jnp.zeros((1, width), jnp.float32)
    for chunk in range(length // rows):
        if chunk * rows == half:

            @pl.when(step > 0)
            def _():
                send_on(step - 1, False)

            @pl.when(step > 1)
            def _():
                send_down(step - 2)

        at = slice(chunk * rows, (chunk + 1) * rows)
        hidden = dot(pick(own_out_ref, other_out_ref, chunk), up, 1, 0) + up_bias_ref[...]
        squared = hidden * hidden
        tanh = jnp.tanh(hidden * (0.7978845608028654 + 0.035677408136300125 * squared))
        gate = 0.5 + 0.5 * tanh
        activated = (hidden * gate).astype(jnp.bfloat16)
        slope = gate + (0.5 * hidden) * (1.0 - tanh * tanh) * (0.7978845608028654 + 0.10703222440890037 * squared)
        act_t[:, at] = activated.T
        grad = (slope * dot(grad_two[at], down, 1, 1)).astype(jnp.bfloat16)
        grad_attended_ref[at] = grad
        bias_sum = bias_sum + jnp.sum(grad.astype(jnp.float32), 0, keepdims=True)
        sum_two[at] += dot(activated, down, 1, 0)
        sum_second[at] += dot(grad, up, 1, 1)

    up_bias_grad_ref[...] = bias_sum
    down_grad = dot(act_t[...], grad_two[...], 1, 0).astype(jnp.bfloat16).reshape(2, 2, -1, model)
    share(core, (down_grad[:, 0], down_grad[:, 1]), down_keep, down_give, step)
    up_grad = dot(second_t[...], grad_attended_ref[...], 1, 0).astype(jnp.bfloat16).reshape(up_keep.shape[1], 2, -1, width)
    share(core, (up_grad[:, 0], up_grad[:, 1]), up_keep, up_give, step)
    for copy in first_copies(step):
        copy.start()

    @pl.when(step == pl.num_programs(0) - 1)
    def _():
        sums = [jnp.zeros((1, model), jnp.float32) for _ in range(4)]
        for chunk in range(length // rows):
            at = slice(chunk * rows, (chunk + 1) * rows)
            branch = grad_middle_ref[at]
            middle = pick(own_ref, other_ref, chunk).astype(jnp.float32) + gate_one * branch
            normed, inverse = norm_rows(middle)
            branch_two = sum_two[at] + down_bias_ref[...]
            output = (middle + gate_two * branch_two).astype(jnp.bfloat16)
            place = (chunk * rows) % half
            (own_out_ref if chunk * rows < half else other_out_ref)[place : place + rows] = output
            cot = live_cot(chunk)
            grad = sum_second[at]
            weighted = grad * normed
            scaled = grad * scaling
            inner = jnp.mean(weighted * scaling, -1, keepdims=True)
            grad_middle = cot + (scaled - jnp.mean(scaled, -1, keepdims=True) - normed * inner) * inverse
            grad_middle_ref[at] = grad_middle
            grad_one = (gate_one * grad_middle).astype(jnp.bfloat16)
            grad_two[at] = grad_one
            act_t[:, at] = attended_ref[at].T
            grad_attended_ref[at] = dot(grad_one, out_weight_ref[...], 1, 1).astype(jnp.bfloat16)
            for i, term in enumerate((grad_middle * branch, grad, weighted, cot * branch_two)):
                sums[i] = sums[i] + jnp.sum(term, 0, keepdims=True)
            if (chunk + 1) * rows == half:
                send_on(last, True)
                send_down(last - 1)
        rows_ref[0:1] = sums[0]
        rows_ref[1:2] = sums[1]
        rows_ref[2:3] = sums[2] * gain_ref[...]
        rows_ref[3:4] = sums[3]
        rows_ref[4:5] = sums[2] * (1.0 + mod_ref[4:5])
        out_grad = dot(act_t[...], grad_two[...], 1, 0).astype(jnp.bfloat16)
        out_grad = out_grad.reshape(out_keep_ref.shape[0], 2, -1, model)
        share(core, (out_grad[:, 0], out_grad[:, 1]), out_keep_ref, out_send_ref, Ellipsis)
        for tile in range(last):
            settle(tile, False)
        settle(last, True)
        for tile in range(tiles):
            ups = [up_last_copy()] if tile == last else up_copies(tile)
            for copy in first_copies(tile) + [down_copy(tile)] + ([] if tile == last else [down_on_copy(tile)]) + ups:
                copy.wait_send()


Z_FLIPS = ("Z", "W", "ZW")


class Links:
    def __init__(self):
        dp = lax.axis_index("dp")
        self.me = lax.axis_index("seq")
        self.bit = {"C": dp % 2, "X": (dp // 2) % 2, "Z": (dp // 4) % 2, "W": (dp // 8) % 2, "Y": self.me}
        jump = {name: size * (1 - 2 * self.bit[name]) for name, size in (("C", 1), ("X", 2), ("Z", 4), ("W", 8))}
        self.partner = {name: (dp + jump[name], self.me) for name in "CXZW"}
        self.partner["ZW"] = (dp + jump["Z"] + jump["W"], self.me)
        self.partner["Y"] = (dp, 1 - self.me)

    def place(self):
        return self.me * 16 + self.bit["X"] * 8 + self.bit["W"] * 4 + self.bit["Z"] * 2 + self.bit["C"]

    def greet(self, names=("C", "X", "Z", "W", "ZW", "Y")):
        barrier = pltpu.get_barrier_semaphore()
        for name in names:
            device = self.partner[name]
            pl.semaphore_signal(barrier, inc=1, device_id=device, device_id_type=pl.DeviceIdType.MESH)
        pl.semaphore_wait(barrier, len(names))


def flips_of(kind):
    return Z_FLIPS if kind == "V" else (kind,)


def remote(source, target, sems, slot, device):
    return pltpu.make_async_remote_copy(
        src_ref=source,
        dst_ref=target,
        send_sem=sems.at[0, slot],
        recv_sem=sems.at[1, slot],
        device_id=device,
        device_id_type=pl.DeviceIdType.MESH,
    )


def piece_scratch(spec):
    _, rows, width, left, order, kind = spec
    count = 1 << len(left)
    shapes = [count] * (1 + ("summed", "given", "made").index(kind))
    for step in order:
        count //= 4 if step == "V" else 2
        shapes += [count * len(flips_of(step))] * 2
    shapes += [1] * 2
    return [pltpu.VMEM((c, rows, width), jnp.bfloat16) for c in shapes]


class Piece:
    def __init__(self, links, refs, spec, sems, slot, source=None, split=False):
        refs = list(refs)
        _, _, _, left, order, kind = spec
        self.links = links
        self.sems = sems
        self.slot = slot
        self.order = list(order)
        self.split = split
        self.left = list(left)
        self.keep = refs.pop(0)
        self.terms = [(self.keep, list(self.left))]
        self.copies = []
        self.flying = []
        if kind != "summed":
            first = refs.pop(0)
            self.source = refs.pop(0) if kind == "made" else source
            copy = (self.source, first, sems, slot, links.partner["C"])
            self.slot += 1
            self.copies.append(copy)
            self.flying = [(copy, first, list(self.left))]
        self.buffers = refs

    def launch(self, source, target, flip):
        copy = (source, target, self.sems, self.slot, self.links.partner[flip])
        self.slot += 1
        remote(*copy).start()
        self.copies.append(copy)
        self.flying.append((copy, target, list(self.left)))

    def begin(self):
        remote(*self.copies[0]).start()

    def arrive(self):
        for copy, target, bits in self.flying:
            remote(*copy).wait_recv()
            self.terms.append((target, bits))
        self.flying = []

    def index(self, bits, values):
        at = 0
        for bit in bits:
            at = at * 2 + values[bit]
        return at

    def add(self, out, flip):
        links = self.links
        rows = out.shape[1]
        block = 48
        for combo in range(1 << len(self.left)):
            values = dict(links.bit)
            for bit in flip:
                values[bit] = 1 - links.bit[bit]
            for place, bit in enumerate(self.left):
                values[bit] = (combo >> (len(self.left) - 1 - place)) & 1
            indices = [self.index(bits, values) for _, bits in self.terms]

            def some(i, carry, indices=indices, combo=combo):
                at = pl.ds(pl.multiple_of(i * block, 16), block)
                total = None
                for (ref, _), index in zip(self.terms, indices):
                    term = ref[index, at, :].astype(jnp.float32)
                    total = term if total is None else total + term
                out[combo, at, :] = total.astype(jnp.bfloat16)
                return carry

            lax.fori_loop(0, rows // block, some, 0)

    def step(self):
        self.arrive()
        kind = self.order.pop(0)
        out, target = self.buffers.pop(0), self.buffers.pop(0)
        for bit in "WZ" if kind == "V" else kind:
            self.left.remove(bit)
        count = 1 << len(self.left)
        for i, flip in enumerate(flips_of(kind)):
            part = pl.ds(i * count, count)
            self.add(out.at[part], flip)
            self.launch(out.at[part], target.at[part], flip)

    def last(self):
        self.arrive()
        self.total, self.got = self.buffers.pop(0), self.buffers.pop(0)
        self.add(self.total, "")
        self.launch(self.total, self.got, "Y")

    def result(self, store):
        remote(*self.flying[0][0]).wait_recv()
        rows = self.total.shape[1]
        total = self.total[0].astype(jnp.float32)
        got = self.got[0].astype(jnp.float32)
        if self.split:
            store(pl.ds(pl.multiple_of(self.links.me * rows, 8), rows), total)
            store(pl.ds(pl.multiple_of((1 - self.links.me) * rows, 8), rows), got)
        else:
            store(slice(0, rows), total + got)


CHUNKS = (3, 2, 1)
BACK_PIECES = (
    ("down", 96, 768, "WZ", "V", "summed"),
    ("upv", 144, 768, "X", "X", "summed"),
    ("upx", 48, 768, "WZ", "V", "summed"),
    ("out", 48, 768, "WZX", "XV", "given"),
    *((f"in{i}", 48, 384 * pairs, "WZX", "XV", "made") for i, pairs in enumerate(CHUNKS)),
)


def copies_of(spec):
    return sum(len(flips_of(kind)) for kind in spec[4]) + 1 + (spec[5] != "summed")


BACK_COPIES = sum(copies_of(spec) for spec in BACK_PIECES)
HOPS = (("C",), Z_FLIPS, ("X",), ("Y",))
RUNNING = "CXZWY"


def spread_copies(links, array, sems, slot, number):
    place = links.place()
    have = (1, 2, 8, 16)[number]
    part = array.at[pl.ds((place // have) * have, have)]
    slot += (0, 1, 4, 5)[number]
    return [remote(part, part, sems, slot + i, links.partner[flip]) for i, flip in enumerate(HOPS[number])]


def start_all(copies):
    for copy in copies:
        copy.start()


def receive_all(copies):
    for copy in copies:
        copy.wait_recv()


def front_kernel(
    tokens_hbm,
    time_ref,
    mod_weight_hbm,
    mod_bias_ref,
    gain_ref,
    weight_hbm,
    cos_hbm,
    sin_hbm,
    first_t_ref,
    qkv_hbm,
    other_hbm,
    mod_ref,
    other_ref,
    own,
    mod_weight,
    weight,
    cos_ref,
    sin_ref,
    qkv,
    sems,
    local_sems,
    store_sems,
):
    rows = T_ROWS
    half, model = own.shape
    blocks = half // rows
    links = Links()

    def exchange(block):
        at = pl.ds(block * rows, rows)
        return remote(tokens_hbm.at[1 - links.me, at], other_ref.at[at], sems, block, links.partner["Y"])

    def fetches():
        pairs = (
            (mod_weight_hbm, mod_weight),
            (tokens_hbm.at[links.me], own),
            (weight_hbm, weight),
            (cos_hbm.at[links.me], cos_ref),
            (sin_hbm.at[links.me], sin_ref),
        )
        return [pltpu.make_async_copy(a, b, local_sems.at[i]) for i, (a, b) in enumerate(pairs)]

    def store(block):
        at = pl.ds(block * rows, rows)
        return pltpu.make_async_copy(qkv.at[at], qkv_hbm.at[at], store_sems.at[block])

    def store_other(block):
        at = pl.ds(block * rows, rows)
        return pltpu.make_async_copy(other_ref.at[at], other_hbm.at[at], store_sems.at[2 * blocks + block])

    for copy in fetches():
        copy.start()
    links.greet(("Y",))
    for block in range(blocks):
        exchange(block).start()
    for copy in fetches():
        copy.wait()
    embedding = time_ref[...].astype(jnp.float32)
    embedding = jnp.where(links.me == 0, embedding[0:1], embedding[1:2])
    embedding = jnp.broadcast_to(embedding, (16, embedding.shape[1])).astype(jnp.bfloat16)
    modulation = dot(embedding, mod_weight[...], 1, 1)[0:1] + mod_bias_ref[...].astype(jnp.float32)
    parts = [modulation[:, i * model : (i + 1) * model] for i in range(6)]
    for i in range(6):
        mod_ref[i : i + 1] = parts[i]
    lane = lax.broadcasted_iota(jnp.int32, (rows, 128), 1)
    scaling = gain_ref[...].astype(jnp.float32) * (1.0 + parts[1])
    for block in range(2 * blocks):
        if block < blocks:
            source = own[block * rows : (block + 1) * rows]
        else:
            exchange(block - blocks).wait_recv()
            source = other_ref[(block - blocks) * rows : (block - blocks + 1) * rows]
            store_other(block - blocks).start()
        at = slice(block * rows, (block + 1) * rows)
        normed, _ = norm_rows(source.astype(jnp.float32))
        first = (normed * scaling + parts[0]).astype(jnp.bfloat16)
        first_t_ref[:, at] = first.T
        for part in range(3):
            projected = dot(first, weight[:, part * model : (part + 1) * model], 1, 0)
            for column in range(model // 128):
                piece = projected[:, column * 128 : (column + 1) * 128]
                if part < 2:
                    piece = piece * cos_ref[at] + swap_halves(piece, lane) * sin_ref[at]
                piece = piece.astype(jnp.bfloat16)
                if part == 0:
                    piece = piece * 0.125
                start = part * model + column * 128
                qkv[at, start : start + 128] = piece
        store(block).start()
    for block in range(2 * blocks):
        store(block).wait()
    for block in range(blocks):
        store_other(block).wait()
        exchange(block).wait_send()


def back_kernel(
    q_ref,
    k_ref,
    v_ref,
    out_ref,
    grad_ref,
    exp_ref,
    inv_ref,
    cos_ref,
    sin_ref,
    first_t_hbm,
    weight_hbm,
    own_hbm,
    other_hbm,
    grad_middle_hbm,
    mod_ref,
    gain_ref,
    down_keep,
    down_tail_hbm,
    upv_keep,
    upx_keep,
    out_keep,
    out_send,
    mid_rows_ref,
    up_bias_ref,
    time_ref,
    mod_weight_hbm,
    other_block_ref,
    _,
    tokens_grad_ref,
    time_grad_ref,
    mod_weight_grad_ref,
    mod_bias_grad_ref,
    gain_grad_ref,
    feed_gain_grad_ref,
    up_bias_grad_ref,
    down_bias_grad_ref,
    down_ref,
    up_ref,
    out_grad_ref,
    in_ref,
    block_ref,
    first_t_ref,
    weight_ref,
    own_ref,
    other_ref,
    grad_middle_ref,
    mod_weight_ref,
    down_tail,
    down_tail_give,
    down_tail_got,
    ds_ref,
    dq_sum,
    proj,
    tokens_stage,
    rows_ref,
    early,
    late,
    running,
    running_got,
    by_vector,
    spread,
    spread_bias,
    turned,
    sems,
    local_sems,
    *buffers,
):
    rows = T_ROWS
    step = pl.program_id(0)
    length = q_ref.shape[0]
    half, model = other_ref.shape
    links = Links()
    core = links.bit["C"]
    pieces = []
    buffers = list(buffers)
    slot = 0
    for spec in BACK_PIECES:
        count = len(piece_scratch(spec))
        source = out_send if spec[0] == "out" else None
        pieces.append(Piece(links, buffers[:count], spec, sems, slot, source, spec[0] == "down"))
        buffers = buffers[count:]
        slot += copies_of(spec)
    down, upv, upx, out, *ins = pieces

    def fetches(first=0, end=11):
        pairs = (
            (upv_keep, upv.keep),
            (down_keep, down.keep.at[pl.ds(0, 3)]),
            (upx_keep, upx.keep),
            (out_keep, out.keep),
            (down_tail_hbm, down_tail),
            (first_t_hbm, first_t_ref),
            (weight_hbm, weight_ref),
            (other_hbm, other_ref),
            (grad_middle_hbm, grad_middle_ref),
            (own_hbm.at[links.me], own_ref),
            (mod_weight_hbm, mod_weight_ref),
        )
        return [pltpu.make_async_copy(a, b, local_sems.at[i]) for i, (a, b) in enumerate(pairs) if first <= i < end]

    place = links.place()
    dp = lax.axis_index("dp")
    early_slot = BACK_COPIES + 6
    quarter = half // 4
    late_slot = early_slot + 6
    running_slot = late_slot + 6
    tail_slot = running_slot + 5

    def running_copy(number):
        partner = links.partner[RUNNING[number]]
        return remote(running.at[number], running_got.at[number], sems, running_slot + number, partner)

    def tail_copy():
        return remote(down_tail_give, down_tail_got, sems, tail_slot, links.partner["X"])

    def block_copy(number):
        at = pl.ds(number * quarter, quarter)
        target = block_ref.at[links.me, at]
        return remote(other_block_ref.at[at], target, sems, BACK_COPIES + number, links.partner["Y"])

    def halves(target, at, first, values):
        middle = model // 2
        target[at, first : first + 1] = values[:, :middle]
        target[at, first + 1 : first + 2] = values[:, middle:]

    @pl.when(step == 0)
    def _():
        links.greet()
        for copy in fetches():
            copy.start()
        out.begin()
        for m in range(4):
            halves(early, place, 2 * m, mid_rows_ref[m : m + 1])
        running[0, 0:2] = mid_rows_ref[4:6]
        for tile in range(up_bias_ref.shape[1] // model):
            running[0, 2 + tile : 3 + tile] = up_bias_ref[:, tile * model : (tile + 1) * model]
        running[0, 6:8] = jnp.zeros((2, model), jnp.float32)
        start_all(spread_copies(links, early, sems, early_slot, 0))
        running_copy(0).start()

    for number in range(4):

        @pl.when(step == number + 1)
        def _(number=number):
            block_copy(number).start()

    def early_arrive(number):
        receive_all(spread_copies(links, early, sems, early_slot, number))

    def early_start(number):
        start_all(spread_copies(links, early, sems, early_slot, number))

    def running_arrive(number):
        running_copy(number).wait_recv()
        running[number + 1] = running[number] + running_got[number]

    def at_step(number):
        return pl.when(step == number)

    def between():
        @at_step(0)
        def _():
            for copy in fetches(0, 5):
                copy.wait()
            down_tail_give[...] = down_tail[1 - links.bit["X"]]
            early_arrive(0)
            running_arrive(0)
            early_start(1)
            running_copy(1).start()
            tail_copy().start()
            upv.step()
            upx.step()

        @at_step(1)
        def _():
            early_arrive(1)
            running_arrive(1)
            early_start(2)
            running_copy(2).start()
            tail_copy().wait_recv()
            kept = down_tail[links.bit["X"]].astype(jnp.float32) + down_tail_got[...].astype(jnp.float32)
            down.keep[3] = kept.astype(jnp.bfloat16)
            down.step()
            out.step()

        @at_step(2)
        def _():
            for copy in fetches(5):
                copy.wait()
            upx.last()
            upv.last()

        @at_step(3)
        def _():
            early_arrive(2)
            running_arrive(2)
            early_start(3)
            running_copy(3).start()
            ins[0].step()

        @at_step(4)
        def _():
            out.step()
            down.last()

        @at_step(5)
        def _():
            running_arrive(3)
            running_copy(4).start()
            ins[1].step()
            ins[0].step()

    lane = lax.broadcasted_iota(jnp.int32, (rows, 128), 1)

    @pl.when(step < 6)
    def _():
        keys = k_ref[...]
        values = v_ref[...]
        scaled = grad_ref[...].astype(jnp.float32) * inv_ref[...]
        products = scaled * out_ref[...].astype(jnp.float32)
        scaled = scaled.astype(jnp.bfloat16)
        scaled_t = scaled.T
        queries_t = q_ref[...].T
        grad_k = []
        grad_v = []
        for head in range(2):
            if head == 1:
                between()
            for chunk in range(length // rows):
                at = slice(chunk * rows, (chunk + 1) * rows)
                mask = (lane < 64) == (head == 0)
                mine = jnp.where(mask, scaled[at], jnp.zeros((rows, 128), jnp.bfloat16))
                row_dots = jnp.sum(jnp.where(mask, products[at], 0.0), -1, keepdims=True)
                grad_p = dot(mine, values, 1, 1)
                grad_s = (exp_ref[head, at].astype(jnp.float32) * (grad_p - row_dots)).astype(jnp.bfloat16)
                ds_ref[at] = grad_s
                grad_q = dot(grad_s, keys, 1, 0) * 0.125
                if head == 0:
                    dq_sum[at] = grad_q
                else:
                    dq_sum[at] = jnp.where(lane < 64, dq_sum[at], grad_q)
            grad_v.append(dot(scaled_t[64 * head : 64 * head + 64], exp_ref[head], 1, 0))
            grad_k.append(dot(queries_t[64 * head : 64 * head + 64], ds_ref[...], 1, 0))
        columns = [pl.ds(pl.multiple_of(part * model + step * 128, 128), 128) for part in range(3)]
        proj[:, columns[2]] = jnp.concatenate(grad_v, 0).astype(jnp.bfloat16).T
        grad_keys = jnp.concatenate(grad_k, 0).astype(jnp.bfloat16).T
        for chunk in range(length // rows):
            at = slice(chunk * rows, (chunk + 1) * rows)
            for part, source in enumerate((dq_sum[at].astype(jnp.bfloat16), grad_keys[at])):
                piece = source.astype(jnp.float32)
                turned = piece * cos_ref[at] - swap_halves(piece, lane) * sin_ref[at]
                proj[at, columns[part]] = turned.astype(jnp.bfloat16)

    starts = [128 * sum(CHUNKS[:i]) for i in range(len(CHUNKS))]

    def weight_part(group):
        piece = ins[group]
        span = 128 * CHUNKS[group]
        for part in range(3):
            column = part * model + starts[group]
            grad = dot(first_t_ref[...], proj[:, column : column + span], 1, 0).astype(jnp.bfloat16)
            grad = grad.reshape(8, 2, -1, span)
            share(core, (grad[:, 0], grad[:, 1]), piece.keep, piece.source, Ellipsis, slice(part * span, (part + 1) * span))
        piece.begin()

    for group, number in enumerate((2, 4, 5)):
        at_step(number)(functools.partial(weight_part, group))

    scaling = gain_ref[...] * (1.0 + mod_ref[1:2])

    def entry(values_ref, base, chunk):
        at = slice(base + chunk * rows, base + (chunk + 1) * rows)
        local = slice(chunk * rows, (chunk + 1) * rows)
        grad = dot(proj[at], weight_ref[...], 1, 1)
        normed, inverse = norm_rows(values_ref[local].astype(jnp.float32))
        weighted = grad * normed
        scaled = grad * scaling
        inner = jnp.mean(weighted * scaling, -1, keepdims=True)
        result = grad_middle_ref[at] + (scaled - jnp.mean(scaled, -1, keepdims=True) - normed * inner) * inverse
        tokens_stage[at] = result.astype(jnp.bfloat16)
        return jnp.concatenate([jnp.sum(grad, 0, keepdims=True), jnp.sum(weighted, 0, keepdims=True)], 0)

    def away(chunk):
        source = tokens_stage.at[pl.ds(half + chunk * rows, rows)]
        target = tokens_grad_ref.at[links.me, pl.ds(chunk * rows, rows)]
        return remote(source, target, sems, BACK_COPIES + 4 + chunk, links.partner["Y"])

    def home():
        return pltpu.make_async_copy(tokens_stage.at[pl.ds(0, half)], tokens_grad_ref.at[links.me], local_sems.at[11])

    def vectors():
        middle = model // 2
        for m in range(6):
            source, row = (late, 2 * m) if m < 2 else (early, 2 * m - 4)
            by_vector[m, :, 0:middle] = source[:, row, :]
            by_vector[m, :, middle:model] = source[:, row + 1, :]
        ones = jnp.ones((32, 128), jnp.float32)
        factors = jnp.concatenate([late[:, 6, 0:128], ones], 1)
        unit = mod_weight_grad_ref.shape[0] // 6
        for part in range(6):
            at = dp * 6 + part
            product = lax.dot_general(
                by_vector[at // 16],
                factors,
                (((0,), (0,)), ((), ())),
                precision=highest,
                preferred_element_type=jnp.float32,
            )
            spread[...] = product
            kept = spread[pl.ds(pl.multiple_of((at % 16) * unit, 8), unit), :]
            mod_weight_grad_ref[part * unit : (part + 1) * unit] = kept[:, 0:128]
            spread_bias[part * unit : (part + 1) * unit] = kept[:, 128:256]
        mod_bias_grad_ref[...] = spread_bias[...].T[0:1]
        base = place % 16
        both = jnp.zeros((2, 128), jnp.float32)
        for m in range(6):
            rest = jnp.concatenate([by_vector[m, pl.ds(base, 1)], by_vector[m, pl.ds(base + 16, 1)]], 0)
            for _ in range(3):
                high = rest.astype(jnp.bfloat16)
                both = both + dot(high, mod_weight_ref[m * model : (m + 1) * model], 1, 0)
                rest = rest - high.astype(jnp.float32)
        time_grad_ref[...] = both
        gains = [jnp.sum(late[:, row, :], 0, keepdims=True) for row in (4, 5)]
        gains = jnp.concatenate(gains, 1)
        turned[...] = jnp.concatenate([running[5, 0:6], gains, gains], 0).T
        narrow = turned[pl.ds(pl.multiple_of(dp * unit, 8), unit), :].T
        feed_gain_grad_ref[...] = narrow[0:1]
        down_bias_grad_ref[...] = narrow[1:2]
        gain_grad_ref[...] = narrow[6:7]
        wide_rows = up_bias_grad_ref.shape[1]
        share_of = model // wide_rows
        wide = turned[pl.ds(pl.multiple_of((dp % share_of) * wide_rows, 8), wide_rows), :].T
        picked = jnp.zeros((1, wide_rows), jnp.float32)
        for tile in range(4):
            picked = jnp.where(dp // share_of == tile, wide[2 + tile : 3 + tile], picked)
        up_bias_grad_ref[...] = picked

    @at_step(6)
    def _():
        rows_ref[...] = entry(other_ref, half, 0)
        ins[2].step()
        away(0).start()
        rows_ref[...] += entry(other_ref, half, 1)
        out.last()
        away(1).start()
        ins[1].step()

    @at_step(7)
    def _():
        rows_ref[...] += entry(own_ref, 0, 0)
        ins[2].step()
        rows_ref[...] += entry(own_ref, 0, 1)
        home().start()
        scaling_one = 1.0 + mod_ref[1:2]
        halves(late, place, 0, rows_ref[0:1])
        halves(late, place, 2, rows_ref[1:2] * gain_ref[...])
        halves(late, place, 4, rows_ref[1:2] * scaling_one)
        embedding = time_ref[...].astype(jnp.float32)
        late[place, 6:7, 0:128] = jnp.where(links.me == 0, embedding[0:1], embedding[1:2])
        start_all(spread_copies(links, late, sems, late_slot, 0))
        hop = iter(range(4))

        def hop_on():
            number = next(hop)
            receive_all(spread_copies(links, late, sems, late_slot, number))
            if number < 3:
                start_all(spread_copies(links, late, sems, late_slot, number + 1))

        early_arrive(3)
        running_arrive(4)
        ins[0].last()
        hop_on()
        ins[1].last()
        hop_on()
        ins[2].last()
        hop_on()
        hop_on()
        vectors()
        for group in range(3):
            def store(at, value, group=group):
                span = 128 * CHUNKS[group]
                for part in range(3):
                    column = part * model + starts[group]
                    in_ref[at, column : column + span] = value[:, part * span : (part + 1) * span]

            ins[group].result(store)

        def store_out(at, value):
            out_grad_ref[at] = value

        out.result(store_out)

        def store_down(at, value):
            down_ref[at] = value

        down.result(store_down)

        def store_up(first):
            def store(at, value):
                count = up_ref.shape[0]
                for tile in range(value.shape[0] // count):
                    columns = slice((first + tile) * model, (first + tile + 1) * model)
                    up_ref[:, columns] = value[tile * count : (tile + 1) * count]

            return store

        upv.result(store_up(0))
        upx.result(store_up(3))
        home().wait()
        for chunk in range(half // rows):
            away(chunk).wait()
        for number in range(4):
            block_copy(number).wait()
        for number in range(4):
            for copy in spread_copies(links, early, sems, early_slot, number) + spread_copies(links, late, sems, late_slot, number):
                copy.wait_send()
        for number in range(5):
            running_copy(number).wait_send()
        tail_copy().wait_send()
        for piece in pieces:
            for copy in piece.copies:
                remote(*copy).wait_send()


def close_kernel(*refs):
    count = len(refs) // 2
    for source, target in zip(refs[:count], refs[count:]):
        target[...] = source[...]


def turn_tables(length):
    inverse = 10000.0 ** (-np.arange(HD // 2, dtype=np.float64) * 2.0 / HD)
    angles = np.arange(length, dtype=np.float64)[:, None] * inverse[None, :]
    cosine = np.tile(np.cos(angles), (1, 4))
    sines = np.sin(angles)
    sines = np.concatenate([-sines, sines, -sines, sines], 1)
    both = [np.stack([t, np.roll(t, -(length // 2), 0)]).astype(np.float32) for t in (cosine, sines)]
    return jnp.asarray(both[0]), jnp.asarray(both[1])


def fast_body(
    tokens,
    time_embedding,
    prefix_length,
    suffix_mask,
    cotangent,
    modulation_weight,
    modulation_bias,
    attention_gain,
    attention_in,
    attention_out,
    feed_gain,
    feed_up,
    feed_up_bias,
    feed_down,
    feed_down_bias,
):
    bf16 = jnp.bfloat16
    f32 = jnp.float32
    _, half, model = tokens.shape
    length = 2 * half
    hidden_width = feed_up.shape[1]
    size = lax.axis_size("dp")
    shape = jax.ShapeDtypeStruct

    packed = [modulation_bias, attention_gain, feed_gain, feed_down_bias, feed_up_bias]
    packed = jnp.concatenate(packed).astype(f32)[None]

    def packed_at(number):
        return pl.BlockSpec((1, model), lambda h: (0, number), pipeline_mode=pl.Buffered(1))

    cosine, sines = turn_tables(length)
    anywhere = pl.BlockSpec(memory_space=pl.ANY)

    def fixed(*dims):
        return pl.BlockSpec(dims, lambda h: (0,) * len(dims), pipeline_mode=pl.Buffered(1))

    first_t, qkv, other, modulation = pl.pallas_call(
        front_kernel,
        grid=(1,),
        in_specs=[
            anywhere,
            fixed(2, 128),
            anywhere,
            fixed(1, 6 * model),
            packed_at(6),
            anywhere,
            anywhere,
            anywhere,
        ],
        out_specs=[fixed(model, length), anywhere, anywhere, fixed(6, model)],
        out_shape=[
            shape((model, length), bf16),
            shape((length, 3 * model), bf16),
            shape((half, model), bf16),
            shape((6, model), f32),
        ],
        scratch_shapes=[
            pltpu.VMEM((half, model), bf16),
            pltpu.VMEM((half, model), bf16),
            pltpu.VMEM((6 * model, 128), bf16),
            pltpu.VMEM((model, 3 * model), bf16),
            pltpu.VMEM((length, 128), f32),
            pltpu.VMEM((length, 128), f32),
            pltpu.VMEM((length, 3 * model), bf16),
            pltpu.SemaphoreType.DMA((2, half // T_ROWS)),
            pltpu.SemaphoreType.DMA((5,)),
            pltpu.SemaphoreType.DMA((3 * half // T_ROWS,)),
        ],
        compiler_params=pltpu.CompilerParams(vmem_limit_bytes=62 * MIB, collective_id=2, has_side_effects=True),
        cost_estimate=pl.CostEstimate(flops=2 * length * model * 3 * model, bytes_accessed=16 * MIB, transcendentals=0),
        name="front",
    )(tokens, time_embedding, modulation_weight, packed, packed, attention_in, cosine, sines)

    def column(k):
        return pl.BlockSpec((length, 128), lambda h: (0, h + k))

    pairs = model // 128
    attended, exps, inverses, own_live, other_live, other_cot = pl.pallas_call(
        attend_kernel,
        grid=(pairs,),
        in_specs=[
            pl.BlockSpec(memory_space=pltpu.SMEM),
            column(0),
            column(pairs),
            column(2 * pairs),
            fixed(2, half),
            anywhere,
        ],
        out_specs=[
            column(0),
            pl.BlockSpec((2, length, length), lambda h: (h, 0, 0)),
            column(0),
            fixed(8, half),
            fixed(8, half),
            anywhere,
        ],
        out_shape=[
            shape((length, model), bf16),
            shape((HEADS, length, length), bf16),
            shape((length, model), f32),
            shape((8, half), f32),
            shape((8, half), f32),
            shape((half, model), bf16),
        ],
        scratch_shapes=[pltpu.VMEM((8, half), f32), pltpu.VMEM((8, half), f32), pltpu.SemaphoreType.DMA((2, 2))],
        compiler_params=pltpu.CompilerParams(vmem_limit_bytes=60 * MIB, collective_id=3, has_side_effects=True),
        cost_estimate=pl.CostEstimate(flops=16 * length * length * model, bytes_accessed=32 * MIB, transcendentals=0),
        name="attend",
    )(prefix_length, qkv, qkv, qkv, suffix_mask, cotangent)

    tiles = 4
    width = hidden_width // tiles
    groups = size // 2
    share_rows = hidden_width // size
    model_rows = model // size
    own_part = pl.BlockSpec((None, half, model), lambda h: (lax.axis_index("seq"), 0, 0), pipeline_mode=pl.Buffered(1))
    up_tile = pl.BlockSpec((model, width), lambda j: (0, j))
    bias_tile = pl.BlockSpec((1, width), lambda j: (0, j))
    down_tile = pl.BlockSpec((width, model), lambda j: (j, 0))
    (
        own_out,
        other_out,
        grad_middle,
        grad_attended,
        mid_rows,
        up_bias_grad,
        down_sum,
        down_tail,
        upv_sum,
        upx_sum,
        out_keep,
        out_send,
    ) = pl.pallas_call(
        middle_kernel,
        grid=(tiles,),
        in_specs=[own_part, fixed(half, model), own_part, fixed(half, model), fixed(8, half), fixed(8, half)]
        + [
            fixed(length, model),
            fixed(6, model),
            packed_at(7),
            fixed(model, model),
            up_tile,
            pl.BlockSpec((1, width), lambda j: (0, j + 9)),
            down_tile,
            packed_at(8),
        ],
        out_specs=[
            own_part,
            fixed(half, model),
            fixed(length, model),
            fixed(length, model),
            fixed(6, model),
            bias_tile,
            fixed(tiles - 1, share_rows // 2, model),
            fixed(2, share_rows // 2, model),
            fixed(2, tiles - 1, model_rows, model),
            fixed(4, model_rows, model),
            fixed(groups, model_rows, model),
            fixed(groups, model_rows, model),
        ],
        out_shape=[shape((2, half, model), bf16), shape((half, model), bf16)]
        + [shape((length, model), f32), shape((length, model), bf16), shape((6, model), f32), shape((1, hidden_width), f32)]
        + [shape((tiles - 1, share_rows // 2, model), bf16), shape((2, share_rows // 2, model), bf16), shape((2, tiles - 1, model_rows, model), bf16)]
        + [shape((4, model_rows, model), bf16)]
        + [shape((groups, model_rows, model), bf16)] * 2,
        scratch_shapes=[
            pltpu.VMEM((model, length), bf16),
            pltpu.VMEM((length, model), bf16),
            pltpu.VMEM((length, model), f32),
            pltpu.VMEM((length, model), f32),
            pltpu.VMEM((width, length), bf16),
        ]
        + [pltpu.VMEM((tiles, groups // tiles, share_rows, model), bf16)] * 3
        + [pltpu.VMEM((tiles, groups, model_rows, model), bf16)] * 3
        + [pltpu.VMEM((tiles, groups // tiles, share_rows // 2, model), bf16)] * 2
        + [pltpu.VMEM((tiles - 1, share_rows // 2, model), bf16)] * 2
        + [pltpu.VMEM((tiles - 1, 3, 2, model_rows, model), bf16)] * 2
        + [pltpu.VMEM((4, model_rows, model), bf16)] * 2
        + [pltpu.SemaphoreType.DMA((2, 7 * tiles))],
        compiler_params=pltpu.CompilerParams(vmem_limit_bytes=63 * MIB, collective_id=1, has_side_effects=True),
        cost_estimate=pl.CostEstimate(
            flops=12 * length * model * hidden_width + 6 * length * model * model, bytes_accessed=36 * MIB, transcendentals=0
        ),
        name="middle",
    )(
        tokens,
        other,
        cotangent,
        other_cot,
        own_live,
        other_live,
        attended,
        modulation,
        packed,
        attention_out,
        feed_up,
        packed,
        feed_down,
        packed,
    )
    merge = (2, (tiles - 1) * model_rows, model)

    def near(k):
        return pl.BlockSpec((length, 128), lambda h: (0, jnp.minimum(h, pairs - 1) + k))

    turn = pl.BlockSpec((None, length, 128), lambda h: (lax.axis_index("seq"), 0, 0), pipeline_mode=pl.Buffered(1))
    scratch = [
        pltpu.VMEM((model, length), bf16),
        pltpu.VMEM((model, 3 * model), bf16),
        pltpu.VMEM((half, model), bf16),
        pltpu.VMEM((half, model), bf16),
        pltpu.VMEM((length, model), f32),
        pltpu.VMEM((6 * model, 128), bf16),
        pltpu.VMEM((2, share_rows // 2, model), bf16),
        pltpu.VMEM((share_rows // 2, model), bf16),
        pltpu.VMEM((share_rows // 2, model), bf16),
        pltpu.VMEM((length, length), bf16),
        pltpu.VMEM((length, 128), f32),
        pltpu.VMEM((length, 3 * model), bf16),
        pltpu.VMEM((length, model), bf16),
        pltpu.VMEM((2, model), f32),
        pltpu.VMEM((2 * size, 8, model // 2), f32),
        pltpu.VMEM((2 * size, 8, model // 2), f32),
        pltpu.VMEM((6, 8, model), f32),
        pltpu.VMEM((5, 8, model), f32),
        pltpu.VMEM((6, 2 * size, model), f32),
        pltpu.VMEM((model, 256), f32),
        pltpu.VMEM((6 * model_rows, 128), f32),
        pltpu.VMEM((model, 8), f32),
        pltpu.SemaphoreType.DMA((2, BACK_COPIES + 24)),
        pltpu.SemaphoreType.DMA((12,)),
    ]
    for spec in BACK_PIECES:
        scratch += piece_scratch(spec)
    def cut(dims):
        if len(dims) == 3:
            return pl.BlockSpec((1, *dims[1:]), lambda i: (i, 0, 0))
        if dims[0] % 16:
            return pl.BlockSpec(dims, lambda i: (0, 0))
        return pl.BlockSpec((dims[0] // 2, dims[1]), lambda i: (i, 0))

    results = pl.pallas_call(
        back_kernel,
        grid=(pairs + 2,),
        in_specs=[
            near(0),
            near(pairs),
            near(2 * pairs),
            near(0),
            near(0),
            pl.BlockSpec((2, length, length), lambda h: (jnp.minimum(h, pairs - 1), 0, 0)),
            near(0),
            turn,
            turn,
            *[anywhere] * 5,
            fixed(6, model),
            packed_at(6),
        ]
        + [anywhere] * 6
        + [fixed(6, model), fixed(1, hidden_width), fixed(2, 128), anywhere, anywhere, anywhere],
        out_specs=[
            anywhere,
            fixed(2, 128),
            fixed(6 * model_rows, 128),
            fixed(1, 6 * model_rows),
            fixed(1, model_rows),
            fixed(1, model_rows),
            fixed(1, hidden_width // size),
            fixed(1, model_rows),
            fixed(hidden_width // size, model),
            fixed(model_rows, hidden_width),
            fixed(model_rows, model),
            fixed(model_rows, 3 * model),
            anywhere,
        ],
        out_shape=[
            shape((2, half, model), bf16),
            shape((2, 128), f32),
            shape((6 * model_rows, 128), f32),
            shape((1, 6 * model_rows), f32),
            shape((1, model_rows), f32),
            shape((1, model_rows), f32),
            shape((1, hidden_width // size), f32),
            shape((1, model_rows), f32),
            shape((hidden_width // size, model), f32),
            shape((model_rows, hidden_width), f32),
            shape((model_rows, model), f32),
            shape((model_rows, 3 * model), f32),
            shape((2, half, model), bf16),
        ],
        input_output_aliases={27: 12},
        scratch_shapes=scratch,
        compiler_params=pltpu.CompilerParams(vmem_limit_bytes=63 * MIB, collective_id=0, has_side_effects=True),
        cost_estimate=pl.CostEstimate(flops=40 * length * length * model, bytes_accessed=60 * MIB, transcendentals=0),
        name="back",
    )(
        qkv,
        qkv,
        qkv,
        attended,
        grad_attended,
        exps,
        inverses,
        cosine,
        sines,
        first_t,
        attention_in,
        tokens,
        other,
        grad_middle,
        modulation,
        packed,
        down_sum,
        down_tail,
        upv_sum.reshape(merge),
        upx_sum,
        out_keep,
        out_send,
        mid_rows,
        up_bias_grad,
        time_embedding,
        modulation_weight,
        other_out,
        own_out,
    )
    (
        tokens_grad,
        time_grad,
        modulation_weight_grad,
        modulation_bias_grad,
        gain_grad,
        feed_gain_grad,
        feed_up_bias_grad,
        feed_down_bias_grad,
        down_grad,
        up_grad,
        out_grad,
        in_grad,
        block_output,
    ) = pl.pallas_call(
        close_kernel,
        grid=(2,),
        in_specs=[cut(r.shape) for r in results],
        out_specs=[cut(r.shape) for r in results],
        out_shape=[shape(r.shape, r.dtype) for r in results],
        compiler_params=params(62),
        name="close",
    )(*results)
    return (
        block_output,
        tokens_grad,
        time_grad,
        modulation_weight_grad,
        modulation_bias_grad[0],
        gain_grad[0],
        in_grad,
        out_grad,
        feed_gain_grad[0],
        up_grad,
        feed_up_bias_grad[0],
        down_grad,
        feed_down_bias_grad[0],
    )


def body(tokens, *rest):
    sequences, half, model = tokens.shape
    size = lax.axis_size("dp")
    fits = model % (16 * size) == 0 and half % T_ROWS == 0
    fits = fits and tokens.shape[1] % MIDDLE_ROWS == 0 and rest[10].shape[1] == 4 * model and size == 16 and lax.axis_size("seq") == 2 and sequences == 2
    return (fast_body if fits else general_body)(tokens, *rest)


def solution(mesh):
    return jax.shard_map(
        body,
        mesh=mesh,
        in_specs=(
            P("dp", "seq", None),
            P("dp", None),
            P("dp"),
            P("dp", "seq"),
            P("dp", "seq", None),
            P(),
            P(),
            P(),
            P(),
            P(),
            P(),
            P(),
            P(),
            P(),
            P(),
        ),
        out_specs=(
            P("dp", "seq", None),
            P("dp", "seq", None),
            P("dp", None),
            P("dp", None),
            P("dp"),
            P("dp"),
            P("dp", None),
            P("dp", None),
            P("dp"),
            P("dp", None),
            P("dp"),
            P("dp", None),
            P("dp"),
        ),
        check_vma=False,
    )
```

```python
import functools
from functools import partial

import jax
import jax.numpy as jnp
import numpy as np
from jax import lax
from jax.experimental import pallas as pl
from jax.experimental.pallas import tpu as pltpu
from jax.sharding import PartitionSpec as P

HEADS = 12
HD = 64


highest = lax.Precision.HIGHEST


def as_sent(shard):

    def short(part):
        return part.astype(jnp.bfloat16) if part.dtype == jnp.float32 else part

    return jax.tree.map(short, shard)


def normalize(values):
    centre = values - jnp.mean(values, -1, keepdims=True)
    spread = jnp.mean(centre * centre, -1, keepdims=True)
    return centre * lax.rsqrt(spread + 1e-05)


def modulate(values, scaling, shifts, scales):
    return normalize(values) * scaling * (1.0 + scales) + shifts


def rotate(values, cosine, sines, direction):
    halves = values.shape[-1] // 2
    former = values[..., :halves]
    latter = values[..., halves:]
    cosine = cosine[None, :, None, :]
    sines = direction * sines[None, :, None, :]
    return jnp.concatenate([former * cosine - latter * sines, latter * cosine + former * sines], -1)


def attend_forward(stacked):
    query_rows = stacked[:, 0]
    key_rows = stacked[:, 1]
    value_rows = stacked[:, 2]
    length = query_rows.shape[0]
    block_rows = min(512, length)
    pieces = []
    logsums = []
    for offset in range(0, length, block_rows):
        query_block = query_rows[offset : offset + block_rows]
        scores = (
            jnp.einsum("qhd,khd->hqk", query_block, key_rows, preferred_element_type=jnp.float32)
            * 0.125
        )
        largest = jnp.max(scores, -1, keepdims=True)
        exponentials = jnp.exp(scores - largest)
        totals = jnp.sum(exponentials, -1, keepdims=True)
        probability = (exponentials / totals).astype(jnp.bfloat16)
        pieces.append(
            jnp.einsum("hqk,khd->qhd", probability, value_rows, preferred_element_type=jnp.float32)
        )
        logsums.append((largest + jnp.log(totals))[..., 0])
    return (jnp.concatenate(pieces, 0).astype(jnp.bfloat16), jnp.concatenate(logsums, 1))


def attend_backward(operands):
    stacked, grad_attended, logsums = operands
    query_rows = stacked[:, 0]
    key_rows = stacked[:, 1]
    value_rows = stacked[:, 2]
    length = query_rows.shape[0]
    block_rows = min(512, length)
    grad_query = []
    grad_keys = jnp.zeros(key_rows.shape, jnp.float32)
    grad_values = jnp.zeros(value_rows.shape, jnp.float32)
    for offset in range(0, length, block_rows):
        query_block = query_rows[offset : offset + block_rows]
        grad_block = grad_attended[offset : offset + block_rows]
        scores = (
            jnp.einsum("qhd,khd->hqk", query_block, key_rows, preferred_element_type=jnp.float32)
            * 0.125
        )
        probability = jnp.exp(scores - logsums[:, offset : offset + block_rows, None])
        grad_probs = jnp.einsum(
            "qhd,khd->hqk", grad_block, value_rows, preferred_element_type=jnp.float32
        )
        row_dots = jnp.sum(probability * grad_probs, -1, keepdims=True)
        grad_scores = (probability * (grad_probs - row_dots)).astype(jnp.bfloat16)
        grad_query.append(
            (
                jnp.einsum(
                    "hqk,khd->qhd", grad_scores, key_rows, preferred_element_type=jnp.float32
                )
                * 0.125
            ).astype(jnp.bfloat16)
        )
        grad_keys = grad_keys + jnp.einsum(
            "hqk,qhd->khd", grad_scores, query_block, preferred_element_type=jnp.float32
        )
        grad_values = grad_values + jnp.einsum(
            "hqk,qhd->khd",
            probability.astype(jnp.bfloat16),
            grad_block,
            preferred_element_type=jnp.float32,
        )
    return jnp.stack(
        [
            jnp.concatenate(grad_query, 0),
            (grad_keys * 0.125).astype(jnp.bfloat16),
            grad_values.astype(jnp.bfloat16),
        ],
        1,
    )


def general_body(
    tokens,
    time_embedding,
    prefix_length,
    suffix_mask,
    cotangent,
    modulation_weight,
    modulation_bias,
    attention_gain,
    attention_in,
    attention_out,
    feed_gain,
    feed_up,
    feed_up_bias,
    feed_down,
    feed_down_bias,
):
    sequences, local_len, model_width = tokens.shape
    groups = lax.axis_size("seq")
    data_size = lax.axis_size("dp")
    length = local_len * groups
    heads_local = HEADS // groups
    group_width = model_width // groups
    modulation = jnp.einsum(
        "sc,oc->so", time_embedding, modulation_weight, preferred_element_type=jnp.float32
    ) + modulation_bias.astype(jnp.float32)
    shift_one, scale_one, gate_one, shift_two, scale_two, gate_two = [
        portion[:, None, :] for portion in jnp.split(modulation, 6, axis=1)
    ]
    inputs = tokens.astype(jnp.float32)
    first_float, first_back = jax.vjp(
        modulate, inputs, attention_gain.astype(jnp.float32), shift_one, scale_one
    )
    first_input = first_float.astype(jnp.bfloat16)
    projected = jnp.einsum(
        "spd,de->spe", first_input, attention_in, preferred_element_type=jnp.float32
    ).reshape(sequences, local_len, 3, HEADS, HD)
    position_ints = lax.axis_index("seq") * local_len + jnp.arange(local_len, dtype=jnp.int32)
    positions = position_ints.astype(jnp.float32)
    inverse = 10000.0 ** (-jnp.arange(HD // 2, dtype=jnp.float32) * 2.0 / HD)
    angles = positions[:, None] * inverse[None, :]
    cosine = jnp.cos(angles)
    sines = jnp.sin(angles)
    rotated = jnp.stack(
        [
            rotate(projected[:, :, 0], cosine, sines, 1.0),
            rotate(projected[:, :, 1], cosine, sines, 1.0),
            projected[:, :, 2],
        ],
        2,
    ).astype(jnp.bfloat16)
    by_heads = lax.all_to_all(
        rotated.reshape(sequences, local_len, 3, groups, group_width),
        "seq",
        split_axis=3,
        concat_axis=1,
        tiled=True,
    )
    by_heads = by_heads.reshape(sequences, length, 3, heads_local, HD)
    attended_heads, logsums = lax.map(attend_forward, by_heads)
    attended = lax.all_to_all(
        as_sent(attended_heads.reshape(sequences, length, 1, group_width)),
        "seq",
        split_axis=1,
        concat_axis=2,
        tiled=True,
    )
    attended = attended.reshape(sequences, local_len, model_width)
    branch_one = jnp.einsum(
        "spd,de->spe", attended, attention_out, preferred_element_type=jnp.float32
    )
    middle = inputs + gate_one * branch_one
    second_float, second_back = jax.vjp(
        modulate, middle, feed_gain.astype(jnp.float32), shift_two, scale_two
    )
    second_input = second_float.astype(jnp.bfloat16)
    hidden = jnp.einsum(
        "spd,df->spf", second_input, feed_up, preferred_element_type=jnp.float32
    ) + feed_up_bias.astype(jnp.float32)
    activated_float, gelu_back = jax.vjp(partial(jax.nn.gelu, approximate=True), hidden)
    activated = activated_float.astype(jnp.bfloat16)
    branch_two = jnp.einsum(
        "spf,fd->spd", activated, feed_down, preferred_element_type=jnp.float32
    ) + feed_down_bias.astype(jnp.float32)
    block_output = (middle + gate_two * branch_two).astype(jnp.bfloat16)
    live_rows = ((position_ints[None, :] >= prefix_length[:, None]) & (suffix_mask == 1)).astype(
        jnp.float32
    )
    grad_output = cotangent.astype(jnp.float32) * live_rows[:, :, None]
    grad_gate_two = jnp.sum(grad_output * branch_two, axis=1)
    grad_branch_two = (gate_two * grad_output).astype(jnp.bfloat16)
    feed_down_bias_grad = jnp.sum(grad_branch_two.astype(jnp.float32), axis=(0, 1))
    feed_down_grad = jnp.einsum(
        "spf,spd->fd", activated, grad_branch_two, preferred_element_type=jnp.float32
    )
    grad_activated = jnp.einsum(
        "spd,fd->spf", grad_branch_two, feed_down, preferred_element_type=jnp.float32
    )
    grad_hidden = gelu_back(grad_activated)[0].astype(jnp.bfloat16)
    feed_up_bias_grad = jnp.sum(grad_hidden.astype(jnp.float32), axis=(0, 1))
    feed_up_grad = jnp.einsum(
        "spd,spf->df", second_input, grad_hidden, preferred_element_type=jnp.float32
    )
    grad_second = jnp.einsum(
        "spf,df->spd", grad_hidden, feed_up, preferred_element_type=jnp.float32
    )
    grad_from_norm, feed_gain_grad, grad_shift_two, grad_scale_two = second_back(grad_second)
    grad_middle = grad_output + grad_from_norm
    grad_gate_one = jnp.sum(grad_middle * branch_one, axis=1)
    grad_branch_one = (gate_one * grad_middle).astype(jnp.bfloat16)
    attention_out_grad = jnp.einsum(
        "spd,spe->de", attended, grad_branch_one, preferred_element_type=jnp.float32
    )
    grad_attended = jnp.einsum(
        "spe,de->spd", grad_branch_one, attention_out, preferred_element_type=jnp.float32
    ).astype(jnp.bfloat16)
    grad_heads = lax.all_to_all(
        grad_attended.reshape(sequences, local_len, groups, group_width),
        "seq",
        split_axis=2,
        concat_axis=1,
        tiled=True,
    )
    grad_heads = grad_heads.reshape(sequences, length, heads_local, HD)
    grad_stacked = lax.map(attend_backward, (by_heads, grad_heads, logsums))
    grad_positions = lax.all_to_all(
        as_sent(grad_stacked.reshape(sequences, length, 3, 1, group_width)),
        "seq",
        split_axis=1,
        concat_axis=3,
        tiled=True,
    )
    grad_positions = grad_positions.reshape(sequences, local_len, 3, HEADS, HD).astype(jnp.float32)
    grad_projected = jnp.stack(
        [
            rotate(grad_positions[:, :, 0], cosine, sines, -1.0),
            rotate(grad_positions[:, :, 1], cosine, sines, -1.0),
            grad_positions[:, :, 2],
        ],
        2,
    ).astype(jnp.bfloat16)
    grad_projected = grad_projected.reshape(sequences, local_len, 3 * model_width)
    attention_in_grad = jnp.einsum(
        "spd,spe->de", first_input, grad_projected, preferred_element_type=jnp.float32
    )
    grad_first = jnp.einsum(
        "spe,de->spd", grad_projected, attention_in, preferred_element_type=jnp.float32
    )
    grad_tokens_norm, attention_gain_grad, grad_shift_one, grad_scale_one = first_back(grad_first)
    tokens_grad = (grad_middle + grad_tokens_norm).astype(jnp.bfloat16)
    grad_modulation = jnp.concatenate(
        [
            grad_shift_one[:, 0],
            grad_scale_one[:, 0],
            grad_gate_one,
            grad_shift_two[:, 0],
            grad_scale_two[:, 0],
            grad_gate_two,
        ],
        1,
    )
    modulation_total = lax.psum(grad_modulation.astype(jnp.bfloat16), "seq").astype(jnp.float32)
    time_grad = jnp.einsum(
        "so,oc->sc", modulation_total, modulation_weight.astype(jnp.float32), precision=highest
    )
    modulation_weight_grad = jnp.einsum(
        "so,sc->oc", grad_modulation, time_embedding.astype(jnp.float32), precision=highest
    )
    modulation_bias_grad = jnp.sum(grad_modulation, axis=0)
    gradients = (
        modulation_weight_grad,
        modulation_bias_grad,
        attention_gain_grad,
        attention_in_grad,
        attention_out_grad,
        feed_gain_grad,
        feed_up_grad,
        feed_up_bias_grad,
        feed_down_grad,
        feed_down_bias_grad,
    )
    flattened = tuple((g.reshape(data_size, -1) for g in gradients))
    shares = lax.psum_scatter(flattened, "dp", scatter_dimension=0, tiled=True)
    summed = jax.tree.map(lambda part: part.astype(jnp.float32), lax.psum(as_sent(shares), "seq"))
    shards = tuple(
        (s.reshape((g.shape[0] // data_size,) + g.shape[1:]) for s, g in zip(summed, gradients))
    )
    return (
        block_output,
        tokens_grad,
        time_grad,
        shards[0],
        shards[1],
        shards[2],
        shards[3],
        shards[4],
        shards[5],
        shards[6],
        shards[7],
        shards[8],
        shards[9],
    )


T_ROWS = 256
FRONT_ROWS = 128
MIDDLE_ROWS = 256
MIB = 1 << 20


def dot(a, b, ca, cb):
    return lax.dot_general(a, b, (((ca,), (cb,)), ((), ())), preferred_element_type=jnp.float32)


def params(limit=60):
    return pltpu.CompilerParams(vmem_limit_bytes=limit * MIB)


def norm_rows(values):
    centre = values - jnp.mean(values, -1, keepdims=True)
    inverse = lax.rsqrt(jnp.mean(centre * centre, -1, keepdims=True) + 1e-05)
    return centre * inverse, inverse


def swap_halves(values, lane):
    left = pltpu.roll(values, 96, 1)
    right = pltpu.roll(values, 32, 1)
    return jnp.where(lane % 64 < 32, left, right)


def attend_kernel(
    prefix_ref,
    q_ref,
    k_ref,
    v_ref,
    mask_ref,
    cot_hbm,
    out_ref,
    exp_ref,
    inv_ref,
    own_live_ref,
    other_live_ref,
    other_cot_hbm,
    give,
    got,
    sems,
):
    rows = 128
    step = pl.program_id(0)
    links = Links()
    half = mask_ref.shape[1]
    partner = links.partner["Y"]

    def exchanges():
        return [
            remote(give, got, sems, 0, partner),
            remote(cot_hbm.at[1 - links.me], other_cot_hbm, sems, 1, partner),
        ]

    @pl.when(step == 0)
    def _():
        position = links.me * half + lax.broadcasted_iota(jnp.int32, (1, half), 1)
        live = [
            jnp.where((position >= prefix_ref[i]) & (mask_ref[i : i + 1] == 1), 1.0, 0.0) for i in range(2)
        ]
        wide = [jnp.broadcast_to(row, (8, half)) for row in live]
        own_live_ref[...] = jnp.where(links.me == 0, wide[0], wide[1])
        give[...] = jnp.where(links.me == 0, wide[1], wide[0])
        links.greet(("Y",))
        start_all(exchanges())

    length = q_ref.shape[0]
    lane = lax.broadcasted_iota(jnp.int32, (rows, 128), 1)
    keys = k_ref[...]
    values = jnp.concatenate([v_ref[...], jnp.ones((length, 128), jnp.bfloat16)], 1)
    for chunk in range(length // rows):
        at = slice(chunk * rows, (chunk + 1) * rows)
        queries = q_ref[at]
        outs = []
        inverses = []
        for head in range(2):
            mine = jnp.where((lane < 64) == (head == 0), queries, jnp.zeros_like(queries))
            scores = dot(mine, keys, 1, 1)
            largest = jnp.max(scores, -1, keepdims=True)
            exps = jnp.exp(scores - largest).astype(jnp.bfloat16)
            exp_ref[head, at] = exps
            summed = dot(exps, values, 1, 0)
            inverse = 1.0 / summed[:, 128:256]
            outs.append(summed[:, 0:128] * inverse)
            inverses.append(inverse)
        out_ref[at] = jnp.where(lane < 64, outs[0], outs[1]).astype(jnp.bfloat16)
        inv_ref[at] = jnp.where(lane < 64, inverses[0], inverses[1])

    @pl.when(step == pl.num_programs(0) - 1)
    def _():
        for copy in exchanges():
            copy.wait()
        other_live_ref[...] = got[...]


def share(core, grad, keep_ref, send_ref, *at):
    first, second = grad
    keep_ref[at] = jnp.where(core == 0, first, second)
    send_ref[at] = jnp.where(core == 0, second, first)


def middle_kernel(
    own_ref,
    other_ref,
    own_cot_ref,
    other_cot_ref,
    own_live_ref,
    other_live_ref,
    attended_ref,
    mod_ref,
    gain_ref,
    out_weight_ref,
    up_ref,
    up_bias_ref,
    down_ref,
    down_bias_ref,
    own_out_ref,
    other_out_ref,
    grad_middle_ref,
    grad_attended_ref,
    rows_ref,
    up_bias_grad_ref,
    down_sum_ref,
    down_tail_ref,
    upv_sum_ref,
    upx_sum_ref,
    out_keep_ref,
    out_send_ref,
    second_t,
    grad_two,
    sum_two,
    sum_second,
    act_t,
    down_keep,
    down_give,
    down_got,
    up_keep,
    up_give,
    up_got,
    down_half,
    down_half_got,
    down_part,
    down_part_got,
    up_part,
    up_part_got,
    up_half,
    up_half_got,
    sems,
):
    rows = MIDDLE_ROWS
    step = pl.program_id(0)
    links = Links()
    core = links.bit["C"]
    tiles = down_keep.shape[0]

    per_tile = 7
    last = tiles - 1

    def first_copies(tile):
        return [
            remote(give.at[tile], got.at[tile], sems, tile * per_tile + i, links.partner["C"])
            for i, (give, got) in enumerate(((down_give, down_got), (up_give, up_got)))
        ]

    def down_copy(tile):
        return remote(down_half.at[tile], down_half_got.at[tile], sems, tile * per_tile + 2, links.partner["Y"])

    def down_on_copy(tile):
        return remote(down_part.at[tile], down_part_got.at[tile], sems, tile * per_tile + 3, links.partner["X"])

    def up_copies(tile):
        return [
            remote(up_part.at[tile, i], up_part_got.at[tile, i], sems, tile * per_tile + 4 + i, links.partner[flip])
            for i, flip in enumerate(Z_FLIPS)
        ]

    def up_last_copy():
        return remote(up_half, up_half_got, sems, last * per_tile + 4, links.partner["X"])

    def total(*terms):
        return sum(term.astype(jnp.float32) for term in terms).astype(jnp.bfloat16)

    half_rows = down_half.shape[2]
    home = pl.ds(pl.multiple_of(links.me * half_rows, 16), half_rows)
    away = pl.ds(pl.multiple_of((1 - links.me) * half_rows, 16), half_rows)
    z_at = links.bit["W"] * 2 + links.bit["Z"]

    def flipped(flip):
        values = {bit: 1 - links.bit[bit] if bit in flip else links.bit[bit] for bit in "WZ"}
        return values["W"] * 2 + values["Z"]

    def send_on(tile, final):
        for copy in first_copies(tile):
            copy.wait_recv()
        for x in range(2):
            down_half[tile, x] = total(down_keep[tile, x, away], down_got[tile, x, away])
        down_copy(tile).start()
        if final:
            for z in range(4):
                other = 2 * z + 1 - links.bit["X"]
                up_half[z] = total(up_keep[tile, other], up_got[tile, other])
            up_last_copy().start()
        else:
            for i, flip in enumerate(Z_FLIPS):
                for x in range(2):
                    other = 2 * flipped(flip) + x
                    up_part[tile, i, x] = total(up_keep[tile, other], up_got[tile, other])
            for copy in up_copies(tile):
                copy.start()

    def send_down(tile):
        down_copy(tile).wait_recv()
        x = 1 - links.bit["X"]
        down_part[tile] = total(down_keep[tile, x, home], down_got[tile, x, home], down_half_got[tile, x])
        down_on_copy(tile).start()

    def settle(tile, final):
        if final:
            down_copy(tile).wait_recv()
            for x in range(2):
                down_tail_ref[x] = total(down_keep[tile, x, home], down_got[tile, x, home], down_half_got[tile, x])
        else:
            down_on_copy(tile).wait_recv()
            x = links.bit["X"]
            terms = (down_keep[tile, x, home], down_got[tile, x, home], down_half_got[tile, x], down_part_got[tile])
            down_sum_ref[tile] = total(*terms)
        if final:
            up_last_copy().wait_recv()
            for z in range(4):
                mine = 2 * z + links.bit["X"]
                upx_sum_ref[z] = total(up_keep[tile, mine], up_got[tile, mine], up_half_got[z])
        else:
            for copy in up_copies(tile):
                copy.wait_recv()
            for x in range(2):
                mine = 2 * z_at + x
                got = [up_part_got[tile, i, x] for i in range(3)]
                upv_sum_ref[x, tile] = total(up_keep[tile, mine], up_got[tile, mine], *got)

    @pl.when(step == 0)
    def _():
        links.greet()

    half, model = own_ref.shape
    length = 2 * half
    scaling = gain_ref[...] * (1.0 + mod_ref[4:5])
    gate_one = mod_ref[2:3]
    shift_two = mod_ref[3:4]
    gate_two = mod_ref[5:6]

    def pick(first_ref, second_ref, chunk):
        at = chunk * rows
        return (first_ref if at < half else second_ref)[at % half : at % half + rows]

    def live_cot(chunk):
        at = (chunk * rows) % half
        live = (own_live_ref if chunk * rows < half else other_live_ref)[...].T[at : at + rows, 0:1]
        return pick(own_cot_ref, other_cot_ref, chunk).astype(jnp.float32) * live

    @pl.when(step == 0)
    def _():
        bias_grad = jnp.zeros((1, model), jnp.float32)
        for chunk in range(length // rows):
            at = slice(chunk * rows, (chunk + 1) * rows)
            branch = dot(attended_ref[at], out_weight_ref[...], 1, 0)
            grad_middle_ref[at] = branch
            sum_two[at] = jnp.zeros((rows, model), jnp.float32)
            sum_second[at] = jnp.zeros((rows, model), jnp.float32)
            middle = pick(own_ref, other_ref, chunk).astype(jnp.float32) + gate_one * branch
            normed, _ = norm_rows(middle)
            rounded = (normed * scaling + shift_two).astype(jnp.bfloat16)
            place = (chunk * rows) % half
            (own_out_ref if chunk * rows < half else other_out_ref)[place : place + rows] = rounded
            second_t[:, at] = rounded.T
            grad = (gate_two * live_cot(chunk)).astype(jnp.bfloat16)
            grad_two[at] = grad
            bias_grad = bias_grad + jnp.sum(grad.astype(jnp.float32), 0, keepdims=True)
        rows_ref[5:6] = bias_grad

    up = up_ref[...]
    down = down_ref[...]
    width = up.shape[1]
    bias_sum = jnp.zeros((1, width), jnp.float32)
    for chunk in range(length // rows):
        if chunk * rows == half:

            @pl.when(step > 0)
            def _():
                send_on(step - 1, False)

            @pl.when(step > 1)
            def _():
                send_down(step - 2)

        at = slice(chunk * rows, (chunk + 1) * rows)
        hidden = dot(pick(own_out_ref, other_out_ref, chunk), up, 1, 0) + up_bias_ref[...]
        squared = hidden * hidden
        tanh = jnp.tanh(hidden * (0.7978845608028654 + 0.035677408136300125 * squared))
        gate = 0.5 + 0.5 * tanh
        activated = (hidden * gate).astype(jnp.bfloat16)
        slope = gate + (0.5 * hidden) * (1.0 - tanh * tanh) * (0.7978845608028654 + 0.10703222440890037 * squared)
        act_t[:, at] = activated.T
        grad = (slope * dot(grad_two[at], down, 1, 1)).astype(jnp.bfloat16)
        grad_attended_ref[at] = grad
        bias_sum = bias_sum + jnp.sum(grad.astype(jnp.float32), 0, keepdims=True)
        sum_two[at] += dot(activated, down, 1, 0)
        sum_second[at] += dot(grad, up, 1, 1)

    up_bias_grad_ref[...] = bias_sum
    down_grad = dot(act_t[...], grad_two[...], 1, 0).astype(jnp.bfloat16).reshape(2, 2, -1, model)
    share(core, (down_grad[:, 0], down_grad[:, 1]), down_keep, down_give, step)
    up_grad = dot(second_t[...], grad_attended_ref[...], 1, 0).astype(jnp.bfloat16).reshape(up_keep.shape[1], 2, -1, width)
    share(core, (up_grad[:, 0], up_grad[:, 1]), up_keep, up_give, step)
    for copy in first_copies(step):
        copy.start()

    @pl.when(step == pl.num_programs(0) - 1)
    def _():
        sums = [jnp.zeros((1, model), jnp.float32) for _ in range(4)]
        for chunk in range(length // rows):
            at = slice(chunk * rows, (chunk + 1) * rows)
            branch = grad_middle_ref[at]
            middle = pick(own_ref, other_ref, chunk).astype(jnp.float32) + gate_one * branch
            normed, inverse = norm_rows(middle)
            branch_two = sum_two[at] + down_bias_ref[...]
            output = (middle + gate_two * branch_two).astype(jnp.bfloat16)
            place = (chunk * rows) % half
            (own_out_ref if chunk * rows < half else other_out_ref)[place : place + rows] = output
            cot = live_cot(chunk)
            grad = sum_second[at]
            weighted = grad * normed
            scaled = grad * scaling
            inner = jnp.mean(weighted * scaling, -1, keepdims=True)
            grad_middle = cot + (scaled - jnp.mean(scaled, -1, keepdims=True) - normed * inner) * inverse
            grad_middle_ref[at] = grad_middle
            grad_one = (gate_one * grad_middle).astype(jnp.bfloat16)
            grad_two[at] = grad_one
            act_t[:, at] = attended_ref[at].T
            grad_attended_ref[at] = dot(grad_one, out_weight_ref[...], 1, 1).astype(jnp.bfloat16)
            for i, term in enumerate((grad_middle * branch, grad, weighted, cot * branch_two)):
                sums[i] = sums[i] + jnp.sum(term, 0, keepdims=True)
            if (chunk + 1) * rows == half:
                send_on(last, True)
                send_down(last - 1)
        rows_ref[0:1] = sums[0]
        rows_ref[1:2] = sums[1]
        rows_ref[2:3] = sums[2] * gain_ref[...]
        rows_ref[3:4] = sums[3]
        rows_ref[4:5] = sums[2] * (1.0 + mod_ref[4:5])
        out_grad = dot(act_t[...], grad_two[...], 1, 0).astype(jnp.bfloat16)
        out_grad = out_grad.reshape(out_keep_ref.shape[0], 2, -1, model)
        share(core, (out_grad[:, 0], out_grad[:, 1]), out_keep_ref, out_send_ref, Ellipsis)
        for tile in range(last):
            settle(tile, False)
        settle(last, True)
        for tile in range(tiles):
            ups = [up_last_copy()] if tile == last else up_copies(tile)
            for copy in first_copies(tile) + [down_copy(tile)] + ([] if tile == last else [down_on_copy(tile)]) + ups:
                copy.wait_send()


Z_FLIPS = ("Z", "W", "ZW")


class Links:
    def __init__(self):
        dp = lax.axis_index("dp")
        self.me = lax.axis_index("seq")
        self.bit = {"C": dp % 2, "X": (dp // 2) % 2, "Z": (dp // 4) % 2, "W": (dp // 8) % 2, "Y": self.me}
        jump = {name: size * (1 - 2 * self.bit[name]) for name, size in (("C", 1), ("X", 2), ("Z", 4), ("W", 8))}
        self.partner = {name: (dp + jump[name], self.me) for name in "CXZW"}
        self.partner["ZW"] = (dp + jump["Z"] + jump["W"], self.me)
        self.partner["Y"] = (dp, 1 - self.me)

    def place(self):
        return self.me * 16 + self.bit["X"] * 8 + self.bit["W"] * 4 + self.bit["Z"] * 2 + self.bit["C"]

    def greet(self, names=("C", "X", "Z", "W", "ZW", "Y")):
        barrier = pltpu.get_barrier_semaphore()
        for name in names:
            device = self.partner[name]
            pl.semaphore_signal(barrier, inc=1, device_id=device, device_id_type=pl.DeviceIdType.MESH)
        pl.semaphore_wait(barrier, len(names))


def flips_of(kind):
    return Z_FLIPS if kind == "V" else (kind,)


def remote(source, target, sems, slot, device):
    return pltpu.make_async_remote_copy(
        src_ref=source,
        dst_ref=target,
        send_sem=sems.at[0, slot],
        recv_sem=sems.at[1, slot],
        device_id=device,
        device_id_type=pl.DeviceIdType.MESH,
    )


def piece_scratch(spec):
    _, rows, width, left, order, kind = spec
    count = 1 << len(left)
    shapes = [count] * (1 + ("summed", "given", "made").index(kind))
    for step in order:
        count //= 4 if step == "V" else 2
        shapes += [count * len(flips_of(step))] * 2
    shapes += [1] * 2
    return [pltpu.VMEM((c, rows, width), jnp.bfloat16) for c in shapes]


class Piece:
    def __init__(self, links, refs, spec, sems, slot, source=None, split=False):
        refs = list(refs)
        _, _, _, left, order, kind = spec
        self.links = links
        self.sems = sems
        self.slot = slot
        self.order = list(order)
        self.split = split
        self.left = list(left)
        self.keep = refs.pop(0)
        self.terms = [(self.keep, list(self.left))]
        self.copies = []
        self.flying = []
        if kind != "summed":
            first = refs.pop(0)
            self.source = refs.pop(0) if kind == "made" else source
            copy = (self.source, first, sems, slot, links.partner["C"])
            self.slot += 1
            self.copies.append(copy)
            self.flying = [(copy, first, list(self.left))]
        self.buffers = refs

    def launch(self, source, target, flip):
        copy = (source, target, self.sems, self.slot, self.links.partner[flip])
        self.slot += 1
        remote(*copy).start()
        self.copies.append(copy)
        self.flying.append((copy, target, list(self.left)))

    def begin(self):
        remote(*self.copies[0]).start()

    def arrive(self):
        for copy, target, bits in self.flying:
            remote(*copy).wait_recv()
            self.terms.append((target, bits))
        self.flying = []

    def index(self, bits, values):
        at = 0
        for bit in bits:
            at = at * 2 + values[bit]
        return at

    def add(self, out, flip):
        links = self.links
        rows = out.shape[1]
        block = 48
        for combo in range(1 << len(self.left)):
            values = dict(links.bit)
            for bit in flip:
                values[bit] = 1 - links.bit[bit]
            for place, bit in enumerate(self.left):
                values[bit] = (combo >> (len(self.left) - 1 - place)) & 1
            indices = [self.index(bits, values) for _, bits in self.terms]

            def some(i, carry, indices=indices, combo=combo):
                at = pl.ds(pl.multiple_of(i * block, 16), block)
                total = None
                for (ref, _), index in zip(self.terms, indices):
                    term = ref[index, at, :].astype(jnp.float32)
                    total = term if total is None else total + term
                out[combo, at, :] = total.astype(jnp.bfloat16)
                return carry

            lax.fori_loop(0, rows // block, some, 0)

    def step(self):
        self.arrive()
        kind = self.order.pop(0)
        out, target = self.buffers.pop(0), self.buffers.pop(0)
        for bit in "WZ" if kind == "V" else kind:
            self.left.remove(bit)
        count = 1 << len(self.left)
        for i, flip in enumerate(flips_of(kind)):
            part = pl.ds(i * count, count)
            self.add(out.at[part], flip)
            self.launch(out.at[part], target.at[part], flip)

    def last(self):
        self.arrive()
        self.total, self.got = self.buffers.pop(0), self.buffers.pop(0)
        self.add(self.total, "")
        self.launch(self.total, self.got, "Y")

    def result(self, store):
        remote(*self.flying[0][0]).wait_recv()
        rows = self.total.shape[1]
        total = self.total[0].astype(jnp.float32)
        got = self.got[0].astype(jnp.float32)
        if self.split:
            store(pl.ds(pl.multiple_of(self.links.me * rows, 8), rows), total)
            store(pl.ds(pl.multiple_of((1 - self.links.me) * rows, 8), rows), got)
        else:
            store(slice(0, rows), total + got)


CHUNKS = (3, 2, 1)
BACK_PIECES = (
    ("down", 96, 768, "WZ", "V", "summed"),
    ("upv", 144, 768, "X", "X", "summed"),
    ("upx", 48, 768, "WZ", "V", "summed"),
    ("out", 48, 768, "WZX", "XV", "given"),
    *((f"in{i}", 48, 384 * pairs, "WZX", "XV", "made") for i, pairs in enumerate(CHUNKS)),
)


def copies_of(spec):
    return sum(len(flips_of(kind)) for kind in spec[4]) + 1 + (spec[5] != "summed")


BACK_COPIES = sum(copies_of(spec) for spec in BACK_PIECES)
HOPS = (("C",), Z_FLIPS, ("X",), ("Y",))
RUNNING = "CXZWY"


def spread_copies(links, array, sems, slot, number):
    place = links.place()
    have = (1, 2, 8, 16)[number]
    part = array.at[pl.ds((place // have) * have, have)]
    slot += (0, 1, 4, 5)[number]
    return [remote(part, part, sems, slot + i, links.partner[flip]) for i, flip in enumerate(HOPS[number])]


def start_all(copies):
    for copy in copies:
        copy.start()


def receive_all(copies):
    for copy in copies:
        copy.wait_recv()


def front_kernel(
    tokens_hbm,
    time_ref,
    mod_weight_hbm,
    mod_bias_ref,
    gain_ref,
    weight_hbm,
    cos_hbm,
    sin_hbm,
    first_t_ref,
    qkv_hbm,
    other_hbm,
    mod_ref,
    other_ref,
    own,
    mod_weight,
    weight,
    cos_ref,
    sin_ref,
    qkv,
    sems,
    local_sems,
    store_sems,
):
    rows = FRONT_ROWS
    half, model = own.shape
    blocks = half // rows
    links = Links()

    def exchange(block):
        at = pl.ds(block * rows, rows)
        return remote(tokens_hbm.at[1 - links.me, at], other_ref.at[at], sems, block, links.partner["Y"])

    def fetches():
        pairs = (
            (mod_weight_hbm, mod_weight),
            (tokens_hbm.at[links.me], own),
            (weight_hbm, weight),
            (cos_hbm.at[links.me], cos_ref),
            (sin_hbm.at[links.me], sin_ref),
        )
        return [pltpu.make_async_copy(a, b, local_sems.at[i]) for i, (a, b) in enumerate(pairs)]

    def store(block):
        at = pl.ds(block * rows, rows)
        return pltpu.make_async_copy(qkv.at[at], qkv_hbm.at[at], store_sems.at[block])

    def store_other(block):
        at = pl.ds(block * rows, rows)
        return pltpu.make_async_copy(other_ref.at[at], other_hbm.at[at], store_sems.at[2 * blocks + block])

    for copy in fetches():
        copy.start()
    links.greet(("Y",))
    for block in range(blocks):
        exchange(block).start()
    for copy in fetches():
        copy.wait()
    embedding = time_ref[...].astype(jnp.float32)
    embedding = jnp.where(links.me == 0, embedding[0:1], embedding[1:2])
    embedding = jnp.broadcast_to(embedding, (16, embedding.shape[1])).astype(jnp.bfloat16)
    modulation = dot(embedding, mod_weight[...], 1, 1)[0:1] + mod_bias_ref[...].astype(jnp.float32)
    parts = [modulation[:, i * model : (i + 1) * model] for i in range(6)]
    for i in range(6):
        mod_ref[i : i + 1] = parts[i]
    lane = lax.broadcasted_iota(jnp.int32, (rows, 128), 1)
    scaling = gain_ref[...].astype(jnp.float32) * (1.0 + parts[1])
    for block in range(2 * blocks):
        if block < blocks:
            source = own[block * rows : (block + 1) * rows]
        else:
            exchange(block - blocks).wait_recv()
            source = other_ref[(block - blocks) * rows : (block - blocks + 1) * rows]
            store_other(block - blocks).start()
        at = slice(block * rows, (block + 1) * rows)
        normed, _ = norm_rows(source.astype(jnp.float32))
        first = (normed * scaling + parts[0]).astype(jnp.bfloat16)
        first_t_ref[:, at] = first.T
        for part in range(3):
            projected = dot(first, weight[:, part * model : (part + 1) * model], 1, 0)
            for column in range(model // 128):
                piece = projected[:, column * 128 : (column + 1) * 128]
                if part < 2:
                    piece = piece * cos_ref[at] + swap_halves(piece, lane) * sin_ref[at]
                piece = piece.astype(jnp.bfloat16)
                if part == 0:
                    piece = piece * 0.125
                start = part * model + column * 128
                qkv[at, start : start + 128] = piece
        store(block).start()
    for block in range(2 * blocks):
        store(block).wait()
    for block in range(blocks):
        store_other(block).wait()
        exchange(block).wait_send()


def back_kernel(
    q_ref,
    k_ref,
    v_ref,
    out_ref,
    grad_ref,
    exp_ref,
    inv_ref,
    cos_ref,
    sin_ref,
    first_t_hbm,
    weight_hbm,
    own_hbm,
    other_hbm,
    grad_middle_hbm,
    mod_ref,
    gain_ref,
    down_keep,
    down_tail_hbm,
    upv_keep,
    upx_keep,
    out_keep,
    out_send,
    mid_rows_ref,
    up_bias_ref,
    time_ref,
    mod_weight_hbm,
    other_block_ref,
    _,
    tokens_grad_ref,
    time_grad_ref,
    mod_weight_grad_ref,
    mod_bias_grad_ref,
    gain_grad_ref,
    feed_gain_grad_ref,
    up_bias_grad_ref,
    down_bias_grad_ref,
    down_ref,
    up_ref,
    out_grad_ref,
    in_ref,
    block_ref,
    first_t_ref,
    weight_ref,
    own_ref,
    other_ref,
    grad_middle_ref,
    mod_weight_ref,
    down_tail,
    down_tail_give,
    down_tail_got,
    ds_ref,
    dq_sum,
    proj,
    tokens_stage,
    rows_ref,
    early,
    late,
    running,
    running_got,
    by_vector,
    spread,
    spread_bias,
    turned,
    sems,
    local_sems,
    *buffers,
):
    rows = T_ROWS
    step = pl.program_id(0)
    length = q_ref.shape[0]
    half, model = other_ref.shape
    links = Links()
    core = links.bit["C"]
    pieces = []
    buffers = list(buffers)
    slot = 0
    for spec in BACK_PIECES:
        count = len(piece_scratch(spec))
        source = out_send if spec[0] == "out" else None
        pieces.append(Piece(links, buffers[:count], spec, sems, slot, source, spec[0] == "down"))
        buffers = buffers[count:]
        slot += copies_of(spec)
    down, upv, upx, out, *ins = pieces

    def fetches(first=0, end=11):
        pairs = (
            (upv_keep, upv.keep),
            (down_keep, down.keep.at[pl.ds(0, 3)]),
            (upx_keep, upx.keep),
            (out_keep, out.keep),
            (down_tail_hbm, down_tail),
            (first_t_hbm, first_t_ref),
            (weight_hbm, weight_ref),
            (other_hbm, other_ref),
            (grad_middle_hbm, grad_middle_ref),
            (own_hbm.at[links.me], own_ref),
            (mod_weight_hbm, mod_weight_ref),
        )
        return [pltpu.make_async_copy(a, b, local_sems.at[i]) for i, (a, b) in enumerate(pairs) if first <= i < end]

    place = links.place()
    dp = lax.axis_index("dp")
    early_slot = BACK_COPIES + 6
    quarter = half // 4
    late_slot = early_slot + 6
    running_slot = late_slot + 6
    tail_slot = running_slot + 5

    def running_copy(number):
        partner = links.partner[RUNNING[number]]
        return remote(running.at[number], running_got.at[number], sems, running_slot + number, partner)

    def tail_copy():
        return remote(down_tail_give, down_tail_got, sems, tail_slot, links.partner["X"])

    def block_copy(number):
        at = pl.ds(number * quarter, quarter)
        target = block_ref.at[links.me, at]
        return remote(other_block_ref.at[at], target, sems, BACK_COPIES + number, links.partner["Y"])

    def halves(target, at, first, values):
        middle = model // 2
        target[at, first : first + 1] = values[:, :middle]
        target[at, first + 1 : first + 2] = values[:, middle:]

    @pl.when(step == 0)
    def _():
        links.greet()
        for copy in fetches():
            copy.start()
        out.begin()
        for m in range(4):
            halves(early, place, 2 * m, mid_rows_ref[m : m + 1])
        running[0, 0:2] = mid_rows_ref[4:6]
        for tile in range(up_bias_ref.shape[1] // model):
            running[0, 2 + tile : 3 + tile] = up_bias_ref[:, tile * model : (tile + 1) * model]
        running[0, 6:8] = jnp.zeros((2, model), jnp.float32)
        start_all(spread_copies(links, early, sems, early_slot, 0))
        running_copy(0).start()

    for number in range(4):

        @pl.when(step == number + 1)
        def _(number=number):
            block_copy(number).start()

    def early_arrive(number):
        receive_all(spread_copies(links, early, sems, early_slot, number))

    def early_start(number):
        start_all(spread_copies(links, early, sems, early_slot, number))

    def running_arrive(number):
        running_copy(number).wait_recv()
        running[number + 1] = running[number] + running_got[number]

    def at_step(number):
        return pl.when(step == number)

    def between():
        @at_step(0)
        def _():
            for copy in fetches(0, 5):
                copy.wait()
            down_tail_give[...] = down_tail[1 - links.bit["X"]]
            early_arrive(0)
            running_arrive(0)
            early_start(1)
            running_copy(1).start()
            tail_copy().start()
            upv.step()
            upx.step()

        @at_step(1)
        def _():
            early_arrive(1)
            running_arrive(1)
            early_start(2)
            running_copy(2).start()
            tail_copy().wait_recv()
            kept = down_tail[links.bit["X"]].astype(jnp.float32) + down_tail_got[...].astype(jnp.float32)
            down.keep[3] = kept.astype(jnp.bfloat16)
            down.step()
            out.step()

        @at_step(2)
        def _():
            for copy in fetches(5):
                copy.wait()
            upx.last()
            upv.last()

        @at_step(3)
        def _():
            early_arrive(2)
            running_arrive(2)
            early_start(3)
            running_copy(3).start()
            ins[0].step()

        @at_step(4)
        def _():
            out.step()
            down.last()

        @at_step(5)
        def _():
            running_arrive(3)
            running_copy(4).start()
            ins[1].step()
            ins[0].step()

    lane = lax.broadcasted_iota(jnp.int32, (rows, 128), 1)

    @pl.when(step < 6)
    def _():
        keys = k_ref[...]
        values = v_ref[...]
        scaled = grad_ref[...].astype(jnp.float32) * inv_ref[...]
        products = scaled * out_ref[...].astype(jnp.float32)
        scaled = scaled.astype(jnp.bfloat16)
        scaled_t = scaled.T
        queries_t = q_ref[...].T
        grad_k = []
        grad_v = []
        for head in range(2):
            if head == 1:
                between()
            for chunk in range(length // rows):
                at = slice(chunk * rows, (chunk + 1) * rows)
                mask = (lane < 64) == (head == 0)
                mine = jnp.where(mask, scaled[at], jnp.zeros((rows, 128), jnp.bfloat16))
                row_dots = jnp.sum(jnp.where(mask, products[at], 0.0), -1, keepdims=True)
                grad_p = dot(mine, values, 1, 1)
                grad_s = (exp_ref[head, at].astype(jnp.float32) * (grad_p - row_dots)).astype(jnp.bfloat16)
                ds_ref[at] = grad_s
                grad_q = dot(grad_s, keys, 1, 0) * 0.125
                if head == 0:
                    dq_sum[at] = grad_q
                else:
                    dq_sum[at] = jnp.where(lane < 64, dq_sum[at], grad_q)
            grad_v.append(dot(scaled_t[64 * head : 64 * head + 64], exp_ref[head], 1, 0))
            grad_k.append(dot(queries_t[64 * head : 64 * head + 64], ds_ref[...], 1, 0))
        columns = [pl.ds(pl.multiple_of(part * model + step * 128, 128), 128) for part in range(3)]
        proj[:, columns[2]] = jnp.concatenate(grad_v, 0).astype(jnp.bfloat16).T
        grad_keys = jnp.concatenate(grad_k, 0).astype(jnp.bfloat16).T
        for chunk in range(length // rows):
            at = slice(chunk * rows, (chunk + 1) * rows)
            for part, source in enumerate((dq_sum[at].astype(jnp.bfloat16), grad_keys[at])):
                piece = source.astype(jnp.float32)
                turned = piece * cos_ref[at] - swap_halves(piece, lane) * sin_ref[at]
                proj[at, columns[part]] = turned.astype(jnp.bfloat16)

    starts = [128 * sum(CHUNKS[:i]) for i in range(len(CHUNKS))]

    def weight_part(group):
        piece = ins[group]
        span = 128 * CHUNKS[group]
        for part in range(3):
            column = part * model + starts[group]
            grad = dot(first_t_ref[...], proj[:, column : column + span], 1, 0).astype(jnp.bfloat16)
            grad = grad.reshape(8, 2, -1, span)
            share(core, (grad[:, 0], grad[:, 1]), piece.keep, piece.source, Ellipsis, slice(part * span, (part + 1) * span))
        piece.begin()

    for group, number in enumerate((2, 4, 5)):
        at_step(number)(functools.partial(weight_part, group))

    scaling = gain_ref[...] * (1.0 + mod_ref[1:2])

    def entry(values_ref, base, chunk):
        at = slice(base + chunk * rows, base + (chunk + 1) * rows)
        local = slice(chunk * rows, (chunk + 1) * rows)
        grad = dot(proj[at], weight_ref[...], 1, 1)
        normed, inverse = norm_rows(values_ref[local].astype(jnp.float32))
        weighted = grad * normed
        scaled = grad * scaling
        inner = jnp.mean(weighted * scaling, -1, keepdims=True)
        result = grad_middle_ref[at] + (scaled - jnp.mean(scaled, -1, keepdims=True) - normed * inner) * inverse
        tokens_stage[at] = result.astype(jnp.bfloat16)
        return jnp.concatenate([jnp.sum(grad, 0, keepdims=True), jnp.sum(weighted, 0, keepdims=True)], 0)

    def away(chunk):
        source = tokens_stage.at[pl.ds(half + chunk * rows, rows)]
        target = tokens_grad_ref.at[links.me, pl.ds(chunk * rows, rows)]
        return remote(source, target, sems, BACK_COPIES + 4 + chunk, links.partner["Y"])

    def home():
        return pltpu.make_async_copy(tokens_stage.at[pl.ds(0, half)], tokens_grad_ref.at[links.me], local_sems.at[11])

    unit = mod_weight_grad_ref.shape[0] // 6
    middle = model // 2

    def time_part(m):
        base = place % 16
        rest = jnp.concatenate([by_vector[m, pl.ds(base, 1)], by_vector[m, pl.ds(base + 16, 1)]], 0)
        both = jnp.zeros((2, 128), jnp.float32)
        for _ in range(3):
            high = rest.astype(jnp.bfloat16)
            both = both + dot(high, mod_weight_ref[m * model : (m + 1) * model], 1, 0)
            rest = rest - high.astype(jnp.float32)
        return both

    def early_vectors():
        for m in range(2, 6):
            by_vector[m, :, 0:middle] = early[:, 2 * m - 4, :]
            by_vector[m, :, middle:model] = early[:, 2 * m - 3, :]
        time_grad_ref[...] = sum(time_part(m) for m in range(2, 6))
        turned[...] = running[5].T
        narrow = turned[pl.ds(pl.multiple_of(dp * unit, 8), unit), :].T
        feed_gain_grad_ref[...] = narrow[0:1]
        down_bias_grad_ref[...] = narrow[1:2]
        wide_rows = up_bias_grad_ref.shape[1]
        share_of = model // wide_rows
        wide = turned[pl.ds(pl.multiple_of((dp % share_of) * wide_rows, 8), wide_rows), :].T
        picked = jnp.zeros((1, wide_rows), jnp.float32)
        for tile in range(4):
            picked = jnp.where(dp // share_of == tile, wide[2 + tile : 3 + tile], picked)
        up_bias_grad_ref[...] = picked

    def late_vectors():
        for m in range(2):
            by_vector[m, :, 0:middle] = late[:, 2 * m, :]
            by_vector[m, :, middle:model] = late[:, 2 * m + 1, :]
        ones = jnp.ones((32, 128), jnp.float32)
        factors = jnp.concatenate([late[:, 6, 0:128], ones], 1)
        for part in range(6):
            at = dp * 6 + part
            spread[...] = lax.dot_general(
                by_vector[at // 16],
                factors,
                (((0,), (0,)), ((), ())),
                precision=highest,
                preferred_element_type=jnp.float32,
            )
            kept = spread[pl.ds(pl.multiple_of((at % 16) * unit, 8), unit), :]
            mod_weight_grad_ref[part * unit : (part + 1) * unit] = kept[:, 0:128]
            spread_bias[part * unit : (part + 1) * unit] = kept[:, 128:256]
        mod_bias_grad_ref[...] = spread_bias[...].T[0:1]
        time_grad_ref[...] += time_part(0) + time_part(1)
        gains = [jnp.sum(late[:, row, :], 0, keepdims=True) for row in (4, 5)]
        turned[...] = jnp.broadcast_to(jnp.concatenate(gains, 1), (8, model)).T
        gain_grad_ref[...] = turned[pl.ds(pl.multiple_of(dp * unit, 8), unit), :].T[0:1]

    @at_step(6)
    def _():
        rows_ref[...] = entry(other_ref, half, 0)
        ins[2].step()
        away(0).start()
        rows_ref[...] += entry(other_ref, half, 1)
        out.last()
        away(1).start()
        ins[1].step()

    @at_step(7)
    def _():
        rows_ref[...] += entry(own_ref, 0, 0)
        ins[2].step()
        rows_ref[...] += entry(own_ref, 0, 1)
        home().start()
        scaling_one = 1.0 + mod_ref[1:2]
        halves(late, place, 0, rows_ref[0:1])
        halves(late, place, 2, rows_ref[1:2] * gain_ref[...])
        halves(late, place, 4, rows_ref[1:2] * scaling_one)
        embedding = time_ref[...].astype(jnp.float32)
        late[place, 6:7, 0:128] = jnp.where(links.me == 0, embedding[0:1], embedding[1:2])
        start_all(spread_copies(links, late, sems, late_slot, 0))
        hop = iter(range(4))

        def hop_on():
            number = next(hop)
            receive_all(spread_copies(links, late, sems, late_slot, number))
            if number < 3:
                start_all(spread_copies(links, late, sems, late_slot, number + 1))

        early_arrive(3)
        running_arrive(4)
        early_vectors()
        ins[0].last()
        hop_on()
        ins[1].last()
        hop_on()
        ins[2].last()
        hop_on()
        hop_on()
        late_vectors()
        for group in range(3):
            def store(at, value, group=group):
                span = 128 * CHUNKS[group]
                for part in range(3):
                    column = part * model + starts[group]
                    in_ref[at, column : column + span] = value[:, part * span : (part + 1) * span]

            ins[group].result(store)

        def store_out(at, value):
            out_grad_ref[at] = value

        out.result(store_out)

        def store_down(at, value):
            down_ref[at] = value

        down.result(store_down)

        def store_up(first):
            def store(at, value):
                count = up_ref.shape[0]
                for tile in range(value.shape[0] // count):
                    columns = slice((first + tile) * model, (first + tile + 1) * model)
                    up_ref[:, columns] = value[tile * count : (tile + 1) * count]

            return store

        upv.result(store_up(0))
        upx.result(store_up(3))
        home().wait()
        for chunk in range(half // rows):
            away(chunk).wait()
        for number in range(4):
            block_copy(number).wait()
        for number in range(4):
            for copy in spread_copies(links, early, sems, early_slot, number) + spread_copies(links, late, sems, late_slot, number):
                copy.wait_send()
        for number in range(5):
            running_copy(number).wait_send()
        tail_copy().wait_send()
        for piece in pieces:
            for copy in piece.copies:
                remote(*copy).wait_send()


def close_kernel(*refs):
    count = len(refs) // 2
    for source, target in zip(refs[:count], refs[count:]):
        target[...] = source[...].reshape(target.shape)


def turn_tables(length):
    inverse = 10000.0 ** (-np.arange(HD // 2, dtype=np.float64) * 2.0 / HD)
    angles = np.arange(length, dtype=np.float64)[:, None] * inverse[None, :]
    cosine = np.tile(np.cos(angles), (1, 4))
    sines = np.sin(angles)
    sines = np.concatenate([-sines, sines, -sines, sines], 1)
    both = [np.stack([t, np.roll(t, -(length // 2), 0)]).astype(np.float32) for t in (cosine, sines)]
    return jnp.asarray(both[0]), jnp.asarray(both[1])


def fast_body(
    tokens,
    time_embedding,
    prefix_length,
    suffix_mask,
    cotangent,
    modulation_weight,
    modulation_bias,
    attention_gain,
    attention_in,
    attention_out,
    feed_gain,
    feed_up,
    feed_up_bias,
    feed_down,
    feed_down_bias,
):
    bf16 = jnp.bfloat16
    f32 = jnp.float32
    _, half, model = tokens.shape
    length = 2 * half
    hidden_width = feed_up.shape[1]
    size = lax.axis_size("dp")
    shape = jax.ShapeDtypeStruct

    packed = [modulation_bias, attention_gain, feed_gain, feed_down_bias, feed_up_bias]
    total = sum(v.shape[0] for v in packed)
    starts = np.cumsum([0] + [v.shape[0] for v in packed])
    packed = sum(
        lax.pad(v.astype(f32), np.float32(0), [(int(a), int(total - a - v.shape[0]), 0)]) for v, a in zip(packed, starts)
    )[None]

    def packed_at(number):
        return pl.BlockSpec((1, model), lambda h: (0, number), pipeline_mode=pl.Buffered(1))

    cosine, sines = turn_tables(length)
    anywhere = pl.BlockSpec(memory_space=pl.ANY)

    def fixed(*dims):
        return pl.BlockSpec(dims, lambda h: (0,) * len(dims), pipeline_mode=pl.Buffered(1))

    first_t, qkv, other, modulation = pl.pallas_call(
        front_kernel,
        grid=(1,),
        in_specs=[
            anywhere,
            fixed(2, 128),
            anywhere,
            fixed(1, 6 * model),
            packed_at(6),
            anywhere,
            anywhere,
            anywhere,
        ],
        out_specs=[fixed(model, length), anywhere, anywhere, fixed(6, model)],
        out_shape=[
            shape((model, length), bf16),
            shape((length, 3 * model), bf16),
            shape((half, model), bf16),
            shape((6, model), f32),
        ],
        scratch_shapes=[
            pltpu.VMEM((half, model), bf16),
            pltpu.VMEM((half, model), bf16),
            pltpu.VMEM((6 * model, 128), bf16),
            pltpu.VMEM((model, 3 * model), bf16),
            pltpu.VMEM((length, 128), f32),
            pltpu.VMEM((length, 128), f32),
            pltpu.VMEM((length, 3 * model), bf16),
            pltpu.SemaphoreType.DMA((2, half // FRONT_ROWS)),
            pltpu.SemaphoreType.DMA((5,)),
            pltpu.SemaphoreType.DMA((3 * half // FRONT_ROWS,)),
        ],
        compiler_params=pltpu.CompilerParams(vmem_limit_bytes=62 * MIB, collective_id=2, has_side_effects=True),
        cost_estimate=pl.CostEstimate(flops=2 * length * model * 3 * model, bytes_accessed=16 * MIB, transcendentals=0),
        name="front",
    )(tokens, time_embedding, modulation_weight, packed, packed, attention_in, cosine, sines)

    def column(k):
        return pl.BlockSpec((length, 128), lambda h: (0, h + k))

    pairs = model // 128
    attended, exps, inverses, own_live, other_live, other_cot = pl.pallas_call(
        attend_kernel,
        grid=(pairs,),
        in_specs=[
            pl.BlockSpec(memory_space=pltpu.SMEM),
            column(0),
            column(pairs),
            column(2 * pairs),
            fixed(2, half),
            anywhere,
        ],
        out_specs=[
            column(0),
            pl.BlockSpec((2, length, length), lambda h: (h, 0, 0)),
            column(0),
            fixed(8, half),
            fixed(8, half),
            anywhere,
        ],
        out_shape=[
            shape((length, model), bf16),
            shape((HEADS, length, length), bf16),
            shape((length, model), f32),
            shape((8, half), f32),
            shape((8, half), f32),
            shape((half, model), bf16),
        ],
        scratch_shapes=[pltpu.VMEM((8, half), f32), pltpu.VMEM((8, half), f32), pltpu.SemaphoreType.DMA((2, 2))],
        compiler_params=pltpu.CompilerParams(vmem_limit_bytes=60 * MIB, collective_id=3, has_side_effects=True),
        cost_estimate=pl.CostEstimate(flops=16 * length * length * model, bytes_accessed=32 * MIB, transcendentals=0),
        name="attend",
    )(prefix_length, qkv, qkv, qkv, suffix_mask, cotangent)

    tiles = 4
    width = hidden_width // tiles
    groups = size // 2
    share_rows = hidden_width // size
    model_rows = model // size
    own_part = pl.BlockSpec((None, half, model), lambda h: (lax.axis_index("seq"), 0, 0), pipeline_mode=pl.Buffered(1))
    up_tile = pl.BlockSpec((model, width), lambda j: (0, j))
    bias_tile = pl.BlockSpec((1, width), lambda j: (0, j))
    down_tile = pl.BlockSpec((width, model), lambda j: (j, 0))
    (
        own_out,
        other_out,
        grad_middle,
        grad_attended,
        mid_rows,
        up_bias_grad,
        down_sum,
        down_tail,
        upv_sum,
        upx_sum,
        out_keep,
        out_send,
    ) = pl.pallas_call(
        middle_kernel,
        grid=(tiles,),
        in_specs=[own_part, fixed(half, model), own_part, fixed(half, model), fixed(8, half), fixed(8, half)]
        + [
            fixed(length, model),
            fixed(6, model),
            packed_at(7),
            fixed(model, model),
            up_tile,
            pl.BlockSpec((1, width), lambda j: (0, j + 9)),
            down_tile,
            packed_at(8),
        ],
        out_specs=[
            own_part,
            fixed(half, model),
            fixed(length, model),
            fixed(length, model),
            fixed(6, model),
            bias_tile,
            fixed(tiles - 1, share_rows // 2, model),
            fixed(2, share_rows // 2, model),
            fixed(2, tiles - 1, model_rows, model),
            fixed(4, model_rows, model),
            fixed(groups, model_rows, model),
            fixed(groups, model_rows, model),
        ],
        out_shape=[shape((2, half, model), bf16), shape((half, model), bf16)]
        + [shape((length, model), f32), shape((length, model), bf16), shape((6, model), f32), shape((1, hidden_width), f32)]
        + [shape((tiles - 1, share_rows // 2, model), bf16), shape((2, share_rows // 2, model), bf16), shape((2, tiles - 1, model_rows, model), bf16)]
        + [shape((4, model_rows, model), bf16)]
        + [shape((groups, model_rows, model), bf16)] * 2,
        scratch_shapes=[
            pltpu.VMEM((model, length), bf16),
            pltpu.VMEM((length, model), bf16),
            pltpu.VMEM((length, model), f32),
            pltpu.VMEM((length, model), f32),
            pltpu.VMEM((width, length), bf16),
        ]
        + [pltpu.VMEM((tiles, groups // tiles, share_rows, model), bf16)] * 3
        + [pltpu.VMEM((tiles, groups, model_rows, model), bf16)] * 3
        + [pltpu.VMEM((tiles, groups // tiles, share_rows // 2, model), bf16)] * 2
        + [pltpu.VMEM((tiles - 1, share_rows // 2, model), bf16)] * 2
        + [pltpu.VMEM((tiles - 1, 3, 2, model_rows, model), bf16)] * 2
        + [pltpu.VMEM((4, model_rows, model), bf16)] * 2
        + [pltpu.SemaphoreType.DMA((2, 7 * tiles))],
        compiler_params=pltpu.CompilerParams(vmem_limit_bytes=63 * MIB, collective_id=1, has_side_effects=True),
        cost_estimate=pl.CostEstimate(
            flops=12 * length * model * hidden_width + 6 * length * model * model, bytes_accessed=36 * MIB, transcendentals=0
        ),
        name="middle",
    )(
        tokens,
        other,
        cotangent,
        other_cot,
        own_live,
        other_live,
        attended,
        modulation,
        packed,
        attention_out,
        feed_up,
        packed,
        feed_down,
        packed,
    )
    merge = (2, (tiles - 1) * model_rows, model)

    def near(k):
        return pl.BlockSpec((length, 128), lambda h: (0, jnp.minimum(h, pairs - 1) + k))

    turn = pl.BlockSpec((None, length, 128), lambda h: (lax.axis_index("seq"), 0, 0), pipeline_mode=pl.Buffered(1))
    scratch = [
        pltpu.VMEM((model, length), bf16),
        pltpu.VMEM((model, 3 * model), bf16),
        pltpu.VMEM((half, model), bf16),
        pltpu.VMEM((half, model), bf16),
        pltpu.VMEM((length, model), f32),
        pltpu.VMEM((6 * model, 128), bf16),
        pltpu.VMEM((2, share_rows // 2, model), bf16),
        pltpu.VMEM((share_rows // 2, model), bf16),
        pltpu.VMEM((share_rows // 2, model), bf16),
        pltpu.VMEM((length, length), bf16),
        pltpu.VMEM((length, 128), f32),
        pltpu.VMEM((length, 3 * model), bf16),
        pltpu.VMEM((length, model), bf16),
        pltpu.VMEM((2, model), f32),
        pltpu.VMEM((2 * size, 8, model // 2), f32),
        pltpu.VMEM((2 * size, 8, model // 2), f32),
        pltpu.VMEM((6, 8, model), f32),
        pltpu.VMEM((5, 8, model), f32),
        pltpu.VMEM((6, 2 * size, model), f32),
        pltpu.VMEM((model, 256), f32),
        pltpu.VMEM((6 * model_rows, 128), f32),
        pltpu.VMEM((model, 8), f32),
        pltpu.SemaphoreType.DMA((2, BACK_COPIES + 24)),
        pltpu.SemaphoreType.DMA((12,)),
    ]
    for spec in BACK_PIECES:
        scratch += piece_scratch(spec)
    def cut(dims):
        if len(dims) == 3:
            return pl.BlockSpec((1, *dims[1:]), lambda i: (i, 0, 0))
        if dims[0] % 16:
            return pl.BlockSpec(dims, lambda i: (0, 0))
        return pl.BlockSpec((dims[0] // 2, dims[1]), lambda i: (i, 0))

    results = pl.pallas_call(
        back_kernel,
        grid=(pairs + 2,),
        in_specs=[
            near(0),
            near(pairs),
            near(2 * pairs),
            near(0),
            near(0),
            pl.BlockSpec((2, length, length), lambda h: (jnp.minimum(h, pairs - 1), 0, 0)),
            near(0),
            turn,
            turn,
            *[anywhere] * 5,
            fixed(6, model),
            packed_at(6),
        ]
        + [anywhere] * 6
        + [fixed(6, model), fixed(1, hidden_width), fixed(2, 128), anywhere, anywhere, anywhere],
        out_specs=[
            anywhere,
            fixed(2, 128),
            fixed(6 * model_rows, 128),
            fixed(1, 6 * model_rows),
            fixed(1, model_rows),
            fixed(1, model_rows),
            fixed(1, hidden_width // size),
            fixed(1, model_rows),
            fixed(hidden_width // size, model),
            fixed(model_rows, hidden_width),
            fixed(model_rows, model),
            fixed(model_rows, 3 * model),
            anywhere,
        ],
        out_shape=[
            shape((2, half, model), bf16),
            shape((2, 128), f32),
            shape((6 * model_rows, 128), f32),
            shape((1, 6 * model_rows), f32),
            shape((1, model_rows), f32),
            shape((1, model_rows), f32),
            shape((1, hidden_width // size), f32),
            shape((1, model_rows), f32),
            shape((hidden_width // size, model), f32),
            shape((model_rows, hidden_width), f32),
            shape((model_rows, model), f32),
            shape((model_rows, 3 * model), f32),
            shape((2, half, model), bf16),
        ],
        input_output_aliases={27: 12},
        scratch_shapes=scratch,
        compiler_params=pltpu.CompilerParams(vmem_limit_bytes=63 * MIB, collective_id=0, has_side_effects=True),
        cost_estimate=pl.CostEstimate(flops=40 * length * length * model, bytes_accessed=60 * MIB, transcendentals=0),
        name="back",
    )(
        qkv,
        qkv,
        qkv,
        attended,
        grad_attended,
        exps,
        inverses,
        cosine,
        sines,
        first_t,
        attention_in,
        tokens,
        other,
        grad_middle,
        modulation,
        packed,
        down_sum,
        down_tail,
        upv_sum.reshape(merge),
        upx_sum,
        out_keep,
        out_send,
        mid_rows,
        up_bias_grad,
        time_embedding,
        modulation_weight,
        other_out,
        own_out,
    )
    (
        tokens_grad,
        time_grad,
        modulation_weight_grad,
        modulation_bias_grad,
        gain_grad,
        feed_gain_grad,
        feed_up_bias_grad,
        feed_down_bias_grad,
        down_grad,
        up_grad,
        out_grad,
        in_grad,
        block_output,
    ) = pl.pallas_call(
        close_kernel,
        grid=(2,),
        in_specs=[cut(r.shape) for r in results],
        out_specs=[pl.BlockSpec(r.shape[1:], lambda i: (0,)) if r.shape[0] == 1 else cut(r.shape) for r in results],
        out_shape=[shape(r.shape[1:] if r.shape[0] == 1 else r.shape, r.dtype) for r in results],
        compiler_params=params(62),
        name="close",
    )(*results)
    return (
        block_output,
        tokens_grad,
        time_grad,
        modulation_weight_grad,
        modulation_bias_grad,
        gain_grad,
        in_grad,
        out_grad,
        feed_gain_grad,
        up_grad,
        feed_up_bias_grad,
        down_grad,
        feed_down_bias_grad,
    )


def body(tokens, *rest):
    sequences, half, model = tokens.shape
    size = lax.axis_size("dp")
    fits = model % (16 * size) == 0 and half % T_ROWS == 0
    fits = fits and tokens.shape[1] % MIDDLE_ROWS == 0 and rest[10].shape[1] == 4 * model and size == 16 and lax.axis_size("seq") == 2 and sequences == 2
    return (fast_body if fits else general_body)(tokens, *rest)


def solution(mesh):
    return jax.shard_map(
        body,
        mesh=mesh,
        in_specs=(
            P("dp", "seq", None),
            P("dp", None),
            P("dp"),
            P("dp", "seq"),
            P("dp", "seq", None),
            P(),
            P(),
            P(),
            P(),
            P(),
            P(),
            P(),
            P(),
            P(),
            P(),
        ),
        out_specs=(
            P("dp", "seq", None),
            P("dp", "seq", None),
            P("dp", None),
            P("dp", None),
            P("dp"),
            P("dp"),
            P("dp", None),
            P("dp", None),
            P("dp"),
            P("dp", None),
            P("dp"),
            P("dp", None),
            P("dp"),
        ),
        check_vma=False,
    )
```

```python
import functools
from functools import partial

import jax
import jax.numpy as jnp
import numpy as np
from jax import lax
from jax.experimental import pallas as pl
from jax.experimental.pallas import tpu as pltpu
from jax.sharding import PartitionSpec as P

HEADS = 12
HD = 64


highest = lax.Precision.HIGHEST


def as_sent(shard):

    def short(part):
        return part.astype(jnp.bfloat16) if part.dtype == jnp.float32 else part

    return jax.tree.map(short, shard)


def normalize(values):
    centre = values - jnp.mean(values, -1, keepdims=True)
    spread = jnp.mean(centre * centre, -1, keepdims=True)
    return centre * lax.rsqrt(spread + 1e-05)


def modulate(values, scaling, shifts, scales):
    return normalize(values) * scaling * (1.0 + scales) + shifts


def rotate(values, cosine, sines, direction):
    halves = values.shape[-1] // 2
    former = values[..., :halves]
    latter = values[..., halves:]
    cosine = cosine[None, :, None, :]
    sines = direction * sines[None, :, None, :]
    return jnp.concatenate([former * cosine - latter * sines, latter * cosine + former * sines], -1)


def attend_forward(stacked):
    query_rows = stacked[:, 0]
    key_rows = stacked[:, 1]
    value_rows = stacked[:, 2]
    length = query_rows.shape[0]
    block_rows = min(512, length)
    pieces = []
    logsums = []
    for offset in range(0, length, block_rows):
        query_block = query_rows[offset : offset + block_rows]
        scores = (
            jnp.einsum("qhd,khd->hqk", query_block, key_rows, preferred_element_type=jnp.float32)
            * 0.125
        )
        largest = jnp.max(scores, -1, keepdims=True)
        exponentials = jnp.exp(scores - largest)
        totals = jnp.sum(exponentials, -1, keepdims=True)
        probability = (exponentials / totals).astype(jnp.bfloat16)
        pieces.append(
            jnp.einsum("hqk,khd->qhd", probability, value_rows, preferred_element_type=jnp.float32)
        )
        logsums.append((largest + jnp.log(totals))[..., 0])
    return (jnp.concatenate(pieces, 0).astype(jnp.bfloat16), jnp.concatenate(logsums, 1))


def attend_backward(operands):
    stacked, grad_attended, logsums = operands
    query_rows = stacked[:, 0]
    key_rows = stacked[:, 1]
    value_rows = stacked[:, 2]
    length = query_rows.shape[0]
    block_rows = min(512, length)
    grad_query = []
    grad_keys = jnp.zeros(key_rows.shape, jnp.float32)
    grad_values = jnp.zeros(value_rows.shape, jnp.float32)
    for offset in range(0, length, block_rows):
        query_block = query_rows[offset : offset + block_rows]
        grad_block = grad_attended[offset : offset + block_rows]
        scores = (
            jnp.einsum("qhd,khd->hqk", query_block, key_rows, preferred_element_type=jnp.float32)
            * 0.125
        )
        probability = jnp.exp(scores - logsums[:, offset : offset + block_rows, None])
        grad_probs = jnp.einsum(
            "qhd,khd->hqk", grad_block, value_rows, preferred_element_type=jnp.float32
        )
        row_dots = jnp.sum(probability * grad_probs, -1, keepdims=True)
        grad_scores = (probability * (grad_probs - row_dots)).astype(jnp.bfloat16)
        grad_query.append(
            (
                jnp.einsum(
                    "hqk,khd->qhd", grad_scores, key_rows, preferred_element_type=jnp.float32
                )
                * 0.125
            ).astype(jnp.bfloat16)
        )
        grad_keys = grad_keys + jnp.einsum(
            "hqk,qhd->khd", grad_scores, query_block, preferred_element_type=jnp.float32
        )
        grad_values = grad_values + jnp.einsum(
            "hqk,qhd->khd",
            probability.astype(jnp.bfloat16),
            grad_block,
            preferred_element_type=jnp.float32,
        )
    return jnp.stack(
        [
            jnp.concatenate(grad_query, 0),
            (grad_keys * 0.125).astype(jnp.bfloat16),
            grad_values.astype(jnp.bfloat16),
        ],
        1,
    )


def general_body(
    tokens,
    time_embedding,
    prefix_length,
    suffix_mask,
    cotangent,
    modulation_weight,
    modulation_bias,
    attention_gain,
    attention_in,
    attention_out,
    feed_gain,
    feed_up,
    feed_up_bias,
    feed_down,
    feed_down_bias,
):
    sequences, local_len, model_width = tokens.shape
    groups = lax.axis_size("seq")
    data_size = lax.axis_size("dp")
    length = local_len * groups
    heads_local = HEADS // groups
    group_width = model_width // groups
    modulation = jnp.einsum(
        "sc,oc->so", time_embedding, modulation_weight, preferred_element_type=jnp.float32
    ) + modulation_bias.astype(jnp.float32)
    shift_one, scale_one, gate_one, shift_two, scale_two, gate_two = [
        portion[:, None, :] for portion in jnp.split(modulation, 6, axis=1)
    ]
    inputs = tokens.astype(jnp.float32)
    first_float, first_back = jax.vjp(
        modulate, inputs, attention_gain.astype(jnp.float32), shift_one, scale_one
    )
    first_input = first_float.astype(jnp.bfloat16)
    projected = jnp.einsum(
        "spd,de->spe", first_input, attention_in, preferred_element_type=jnp.float32
    ).reshape(sequences, local_len, 3, HEADS, HD)
    position_ints = lax.axis_index("seq") * local_len + jnp.arange(local_len, dtype=jnp.int32)
    positions = position_ints.astype(jnp.float32)
    inverse = 10000.0 ** (-jnp.arange(HD // 2, dtype=jnp.float32) * 2.0 / HD)
    angles = positions[:, None] * inverse[None, :]
    cosine = jnp.cos(angles)
    sines = jnp.sin(angles)
    rotated = jnp.stack(
        [
            rotate(projected[:, :, 0], cosine, sines, 1.0),
            rotate(projected[:, :, 1], cosine, sines, 1.0),
            projected[:, :, 2],
        ],
        2,
    ).astype(jnp.bfloat16)
    by_heads = lax.all_to_all(
        rotated.reshape(sequences, local_len, 3, groups, group_width),
        "seq",
        split_axis=3,
        concat_axis=1,
        tiled=True,
    )
    by_heads = by_heads.reshape(sequences, length, 3, heads_local, HD)
    attended_heads, logsums = lax.map(attend_forward, by_heads)
    attended = lax.all_to_all(
        as_sent(attended_heads.reshape(sequences, length, 1, group_width)),
        "seq",
        split_axis=1,
        concat_axis=2,
        tiled=True,
    )
    attended = attended.reshape(sequences, local_len, model_width)
    branch_one = jnp.einsum(
        "spd,de->spe", attended, attention_out, preferred_element_type=jnp.float32
    )
    middle = inputs + gate_one * branch_one
    second_float, second_back = jax.vjp(
        modulate, middle, feed_gain.astype(jnp.float32), shift_two, scale_two
    )
    second_input = second_float.astype(jnp.bfloat16)
    hidden = jnp.einsum(
        "spd,df->spf", second_input, feed_up, preferred_element_type=jnp.float32
    ) + feed_up_bias.astype(jnp.float32)
    activated_float, gelu_back = jax.vjp(partial(jax.nn.gelu, approximate=True), hidden)
    activated = activated_float.astype(jnp.bfloat16)
    branch_two = jnp.einsum(
        "spf,fd->spd", activated, feed_down, preferred_element_type=jnp.float32
    ) + feed_down_bias.astype(jnp.float32)
    block_output = (middle + gate_two * branch_two).astype(jnp.bfloat16)
    live_rows = ((position_ints[None, :] >= prefix_length[:, None]) & (suffix_mask == 1)).astype(
        jnp.float32
    )
    grad_output = cotangent.astype(jnp.float32) * live_rows[:, :, None]
    grad_gate_two = jnp.sum(grad_output * branch_two, axis=1)
    grad_branch_two = (gate_two * grad_output).astype(jnp.bfloat16)
    feed_down_bias_grad = jnp.sum(grad_branch_two.astype(jnp.float32), axis=(0, 1))
    feed_down_grad = jnp.einsum(
        "spf,spd->fd", activated, grad_branch_two, preferred_element_type=jnp.float32
    )
    grad_activated = jnp.einsum(
        "spd,fd->spf", grad_branch_two, feed_down, preferred_element_type=jnp.float32
    )
    grad_hidden = gelu_back(grad_activated)[0].astype(jnp.bfloat16)
    feed_up_bias_grad = jnp.sum(grad_hidden.astype(jnp.float32), axis=(0, 1))
    feed_up_grad = jnp.einsum(
        "spd,spf->df", second_input, grad_hidden, preferred_element_type=jnp.float32
    )
    grad_second = jnp.einsum(
        "spf,df->spd", grad_hidden, feed_up, preferred_element_type=jnp.float32
    )
    grad_from_norm, feed_gain_grad, grad_shift_two, grad_scale_two = second_back(grad_second)
    grad_middle = grad_output + grad_from_norm
    grad_gate_one = jnp.sum(grad_middle * branch_one, axis=1)
    grad_branch_one = (gate_one * grad_middle).astype(jnp.bfloat16)
    attention_out_grad = jnp.einsum(
        "spd,spe->de", attended, grad_branch_one, preferred_element_type=jnp.float32
    )
    grad_attended = jnp.einsum(
        "spe,de->spd", grad_branch_one, attention_out, preferred_element_type=jnp.float32
    ).astype(jnp.bfloat16)
    grad_heads = lax.all_to_all(
        grad_attended.reshape(sequences, local_len, groups, group_width),
        "seq",
        split_axis=2,
        concat_axis=1,
        tiled=True,
    )
    grad_heads = grad_heads.reshape(sequences, length, heads_local, HD)
    grad_stacked = lax.map(attend_backward, (by_heads, grad_heads, logsums))
    grad_positions = lax.all_to_all(
        as_sent(grad_stacked.reshape(sequences, length, 3, 1, group_width)),
        "seq",
        split_axis=1,
        concat_axis=3,
        tiled=True,
    )
    grad_positions = grad_positions.reshape(sequences, local_len, 3, HEADS, HD).astype(jnp.float32)
    grad_projected = jnp.stack(
        [
            rotate(grad_positions[:, :, 0], cosine, sines, -1.0),
            rotate(grad_positions[:, :, 1], cosine, sines, -1.0),
            grad_positions[:, :, 2],
        ],
        2,
    ).astype(jnp.bfloat16)
    grad_projected = grad_projected.reshape(sequences, local_len, 3 * model_width)
    attention_in_grad = jnp.einsum(
        "spd,spe->de", first_input, grad_projected, preferred_element_type=jnp.float32
    )
    grad_first = jnp.einsum(
        "spe,de->spd", grad_projected, attention_in, preferred_element_type=jnp.float32
    )
    grad_tokens_norm, attention_gain_grad, grad_shift_one, grad_scale_one = first_back(grad_first)
    tokens_grad = (grad_middle + grad_tokens_norm).astype(jnp.bfloat16)
    grad_modulation = jnp.concatenate(
        [
            grad_shift_one[:, 0],
            grad_scale_one[:, 0],
            grad_gate_one,
            grad_shift_two[:, 0],
            grad_scale_two[:, 0],
            grad_gate_two,
        ],
        1,
    )
    modulation_total = lax.psum(grad_modulation.astype(jnp.bfloat16), "seq").astype(jnp.float32)
    time_grad = jnp.einsum(
        "so,oc->sc", modulation_total, modulation_weight.astype(jnp.float32), precision=highest
    )
    modulation_weight_grad = jnp.einsum(
        "so,sc->oc", grad_modulation, time_embedding.astype(jnp.float32), precision=highest
    )
    modulation_bias_grad = jnp.sum(grad_modulation, axis=0)
    gradients = (
        modulation_weight_grad,
        modulation_bias_grad,
        attention_gain_grad,
        attention_in_grad,
        attention_out_grad,
        feed_gain_grad,
        feed_up_grad,
        feed_up_bias_grad,
        feed_down_grad,
        feed_down_bias_grad,
    )
    flattened = tuple((g.reshape(data_size, -1) for g in gradients))
    shares = lax.psum_scatter(flattened, "dp", scatter_dimension=0, tiled=True)
    summed = jax.tree.map(lambda part: part.astype(jnp.float32), lax.psum(as_sent(shares), "seq"))
    shards = tuple(
        (s.reshape((g.shape[0] // data_size,) + g.shape[1:]) for s, g in zip(summed, gradients))
    )
    return (
        block_output,
        tokens_grad,
        time_grad,
        shards[0],
        shards[1],
        shards[2],
        shards[3],
        shards[4],
        shards[5],
        shards[6],
        shards[7],
        shards[8],
        shards[9],
    )


T_ROWS = 256
FRONT_ROWS = 128
MIDDLE_ROWS = 256
MIB = 1 << 20


def dot(a, b, ca, cb):
    return lax.dot_general(a, b, (((ca,), (cb,)), ((), ())), preferred_element_type=jnp.float32)


def params(limit=60):
    return pltpu.CompilerParams(vmem_limit_bytes=limit * MIB)


def norm_rows(values):
    centre = values - jnp.mean(values, -1, keepdims=True)
    inverse = lax.rsqrt(jnp.mean(centre * centre, -1, keepdims=True) + 1e-05)
    return centre * inverse, inverse


def swap_halves(values, lane):
    left = pltpu.roll(values, 96, 1)
    right = pltpu.roll(values, 32, 1)
    return jnp.where(lane % 64 < 32, left, right)


def attend_kernel(
    prefix_ref,
    q_ref,
    k_ref,
    v_ref,
    mask_ref,
    cot_hbm,
    out_ref,
    exp_ref,
    inv_ref,
    own_live_ref,
    other_live_ref,
    other_cot_hbm,
    give,
    got,
    sems,
):
    rows = 128
    step = pl.program_id(0)
    links = Links()
    half = mask_ref.shape[1]
    partner = links.partner["Y"]

    def exchanges():
        return [
            remote(give, got, sems, 0, partner),
            remote(cot_hbm.at[1 - links.me], other_cot_hbm, sems, 1, partner),
        ]

    @pl.when(step == 0)
    def _():
        position = links.me * half + lax.broadcasted_iota(jnp.int32, (1, half), 1)
        live = [
            jnp.where((position >= prefix_ref[i]) & (mask_ref[i : i + 1] == 1), 1.0, 0.0) for i in range(2)
        ]
        wide = [jnp.broadcast_to(row, (8, half)) for row in live]
        own_live_ref[...] = jnp.where(links.me == 0, wide[0], wide[1])
        give[...] = jnp.where(links.me == 0, wide[1], wide[0])
        links.greet(("Y",))
        start_all(exchanges())

    length = q_ref.shape[0]
    lane = lax.broadcasted_iota(jnp.int32, (rows, 128), 1)
    keys = k_ref[...]
    values = jnp.concatenate([v_ref[...], jnp.ones((length, 128), jnp.bfloat16)], 1)
    for chunk in range(length // rows):
        at = slice(chunk * rows, (chunk + 1) * rows)
        queries = q_ref[at]
        outs = []
        inverses = []
        for head in range(2):
            mine = jnp.where((lane < 64) == (head == 0), queries, jnp.zeros_like(queries))
            scores = dot(mine, keys, 1, 1)
            largest = jnp.max(scores, -1, keepdims=True)
            exps = jnp.exp(scores - largest).astype(jnp.bfloat16)
            exp_ref[head, at] = exps
            summed = dot(exps, values, 1, 0)
            inverse = 1.0 / summed[:, 128:256]
            outs.append(summed[:, 0:128] * inverse)
            inverses.append(inverse)
        out_ref[at] = jnp.where(lane < 64, outs[0], outs[1]).astype(jnp.bfloat16)
        inv_ref[at] = jnp.where(lane < 64, inverses[0], inverses[1])

    @pl.when(step == pl.num_programs(0) - 1)
    def _():
        for copy in exchanges():
            copy.wait()
        other_live_ref[...] = got[...]


def share(core, grad, keep_ref, send_ref, *at):
    first, second = grad
    keep_ref[at] = jnp.where(core == 0, first, second)
    send_ref[at] = jnp.where(core == 0, second, first)


def middle_kernel(
    own_ref,
    other_ref,
    own_cot_ref,
    other_cot_ref,
    own_live_ref,
    other_live_ref,
    attended_ref,
    mod_ref,
    gain_ref,
    out_weight_ref,
    up_ref,
    up_bias_ref,
    down_ref,
    down_bias_ref,
    own_out_ref,
    other_out_ref,
    grad_middle_ref,
    grad_attended_ref,
    rows_ref,
    up_bias_grad_ref,
    down_sum_ref,
    down_tail_ref,
    upv_sum_ref,
    upx_sum_ref,
    out_keep_ref,
    out_send_ref,
    second_t,
    grad_two,
    sum_two,
    sum_second,
    act_t,
    down_keep,
    down_give,
    down_got,
    up_keep,
    up_give,
    up_got,
    down_half,
    down_half_got,
    down_part,
    down_part_got,
    up_part,
    up_part_got,
    up_half,
    up_half_got,
    sems,
):
    rows = MIDDLE_ROWS
    step = pl.program_id(0)
    links = Links()
    core = links.bit["C"]
    tiles = down_keep.shape[0]

    per_tile = 7
    last = tiles - 1

    def first_copies(tile):
        return [
            remote(give.at[tile], got.at[tile], sems, tile * per_tile + i, links.partner["C"])
            for i, (give, got) in enumerate(((down_give, down_got), (up_give, up_got)))
        ]

    def down_copy(tile):
        return remote(down_half.at[tile], down_half_got.at[tile], sems, tile * per_tile + 2, links.partner["Y"])

    def down_on_copy(tile):
        return remote(down_part.at[tile], down_part_got.at[tile], sems, tile * per_tile + 3, links.partner["X"])

    def up_copies(tile):
        return [
            remote(up_part.at[tile, i], up_part_got.at[tile, i], sems, tile * per_tile + 4 + i, links.partner[flip])
            for i, flip in enumerate(Z_FLIPS)
        ]

    def up_last_copy():
        return remote(up_half, up_half_got, sems, last * per_tile + 4, links.partner["X"])

    def total(*terms):
        return sum(term.astype(jnp.float32) for term in terms).astype(jnp.bfloat16)

    half_rows = down_half.shape[2]
    home = pl.ds(pl.multiple_of(links.me * half_rows, 16), half_rows)
    away = pl.ds(pl.multiple_of((1 - links.me) * half_rows, 16), half_rows)
    z_at = links.bit["W"] * 2 + links.bit["Z"]

    def flipped(flip):
        values = {bit: 1 - links.bit[bit] if bit in flip else links.bit[bit] for bit in "WZ"}
        return values["W"] * 2 + values["Z"]

    def send_on(tile, final):
        for copy in first_copies(tile):
            copy.wait_recv()
        for x in range(2):
            down_half[tile, x] = total(down_keep[tile, x, away], down_got[tile, x, away])
        down_copy(tile).start()
        if final:
            for z in range(4):
                other = 2 * z + 1 - links.bit["X"]
                up_half[z] = total(up_keep[tile, other], up_got[tile, other])
            up_last_copy().start()
        else:
            for i, flip in enumerate(Z_FLIPS):
                for x in range(2):
                    other = 2 * flipped(flip) + x
                    up_part[tile, i, x] = total(up_keep[tile, other], up_got[tile, other])
            for copy in up_copies(tile):
                copy.start()

    def send_down(tile):
        down_copy(tile).wait_recv()
        x = 1 - links.bit["X"]
        down_part[tile] = total(down_keep[tile, x, home], down_got[tile, x, home], down_half_got[tile, x])
        down_on_copy(tile).start()

    def settle(tile, final):
        if final:
            down_copy(tile).wait_recv()
            for x in range(2):
                down_tail_ref[x] = total(down_keep[tile, x, home], down_got[tile, x, home], down_half_got[tile, x])
        else:
            down_on_copy(tile).wait_recv()
            x = links.bit["X"]
            terms = (down_keep[tile, x, home], down_got[tile, x, home], down_half_got[tile, x], down_part_got[tile])
            down_sum_ref[tile] = total(*terms)
        if final:
            up_last_copy().wait_recv()
            for z in range(4):
                mine = 2 * z + links.bit["X"]
                upx_sum_ref[z] = total(up_keep[tile, mine], up_got[tile, mine], up_half_got[z])
        else:
            for copy in up_copies(tile):
                copy.wait_recv()
            for x in range(2):
                mine = 2 * z_at + x
                got = [up_part_got[tile, i, x] for i in range(3)]
                upv_sum_ref[x, tile] = total(up_keep[tile, mine], up_got[tile, mine], *got)

    @pl.when(step == 0)
    def _():
        links.greet()

    half, model = own_ref.shape
    length = 2 * half
    scaling = gain_ref[...] * (1.0 + mod_ref[4:5])
    gate_one = mod_ref[2:3]
    shift_two = mod_ref[3:4]
    gate_two = mod_ref[5:6]

    def pick(first_ref, second_ref, chunk):
        at = chunk * rows
        return (first_ref if at < half else second_ref)[at % half : at % half + rows]

    def live_cot(chunk):
        at = (chunk * rows) % half
        live = (own_live_ref if chunk * rows < half else other_live_ref)[...].T[at : at + rows, 0:1]
        return pick(own_cot_ref, other_cot_ref, chunk).astype(jnp.float32) * live

    @pl.when(step == 0)
    def _():
        bias_grad = jnp.zeros((1, model), jnp.float32)
        for chunk in range(length // rows):
            at = slice(chunk * rows, (chunk + 1) * rows)
            branch = dot(attended_ref[at], out_weight_ref[...], 1, 0)
            grad_middle_ref[at] = branch
            sum_two[at] = jnp.zeros((rows, model), jnp.float32)
            sum_second[at] = jnp.zeros((rows, model), jnp.float32)
            middle = pick(own_ref, other_ref, chunk).astype(jnp.float32) + gate_one * branch
            normed, _ = norm_rows(middle)
            rounded = (normed * scaling + shift_two).astype(jnp.bfloat16)
            place = (chunk * rows) % half
            (own_out_ref if chunk * rows < half else other_out_ref)[place : place + rows] = rounded
            second_t[:, at] = rounded.T
            grad = (gate_two * live_cot(chunk)).astype(jnp.bfloat16)
            grad_two[at] = grad
            bias_grad = bias_grad + jnp.sum(grad.astype(jnp.float32), 0, keepdims=True)
        rows_ref[5:6] = bias_grad

    up = up_ref[...]
    down = down_ref[...]
    width = up.shape[1]
    bias_sum = jnp.zeros((1, width), jnp.float32)
    for chunk in range(length // rows):
        if chunk == 1:

            @pl.when(step > 0)
            def _():
                send_on(step - 1, False)

            @pl.when(step > 1)
            def _():
                send_down(step - 2)

        at = slice(chunk * rows, (chunk + 1) * rows)
        hidden = dot(pick(own_out_ref, other_out_ref, chunk), up, 1, 0) + up_bias_ref[...]
        squared = hidden * hidden
        tanh = jnp.tanh(hidden * (0.7978845608028654 + 0.035677408136300125 * squared))
        gate = 0.5 + 0.5 * tanh
        activated = (hidden * gate).astype(jnp.bfloat16)
        slope = gate + (0.5 * hidden) * (1.0 - tanh * tanh) * (0.7978845608028654 + 0.10703222440890037 * squared)
        act_t[:, at] = activated.T
        grad = (slope * dot(grad_two[at], down, 1, 1)).astype(jnp.bfloat16)
        grad_attended_ref[at] = grad
        bias_sum = bias_sum + jnp.sum(grad.astype(jnp.float32), 0, keepdims=True)
        sum_two[at] += dot(activated, down, 1, 0)
        sum_second[at] += dot(grad, up, 1, 1)

    up_bias_grad_ref[...] = bias_sum
    down_grad = dot(act_t[...], grad_two[...], 1, 0).astype(jnp.bfloat16).reshape(2, 2, -1, model)
    share(core, (down_grad[:, 0], down_grad[:, 1]), down_keep, down_give, step)
    up_grad = dot(second_t[...], grad_attended_ref[...], 1, 0).astype(jnp.bfloat16).reshape(up_keep.shape[1], 2, -1, width)
    share(core, (up_grad[:, 0], up_grad[:, 1]), up_keep, up_give, step)
    for copy in first_copies(step):
        copy.start()

    @pl.when(step == pl.num_programs(0) - 1)
    def _():
        sums = [jnp.zeros((1, model), jnp.float32) for _ in range(4)]
        for chunk in range(length // rows):
            at = slice(chunk * rows, (chunk + 1) * rows)
            branch = grad_middle_ref[at]
            middle = pick(own_ref, other_ref, chunk).astype(jnp.float32) + gate_one * branch
            normed, inverse = norm_rows(middle)
            branch_two = sum_two[at] + down_bias_ref[...]
            output = (middle + gate_two * branch_two).astype(jnp.bfloat16)
            place = (chunk * rows) % half
            (own_out_ref if chunk * rows < half else other_out_ref)[place : place + rows] = output
            cot = live_cot(chunk)
            grad = sum_second[at]
            weighted = grad * normed
            scaled = grad * scaling
            inner = jnp.mean(weighted * scaling, -1, keepdims=True)
            grad_middle = cot + (scaled - jnp.mean(scaled, -1, keepdims=True) - normed * inner) * inverse
            grad_middle_ref[at] = grad_middle
            grad_one = (gate_one * grad_middle).astype(jnp.bfloat16)
            grad_two[at] = grad_one
            act_t[:, at] = attended_ref[at].T
            grad_attended_ref[at] = dot(grad_one, out_weight_ref[...], 1, 1).astype(jnp.bfloat16)
            for i, term in enumerate((grad_middle * branch, grad, weighted, cot * branch_two)):
                sums[i] = sums[i] + jnp.sum(term, 0, keepdims=True)
            if chunk == 0:
                send_on(last, True)
                send_down(last - 1)
        rows_ref[0:1] = sums[0]
        rows_ref[1:2] = sums[1]
        rows_ref[2:3] = sums[2] * gain_ref[...]
        rows_ref[3:4] = sums[3]
        rows_ref[4:5] = sums[2] * (1.0 + mod_ref[4:5])
        out_grad = dot(act_t[...], grad_two[...], 1, 0).astype(jnp.bfloat16)
        out_grad = out_grad.reshape(out_keep_ref.shape[0], 2, -1, model)
        share(core, (out_grad[:, 0], out_grad[:, 1]), out_keep_ref, out_send_ref, Ellipsis)
        for tile in range(last):
            settle(tile, False)
        settle(last, True)
        for tile in range(tiles):
            ups = [up_last_copy()] if tile == last else up_copies(tile)
            for copy in first_copies(tile) + [down_copy(tile)] + ([] if tile == last else [down_on_copy(tile)]) + ups:
                copy.wait_send()


Z_FLIPS = ("Z", "W", "ZW")


class Links:
    def __init__(self):
        dp = lax.axis_index("dp")
        self.me = lax.axis_index("seq")
        self.bit = {"C": dp % 2, "X": (dp // 2) % 2, "Z": (dp // 4) % 2, "W": (dp // 8) % 2, "Y": self.me}
        jump = {name: size * (1 - 2 * self.bit[name]) for name, size in (("C", 1), ("X", 2), ("Z", 4), ("W", 8))}
        self.partner = {name: (dp + jump[name], self.me) for name in "CXZW"}
        self.partner["ZW"] = (dp + jump["Z"] + jump["W"], self.me)
        self.partner["Y"] = (dp, 1 - self.me)

    def place(self):
        return self.me * 16 + self.bit["X"] * 8 + self.bit["W"] * 4 + self.bit["Z"] * 2 + self.bit["C"]

    def greet(self, names=("C", "X", "Z", "W", "ZW", "Y")):
        barrier = pltpu.get_barrier_semaphore()
        for name in names:
            device = self.partner[name]
            pl.semaphore_signal(barrier, inc=1, device_id=device, device_id_type=pl.DeviceIdType.MESH)
        pl.semaphore_wait(barrier, len(names))


def flips_of(kind):
    return Z_FLIPS if kind == "V" else (kind,)


def remote(source, target, sems, slot, device):
    return pltpu.make_async_remote_copy(
        src_ref=source,
        dst_ref=target,
        send_sem=sems.at[0, slot],
        recv_sem=sems.at[1, slot],
        device_id=device,
        device_id_type=pl.DeviceIdType.MESH,
    )


def piece_scratch(spec):
    _, rows, width, left, order, kind = spec
    count = 1 << len(left)
    shapes = [count] * (1 + ("summed", "given", "made").index(kind))
    for step in order:
        count //= 4 if step == "V" else 2
        shapes += [count * len(flips_of(step))] * 2
    shapes += [1] * 2
    return [pltpu.VMEM((c, rows, width), jnp.bfloat16) for c in shapes]


class Piece:
    def __init__(self, links, refs, spec, sems, slot, source=None, split=False):
        refs = list(refs)
        _, _, _, left, order, kind = spec
        self.links = links
        self.sems = sems
        self.slot = slot
        self.order = list(order)
        self.split = split
        self.left = list(left)
        self.keep = refs.pop(0)
        self.terms = [(self.keep, list(self.left))]
        self.copies = []
        self.flying = []
        if kind != "summed":
            first = refs.pop(0)
            self.source = refs.pop(0) if kind == "made" else source
            copy = (self.source, first, sems, slot, links.partner["C"])
            self.slot += 1
            self.copies.append(copy)
            self.flying = [(copy, first, list(self.left))]
        self.buffers = refs

    def launch(self, source, target, flip):
        copy = (source, target, self.sems, self.slot, self.links.partner[flip])
        self.slot += 1
        remote(*copy).start()
        self.copies.append(copy)
        self.flying.append((copy, target, list(self.left)))

    def begin(self):
        remote(*self.copies[0]).start()

    def arrive(self):
        for copy, target, bits in self.flying:
            remote(*copy).wait_recv()
            self.terms.append((target, bits))
        self.flying = []

    def index(self, bits, values):
        at = 0
        for bit in bits:
            at = at * 2 + values[bit]
        return at

    def add(self, out, flip):
        links = self.links
        rows = out.shape[1]
        block = 48
        for combo in range(1 << len(self.left)):
            values = dict(links.bit)
            for bit in flip:
                values[bit] = 1 - links.bit[bit]
            for place, bit in enumerate(self.left):
                values[bit] = (combo >> (len(self.left) - 1 - place)) & 1
            indices = [self.index(bits, values) for _, bits in self.terms]

            def some(i, carry, indices=indices, combo=combo):
                at = pl.ds(pl.multiple_of(i * block, 16), block)
                total = None
                for (ref, _), index in zip(self.terms, indices):
                    term = ref[index, at, :].astype(jnp.float32)
                    total = term if total is None else total + term
                out[combo, at, :] = total.astype(jnp.bfloat16)
                return carry

            lax.fori_loop(0, rows // block, some, 0)

    def step(self):
        self.arrive()
        kind = self.order.pop(0)
        out, target = self.buffers.pop(0), self.buffers.pop(0)
        for bit in "WZ" if kind == "V" else kind:
            self.left.remove(bit)
        count = 1 << len(self.left)
        for i, flip in enumerate(flips_of(kind)):
            part = pl.ds(i * count, count)
            self.add(out.at[part], flip)
            self.launch(out.at[part], target.at[part], flip)

    def last(self):
        self.arrive()
        self.total, self.got = self.buffers.pop(0), self.buffers.pop(0)
        self.add(self.total, "")
        self.launch(self.total, self.got, "Y")

    def result(self, store):
        remote(*self.flying[0][0]).wait_recv()
        rows = self.total.shape[1]
        total = self.total[0].astype(jnp.float32)
        got = self.got[0].astype(jnp.float32)
        if self.split:
            store(pl.ds(pl.multiple_of(self.links.me * rows, 8), rows), total)
            store(pl.ds(pl.multiple_of((1 - self.links.me) * rows, 8), rows), got)
        else:
            store(slice(0, rows), total + got)


CHUNKS = (3, 2, 1)
BACK_PIECES = (
    ("down", 96, 768, "WZ", "V", "summed"),
    ("upv", 144, 768, "X", "X", "summed"),
    ("upx", 48, 768, "WZ", "V", "summed"),
    ("out", 48, 768, "WZX", "XV", "given"),
    *((f"in{i}", 48, 384 * pairs, "WZX", "XV", "made") for i, pairs in enumerate(CHUNKS)),
)


def copies_of(spec):
    return sum(len(flips_of(kind)) for kind in spec[4]) + 1 + (spec[5] != "summed")


BACK_COPIES = sum(copies_of(spec) for spec in BACK_PIECES)
HOPS = (("C",), Z_FLIPS, ("X",), ("Y",))
RUNNING = "CXZWY"


def spread_copies(links, array, sems, slot, number):
    place = links.place()
    have = (1, 2, 8, 16)[number]
    part = array.at[pl.ds((place // have) * have, have)]
    slot += (0, 1, 4, 5)[number]
    return [remote(part, part, sems, slot + i, links.partner[flip]) for i, flip in enumerate(HOPS[number])]


def start_all(copies):
    for copy in copies:
        copy.start()


def receive_all(copies):
    for copy in copies:
        copy.wait_recv()


def front_kernel(
    tokens_hbm,
    time_ref,
    mod_weight_hbm,
    mod_bias_ref,
    gain_ref,
    weight_hbm,
    cos_hbm,
    sin_hbm,
    first_t_ref,
    qkv_hbm,
    other_hbm,
    mod_ref,
    other_ref,
    own,
    mod_weight,
    weight,
    cos_ref,
    sin_ref,
    qkv,
    sems,
    local_sems,
    store_sems,
):
    rows = FRONT_ROWS
    half, model = own.shape
    blocks = half // rows
    links = Links()

    def exchange(block):
        at = pl.ds(block * rows, rows)
        return remote(tokens_hbm.at[1 - links.me, at], other_ref.at[at], sems, block, links.partner["Y"])

    def fetches():
        pairs = (
            (mod_weight_hbm, mod_weight),
            (tokens_hbm.at[links.me], own),
            (weight_hbm, weight),
            (cos_hbm.at[links.me], cos_ref),
            (sin_hbm.at[links.me], sin_ref),
        )
        return [pltpu.make_async_copy(a, b, local_sems.at[i]) for i, (a, b) in enumerate(pairs)]

    def store(block):
        at = pl.ds(block * rows, rows)
        return pltpu.make_async_copy(qkv.at[at], qkv_hbm.at[at], store_sems.at[block])

    def store_other(block):
        at = pl.ds(block * rows, rows)
        return pltpu.make_async_copy(other_ref.at[at], other_hbm.at[at], store_sems.at[2 * blocks + block])

    for copy in fetches():
        copy.start()
    links.greet(("Y",))
    for block in range(blocks):
        exchange(block).start()
    for copy in fetches():
        copy.wait()
    embedding = time_ref[...].astype(jnp.float32)
    embedding = jnp.where(links.me == 0, embedding[0:1], embedding[1:2])
    embedding = jnp.broadcast_to(embedding, (16, embedding.shape[1])).astype(jnp.bfloat16)
    modulation = dot(embedding, mod_weight[...], 1, 1)[0:1] + mod_bias_ref[...].astype(jnp.float32)
    parts = [modulation[:, i * model : (i + 1) * model] for i in range(6)]
    for i in range(6):
        mod_ref[i : i + 1] = parts[i]
    lane = lax.broadcasted_iota(jnp.int32, (rows, 128), 1)
    scaling = gain_ref[...].astype(jnp.float32) * (1.0 + parts[1])
    for block in range(2 * blocks):
        if block < blocks:
            source = own[block * rows : (block + 1) * rows]
        else:
            exchange(block - blocks).wait_recv()
            source = other_ref[(block - blocks) * rows : (block - blocks + 1) * rows]
            store_other(block - blocks).start()
        at = slice(block * rows, (block + 1) * rows)
        normed, _ = norm_rows(source.astype(jnp.float32))
        first = (normed * scaling + parts[0]).astype(jnp.bfloat16)
        first_t_ref[:, at] = first.T
        for part in range(3):
            projected = dot(first, weight[:, part * model : (part + 1) * model], 1, 0)
            for column in range(model // 128):
                piece = projected[:, column * 128 : (column + 1) * 128]
                if part < 2:
                    piece = piece * cos_ref[at] + swap_halves(piece, lane) * sin_ref[at]
                piece = piece.astype(jnp.bfloat16)
                if part == 0:
                    piece = piece * 0.125
                start = part * model + column * 128
                qkv[at, start : start + 128] = piece
        store(block).start()
    for block in range(2 * blocks):
        store(block).wait()
    for block in range(blocks):
        store_other(block).wait()
        exchange(block).wait_send()


def back_kernel(
    q_ref,
    k_ref,
    v_ref,
    out_ref,
    grad_ref,
    exp_ref,
    inv_ref,
    cos_ref,
    sin_ref,
    first_t_hbm,
    weight_hbm,
    own_hbm,
    other_hbm,
    grad_middle_hbm,
    mod_ref,
    gain_ref,
    down_keep,
    down_tail_hbm,
    upv_keep,
    upx_keep,
    out_keep,
    out_send,
    mid_rows_ref,
    up_bias_ref,
    time_ref,
    mod_weight_hbm,
    other_block_ref,
    _,
    tokens_grad_ref,
    time_grad_ref,
    mod_weight_grad_ref,
    mod_bias_grad_ref,
    gain_grad_ref,
    feed_gain_grad_ref,
    up_bias_grad_ref,
    down_bias_grad_ref,
    down_ref,
    up_ref,
    out_grad_ref,
    in_ref,
    block_ref,
    first_t_ref,
    weight_ref,
    own_ref,
    other_ref,
    grad_middle_ref,
    mod_weight_ref,
    down_tail,
    down_tail_give,
    down_tail_got,
    ds_ref,
    dq_sum,
    proj,
    tokens_stage,
    rows_ref,
    early,
    late,
    running,
    running_got,
    by_vector,
    spread,
    spread_bias,
    turned,
    sems,
    local_sems,
    *buffers,
):
    rows = T_ROWS
    step = pl.program_id(0)
    length = q_ref.shape[0]
    half, model = other_ref.shape
    links = Links()
    core = links.bit["C"]
    pieces = []
    buffers = list(buffers)
    slot = 0
    for spec in BACK_PIECES:
        count = len(piece_scratch(spec))
        source = out_send if spec[0] == "out" else None
        pieces.append(Piece(links, buffers[:count], spec, sems, slot, source, spec[0] == "down"))
        buffers = buffers[count:]
        slot += copies_of(spec)
    down, upv, upx, out, *ins = pieces

    def fetches(first=0, end=11):
        pairs = (
            (upv_keep, upv.keep),
            (down_keep, down.keep.at[pl.ds(0, 3)]),
            (upx_keep, upx.keep),
            (out_keep, out.keep),
            (down_tail_hbm, down_tail),
            (first_t_hbm, first_t_ref),
            (weight_hbm, weight_ref),
            (other_hbm, other_ref),
            (grad_middle_hbm, grad_middle_ref),
            (own_hbm.at[links.me], own_ref),
            (mod_weight_hbm, mod_weight_ref),
        )
        return [pltpu.make_async_copy(a, b, local_sems.at[i]) for i, (a, b) in enumerate(pairs) if first <= i < end]

    place = links.place()
    dp = lax.axis_index("dp")
    early_slot = BACK_COPIES + 6
    quarter = half // 4
    late_slot = early_slot + 6
    running_slot = late_slot + 6
    tail_slot = running_slot + 5

    def running_copy(number):
        partner = links.partner[RUNNING[number]]
        return remote(running.at[number], running_got.at[number], sems, running_slot + number, partner)

    def tail_copy():
        return remote(down_tail_give, down_tail_got, sems, tail_slot, links.partner["X"])

    def block_copy(number):
        at = pl.ds(number * quarter, quarter)
        target = block_ref.at[links.me, at]
        return remote(other_block_ref.at[at], target, sems, BACK_COPIES + number, links.partner["Y"])

    def halves(target, at, first, values):
        middle = model // 2
        target[at, first : first + 1] = values[:, :middle]
        target[at, first + 1 : first + 2] = values[:, middle:]

    @pl.when(step == 0)
    def _():
        links.greet()
        for copy in fetches():
            copy.start()
        out.begin()
        for m in range(4):
            halves(early, place, 2 * m, mid_rows_ref[m : m + 1])
        running[0, 0:2] = mid_rows_ref[4:6]
        for tile in range(up_bias_ref.shape[1] // model):
            running[0, 2 + tile : 3 + tile] = up_bias_ref[:, tile * model : (tile + 1) * model]
        running[0, 6:8] = jnp.zeros((2, model), jnp.float32)
        start_all(spread_copies(links, early, sems, early_slot, 0))
        running_copy(0).start()

    for number in range(4):

        @pl.when(step == number + 1)
        def _(number=number):
            block_copy(number).start()

    def early_arrive(number):
        receive_all(spread_copies(links, early, sems, early_slot, number))

    def early_start(number):
        start_all(spread_copies(links, early, sems, early_slot, number))

    def running_arrive(number):
        running_copy(number).wait_recv()
        running[number + 1] = running[number] + running_got[number]

    def at_step(number):
        return pl.when(step == number)

    def between():
        @at_step(0)
        def _():
            for copy in fetches(0, 5):
                copy.wait()
            down_tail_give[...] = down_tail[1 - links.bit["X"]]
            early_arrive(0)
            running_arrive(0)
            early_start(1)
            running_copy(1).start()
            tail_copy().start()
            upv.step()
            upx.step()

        @at_step(1)
        def _():
            early_arrive(1)
            running_arrive(1)
            early_start(2)
            running_copy(2).start()
            tail_copy().wait_recv()
            kept = down_tail[links.bit["X"]].astype(jnp.float32) + down_tail_got[...].astype(jnp.float32)
            down.keep[3] = kept.astype(jnp.bfloat16)
            down.step()
            out.step()

        @at_step(2)
        def _():
            for copy in fetches(5):
                copy.wait()
            upx.last()
            upv.last()

        @at_step(3)
        def _():
            early_arrive(2)
            running_arrive(2)
            early_start(3)
            running_copy(3).start()
            ins[0].step()

        @at_step(4)
        def _():
            out.step()
            down.last()

        @at_step(5)
        def _():
            running_arrive(3)
            running_copy(4).start()
            ins[1].step()
            ins[0].step()

    lane = lax.broadcasted_iota(jnp.int32, (rows, 128), 1)

    @pl.when(step < 6)
    def _():
        keys = k_ref[...]
        values = v_ref[...]
        scaled = grad_ref[...].astype(jnp.float32) * inv_ref[...]
        products = scaled * out_ref[...].astype(jnp.float32)
        scaled = scaled.astype(jnp.bfloat16)
        scaled_t = scaled.T
        queries_t = q_ref[...].T
        grad_k = []
        grad_v = []
        for head in range(2):
            if head == 1:
                between()
            for chunk in range(length // rows):
                at = slice(chunk * rows, (chunk + 1) * rows)
                mask = (lane < 64) == (head == 0)
                mine = jnp.where(mask, scaled[at], jnp.zeros((rows, 128), jnp.bfloat16))
                row_dots = jnp.sum(jnp.where(mask, products[at], 0.0), -1, keepdims=True)
                grad_p = dot(mine, values, 1, 1)
                grad_s = (exp_ref[head, at].astype(jnp.float32) * (grad_p - row_dots)).astype(jnp.bfloat16)
                ds_ref[at] = grad_s
                grad_q = dot(grad_s, keys, 1, 0) * 0.125
                if head == 0:
                    dq_sum[at] = grad_q
                else:
                    dq_sum[at] = jnp.where(lane < 64, dq_sum[at], grad_q)
            grad_v.append(dot(scaled_t[64 * head : 64 * head + 64], exp_ref[head], 1, 0))
            grad_k.append(dot(queries_t[64 * head : 64 * head + 64], ds_ref[...], 1, 0))
        columns = [pl.ds(pl.multiple_of(part * model + step * 128, 128), 128) for part in range(3)]
        proj[:, columns[2]] = jnp.concatenate(grad_v, 0).astype(jnp.bfloat16).T
        grad_keys = jnp.concatenate(grad_k, 0).astype(jnp.bfloat16).T
        for chunk in range(length // rows):
            at = slice(chunk * rows, (chunk + 1) * rows)
            for part, source in enumerate((dq_sum[at].astype(jnp.bfloat16), grad_keys[at])):
                piece = source.astype(jnp.float32)
                turned = piece * cos_ref[at] - swap_halves(piece, lane) * sin_ref[at]
                proj[at, columns[part]] = turned.astype(jnp.bfloat16)

    starts = [128 * sum(CHUNKS[:i]) for i in range(len(CHUNKS))]

    def weight_part(group):
        piece = ins[group]
        span = 128 * CHUNKS[group]
        for part in range(3):
            column = part * model + starts[group]
            grad = dot(first_t_ref[...], proj[:, column : column + span], 1, 0).astype(jnp.bfloat16)
            grad = grad.reshape(8, 2, -1, span)
            share(core, (grad[:, 0], grad[:, 1]), piece.keep, piece.source, Ellipsis, slice(part * span, (part + 1) * span))
        piece.begin()

    for group, number in enumerate((2, 4, 5)):
        at_step(number)(functools.partial(weight_part, group))

    scaling = gain_ref[...] * (1.0 + mod_ref[1:2])

    def entry(values_ref, base, chunk):
        at = slice(base + chunk * rows, base + (chunk + 1) * rows)
        local = slice(chunk * rows, (chunk + 1) * rows)
        grad = dot(proj[at], weight_ref[...], 1, 1)
        normed, inverse = norm_rows(values_ref[local].astype(jnp.float32))
        weighted = grad * normed
        scaled = grad * scaling
        inner = jnp.mean(weighted * scaling, -1, keepdims=True)
        result = grad_middle_ref[at] + (scaled - jnp.mean(scaled, -1, keepdims=True) - normed * inner) * inverse
        tokens_stage[at] = result.astype(jnp.bfloat16)
        return jnp.concatenate([jnp.sum(grad, 0, keepdims=True), jnp.sum(weighted, 0, keepdims=True)], 0)

    def away(chunk):
        source = tokens_stage.at[pl.ds(half + chunk * rows, rows)]
        target = tokens_grad_ref.at[links.me, pl.ds(chunk * rows, rows)]
        return remote(source, target, sems, BACK_COPIES + 4 + chunk, links.partner["Y"])

    def home():
        return pltpu.make_async_copy(tokens_stage.at[pl.ds(0, half)], tokens_grad_ref.at[links.me], local_sems.at[11])

    unit = mod_weight_grad_ref.shape[0] // 6
    middle = model // 2

    def time_part(m):
        base = place % 16
        rest = jnp.concatenate([by_vector[m, pl.ds(base, 1)], by_vector[m, pl.ds(base + 16, 1)]], 0)
        both = jnp.zeros((2, 128), jnp.float32)
        for _ in range(3):
            high = rest.astype(jnp.bfloat16)
            both = both + dot(high, mod_weight_ref[m * model : (m + 1) * model], 1, 0)
            rest = rest - high.astype(jnp.float32)
        return both

    def early_vectors():
        for m in range(2, 6):
            by_vector[m, :, 0:middle] = early[:, 2 * m - 4, :]
            by_vector[m, :, middle:model] = early[:, 2 * m - 3, :]
        time_grad_ref[...] = sum(time_part(m) for m in range(2, 6))
        turned[...] = running[5].T
        narrow = turned[pl.ds(pl.multiple_of(dp * unit, 8), unit), :].T
        feed_gain_grad_ref[...] = narrow[0:1]
        down_bias_grad_ref[...] = narrow[1:2]
        wide_rows = up_bias_grad_ref.shape[1]
        share_of = model // wide_rows
        wide = turned[pl.ds(pl.multiple_of((dp % share_of) * wide_rows, 8), wide_rows), :].T
        picked = jnp.zeros((1, wide_rows), jnp.float32)
        for tile in range(4):
            picked = jnp.where(dp // share_of == tile, wide[2 + tile : 3 + tile], picked)
        up_bias_grad_ref[...] = picked

    def late_vectors():
        for m in range(2):
            by_vector[m, :, 0:middle] = late[:, 2 * m, :]
            by_vector[m, :, middle:model] = late[:, 2 * m + 1, :]
        ones = jnp.ones((32, 128), jnp.float32)
        factors = jnp.concatenate([late[:, 6, 0:128], ones], 1)
        for part in range(6):
            at = dp * 6 + part
            spread[...] = lax.dot_general(
                by_vector[at // 16],
                factors,
                (((0,), (0,)), ((), ())),
                precision=highest,
                preferred_element_type=jnp.float32,
            )
            kept = spread[pl.ds(pl.multiple_of((at % 16) * unit, 8), unit), :]
            mod_weight_grad_ref[part * unit : (part + 1) * unit] = kept[:, 0:128]
            spread_bias[part * unit : (part + 1) * unit] = kept[:, 128:256]
        mod_bias_grad_ref[...] = spread_bias[...].T[0:1]
        time_grad_ref[...] += time_part(0) + time_part(1)
        gains = [jnp.sum(late[:, row, :], 0, keepdims=True) for row in (4, 5)]
        turned[...] = jnp.broadcast_to(jnp.concatenate(gains, 1), (8, model)).T
        gain_grad_ref[...] = turned[pl.ds(pl.multiple_of(dp * unit, 8), unit), :].T[0:1]

    @at_step(6)
    def _():
        rows_ref[...] = entry(other_ref, half, 0)
        ins[2].step()
        away(0).start()
        rows_ref[...] += entry(other_ref, half, 1)
        out.last()
        away(1).start()
        ins[1].step()

    @at_step(7)
    def _():
        rows_ref[...] += entry(own_ref, 0, 0)
        ins[2].step()
        rows_ref[...] += entry(own_ref, 0, 1)
        home().start()
        scaling_one = 1.0 + mod_ref[1:2]
        halves(late, place, 0, rows_ref[0:1])
        halves(late, place, 2, rows_ref[1:2] * gain_ref[...])
        halves(late, place, 4, rows_ref[1:2] * scaling_one)
        embedding = time_ref[...].astype(jnp.float32)
        late[place, 6:7, 0:128] = jnp.where(links.me == 0, embedding[0:1], embedding[1:2])
        start_all(spread_copies(links, late, sems, late_slot, 0))
        hop = iter(range(4))

        def hop_on():
            number = next(hop)
            receive_all(spread_copies(links, late, sems, late_slot, number))
            if number < 3:
                start_all(spread_copies(links, late, sems, late_slot, number + 1))

        hop_on()
        early_arrive(3)
        running_arrive(4)
        early_vectors()
        ins[0].last()
        hop_on()
        ins[1].last()
        hop_on()
        ins[2].last()
        hop_on()
        late_vectors()
        for group in range(3):
            def store(at, value, group=group):
                span = 128 * CHUNKS[group]
                for part in range(3):
                    column = part * model + starts[group]
                    in_ref[at, column : column + span] = value[:, part * span : (part + 1) * span]

            ins[group].result(store)

        def store_out(at, value):
            out_grad_ref[at] = value

        out.result(store_out)

        def store_down(at, value):
            down_ref[at] = value

        down.result(store_down)

        def store_up(first):
            def store(at, value):
                count = up_ref.shape[0]
                for tile in range(value.shape[0] // count):
                    columns = slice((first + tile) * model, (first + tile + 1) * model)
                    up_ref[:, columns] = value[tile * count : (tile + 1) * count]

            return store

        upv.result(store_up(0))
        upx.result(store_up(3))
        home().wait()
        for chunk in range(half // rows):
            away(chunk).wait()
        for number in range(4):
            block_copy(number).wait()
        for number in range(4):
            for copy in spread_copies(links, early, sems, early_slot, number) + spread_copies(links, late, sems, late_slot, number):
                copy.wait_send()
        for number in range(5):
            running_copy(number).wait_send()
        tail_copy().wait_send()
        for piece in pieces:
            for copy in piece.copies:
                remote(*copy).wait_send()


def close_kernel(*refs):
    count = len(refs) // 2
    for source, target in zip(refs[:count], refs[count:]):
        target[...] = source[...].reshape(target.shape)


def turn_tables(length):
    inverse = 10000.0 ** (-np.arange(HD // 2, dtype=np.float64) * 2.0 / HD)
    angles = np.arange(length, dtype=np.float64)[:, None] * inverse[None, :]
    cosine = np.tile(np.cos(angles), (1, 4))
    sines = np.sin(angles)
    sines = np.concatenate([-sines, sines, -sines, sines], 1)
    both = [np.stack([t, np.roll(t, -(length // 2), 0)]).astype(np.float32) for t in (cosine, sines)]
    return jnp.asarray(both[0]), jnp.asarray(both[1])


def fast_body(
    tokens,
    time_embedding,
    prefix_length,
    suffix_mask,
    cotangent,
    modulation_weight,
    modulation_bias,
    attention_gain,
    attention_in,
    attention_out,
    feed_gain,
    feed_up,
    feed_up_bias,
    feed_down,
    feed_down_bias,
):
    bf16 = jnp.bfloat16
    f32 = jnp.float32
    _, half, model = tokens.shape
    length = 2 * half
    hidden_width = feed_up.shape[1]
    size = lax.axis_size("dp")
    shape = jax.ShapeDtypeStruct

    packed = [modulation_bias, attention_gain, feed_gain, feed_down_bias, feed_up_bias]
    total = sum(v.shape[0] for v in packed)
    starts = np.cumsum([0] + [v.shape[0] for v in packed])
    packed = sum(
        lax.pad(v.astype(f32), np.float32(0), [(int(a), int(total - a - v.shape[0]), 0)]) for v, a in zip(packed, starts)
    )[None]

    def packed_at(number):
        return pl.BlockSpec((1, model), lambda h: (0, number), pipeline_mode=pl.Buffered(1))

    cosine, sines = turn_tables(length)
    anywhere = pl.BlockSpec(memory_space=pl.ANY)

    def fixed(*dims):
        return pl.BlockSpec(dims, lambda h: (0,) * len(dims), pipeline_mode=pl.Buffered(1))

    first_t, qkv, other, modulation = pl.pallas_call(
        front_kernel,
        grid=(1,),
        in_specs=[
            anywhere,
            fixed(2, 128),
            anywhere,
            fixed(1, 6 * model),
            packed_at(6),
            anywhere,
            anywhere,
            anywhere,
        ],
        out_specs=[fixed(model, length), anywhere, anywhere, fixed(6, model)],
        out_shape=[
            shape((model, length), bf16),
            shape((length, 3 * model), bf16),
            shape((half, model), bf16),
            shape((6, model), f32),
        ],
        scratch_shapes=[
            pltpu.VMEM((half, model), bf16),
            pltpu.VMEM((half, model), bf16),
            pltpu.VMEM((6 * model, 128), bf16),
            pltpu.VMEM((model, 3 * model), bf16),
            pltpu.VMEM((length, 128), f32),
            pltpu.VMEM((length, 128), f32),
            pltpu.VMEM((length, 3 * model), bf16),
            pltpu.SemaphoreType.DMA((2, half // FRONT_ROWS)),
            pltpu.SemaphoreType.DMA((5,)),
            pltpu.SemaphoreType.DMA((3 * half // FRONT_ROWS,)),
        ],
        compiler_params=pltpu.CompilerParams(vmem_limit_bytes=62 * MIB, collective_id=2, has_side_effects=True),
        cost_estimate=pl.CostEstimate(flops=2 * length * model * 3 * model, bytes_accessed=16 * MIB, transcendentals=0),
        name="front",
    )(tokens, time_embedding, modulation_weight, packed, packed, attention_in, cosine, sines)

    def column(k):
        return pl.BlockSpec((length, 128), lambda h: (0, h + k))

    pairs = model // 128
    attended, exps, inverses, own_live, other_live, other_cot = pl.pallas_call(
        attend_kernel,
        grid=(pairs,),
        in_specs=[
            pl.BlockSpec(memory_space=pltpu.SMEM),
            column(0),
            column(pairs),
            column(2 * pairs),
            fixed(2, half),
            anywhere,
        ],
        out_specs=[
            column(0),
            pl.BlockSpec((2, length, length), lambda h: (h, 0, 0)),
            column(0),
            fixed(8, half),
            fixed(8, half),
            anywhere,
        ],
        out_shape=[
            shape((length, model), bf16),
            shape((HEADS, length, length), bf16),
            shape((length, model), f32),
            shape((8, half), f32),
            shape((8, half), f32),
            shape((half, model), bf16),
        ],
        scratch_shapes=[pltpu.VMEM((8, half), f32), pltpu.VMEM((8, half), f32), pltpu.SemaphoreType.DMA((2, 2))],
        compiler_params=pltpu.CompilerParams(vmem_limit_bytes=60 * MIB, collective_id=3, has_side_effects=True),
        cost_estimate=pl.CostEstimate(flops=16 * length * length * model, bytes_accessed=32 * MIB, transcendentals=0),
        name="attend",
    )(prefix_length, qkv, qkv, qkv, suffix_mask, cotangent)

    tiles = 4
    width = hidden_width // tiles
    groups = size // 2
    share_rows = hidden_width // size
    model_rows = model // size
    own_part = pl.BlockSpec((None, half, model), lambda h: (lax.axis_index("seq"), 0, 0), pipeline_mode=pl.Buffered(1))
    up_tile = pl.BlockSpec((model, width), lambda j: (0, j))
    bias_tile = pl.BlockSpec((1, width), lambda j: (0, j))
    down_tile = pl.BlockSpec((width, model), lambda j: (j, 0))
    (
        own_out,
        other_out,
        grad_middle,
        grad_attended,
        mid_rows,
        up_bias_grad,
        down_sum,
        down_tail,
        upv_sum,
        upx_sum,
        out_keep,
        out_send,
    ) = pl.pallas_call(
        middle_kernel,
        grid=(tiles,),
        in_specs=[own_part, fixed(half, model), own_part, fixed(half, model), fixed(8, half), fixed(8, half)]
        + [
            fixed(length, model),
            fixed(6, model),
            packed_at(7),
            fixed(model, model),
            up_tile,
            pl.BlockSpec((1, width), lambda j: (0, j + 9)),
            down_tile,
            packed_at(8),
        ],
        out_specs=[
            own_part,
            fixed(half, model),
            fixed(length, model),
            fixed(length, model),
            fixed(6, model),
            bias_tile,
            fixed(tiles - 1, share_rows // 2, model),
            fixed(2, share_rows // 2, model),
            fixed(2, tiles - 1, model_rows, model),
            fixed(4, model_rows, model),
            fixed(groups, model_rows, model),
            fixed(groups, model_rows, model),
        ],
        out_shape=[shape((2, half, model), bf16), shape((half, model), bf16)]
        + [shape((length, model), f32), shape((length, model), bf16), shape((6, model), f32), shape((1, hidden_width), f32)]
        + [shape((tiles - 1, share_rows // 2, model), bf16), shape((2, share_rows // 2, model), bf16), shape((2, tiles - 1, model_rows, model), bf16)]
        + [shape((4, model_rows, model), bf16)]
        + [shape((groups, model_rows, model), bf16)] * 2,
        scratch_shapes=[
            pltpu.VMEM((model, length), bf16),
            pltpu.VMEM((length, model), bf16),
            pltpu.VMEM((length, model), f32),
            pltpu.VMEM((length, model), f32),
            pltpu.VMEM((width, length), bf16),
        ]
        + [pltpu.VMEM((tiles, groups // tiles, share_rows, model), bf16)] * 3
        + [pltpu.VMEM((tiles, groups, model_rows, model), bf16)] * 3
        + [pltpu.VMEM((tiles, groups // tiles, share_rows // 2, model), bf16)] * 2
        + [pltpu.VMEM((tiles - 1, share_rows // 2, model), bf16)] * 2
        + [pltpu.VMEM((tiles - 1, 3, 2, model_rows, model), bf16)] * 2
        + [pltpu.VMEM((4, model_rows, model), bf16)] * 2
        + [pltpu.SemaphoreType.DMA((2, 7 * tiles))],
        compiler_params=pltpu.CompilerParams(vmem_limit_bytes=63 * MIB, collective_id=1, has_side_effects=True),
        cost_estimate=pl.CostEstimate(
            flops=12 * length * model * hidden_width + 6 * length * model * model, bytes_accessed=36 * MIB, transcendentals=0
        ),
        name="middle",
    )(
        tokens,
        other,
        cotangent,
        other_cot,
        own_live,
        other_live,
        attended,
        modulation,
        packed,
        attention_out,
        feed_up,
        packed,
        feed_down,
        packed,
    )
    merge = (2, (tiles - 1) * model_rows, model)

    def near(k):
        return pl.BlockSpec((length, 128), lambda h: (0, jnp.minimum(h, pairs - 1) + k))

    turn = pl.BlockSpec((None, length, 128), lambda h: (lax.axis_index("seq"), 0, 0), pipeline_mode=pl.Buffered(1))
    scratch = [
        pltpu.VMEM((model, length), bf16),
        pltpu.VMEM((model, 3 * model), bf16),
        pltpu.VMEM((half, model), bf16),
        pltpu.VMEM((half, model), bf16),
        pltpu.VMEM((length, model), f32),
        pltpu.VMEM((6 * model, 128), bf16),
        pltpu.VMEM((2, share_rows // 2, model), bf16),
        pltpu.VMEM((share_rows // 2, model), bf16),
        pltpu.VMEM((share_rows // 2, model), bf16),
        pltpu.VMEM((length, length), bf16),
        pltpu.VMEM((length, 128), f32),
        pltpu.VMEM((length, 3 * model), bf16),
        pltpu.VMEM((length, model), bf16),
        pltpu.VMEM((2, model), f32),
        pltpu.VMEM((2 * size, 8, model // 2), f32),
        pltpu.VMEM((2 * size, 8, model // 2), f32),
        pltpu.VMEM((6, 8, model), f32),
        pltpu.VMEM((5, 8, model), f32),
        pltpu.VMEM((6, 2 * size, model), f32),
        pltpu.VMEM((model, 256), f32),
        pltpu.VMEM((6 * model_rows, 128), f32),
        pltpu.VMEM((model, 8), f32),
        pltpu.SemaphoreType.DMA((2, BACK_COPIES + 24)),
        pltpu.SemaphoreType.DMA((12,)),
    ]
    for spec in BACK_PIECES:
        scratch += piece_scratch(spec)
    def cut(dims):
        if len(dims) == 3:
            return pl.BlockSpec((1, *dims[1:]), lambda i: (i, 0, 0))
        if dims[0] % 16:
            return pl.BlockSpec(dims, lambda i: (0, 0))
        return pl.BlockSpec((dims[0] // 2, dims[1]), lambda i: (i, 0))

    results = pl.pallas_call(
        back_kernel,
        grid=(pairs + 2,),
        in_specs=[
            near(0),
            near(pairs),
            near(2 * pairs),
            near(0),
            near(0),
            pl.BlockSpec((2, length, length), lambda h: (jnp.minimum(h, pairs - 1), 0, 0)),
            near(0),
            turn,
            turn,
            *[anywhere] * 5,
            fixed(6, model),
            packed_at(6),
        ]
        + [anywhere] * 6
        + [fixed(6, model), fixed(1, hidden_width), fixed(2, 128), anywhere, anywhere, anywhere],
        out_specs=[
            anywhere,
            fixed(2, 128),
            fixed(6 * model_rows, 128),
            fixed(1, 6 * model_rows),
            fixed(1, model_rows),
            fixed(1, model_rows),
            fixed(1, hidden_width // size),
            fixed(1, model_rows),
            fixed(hidden_width // size, model),
            fixed(model_rows, hidden_width),
            fixed(model_rows, model),
            fixed(model_rows, 3 * model),
            anywhere,
        ],
        out_shape=[
            shape((2, half, model), bf16),
            shape((2, 128), f32),
            shape((6 * model_rows, 128), f32),
            shape((1, 6 * model_rows), f32),
            shape((1, model_rows), f32),
            shape((1, model_rows), f32),
            shape((1, hidden_width // size), f32),
            shape((1, model_rows), f32),
            shape((hidden_width // size, model), f32),
            shape((model_rows, hidden_width), f32),
            shape((model_rows, model), f32),
            shape((model_rows, 3 * model), f32),
            shape((2, half, model), bf16),
        ],
        input_output_aliases={27: 12},
        scratch_shapes=scratch,
        compiler_params=pltpu.CompilerParams(vmem_limit_bytes=63 * MIB, collective_id=0, has_side_effects=True),
        cost_estimate=pl.CostEstimate(flops=40 * length * length * model, bytes_accessed=60 * MIB, transcendentals=0),
        name="back",
    )(
        qkv,
        qkv,
        qkv,
        attended,
        grad_attended,
        exps,
        inverses,
        cosine,
        sines,
        first_t,
        attention_in,
        tokens,
        other,
        grad_middle,
        modulation,
        packed,
        down_sum,
        down_tail,
        upv_sum.reshape(merge),
        upx_sum,
        out_keep,
        out_send,
        mid_rows,
        up_bias_grad,
        time_embedding,
        modulation_weight,
        other_out,
        own_out,
    )
    (
        tokens_grad,
        time_grad,
        modulation_weight_grad,
        modulation_bias_grad,
        gain_grad,
        feed_gain_grad,
        feed_up_bias_grad,
        feed_down_bias_grad,
        down_grad,
        up_grad,
        out_grad,
        in_grad,
        block_output,
    ) = pl.pallas_call(
        close_kernel,
        grid=(2,),
        in_specs=[cut(r.shape) for r in results],
        out_specs=[pl.BlockSpec(r.shape[1:], lambda i: (0,)) if r.shape[0] == 1 else cut(r.shape) for r in results],
        out_shape=[shape(r.shape[1:] if r.shape[0] == 1 else r.shape, r.dtype) for r in results],
        compiler_params=params(62),
        name="close",
    )(*results)
    return (
        block_output,
        tokens_grad,
        time_grad,
        modulation_weight_grad,
        modulation_bias_grad,
        gain_grad,
        in_grad,
        out_grad,
        feed_gain_grad,
        up_grad,
        feed_up_bias_grad,
        down_grad,
        feed_down_bias_grad,
    )


def body(tokens, *rest):
    sequences, half, model = tokens.shape
    size = lax.axis_size("dp")
    fits = model % (16 * size) == 0 and half % T_ROWS == 0
    fits = fits and tokens.shape[1] % MIDDLE_ROWS == 0 and rest[10].shape[1] == 4 * model and size == 16 and lax.axis_size("seq") == 2 and sequences == 2
    return (fast_body if fits else general_body)(tokens, *rest)


def solution(mesh):
    return jax.shard_map(
        body,
        mesh=mesh,
        in_specs=(
            P("dp", "seq", None),
            P("dp", None),
            P("dp"),
            P("dp", "seq"),
            P("dp", "seq", None),
            P(),
            P(),
            P(),
            P(),
            P(),
            P(),
            P(),
            P(),
            P(),
            P(),
        ),
        out_specs=(
            P("dp", "seq", None),
            P("dp", "seq", None),
            P("dp", None),
            P("dp", None),
            P("dp"),
            P("dp"),
            P("dp", None),
            P("dp", None),
            P("dp"),
            P("dp", None),
            P("dp"),
            P("dp", None),
            P("dp"),
        ),
        check_vma=False,
    )
```

```python
import functools
from functools import partial

import jax
import jax.numpy as jnp
import numpy as np
from jax import lax
from jax.experimental import pallas as pl
from jax.experimental.pallas import tpu as pltpu
from jax.sharding import PartitionSpec as P

HEADS = 12
HD = 64


highest = lax.Precision.HIGHEST


def as_sent(shard):

    def short(part):
        return part.astype(jnp.bfloat16) if part.dtype == jnp.float32 else part

    return jax.tree.map(short, shard)


def normalize(values):
    centre = values - jnp.mean(values, -1, keepdims=True)
    spread = jnp.mean(centre * centre, -1, keepdims=True)
    return centre * lax.rsqrt(spread + 1e-05)


def modulate(values, scaling, shifts, scales):
    return normalize(values) * scaling * (1.0 + scales) + shifts


def rotate(values, cosine, sines, direction):
    halves = values.shape[-1] // 2
    former = values[..., :halves]
    latter = values[..., halves:]
    cosine = cosine[None, :, None, :]
    sines = direction * sines[None, :, None, :]
    return jnp.concatenate([former * cosine - latter * sines, latter * cosine + former * sines], -1)


def attend_forward(stacked):
    query_rows = stacked[:, 0]
    key_rows = stacked[:, 1]
    value_rows = stacked[:, 2]
    length = query_rows.shape[0]
    block_rows = min(512, length)
    pieces = []
    logsums = []
    for offset in range(0, length, block_rows):
        query_block = query_rows[offset : offset + block_rows]
        scores = (
            jnp.einsum("qhd,khd->hqk", query_block, key_rows, preferred_element_type=jnp.float32)
            * 0.125
        )
        largest = jnp.max(scores, -1, keepdims=True)
        exponentials = jnp.exp(scores - largest)
        totals = jnp.sum(exponentials, -1, keepdims=True)
        probability = (exponentials / totals).astype(jnp.bfloat16)
        pieces.append(
            jnp.einsum("hqk,khd->qhd", probability, value_rows, preferred_element_type=jnp.float32)
        )
        logsums.append((largest + jnp.log(totals))[..., 0])
    return (jnp.concatenate(pieces, 0).astype(jnp.bfloat16), jnp.concatenate(logsums, 1))


def attend_backward(operands):
    stacked, grad_attended, logsums = operands
    query_rows = stacked[:, 0]
    key_rows = stacked[:, 1]
    value_rows = stacked[:, 2]
    length = query_rows.shape[0]
    block_rows = min(512, length)
    grad_query = []
    grad_keys = jnp.zeros(key_rows.shape, jnp.float32)
    grad_values = jnp.zeros(value_rows.shape, jnp.float32)
    for offset in range(0, length, block_rows):
        query_block = query_rows[offset : offset + block_rows]
        grad_block = grad_attended[offset : offset + block_rows]
        scores = (
            jnp.einsum("qhd,khd->hqk", query_block, key_rows, preferred_element_type=jnp.float32)
            * 0.125
        )
        probability = jnp.exp(scores - logsums[:, offset : offset + block_rows, None])
        grad_probs = jnp.einsum(
            "qhd,khd->hqk", grad_block, value_rows, preferred_element_type=jnp.float32
        )
        row_dots = jnp.sum(probability * grad_probs, -1, keepdims=True)
        grad_scores = (probability * (grad_probs - row_dots)).astype(jnp.bfloat16)
        grad_query.append(
            (
                jnp.einsum(
                    "hqk,khd->qhd", grad_scores, key_rows, preferred_element_type=jnp.float32
                )
                * 0.125
            ).astype(jnp.bfloat16)
        )
        grad_keys = grad_keys + jnp.einsum(
            "hqk,qhd->khd", grad_scores, query_block, preferred_element_type=jnp.float32
        )
        grad_values = grad_values + jnp.einsum(
            "hqk,qhd->khd",
            probability.astype(jnp.bfloat16),
            grad_block,
            preferred_element_type=jnp.float32,
        )
    return jnp.stack(
        [
            jnp.concatenate(grad_query, 0),
            (grad_keys * 0.125).astype(jnp.bfloat16),
            grad_values.astype(jnp.bfloat16),
        ],
        1,
    )


def general_body(
    tokens,
    time_embedding,
    prefix_length,
    suffix_mask,
    cotangent,
    modulation_weight,
    modulation_bias,
    attention_gain,
    attention_in,
    attention_out,
    feed_gain,
    feed_up,
    feed_up_bias,
    feed_down,
    feed_down_bias,
):
    sequences, local_len, model_width = tokens.shape
    groups = lax.axis_size("seq")
    data_size = lax.axis_size("dp")
    length = local_len * groups
    heads_local = HEADS // groups
    group_width = model_width // groups
    modulation = jnp.einsum(
        "sc,oc->so", time_embedding, modulation_weight, preferred_element_type=jnp.float32
    ) + modulation_bias.astype(jnp.float32)
    shift_one, scale_one, gate_one, shift_two, scale_two, gate_two = [
        portion[:, None, :] for portion in jnp.split(modulation, 6, axis=1)
    ]
    inputs = tokens.astype(jnp.float32)
    first_float, first_back = jax.vjp(
        modulate, inputs, attention_gain.astype(jnp.float32), shift_one, scale_one
    )
    first_input = first_float.astype(jnp.bfloat16)
    projected = jnp.einsum(
        "spd,de->spe", first_input, attention_in, preferred_element_type=jnp.float32
    ).reshape(sequences, local_len, 3, HEADS, HD)
    position_ints = lax.axis_index("seq") * local_len + jnp.arange(local_len, dtype=jnp.int32)
    positions = position_ints.astype(jnp.float32)
    inverse = 10000.0 ** (-jnp.arange(HD // 2, dtype=jnp.float32) * 2.0 / HD)
    angles = positions[:, None] * inverse[None, :]
    cosine = jnp.cos(angles)
    sines = jnp.sin(angles)
    rotated = jnp.stack(
        [
            rotate(projected[:, :, 0], cosine, sines, 1.0),
            rotate(projected[:, :, 1], cosine, sines, 1.0),
            projected[:, :, 2],
        ],
        2,
    ).astype(jnp.bfloat16)
    by_heads = lax.all_to_all(
        rotated.reshape(sequences, local_len, 3, groups, group_width),
        "seq",
        split_axis=3,
        concat_axis=1,
        tiled=True,
    )
    by_heads = by_heads.reshape(sequences, length, 3, heads_local, HD)
    attended_heads, logsums = lax.map(attend_forward, by_heads)
    attended = lax.all_to_all(
        as_sent(attended_heads.reshape(sequences, length, 1, group_width)),
        "seq",
        split_axis=1,
        concat_axis=2,
        tiled=True,
    )
    attended = attended.reshape(sequences, local_len, model_width)
    branch_one = jnp.einsum(
        "spd,de->spe", attended, attention_out, preferred_element_type=jnp.float32
    )
    middle = inputs + gate_one * branch_one
    second_float, second_back = jax.vjp(
        modulate, middle, feed_gain.astype(jnp.float32), shift_two, scale_two
    )
    second_input = second_float.astype(jnp.bfloat16)
    hidden = jnp.einsum(
        "spd,df->spf", second_input, feed_up, preferred_element_type=jnp.float32
    ) + feed_up_bias.astype(jnp.float32)
    activated_float, gelu_back = jax.vjp(partial(jax.nn.gelu, approximate=True), hidden)
    activated = activated_float.astype(jnp.bfloat16)
    branch_two = jnp.einsum(
        "spf,fd->spd", activated, feed_down, preferred_element_type=jnp.float32
    ) + feed_down_bias.astype(jnp.float32)
    block_output = (middle + gate_two * branch_two).astype(jnp.bfloat16)
    live_rows = ((position_ints[None, :] >= prefix_length[:, None]) & (suffix_mask == 1)).astype(
        jnp.float32
    )
    grad_output = cotangent.astype(jnp.float32) * live_rows[:, :, None]
    grad_gate_two = jnp.sum(grad_output * branch_two, axis=1)
    grad_branch_two = (gate_two * grad_output).astype(jnp.bfloat16)
    feed_down_bias_grad = jnp.sum(grad_branch_two.astype(jnp.float32), axis=(0, 1))
    feed_down_grad = jnp.einsum(
        "spf,spd->fd", activated, grad_branch_two, preferred_element_type=jnp.float32
    )
    grad_activated = jnp.einsum(
        "spd,fd->spf", grad_branch_two, feed_down, preferred_element_type=jnp.float32
    )
    grad_hidden = gelu_back(grad_activated)[0].astype(jnp.bfloat16)
    feed_up_bias_grad = jnp.sum(grad_hidden.astype(jnp.float32), axis=(0, 1))
    feed_up_grad = jnp.einsum(
        "spd,spf->df", second_input, grad_hidden, preferred_element_type=jnp.float32
    )
    grad_second = jnp.einsum(
        "spf,df->spd", grad_hidden, feed_up, preferred_element_type=jnp.float32
    )
    grad_from_norm, feed_gain_grad, grad_shift_two, grad_scale_two = second_back(grad_second)
    grad_middle = grad_output + grad_from_norm
    grad_gate_one = jnp.sum(grad_middle * branch_one, axis=1)
    grad_branch_one = (gate_one * grad_middle).astype(jnp.bfloat16)
    attention_out_grad = jnp.einsum(
        "spd,spe->de", attended, grad_branch_one, preferred_element_type=jnp.float32
    )
    grad_attended = jnp.einsum(
        "spe,de->spd", grad_branch_one, attention_out, preferred_element_type=jnp.float32
    ).astype(jnp.bfloat16)
    grad_heads = lax.all_to_all(
        grad_attended.reshape(sequences, local_len, groups, group_width),
        "seq",
        split_axis=2,
        concat_axis=1,
        tiled=True,
    )
    grad_heads = grad_heads.reshape(sequences, length, heads_local, HD)
    grad_stacked = lax.map(attend_backward, (by_heads, grad_heads, logsums))
    grad_positions = lax.all_to_all(
        as_sent(grad_stacked.reshape(sequences, length, 3, 1, group_width)),
        "seq",
        split_axis=1,
        concat_axis=3,
        tiled=True,
    )
    grad_positions = grad_positions.reshape(sequences, local_len, 3, HEADS, HD).astype(jnp.float32)
    grad_projected = jnp.stack(
        [
            rotate(grad_positions[:, :, 0], cosine, sines, -1.0),
            rotate(grad_positions[:, :, 1], cosine, sines, -1.0),
            grad_positions[:, :, 2],
        ],
        2,
    ).astype(jnp.bfloat16)
    grad_projected = grad_projected.reshape(sequences, local_len, 3 * model_width)
    attention_in_grad = jnp.einsum(
        "spd,spe->de", first_input, grad_projected, preferred_element_type=jnp.float32
    )
    grad_first = jnp.einsum(
        "spe,de->spd", grad_projected, attention_in, preferred_element_type=jnp.float32
    )
    grad_tokens_norm, attention_gain_grad, grad_shift_one, grad_scale_one = first_back(grad_first)
    tokens_grad = (grad_middle + grad_tokens_norm).astype(jnp.bfloat16)
    grad_modulation = jnp.concatenate(
        [
            grad_shift_one[:, 0],
            grad_scale_one[:, 0],
            grad_gate_one,
            grad_shift_two[:, 0],
            grad_scale_two[:, 0],
            grad_gate_two,
        ],
        1,
    )
    modulation_total = lax.psum(grad_modulation.astype(jnp.bfloat16), "seq").astype(jnp.float32)
    time_grad = jnp.einsum(
        "so,oc->sc", modulation_total, modulation_weight.astype(jnp.float32), precision=highest
    )
    modulation_weight_grad = jnp.einsum(
        "so,sc->oc", grad_modulation, time_embedding.astype(jnp.float32), precision=highest
    )
    modulation_bias_grad = jnp.sum(grad_modulation, axis=0)
    gradients = (
        modulation_weight_grad,
        modulation_bias_grad,
        attention_gain_grad,
        attention_in_grad,
        attention_out_grad,
        feed_gain_grad,
        feed_up_grad,
        feed_up_bias_grad,
        feed_down_grad,
        feed_down_bias_grad,
    )
    flattened = tuple((g.reshape(data_size, -1) for g in gradients))
    shares = lax.psum_scatter(flattened, "dp", scatter_dimension=0, tiled=True)
    summed = jax.tree.map(lambda part: part.astype(jnp.float32), lax.psum(as_sent(shares), "seq"))
    shards = tuple(
        (s.reshape((g.shape[0] // data_size,) + g.shape[1:]) for s, g in zip(summed, gradients))
    )
    return (
        block_output,
        tokens_grad,
        time_grad,
        shards[0],
        shards[1],
        shards[2],
        shards[3],
        shards[4],
        shards[5],
        shards[6],
        shards[7],
        shards[8],
        shards[9],
    )


T_ROWS = 256
FRONT_ROWS = 128
MIDDLE_ROWS = 256
MIB = 1 << 20


def dot(a, b, ca, cb):
    return lax.dot_general(a, b, (((ca,), (cb,)), ((), ())), preferred_element_type=jnp.float32)


def params(limit=60):
    return pltpu.CompilerParams(vmem_limit_bytes=limit * MIB)


def norm_rows(values):
    centre = values - jnp.mean(values, -1, keepdims=True)
    inverse = lax.rsqrt(jnp.mean(centre * centre, -1, keepdims=True) + 1e-05)
    return centre * inverse, inverse


def swap_halves(values, lane):
    left = pltpu.roll(values, 96, 1)
    right = pltpu.roll(values, 32, 1)
    return jnp.where(lane % 64 < 32, left, right)


def attend_kernel(
    prefix_ref,
    q_ref,
    k_ref,
    v_ref,
    mask_ref,
    cot_hbm,
    out_ref,
    exp_ref,
    inv_ref,
    own_live_ref,
    other_live_ref,
    other_cot_hbm,
    give,
    got,
    sems,
):
    rows = 128
    step = pl.program_id(0)
    links = Links()
    half = mask_ref.shape[1]
    partner = links.partner["Y"]

    def exchanges():
        return [
            remote(give, got, sems, 0, partner),
            remote(cot_hbm.at[1 - links.me], other_cot_hbm, sems, 1, partner),
        ]

    @pl.when(step == 0)
    def _():
        position = links.me * half + lax.broadcasted_iota(jnp.int32, (1, half), 1)
        live = [
            jnp.where((position >= prefix_ref[i]) & (mask_ref[i : i + 1] == 1), 1.0, 0.0) for i in range(2)
        ]
        wide = [jnp.broadcast_to(row, (8, half)) for row in live]
        own_live_ref[...] = jnp.where(links.me == 0, wide[0], wide[1])
        give[...] = jnp.where(links.me == 0, wide[1], wide[0])
        links.greet(("Y",))
        start_all(exchanges())

    length = q_ref.shape[0]
    lane = lax.broadcasted_iota(jnp.int32, (rows, 128), 1)
    keys = k_ref[...]
    values = jnp.concatenate([v_ref[...], jnp.ones((length, 128), jnp.bfloat16)], 1)
    for chunk in range(length // rows):
        at = slice(chunk * rows, (chunk + 1) * rows)
        queries = q_ref[at]
        outs = []
        inverses = []
        for head in range(2):
            mine = jnp.where((lane < 64) == (head == 0), queries, jnp.zeros_like(queries))
            scores = dot(mine, keys, 1, 1)
            largest = jnp.max(scores, -1, keepdims=True)
            exps = jnp.exp(scores - largest).astype(jnp.bfloat16)
            exp_ref[head, at] = exps
            summed = dot(exps, values, 1, 0)
            inverse = 1.0 / summed[:, 128:256]
            outs.append(summed[:, 0:128] * inverse)
            inverses.append(inverse)
        out_ref[at] = jnp.where(lane < 64, outs[0], outs[1]).astype(jnp.bfloat16)
        inv_ref[at] = jnp.where(lane < 64, inverses[0], inverses[1])

    @pl.when(step == pl.num_programs(0) - 1)
    def _():
        for copy in exchanges():
            copy.wait()
        other_live_ref[...] = got[...]


def share(core, grad, keep_ref, send_ref, *at):
    first, second = grad
    keep_ref[at] = jnp.where(core == 0, first, second)
    send_ref[at] = jnp.where(core == 0, second, first)


def middle_kernel(
    own_ref,
    other_ref,
    own_cot_ref,
    other_cot_ref,
    own_live_ref,
    other_live_ref,
    attended_ref,
    mod_ref,
    gain_ref,
    out_weight_ref,
    up_ref,
    up_bias_ref,
    down_ref,
    down_bias_ref,
    own_out_ref,
    other_out_ref,
    grad_middle_ref,
    grad_attended_ref,
    rows_ref,
    up_bias_grad_ref,
    down_sum_ref,
    down_tail_ref,
    upv_sum_ref,
    upx_sum_ref,
    out_keep_ref,
    out_send_ref,
    second_t,
    grad_two,
    sum_two,
    sum_second,
    act_t,
    down_keep,
    down_give,
    down_got,
    up_keep,
    up_give,
    up_got,
    down_half,
    down_half_got,
    down_part,
    down_part_got,
    up_part,
    up_part_got,
    up_half,
    up_half_got,
    sems,
):
    rows = MIDDLE_ROWS
    step = pl.program_id(0)
    links = Links()
    core = links.bit["C"]
    tiles = down_keep.shape[0]

    per_tile = 7
    last = tiles - 1

    def first_copies(tile):
        return [
            remote(give.at[tile], got.at[tile], sems, tile * per_tile + i, links.partner["C"])
            for i, (give, got) in enumerate(((down_give, down_got), (up_give, up_got)))
        ]

    def down_copy(tile):
        return remote(down_half.at[tile], down_half_got.at[tile], sems, tile * per_tile + 2, links.partner["Y"])

    def down_on_copy(tile):
        return remote(down_part.at[tile], down_part_got.at[tile], sems, tile * per_tile + 3, links.partner["X"])

    def up_copies(tile):
        return [
            remote(up_part.at[tile, i], up_part_got.at[tile, i], sems, tile * per_tile + 4 + i, links.partner[flip])
            for i, flip in enumerate(Z_FLIPS)
        ]

    def up_last_copy():
        return remote(up_half, up_half_got, sems, last * per_tile + 4, links.partner["X"])

    def total(*terms):
        return sum(term.astype(jnp.float32) for term in terms).astype(jnp.bfloat16)

    half_rows = down_half.shape[2]
    home = pl.ds(pl.multiple_of(links.me * half_rows, 16), half_rows)
    away = pl.ds(pl.multiple_of((1 - links.me) * half_rows, 16), half_rows)
    z_at = links.bit["W"] * 2 + links.bit["Z"]

    def flipped(flip):
        values = {bit: 1 - links.bit[bit] if bit in flip else links.bit[bit] for bit in "WZ"}
        return values["W"] * 2 + values["Z"]

    def send_on(tile, final):
        for copy in first_copies(tile):
            copy.wait_recv()
        for x in range(2):
            down_half[tile, x] = total(down_keep[tile, x, away], down_got[tile, x, away])
        down_copy(tile).start()
        if final:
            for z in range(4):
                other = 2 * z + 1 - links.bit["X"]
                up_half[z] = total(up_keep[tile, other], up_got[tile, other])
            up_last_copy().start()
        else:
            for i, flip in enumerate(Z_FLIPS):
                for x in range(2):
                    other = 2 * flipped(flip) + x
                    up_part[tile, i, x] = total(up_keep[tile, other], up_got[tile, other])
            for copy in up_copies(tile):
                copy.start()

    def send_down(tile):
        down_copy(tile).wait_recv()
        x = 1 - links.bit["X"]
        down_part[tile] = total(down_keep[tile, x, home], down_got[tile, x, home], down_half_got[tile, x])
        down_on_copy(tile).start()

    def settle(tile, final):
        if final:
            down_copy(tile).wait_recv()
            for x in range(2):
                down_tail_ref[x] = total(down_keep[tile, x, home], down_got[tile, x, home], down_half_got[tile, x])
        else:
            down_on_copy(tile).wait_recv()
            x = links.bit["X"]
            terms = (down_keep[tile, x, home], down_got[tile, x, home], down_half_got[tile, x], down_part_got[tile])
            down_sum_ref[tile] = total(*terms)
        if final:
            up_last_copy().wait_recv()
            for z in range(4):
                mine = 2 * z + links.bit["X"]
                upx_sum_ref[z] = total(up_keep[tile, mine], up_got[tile, mine], up_half_got[z])
        else:
            for copy in up_copies(tile):
                copy.wait_recv()
            for x in range(2):
                mine = 2 * z_at + x
                got = [up_part_got[tile, i, x] for i in range(3)]
                upv_sum_ref[x, tile] = total(up_keep[tile, mine], up_got[tile, mine], *got)

    @pl.when(step == 0)
    def _():
        links.greet()

    half, model = own_ref.shape
    length = 2 * half
    scaling = gain_ref[...] * (1.0 + mod_ref[4:5])
    gate_one = mod_ref[2:3]
    shift_two = mod_ref[3:4]
    gate_two = mod_ref[5:6]

    def pick(first_ref, second_ref, chunk):
        at = chunk * rows
        return (first_ref if at < half else second_ref)[at % half : at % half + rows]

    def live_cot(chunk):
        at = (chunk * rows) % half
        live = (own_live_ref if chunk * rows < half else other_live_ref)[...].T[at : at + rows, 0:1]
        return pick(own_cot_ref, other_cot_ref, chunk).astype(jnp.float32) * live

    @pl.when(step == 0)
    def _():
        bias_grad = jnp.zeros((1, model), jnp.float32)
        for chunk in range(length // rows):
            at = slice(chunk * rows, (chunk + 1) * rows)
            branch = dot(attended_ref[at], out_weight_ref[...], 1, 0)
            grad_middle_ref[at] = branch
            sum_two[at] = jnp.zeros((rows, model), jnp.float32)
            sum_second[at] = jnp.zeros((rows, model), jnp.float32)
            middle = pick(own_ref, other_ref, chunk).astype(jnp.float32) + gate_one * branch
            normed, _ = norm_rows(middle)
            rounded = (normed * scaling + shift_two).astype(jnp.bfloat16)
            place = (chunk * rows) % half
            (own_out_ref if chunk * rows < half else other_out_ref)[place : place + rows] = rounded
            second_t[:, at] = rounded.T
            grad = (gate_two * live_cot(chunk)).astype(jnp.bfloat16)
            grad_two[at] = grad
            bias_grad = bias_grad + jnp.sum(grad.astype(jnp.float32), 0, keepdims=True)
        rows_ref[5:6] = bias_grad

    up = up_ref[...]
    down = down_ref[...]
    width = up.shape[1]
    bias_sum = jnp.zeros((1, width), jnp.float32)
    for chunk in range(length // rows):
        if chunk == 1:

            @pl.when(step > 0)
            def _():
                send_on(step - 1, False)

            @pl.when(step > 1)
            def _():
                send_down(step - 2)

        at = slice(chunk * rows, (chunk + 1) * rows)
        hidden = dot(pick(own_out_ref, other_out_ref, chunk), up, 1, 0) + up_bias_ref[...]
        squared = hidden * hidden
        tanh = jnp.tanh(hidden * (0.7978845608028654 + 0.035677408136300125 * squared))
        gate = 0.5 + 0.5 * tanh
        activated = (hidden * gate).astype(jnp.bfloat16)
        slope = gate + (0.5 * hidden) * (1.0 - tanh * tanh) * (0.7978845608028654 + 0.10703222440890037 * squared)
        act_t[:, at] = activated.T
        grad = (slope * dot(grad_two[at], down, 1, 1)).astype(jnp.bfloat16)
        grad_attended_ref[at] = grad
        bias_sum = bias_sum + jnp.sum(grad.astype(jnp.float32), 0, keepdims=True)
        sum_two[at] += dot(activated, down, 1, 0)
        sum_second[at] += dot(grad, up, 1, 1)

    up_bias_grad_ref[...] = bias_sum
    down_grad = dot(act_t[...], grad_two[...], 1, 0).astype(jnp.bfloat16).reshape(2, 2, -1, model)
    share(core, (down_grad[:, 0], down_grad[:, 1]), down_keep, down_give, step)
    up_grad = dot(second_t[...], grad_attended_ref[...], 1, 0).astype(jnp.bfloat16).reshape(up_keep.shape[1], 2, -1, width)
    share(core, (up_grad[:, 0], up_grad[:, 1]), up_keep, up_give, step)
    for copy in first_copies(step):
        copy.start()

    @pl.when(step == pl.num_programs(0) - 1)
    def _():
        sums = [jnp.zeros((1, model), jnp.float32) for _ in range(4)]
        for chunk in range(length // rows):
            at = slice(chunk * rows, (chunk + 1) * rows)
            branch = grad_middle_ref[at]
            middle = pick(own_ref, other_ref, chunk).astype(jnp.float32) + gate_one * branch
            normed, inverse = norm_rows(middle)
            branch_two = sum_two[at] + down_bias_ref[...]
            output = (middle + gate_two * branch_two).astype(jnp.bfloat16)
            place = (chunk * rows) % half
            (own_out_ref if chunk * rows < half else other_out_ref)[place : place + rows] = output
            cot = live_cot(chunk)
            grad = sum_second[at]
            weighted = grad * normed
            scaled = grad * scaling
            inner = jnp.mean(weighted * scaling, -1, keepdims=True)
            grad_middle = cot + (scaled - jnp.mean(scaled, -1, keepdims=True) - normed * inner) * inverse
            grad_middle_ref[at] = grad_middle
            grad_one = (gate_one * grad_middle).astype(jnp.bfloat16)
            grad_two[at] = grad_one
            act_t[:, at] = attended_ref[at].T
            grad_attended_ref[at] = dot(grad_one, out_weight_ref[...], 1, 1).astype(jnp.bfloat16)
            for i, term in enumerate((grad_middle * branch, grad, weighted, cot * branch_two)):
                sums[i] = sums[i] + jnp.sum(term, 0, keepdims=True)
            if chunk == 0:
                send_on(last, True)
                send_down(last - 1)
        rows_ref[0:1] = sums[0]
        rows_ref[1:2] = sums[1]
        rows_ref[2:3] = sums[2] * gain_ref[...]
        rows_ref[3:4] = sums[3]
        rows_ref[4:5] = sums[2] * (1.0 + mod_ref[4:5])
        out_grad = dot(act_t[...], grad_two[...], 1, 0).astype(jnp.bfloat16)
        out_grad = out_grad.reshape(out_keep_ref.shape[0], 2, -1, model)
        share(core, (out_grad[:, 0], out_grad[:, 1]), out_keep_ref, out_send_ref, Ellipsis)
        for tile in range(last):
            settle(tile, False)
        settle(last, True)
        for tile in range(tiles):
            ups = [up_last_copy()] if tile == last else up_copies(tile)
            for copy in first_copies(tile) + [down_copy(tile)] + ([] if tile == last else [down_on_copy(tile)]) + ups:
                copy.wait_send()


Z_FLIPS = ("Z", "W", "ZW")


class Links:
    def __init__(self):
        dp = lax.axis_index("dp")
        self.me = lax.axis_index("seq")
        self.bit = {"C": dp % 2, "X": (dp // 2) % 2, "Z": (dp // 4) % 2, "W": (dp // 8) % 2, "Y": self.me}
        jump = {name: size * (1 - 2 * self.bit[name]) for name, size in (("C", 1), ("X", 2), ("Z", 4), ("W", 8))}
        self.partner = {name: (dp + jump[name], self.me) for name in "CXZW"}
        self.partner["ZW"] = (dp + jump["Z"] + jump["W"], self.me)
        self.partner["Y"] = (dp, 1 - self.me)

    def place(self):
        return self.me * 16 + self.bit["X"] * 8 + self.bit["W"] * 4 + self.bit["Z"] * 2 + self.bit["C"]

    def greet(self, names=("C", "X", "Z", "W", "ZW", "Y")):
        barrier = pltpu.get_barrier_semaphore()
        for name in names:
            device = self.partner[name]
            pl.semaphore_signal(barrier, inc=1, device_id=device, device_id_type=pl.DeviceIdType.MESH)
        pl.semaphore_wait(barrier, len(names))


def flips_of(kind):
    return Z_FLIPS if kind == "V" else (kind,)


def remote(source, target, sems, slot, device):
    return pltpu.make_async_remote_copy(
        src_ref=source,
        dst_ref=target,
        send_sem=sems.at[0, slot],
        recv_sem=sems.at[1, slot],
        device_id=device,
        device_id_type=pl.DeviceIdType.MESH,
    )


def piece_scratch(spec):
    _, rows, width, left, order, kind = spec
    count = 1 << len(left)
    shapes = [count] * (1 + ("summed", "given", "made").index(kind))
    for step in order:
        count //= 4 if step == "V" else 2
        shapes += [count * len(flips_of(step))] * 2
    shapes += [1] * 2
    return [pltpu.VMEM((c, rows, width), jnp.bfloat16) for c in shapes]


class Piece:
    def __init__(self, links, refs, spec, sems, slot, source=None, split=False):
        refs = list(refs)
        _, _, _, left, order, kind = spec
        self.links = links
        self.sems = sems
        self.slot = slot
        self.order = list(order)
        self.split = split
        self.left = list(left)
        self.keep = refs.pop(0)
        self.terms = [(self.keep, list(self.left))]
        self.copies = []
        self.flying = []
        if kind != "summed":
            first = refs.pop(0)
            self.source = refs.pop(0) if kind == "made" else source
            copy = (self.source, first, sems, slot, links.partner["C"])
            self.slot += 1
            self.copies.append(copy)
            self.flying = [(copy, first, list(self.left))]
        self.buffers = refs

    def launch(self, source, target, flip):
        copy = (source, target, self.sems, self.slot, self.links.partner[flip])
        self.slot += 1
        remote(*copy).start()
        self.copies.append(copy)
        self.flying.append((copy, target, list(self.left)))

    def begin(self):
        remote(*self.copies[0]).start()

    def arrive(self):
        for copy, target, bits in self.flying:
            remote(*copy).wait_recv()
            self.terms.append((target, bits))
        self.flying = []

    def index(self, bits, values):
        at = 0
        for bit in bits:
            at = at * 2 + values[bit]
        return at

    def add(self, out, flip):
        links = self.links
        rows = out.shape[1]
        block = 48
        for combo in range(1 << len(self.left)):
            values = dict(links.bit)
            for bit in flip:
                values[bit] = 1 - links.bit[bit]
            for place, bit in enumerate(self.left):
                values[bit] = (combo >> (len(self.left) - 1 - place)) & 1
            indices = [self.index(bits, values) for _, bits in self.terms]

            def some(i, carry, indices=indices, combo=combo):
                at = pl.ds(pl.multiple_of(i * block, 16), block)
                total = None
                for (ref, _), index in zip(self.terms, indices):
                    term = ref[index, at, :].astype(jnp.float32)
                    total = term if total is None else total + term
                out[combo, at, :] = total.astype(jnp.bfloat16)
                return carry

            lax.fori_loop(0, rows // block, some, 0)

    def step(self):
        self.arrive()
        kind = self.order.pop(0)
        out, target = self.buffers.pop(0), self.buffers.pop(0)
        for bit in "WZ" if kind == "V" else kind:
            self.left.remove(bit)
        count = 1 << len(self.left)
        for i, flip in enumerate(flips_of(kind)):
            part = pl.ds(i * count, count)
            self.add(out.at[part], flip)
            self.launch(out.at[part], target.at[part], flip)

    def last(self):
        self.arrive()
        self.total, self.got = self.buffers.pop(0), self.buffers.pop(0)
        self.add(self.total, "")
        self.launch(self.total, self.got, "Y")

    def result(self, store):
        remote(*self.flying[0][0]).wait_recv()
        rows = self.total.shape[1]
        total = self.total[0].astype(jnp.float32)
        got = self.got[0].astype(jnp.float32)
        if self.split:
            store(pl.ds(pl.multiple_of(self.links.me * rows, 8), rows), total)
            store(pl.ds(pl.multiple_of((1 - self.links.me) * rows, 8), rows), got)
        else:
            store(slice(0, rows), total + got)


CHUNKS = (3, 2, 1)
BACK_PIECES = (
    ("down", 96, 768, "WZ", "V", "summed"),
    ("upv", 144, 768, "X", "X", "summed"),
    ("upx", 48, 768, "WZ", "V", "summed"),
    ("out", 48, 768, "WZX", "XV", "given"),
    *((f"in{i}", 48, 384 * pairs, "WZX", "XV", "made") for i, pairs in enumerate(CHUNKS)),
)


def copies_of(spec):
    return sum(len(flips_of(kind)) for kind in spec[4]) + 1 + (spec[5] != "summed")


BACK_COPIES = sum(copies_of(spec) for spec in BACK_PIECES)
HOPS = (("C",), Z_FLIPS, ("X",), ("Y",))
RUNNING = "CXZWY"


def spread_copies(links, array, sems, slot, number):
    place = links.place()
    have = (1, 2, 8, 16)[number]
    part = array.at[pl.ds((place // have) * have, have)]
    slot += (0, 1, 4, 5)[number]
    return [remote(part, part, sems, slot + i, links.partner[flip]) for i, flip in enumerate(HOPS[number])]


def start_all(copies):
    for copy in copies:
        copy.start()


def receive_all(copies):
    for copy in copies:
        copy.wait_recv()


def front_kernel(
    tokens_hbm,
    time_ref,
    mod_weight_hbm,
    mod_bias_ref,
    gain_ref,
    weight_hbm,
    cos_hbm,
    sin_hbm,
    first_t_ref,
    qkv_hbm,
    other_hbm,
    mod_ref,
    other_ref,
    own,
    mod_weight,
    weight,
    cos_ref,
    sin_ref,
    qkv,
    sems,
    local_sems,
    store_sems,
):
    rows = FRONT_ROWS
    half, model = own.shape
    blocks = half // rows
    links = Links()

    def exchange(block):
        at = pl.ds(block * rows, rows)
        return remote(tokens_hbm.at[1 - links.me, at], other_ref.at[at], sems, block, links.partner["Y"])

    def fetches():
        pairs = (
            (mod_weight_hbm, mod_weight),
            (tokens_hbm.at[links.me], own),
            (weight_hbm, weight),
            (cos_hbm.at[links.me], cos_ref),
            (sin_hbm.at[links.me], sin_ref),
        )
        return [pltpu.make_async_copy(a, b, local_sems.at[i]) for i, (a, b) in enumerate(pairs)]

    def store(block):
        at = pl.ds(block * rows, rows)
        return pltpu.make_async_copy(qkv.at[at], qkv_hbm.at[at], store_sems.at[block])

    def store_other(block):
        at = pl.ds(block * rows, rows)
        return pltpu.make_async_copy(other_ref.at[at], other_hbm.at[at], store_sems.at[2 * blocks + block])

    for copy in fetches():
        copy.start()
    links.greet(("Y",))
    for block in range(blocks):
        exchange(block).start()
    for copy in fetches():
        copy.wait()
    embedding = time_ref[...].astype(jnp.float32)
    embedding = jnp.where(links.me == 0, embedding[0:1], embedding[1:2])
    embedding = jnp.broadcast_to(embedding, (16, embedding.shape[1])).astype(jnp.bfloat16)
    modulation = dot(embedding, mod_weight[...], 1, 1)[0:1] + mod_bias_ref[...].astype(jnp.float32)
    parts = [modulation[:, i * model : (i + 1) * model] for i in range(6)]
    for i in range(6):
        mod_ref[i : i + 1] = parts[i]
    lane = lax.broadcasted_iota(jnp.int32, (rows, 128), 1)
    scaling = gain_ref[...].astype(jnp.float32) * (1.0 + parts[1])
    for block in range(2 * blocks):
        if block < blocks:
            source = own[block * rows : (block + 1) * rows]
        else:
            exchange(block - blocks).wait_recv()
            source = other_ref[(block - blocks) * rows : (block - blocks + 1) * rows]
            store_other(block - blocks).start()
        at = slice(block * rows, (block + 1) * rows)
        normed, _ = norm_rows(source.astype(jnp.float32))
        first = (normed * scaling + parts[0]).astype(jnp.bfloat16)
        first_t_ref[:, at] = first.T
        for part in range(3):
            projected = dot(first, weight[:, part * model : (part + 1) * model], 1, 0)
            for column in range(model // 128):
                piece = projected[:, column * 128 : (column + 1) * 128]
                if part < 2:
                    piece = piece * cos_ref[at] + swap_halves(piece, lane) * sin_ref[at]
                piece = piece.astype(jnp.bfloat16)
                if part == 0:
                    piece = piece * 0.125
                start = part * model + column * 128
                qkv[at, start : start + 128] = piece
        store(block).start()
    for block in range(2 * blocks):
        store(block).wait()
    for block in range(blocks):
        store_other(block).wait()
        exchange(block).wait_send()


def back_kernel(
    q_ref,
    k_ref,
    v_ref,
    out_ref,
    grad_ref,
    exp_ref,
    inv_ref,
    cos_ref,
    sin_ref,
    first_t_hbm,
    weight_hbm,
    own_hbm,
    other_hbm,
    grad_middle_hbm,
    mod_ref,
    gain_ref,
    down_keep,
    down_tail_hbm,
    upv_keep,
    upx_keep,
    out_keep,
    out_send,
    mid_rows_ref,
    up_bias_ref,
    time_ref,
    mod_weight_hbm,
    other_block_ref,
    _,
    tokens_grad_ref,
    time_grad_ref,
    mod_weight_grad_ref,
    mod_bias_grad_ref,
    gain_grad_ref,
    feed_gain_grad_ref,
    up_bias_grad_ref,
    down_bias_grad_ref,
    down_ref,
    up_ref,
    out_grad_ref,
    in_ref,
    block_ref,
    first_t_ref,
    weight_ref,
    own_ref,
    other_ref,
    grad_middle_ref,
    mod_weight_ref,
    down_tail,
    down_tail_give,
    down_tail_got,
    ds_ref,
    dq_sum,
    proj,
    tokens_stage,
    rows_ref,
    early,
    late,
    running,
    running_got,
    by_vector,
    spread,
    spread_bias,
    turned,
    sems,
    local_sems,
    *buffers,
):
    rows = T_ROWS
    step = pl.program_id(0)
    length = q_ref.shape[0]
    half, model = other_ref.shape
    links = Links()
    core = links.bit["C"]
    pieces = []
    buffers = list(buffers)
    slot = 0
    for spec in BACK_PIECES:
        count = len(piece_scratch(spec))
        source = out_send if spec[0] == "out" else None
        pieces.append(Piece(links, buffers[:count], spec, sems, slot, source, spec[0] == "down"))
        buffers = buffers[count:]
        slot += copies_of(spec)
    down, upv, upx, out, *ins = pieces

    def fetches(first=0, end=11):
        pairs = (
            (upv_keep, upv.keep),
            (down_keep, down.keep.at[pl.ds(0, 3)]),
            (upx_keep, upx.keep),
            (out_keep, out.keep),
            (down_tail_hbm, down_tail),
            (first_t_hbm, first_t_ref),
            (weight_hbm, weight_ref),
            (other_hbm, other_ref),
            (grad_middle_hbm, grad_middle_ref),
            (own_hbm.at[links.me], own_ref),
            (mod_weight_hbm, mod_weight_ref),
        )
        return [pltpu.make_async_copy(a, b, local_sems.at[i]) for i, (a, b) in enumerate(pairs) if first <= i < end]

    place = links.place()
    dp = lax.axis_index("dp")
    early_slot = BACK_COPIES + 6
    quarter = half // 4
    late_slot = early_slot + 6
    running_slot = late_slot + 6
    tail_slot = running_slot + 5

    def running_copy(number):
        partner = links.partner[RUNNING[number]]
        return remote(running.at[number], running_got.at[number], sems, running_slot + number, partner)

    def tail_copy():
        return remote(down_tail_give, down_tail_got, sems, tail_slot, links.partner["X"])

    def block_copy(number):
        at = pl.ds(number * quarter, quarter)
        target = block_ref.at[links.me, at]
        return remote(other_block_ref.at[at], target, sems, BACK_COPIES + number, links.partner["Y"])

    def halves(target, at, first, values):
        middle = model // 2
        target[at, first : first + 1] = values[:, :middle]
        target[at, first + 1 : first + 2] = values[:, middle:]

    @pl.when(step == 0)
    def _():
        links.greet()
        for copy in fetches():
            copy.start()
        out.begin()
        for m in range(4):
            halves(early, place, 2 * m, mid_rows_ref[m : m + 1])
        running[0, 0:2] = mid_rows_ref[4:6]
        for tile in range(up_bias_ref.shape[1] // model):
            running[0, 2 + tile : 3 + tile] = up_bias_ref[:, tile * model : (tile + 1) * model]
        running[0, 6:8] = jnp.zeros((2, model), jnp.float32)
        start_all(spread_copies(links, early, sems, early_slot, 0))
        running_copy(0).start()

    for number in range(4):

        @pl.when(step == number + 1)
        def _(number=number):
            block_copy(number).start()

    def early_arrive(number):
        receive_all(spread_copies(links, early, sems, early_slot, number))

    def early_start(number):
        start_all(spread_copies(links, early, sems, early_slot, number))

    def running_arrive(number):
        running_copy(number).wait_recv()
        running[number + 1] = running[number] + running_got[number]

    def at_step(number):
        return pl.when(step == number)

    def between():
        @at_step(0)
        def _():
            for copy in fetches(0, 5):
                copy.wait()
            down_tail_give[...] = down_tail[1 - links.bit["X"]]
            early_arrive(0)
            running_arrive(0)
            early_start(1)
            running_copy(1).start()
            tail_copy().start()
            upv.step()
            upx.step()

        @at_step(1)
        def _():
            early_arrive(1)
            running_arrive(1)
            early_start(2)
            running_copy(2).start()
            tail_copy().wait_recv()
            kept = down_tail[links.bit["X"]].astype(jnp.float32) + down_tail_got[...].astype(jnp.float32)
            down.keep[3] = kept.astype(jnp.bfloat16)
            down.step()
            out.step()

        @at_step(2)
        def _():
            for copy in fetches(5):
                copy.wait()
            upx.last()
            upv.last()

        @at_step(3)
        def _():
            early_arrive(2)
            running_arrive(2)
            early_start(3)
            running_copy(3).start()
            ins[0].step()

        @at_step(4)
        def _():
            out.step()
            down.last()

        @at_step(5)
        def _():
            running_arrive(3)
            running_copy(4).start()
            ins[1].step()
            ins[0].step()

    lane = lax.broadcasted_iota(jnp.int32, (rows, 128), 1)

    @pl.when(step < 6)
    def _():
        keys = k_ref[...]
        values = v_ref[...]
        scaled = grad_ref[...].astype(jnp.float32) * inv_ref[...]
        products = scaled * out_ref[...].astype(jnp.float32)
        scaled = scaled.astype(jnp.bfloat16)
        scaled_t = scaled.T
        queries_t = q_ref[...].T
        grad_k = []
        grad_v = []
        for head in range(2):
            if head == 1:
                between()
            for chunk in range(length // rows):
                at = slice(chunk * rows, (chunk + 1) * rows)
                mask = (lane < 64) == (head == 0)
                mine = jnp.where(mask, scaled[at], jnp.zeros((rows, 128), jnp.bfloat16))
                row_dots = jnp.sum(jnp.where(mask, products[at], 0.0), -1, keepdims=True)
                grad_p = dot(mine, values, 1, 1)
                grad_s = (exp_ref[head, at].astype(jnp.float32) * (grad_p - row_dots)).astype(jnp.bfloat16)
                ds_ref[at] = grad_s
                grad_q = dot(grad_s, keys, 1, 0) * 0.125
                if head == 0:
                    dq_sum[at] = grad_q
                else:
                    dq_sum[at] = jnp.where(lane < 64, dq_sum[at], grad_q)
            grad_v.append(dot(scaled_t[64 * head : 64 * head + 64], exp_ref[head], 1, 0))
            grad_k.append(dot(queries_t[64 * head : 64 * head + 64], ds_ref[...], 1, 0))
        columns = [pl.ds(pl.multiple_of(part * model + step * 128, 128), 128) for part in range(3)]
        proj[:, columns[2]] = jnp.concatenate(grad_v, 0).astype(jnp.bfloat16).T
        grad_keys = jnp.concatenate(grad_k, 0).astype(jnp.bfloat16).T
        for chunk in range(length // rows):
            at = slice(chunk * rows, (chunk + 1) * rows)
            for part, source in enumerate((dq_sum[at].astype(jnp.bfloat16), grad_keys[at])):
                piece = source.astype(jnp.float32)
                turned = piece * cos_ref[at] - swap_halves(piece, lane) * sin_ref[at]
                proj[at, columns[part]] = turned.astype(jnp.bfloat16)

    starts = [128 * sum(CHUNKS[:i]) for i in range(len(CHUNKS))]

    def weight_part(group):
        piece = ins[group]
        span = 128 * CHUNKS[group]
        for part in range(3):
            column = part * model + starts[group]
            grad = dot(first_t_ref[...], proj[:, column : column + span], 1, 0).astype(jnp.bfloat16)
            grad = grad.reshape(8, 2, -1, span)
            share(core, (grad[:, 0], grad[:, 1]), piece.keep, piece.source, Ellipsis, slice(part * span, (part + 1) * span))
        piece.begin()

    for group, number in enumerate((2, 4, 5)):
        at_step(number)(functools.partial(weight_part, group))

    scaling = gain_ref[...] * (1.0 + mod_ref[1:2])

    def entry(values_ref, base, chunk):
        at = slice(base + chunk * rows, base + (chunk + 1) * rows)
        local = slice(chunk * rows, (chunk + 1) * rows)
        grad = dot(proj[at], weight_ref[...], 1, 1)
        normed, inverse = norm_rows(values_ref[local].astype(jnp.float32))
        weighted = grad * normed
        scaled = grad * scaling
        inner = jnp.mean(weighted * scaling, -1, keepdims=True)
        result = grad_middle_ref[at] + (scaled - jnp.mean(scaled, -1, keepdims=True) - normed * inner) * inverse
        tokens_stage[at] = result.astype(jnp.bfloat16)
        return jnp.concatenate([jnp.sum(grad, 0, keepdims=True), jnp.sum(weighted, 0, keepdims=True)], 0)

    def away(chunk):
        source = tokens_stage.at[pl.ds(half + chunk * rows, rows)]
        target = tokens_grad_ref.at[links.me, pl.ds(chunk * rows, rows)]
        return remote(source, target, sems, BACK_COPIES + 4 + chunk, links.partner["Y"])

    def home():
        return pltpu.make_async_copy(tokens_stage.at[pl.ds(0, half)], tokens_grad_ref.at[links.me], local_sems.at[11])

    unit = mod_weight_grad_ref.shape[0] // 6
    middle = model // 2

    def time_part(m):
        base = place % 16
        rest = jnp.concatenate([by_vector[m, pl.ds(base, 1)], by_vector[m, pl.ds(base + 16, 1)]], 0)
        both = jnp.zeros((2, 128), jnp.float32)
        for _ in range(3):
            high = rest.astype(jnp.bfloat16)
            both = both + dot(high, mod_weight_ref[m * model : (m + 1) * model], 1, 0)
            rest = rest - high.astype(jnp.float32)
        return both

    def early_vectors():
        for m in range(2, 6):
            by_vector[m, :, 0:middle] = early[:, 2 * m - 4, :]
            by_vector[m, :, middle:model] = early[:, 2 * m - 3, :]
        time_grad_ref[...] = sum(time_part(m) for m in range(2, 6))
        turned[...] = running[5].T
        narrow = turned[pl.ds(pl.multiple_of(dp * unit, 8), unit), :].T
        feed_gain_grad_ref[...] = narrow[0:1]
        down_bias_grad_ref[...] = narrow[1:2]
        wide_rows = up_bias_grad_ref.shape[1]
        share_of = model // wide_rows
        wide = turned[pl.ds(pl.multiple_of((dp % share_of) * wide_rows, 8), wide_rows), :].T
        picked = jnp.zeros((1, wide_rows), jnp.float32)
        for tile in range(4):
            picked = jnp.where(dp // share_of == tile, wide[2 + tile : 3 + tile], picked)
        up_bias_grad_ref[...] = picked

    def late_vectors():
        for m in range(2):
            by_vector[m, :, 0:middle] = late[:, 2 * m, :]
            by_vector[m, :, middle:model] = late[:, 2 * m + 1, :]
        ones = jnp.ones((32, 128), jnp.float32)
        factors = jnp.concatenate([late[:, 6, 0:128], ones], 1)
        for part in range(6):
            at = dp * 6 + part
            spread[...] = lax.dot_general(
                by_vector[at // 16],
                factors,
                (((0,), (0,)), ((), ())),
                precision=highest,
                preferred_element_type=jnp.float32,
            )
            kept = spread[pl.ds(pl.multiple_of((at % 16) * unit, 8), unit), :]
            mod_weight_grad_ref[part * unit : (part + 1) * unit] = kept[:, 0:128]
            spread_bias[part * unit : (part + 1) * unit] = kept[:, 128:256]
        mod_bias_grad_ref[...] = spread_bias[...].T[0:1]
        time_grad_ref[...] += time_part(0) + time_part(1)
        gains = [jnp.sum(late[:, row, :], 0, keepdims=True) for row in (4, 5)]
        turned[...] = jnp.broadcast_to(jnp.concatenate(gains, 1), (8, model)).T
        gain_grad_ref[...] = turned[pl.ds(pl.multiple_of(dp * unit, 8), unit), :].T[0:1]

    @at_step(6)
    def _():
        rows_ref[...] = entry(other_ref, half, 0)
        ins[2].step()
        away(0).start()
        rows_ref[...] += entry(other_ref, half, 1)
        out.last()
        away(1).start()
        ins[1].step()

    @at_step(7)
    def _():
        rows_ref[...] += entry(own_ref, 0, 0)
        ins[2].step()
        rows_ref[...] += entry(own_ref, 0, 1)
        home().start()
        scaling_one = 1.0 + mod_ref[1:2]
        halves(late, place, 0, rows_ref[0:1])
        halves(late, place, 2, rows_ref[1:2] * gain_ref[...])
        halves(late, place, 4, rows_ref[1:2] * scaling_one)
        embedding = time_ref[...].astype(jnp.float32)
        late[place, 6:7, 0:128] = jnp.where(links.me == 0, embedding[0:1], embedding[1:2])
        start_all(spread_copies(links, late, sems, late_slot, 0))
        hop = iter(range(4))

        def hop_on():
            number = next(hop)
            receive_all(spread_copies(links, late, sems, late_slot, number))
            if number < 3:
                start_all(spread_copies(links, late, sems, late_slot, number + 1))

        hop_on()
        early_arrive(3)
        running_arrive(4)
        early_vectors()
        ins[0].last()
        hop_on()
        ins[1].last()
        hop_on()
        ins[2].last()
        hop_on()
        late_vectors()
        for group in range(3):
            def store(at, value, group=group):
                span = 128 * CHUNKS[group]
                for part in range(3):
                    column = part * model + starts[group]
                    in_ref[at, column : column + span] = value[:, part * span : (part + 1) * span]

            ins[group].result(store)

        def store_out(at, value):
            out_grad_ref[at] = value

        out.result(store_out)

        def store_down(at, value):
            down_ref[at] = value

        down.result(store_down)

        def store_up(first):
            def store(at, value):
                count = up_ref.shape[0]
                for tile in range(value.shape[0] // count):
                    columns = slice((first + tile) * model, (first + tile + 1) * model)
                    up_ref[:, columns] = value[tile * count : (tile + 1) * count]

            return store

        upv.result(store_up(0))
        upx.result(store_up(3))
        home().wait()
        for chunk in range(half // rows):
            away(chunk).wait()
        for number in range(4):
            block_copy(number).wait()
        for number in range(4):
            for copy in spread_copies(links, early, sems, early_slot, number) + spread_copies(links, late, sems, late_slot, number):
                copy.wait_send()
        for number in range(5):
            running_copy(number).wait_send()
        tail_copy().wait_send()
        for piece in pieces:
            for copy in piece.copies:
                remote(*copy).wait_send()


def close_kernel(*refs):
    count = len(refs) // 2
    for source, target in zip(refs[:count], refs[count:]):
        target[...] = source[...].reshape(target.shape)


def turn_tables(length):
    inverse = 10000.0 ** (-np.arange(HD // 2, dtype=np.float64) * 2.0 / HD)
    angles = np.arange(length, dtype=np.float64)[:, None] * inverse[None, :]
    cosine = np.tile(np.cos(angles), (1, 4))
    sines = np.sin(angles)
    sines = np.concatenate([-sines, sines, -sines, sines], 1)
    both = [np.stack([t, np.roll(t, -(length // 2), 0)]).astype(np.float32) for t in (cosine, sines)]
    return jnp.asarray(both[0]), jnp.asarray(both[1])


def fast_body(
    tokens,
    time_embedding,
    prefix_length,
    suffix_mask,
    cotangent,
    modulation_weight,
    modulation_bias,
    attention_gain,
    attention_in,
    attention_out,
    feed_gain,
    feed_up,
    feed_up_bias,
    feed_down,
    feed_down_bias,
):
    bf16 = jnp.bfloat16
    f32 = jnp.float32
    _, half, model = tokens.shape
    length = 2 * half
    hidden_width = feed_up.shape[1]
    size = lax.axis_size("dp")
    shape = jax.ShapeDtypeStruct

    packed = [modulation_bias, attention_gain, feed_gain, feed_down_bias, feed_up_bias]
    total = sum(v.shape[0] for v in packed)
    starts = np.cumsum([0] + [v.shape[0] for v in packed])
    packed = sum(
        lax.pad(v.astype(f32), np.float32(0), [(int(a), int(total - a - v.shape[0]), 0)]) for v, a in zip(packed, starts)
    )[None]

    def packed_at(number):
        return pl.BlockSpec((1, model), lambda h: (0, number), pipeline_mode=pl.Buffered(1))

    cosine, sines = turn_tables(length)
    anywhere = pl.BlockSpec(memory_space=pl.ANY)

    def fixed(*dims):
        return pl.BlockSpec(dims, lambda h: (0,) * len(dims), pipeline_mode=pl.Buffered(1))

    first_t, qkv, other, modulation = pl.pallas_call(
        front_kernel,
        grid=(1,),
        in_specs=[
            anywhere,
            fixed(2, 128),
            anywhere,
            fixed(1, 6 * model),
            packed_at(6),
            anywhere,
            anywhere,
            anywhere,
        ],
        out_specs=[fixed(model, length), anywhere, anywhere, fixed(6, model)],
        out_shape=[
            shape((model, length), bf16),
            shape((length, 3 * model), bf16),
            shape((half, model), bf16),
            shape((6, model), f32),
        ],
        scratch_shapes=[
            pltpu.VMEM((half, model), bf16),
            pltpu.VMEM((half, model), bf16),
            pltpu.VMEM((6 * model, 128), bf16),
            pltpu.VMEM((model, 3 * model), bf16),
            pltpu.VMEM((length, 128), f32),
            pltpu.VMEM((length, 128), f32),
            pltpu.VMEM((length, 3 * model), bf16),
            pltpu.SemaphoreType.DMA((2, half // FRONT_ROWS)),
            pltpu.SemaphoreType.DMA((5,)),
            pltpu.SemaphoreType.DMA((3 * half // FRONT_ROWS,)),
        ],
        compiler_params=pltpu.CompilerParams(vmem_limit_bytes=62 * MIB, collective_id=2, has_side_effects=True),
        cost_estimate=pl.CostEstimate(flops=2 * length * model * 3 * model, bytes_accessed=16 * MIB, transcendentals=0),
        name="front",
    )(tokens, time_embedding, modulation_weight, packed, packed, attention_in, cosine, sines)

    def column(k):
        return pl.BlockSpec((length, 128), lambda h: (0, h + k))

    pairs = model // 128
    attended, exps, inverses, own_live, other_live, other_cot = pl.pallas_call(
        attend_kernel,
        grid=(pairs,),
        in_specs=[
            pl.BlockSpec(memory_space=pltpu.SMEM),
            column(0),
            column(pairs),
            column(2 * pairs),
            fixed(2, half),
            anywhere,
        ],
        out_specs=[
            column(0),
            pl.BlockSpec((2, length, length), lambda h: (h, 0, 0)),
            column(0),
            fixed(8, half),
            fixed(8, half),
            anywhere,
        ],
        out_shape=[
            shape((length, model), bf16),
            shape((HEADS, length, length), bf16),
            shape((length, model), f32),
            shape((8, half), f32),
            shape((8, half), f32),
            shape((half, model), bf16),
        ],
        scratch_shapes=[pltpu.VMEM((8, half), f32), pltpu.VMEM((8, half), f32), pltpu.SemaphoreType.DMA((2, 2))],
        compiler_params=pltpu.CompilerParams(vmem_limit_bytes=60 * MIB, collective_id=3, has_side_effects=True),
        cost_estimate=pl.CostEstimate(flops=16 * length * length * model, bytes_accessed=32 * MIB, transcendentals=0),
        name="attend",
    )(prefix_length, qkv, qkv, qkv, suffix_mask, cotangent)

    tiles = 4
    width = hidden_width // tiles
    groups = size // 2
    share_rows = hidden_width // size
    model_rows = model // size
    own_part = pl.BlockSpec((None, half, model), lambda h: (lax.axis_index("seq"), 0, 0), pipeline_mode=pl.Buffered(1))
    up_tile = pl.BlockSpec((model, width), lambda j: (0, j))
    bias_tile = pl.BlockSpec((1, width), lambda j: (0, j))
    down_tile = pl.BlockSpec((width, model), lambda j: (j, 0))
    (
        own_out,
        other_out,
        grad_middle,
        grad_attended,
        mid_rows,
        up_bias_grad,
        down_sum,
        down_tail,
        upv_sum,
        upx_sum,
        out_keep,
        out_send,
    ) = pl.pallas_call(
        middle_kernel,
        grid=(tiles,),
        in_specs=[own_part, fixed(half, model), own_part, fixed(half, model), fixed(8, half), fixed(8, half)]
        + [
            fixed(length, model),
            fixed(6, model),
            packed_at(7),
            fixed(model, model),
            up_tile,
            pl.BlockSpec((1, width), lambda j: (0, j + 9)),
            down_tile,
            packed_at(8),
        ],
        out_specs=[
            own_part,
            fixed(half, model),
            fixed(length, model),
            fixed(length, model),
            fixed(6, model),
            bias_tile,
            fixed(tiles - 1, share_rows // 2, model),
            fixed(2, share_rows // 2, model),
            fixed(2, tiles - 1, model_rows, model),
            fixed(4, model_rows, model),
            fixed(groups, model_rows, model),
            fixed(groups, model_rows, model),
        ],
        out_shape=[shape((2, half, model), bf16), shape((half, model), bf16)]
        + [shape((length, model), f32), shape((length, model), bf16), shape((6, model), f32), shape((1, hidden_width), f32)]
        + [shape((tiles - 1, share_rows // 2, model), bf16), shape((2, share_rows // 2, model), bf16), shape((2, tiles - 1, model_rows, model), bf16)]
        + [shape((4, model_rows, model), bf16)]
        + [shape((groups, model_rows, model), bf16)] * 2,
        scratch_shapes=[
            pltpu.VMEM((model, length), bf16),
            pltpu.VMEM((length, model), bf16),
            pltpu.VMEM((length, model), f32),
            pltpu.VMEM((length, model), f32),
            pltpu.VMEM((width, length), bf16),
        ]
        + [pltpu.VMEM((tiles, groups // tiles, share_rows, model), bf16)] * 3
        + [pltpu.VMEM((tiles, groups, model_rows, model), bf16)] * 3
        + [pltpu.VMEM((tiles, groups // tiles, share_rows // 2, model), bf16)] * 2
        + [pltpu.VMEM((tiles - 1, share_rows // 2, model), bf16)] * 2
        + [pltpu.VMEM((tiles - 1, 3, 2, model_rows, model), bf16)] * 2
        + [pltpu.VMEM((4, model_rows, model), bf16)] * 2
        + [pltpu.SemaphoreType.DMA((2, 7 * tiles))],
        compiler_params=pltpu.CompilerParams(vmem_limit_bytes=63 * MIB, collective_id=1, has_side_effects=True),
        cost_estimate=pl.CostEstimate(
            flops=12 * length * model * hidden_width + 6 * length * model * model, bytes_accessed=36 * MIB, transcendentals=0
        ),
        name="middle",
    )(
        tokens,
        other,
        cotangent,
        other_cot,
        own_live,
        other_live,
        attended,
        modulation,
        packed,
        attention_out,
        feed_up,
        packed,
        feed_down,
        packed,
    )
    merge = (2, (tiles - 1) * model_rows, model)

    def near(k):
        return pl.BlockSpec((length, 128), lambda h: (0, jnp.minimum(h, pairs - 1) + k))

    turn = pl.BlockSpec((None, length, 128), lambda h: (lax.axis_index("seq"), 0, 0), pipeline_mode=pl.Buffered(1))
    scratch = [
        pltpu.VMEM((model, length), bf16),
        pltpu.VMEM((model, 3 * model), bf16),
        pltpu.VMEM((half, model), bf16),
        pltpu.VMEM((half, model), bf16),
        pltpu.VMEM((length, model), f32),
        pltpu.VMEM((6 * model, 128), bf16),
        pltpu.VMEM((2, share_rows // 2, model), bf16),
        pltpu.VMEM((share_rows // 2, model), bf16),
        pltpu.VMEM((share_rows // 2, model), bf16),
        pltpu.VMEM((length, length), bf16),
        pltpu.VMEM((length, 128), f32),
        pltpu.VMEM((length, 3 * model), bf16),
        pltpu.VMEM((length, model), bf16),
        pltpu.VMEM((2, model), f32),
        pltpu.VMEM((2 * size, 8, model // 2), f32),
        pltpu.VMEM((2 * size, 8, model // 2), f32),
        pltpu.VMEM((6, 8, model), f32),
        pltpu.VMEM((5, 8, model), f32),
        pltpu.VMEM((6, 2 * size, model), f32),
        pltpu.VMEM((model, 256), f32),
        pltpu.VMEM((6 * model_rows, 128), f32),
        pltpu.VMEM((model, 8), f32),
        pltpu.SemaphoreType.DMA((2, BACK_COPIES + 24)),
        pltpu.SemaphoreType.DMA((12,)),
    ]
    for spec in BACK_PIECES:
        scratch += piece_scratch(spec)
    def cut(dims):
        if len(dims) == 3:
            return pl.BlockSpec((1, dims[1] // 2, dims[2]), lambda i: (i // 2, i % 2, 0))
        if dims[0] % 16:
            return pl.BlockSpec(dims, lambda i: (0, 0))
        return pl.BlockSpec((dims[0] // 2, dims[1]), lambda i: (i // 2, 0))

    results = pl.pallas_call(
        back_kernel,
        grid=(pairs + 2,),
        in_specs=[
            near(0),
            near(pairs),
            near(2 * pairs),
            near(0),
            near(0),
            pl.BlockSpec((2, length, length), lambda h: (jnp.minimum(h, pairs - 1), 0, 0)),
            near(0),
            turn,
            turn,
            *[anywhere] * 5,
            fixed(6, model),
            packed_at(6),
        ]
        + [anywhere] * 6
        + [fixed(6, model), fixed(1, hidden_width), fixed(2, 128), anywhere, anywhere, anywhere],
        out_specs=[
            anywhere,
            fixed(2, 128),
            fixed(6 * model_rows, 128),
            fixed(1, 6 * model_rows),
            fixed(1, model_rows),
            fixed(1, model_rows),
            fixed(1, hidden_width // size),
            fixed(1, model_rows),
            fixed(hidden_width // size, model),
            fixed(model_rows, hidden_width),
            fixed(model_rows, model),
            fixed(model_rows, 3 * model),
            anywhere,
        ],
        out_shape=[
            shape((2, half, model), bf16),
            shape((2, 128), f32),
            shape((6 * model_rows, 128), f32),
            shape((1, 6 * model_rows), f32),
            shape((1, model_rows), f32),
            shape((1, model_rows), f32),
            shape((1, hidden_width // size), f32),
            shape((1, model_rows), f32),
            shape((hidden_width // size, model), f32),
            shape((model_rows, hidden_width), f32),
            shape((model_rows, model), f32),
            shape((model_rows, 3 * model), f32),
            shape((2, half, model), bf16),
        ],
        input_output_aliases={27: 12},
        scratch_shapes=scratch,
        compiler_params=pltpu.CompilerParams(vmem_limit_bytes=63 * MIB, collective_id=0, has_side_effects=True),
        cost_estimate=pl.CostEstimate(flops=40 * length * length * model, bytes_accessed=60 * MIB, transcendentals=0),
        name="back",
    )(
        qkv,
        qkv,
        qkv,
        attended,
        grad_attended,
        exps,
        inverses,
        cosine,
        sines,
        first_t,
        attention_in,
        tokens,
        other,
        grad_middle,
        modulation,
        packed,
        down_sum,
        down_tail,
        upv_sum.reshape(merge),
        upx_sum,
        out_keep,
        out_send,
        mid_rows,
        up_bias_grad,
        time_embedding,
        modulation_weight,
        other_out,
        own_out,
    )
    (
        tokens_grad,
        time_grad,
        modulation_weight_grad,
        modulation_bias_grad,
        gain_grad,
        feed_gain_grad,
        feed_up_bias_grad,
        feed_down_bias_grad,
        down_grad,
        up_grad,
        out_grad,
        in_grad,
        block_output,
    ) = pl.pallas_call(
        close_kernel,
        grid=(4,),
        in_specs=[cut(r.shape) for r in results],
        out_specs=[pl.BlockSpec(r.shape[1:], lambda i: (0,)) if r.shape[0] == 1 else cut(r.shape) for r in results],
        out_shape=[shape(r.shape[1:] if r.shape[0] == 1 else r.shape, r.dtype) for r in results],
        compiler_params=params(62),
        name="close",
    )(*results)
    return (
        block_output,
        tokens_grad,
        time_grad,
        modulation_weight_grad,
        modulation_bias_grad,
        gain_grad,
        in_grad,
        out_grad,
        feed_gain_grad,
        up_grad,
        feed_up_bias_grad,
        down_grad,
        feed_down_bias_grad,
    )


def body(tokens, *rest):
    sequences, half, model = tokens.shape
    size = lax.axis_size("dp")
    fits = model % (16 * size) == 0 and half % T_ROWS == 0
    fits = fits and tokens.shape[1] % MIDDLE_ROWS == 0 and rest[10].shape[1] == 4 * model and size == 16 and lax.axis_size("seq") == 2 and sequences == 2
    return (fast_body if fits else general_body)(tokens, *rest)


def solution(mesh):
    return jax.shard_map(
        body,
        mesh=mesh,
        in_specs=(
            P("dp", "seq", None),
            P("dp", None),
            P("dp"),
            P("dp", "seq"),
            P("dp", "seq", None),
            P(),
            P(),
            P(),
            P(),
            P(),
            P(),
            P(),
            P(),
            P(),
            P(),
        ),
        out_specs=(
            P("dp", "seq", None),
            P("dp", "seq", None),
            P("dp", None),
            P("dp", None),
            P("dp"),
            P("dp"),
            P("dp", None),
            P("dp", None),
            P("dp"),
            P("dp", None),
            P("dp"),
            P("dp", None),
            P("dp"),
        ),
        check_vma=False,
    )
```
